32 devices in a mesh: dp: 8 (over z, x), tensor: 4 (over y, core).
Axes of the slice: x: 2, y: 2, z: 4, core: 2. Of those that a mesh axis runs over, the one named last changes fastest.
Arguments:
- enc_x: bfloat16 [4096, 1472], P(('dp', 'tensor')), may hold values from -6 to 6
- dec_x: bfloat16 [768, 1472], P(('dp', 'tensor')), may hold values from -6 to 6
- dec_cot: bfloat16 [768, 1472], P(('dp', 'tensor')), may hold values from -6 to 6
- item_count: int32 [8], P('dp'), may hold values from 1 to 4, as said below
- enc_mask: int32 [4096], P('dp'), may hold values from 0 to 1, as said below
- dec_mask: int32 [768], P('dp'), may hold values from 0 to 1, as said below
- enc_buckets: int32 [1023], replicated, may hold values from 0 to 31
- dec_buckets: int32 [96], replicated, may hold values from 0 to 31
- gains: float32 [6, 1472], replicated, may hold values from 0.25 to 1.75
- tables: float32 [2, 32, 6], replicated, may hold values from -4 to 4
- attn_qk: bfloat16 [3, 1472, 768], replicated, may hold values from -0.0625 to 0.0625
- attn_vo: bfloat16 [3, 1472, 768], replicated, may hold values from -0.5 to 0.5
- ff_in: bfloat16 [2, 2, 1472, 3584], P(None, None, None, 'tensor'), may hold values from -0.15625 to 0.15625
- ff_out: bfloat16 [2, 3584, 1472], P(None, 'tensor'), may hold values from -0.09375 to 0.09375
Outputs:
- dec_out: bfloat16 [768, 1472], P(('dp', 'tensor'))
- enc_grad: float32 [4096, 1472], P(('dp', 'tensor'))
- dec_grad: float32 [768, 1472], P(('dp', 'tensor'))
- gains_grad: float32 [6, 1472], replicated
- tables_grad: float32 [2, 32, 6], replicated
- qk_grad: float32 [3, 1472, 768], P(None, 'dp')
- vo_grad: float32 [3, 1472, 768], P(None, 'dp')
- ffin_grad: float32 [2, 2, 1472, 3584], P(None, None, 'dp', 'tensor')
- ffout_grad: float32 [2, 3584, 1472], P(None, 'tensor', 'dp')
The draws below stay inside these ranges and needn't reach their ends.
Inputs may be any that keep to these rules, and one draw needn't show every extreme that they name: `item_count`: each entry is 1, 2 or 4, the number of equal items that a group's encoder rows and its target rows are cut into; every draw has a group with 1 item and one with 4. `enc_mask`: in each item the ones are a prefix holding at least half of the item (rounded down), never none. `dec_mask`: in each item the ones are a prefix holding at least half of the item (rounded down), never none. `enc_buckets`: entry k is the bucket of key place minus query place equal to k - 511. `dec_buckets`: entry k is the bucket of a key k places before its query.
All inputs are finite; a program needn't handle non-finite values.
Results may differ from the reference program's by a relative error of at most 0.03.
Values may be sent and summed in bfloat16 or wider, within the bound.
A program may use at most 256 MiB of HBM per device.

```python
import jax
import jax.numpy as jnp
from jax import lax

D = 1472
HEADS = 6
HEAD = 64
FF = 3584
BUCKETS = 32
ENC_TOK = 512
INNER = 384
DEC_TOK = 96
ENC_ALL = 4096
DEC_ALL = 768
N_DP = 8


def count_exponents(key):
    base = jax.random.fold_in(key, 101)
    exponent = jax.random.randint(jax.random.fold_in(base, 1), (N_DP,), 0, 3)
    first = jax.random.randint(jax.random.fold_in(base, 2), (), 0, N_DP)
    second = (first + 1 + jax.random.randint(jax.random.fold_in(base, 3), (), 0, N_DP - 1)) % N_DP
    places = jnp.arange(N_DP)
    exponent = jnp.where(places == first, 0, exponent)
    return jnp.where(places == second, 2, exponent)


def item_counts(key):
    exponent = count_exponents(key)
    return jnp.where(exponent == 0, 1, jnp.where(exponent == 1, 2, 4)).astype(jnp.int32)


def padding(key, counts, length):
    item_len = (length // counts)[:, None]
    kept = jax.random.randint(key, (N_DP, 4), item_len // 2, item_len + 1)
    kept = jnp.maximum(kept, 1)
    places = jnp.arange(length)[None, :]
    item = places // item_len
    inside = places % item_len
    limit = jnp.take_along_axis(kept, item, axis=1)
    return (inside < limit).astype(jnp.int32).reshape(-1)


def draw_item_count(key, part):
    counts = item_counts(key)
    return counts


def draw_enc_mask(key, part):
    counts = item_counts(key)
    key = jax.random.fold_in(key, 7)
    return padding(key, counts, ENC_TOK)


def draw_dec_mask(key, part):
    counts = item_counts(key)
    key = jax.random.fold_in(key, 9)
    return padding(key, counts, DEC_TOK)


def touch_ends(entries, rng, low, high):
    longest = entries.shape.index(max(entries.shape))
    spots = []
    for shift in (0, 1):
        where = [jax.random.randint(jax.random.fold_in(rng, axis), (), 0, length) for axis, length in enumerate(entries.shape)]
        where[longest] = (where[longest] + shift) % entries.shape[longest]
        spots.append(tuple(where))
    return entries.at[spots[0]].set(low).at[spots[1]].set(high)


def block_scale(rng, dims, shards, low, top_value):
    level, own = 1.0, jax.random.fold_in(rng, 6)
    for dim, parts in shards:
        steps = jnp.exp(jax.random.uniform(jax.random.fold_in(own, dim), (parts,), jnp.float32, low / len(shards), top_value / len(shards)))
        level = level * jnp.repeat(steps, dims[dim] // parts).reshape([-1 if axis == dim else 1 for axis in range(len(dims))])
    return level


def centred(key, dims, width, reach, split=(), held_as=jnp.bfloat16):
    values = width * jax.random.normal(key, dims, jnp.float32)
    if split:
        values = values * block_scale(key, dims, split, -0.22, 0.18)
    return jnp.clip(values, -reach, reach).astype(held_as)


def setup_inputs(seed: int = 0) -> dict:
    seeds = jax.random.split(jax.random.key(seed), 15)
    return {
        "enc_x": centred(seeds[0], (ENC_ALL, D), 1.0, 6.0, ((0, 32),)),
        "dec_x": centred(seeds[1], (DEC_ALL, D), 1.0, 6.0, ((0, 32),)),
        "dec_cot": centred(seeds[2], (DEC_ALL, D), 1.0, 6.0, ((0, 32),)),
        "item_count": draw_item_count(jax.random.fold_in(seeds[14], 71), 0),
        "enc_mask": draw_enc_mask(jax.random.fold_in(seeds[14], 71), 0),
        "dec_mask": draw_dec_mask(jax.random.fold_in(seeds[14], 71), 0),
        "enc_buckets": touch_ends(jax.random.randint(seeds[6], (2 * ENC_TOK - 1,), 0, BUCKETS), jax.random.fold_in(seeds[6], 1), 0, BUCKETS - 1).astype(jnp.int32),
        "dec_buckets": touch_ends(jax.random.randint(seeds[7], (DEC_TOK,), 0, BUCKETS), jax.random.fold_in(seeds[7], 1), 0, BUCKETS - 1).astype(jnp.int32),
        "gains": jnp.clip(1.0 + 0.15 * jax.random.normal(seeds[8], (6, D), jnp.float32), 0.25, 1.75),
        "tables": centred(seeds[9], (2, BUCKETS, HEADS), 1.0, 4.0, (), jnp.float32),
        "attn_qk": centred(seeds[10], (3, D, 2 * INNER), (5 * D) ** -0.5, 0.0625),
        "attn_vo": centred(seeds[11], (3, D, 2 * INNER), (2 * HEAD) ** -0.5, 0.5),
        "ff_in": centred(seeds[12], (2, 2, D, FF), D ** -0.5, 0.15625, ((3, 4),)),
        "ff_out": centred(seeds[13], (2, FF, D), FF ** -0.5, 0.09375, ((1, 4),)),
    }


HIGH = lax.Precision.HIGHEST
EPSILON = 1e-06
MASKED = -1000000000.0

@jax.custom_vjp
def low(v):
    return lax.optimization_barrier(v.astype(jnp.bfloat16)).astype(jnp.float32)

@jax.custom_vjp
def low_back(v):
    return v

def low_keep(v):
    return (low(v), None)

def low_pass(kept, grad):
    return (grad,)

def back_keep(v):
    return (v, None)

def back_low(kept, grad):
    return (low(grad),)
low.defvjp(low_keep, low_pass)
low_back.defvjp(back_keep, back_low)

def product(left, right):
    return jnp.dot(left, right, precision=HIGH)

def norm_gain(rows, gain):
    return rows * lax.rsqrt(lax.optimization_barrier(jnp.mean(rows * rows, axis=-1, keepdims=True)) + EPSILON) * gain

def split_heads(matrix):
    return matrix.reshape(matrix.shape[0], HEADS, HEAD)

def attention(query_rows, key_rows, weight_qk, weight_vo, bias, allowed):
    inner = HEADS * HEAD
    queries = split_heads(low(low_back(product(query_rows, weight_qk[:, :inner]))))
    keys = split_heads(low(low_back(product(key_rows, weight_qk[:, inner:]))))
    values = split_heads(low(low_back(product(key_rows, weight_vo[:, :inner]))))
    raw = jnp.einsum('rhd,shd->hrs', queries, keys, precision=HIGH) + bias
    scores = low_back(jnp.where(allowed[None], raw, MASKED))
    weights = low(jax.nn.softmax(scores, axis=-1))
    mixed = jnp.einsum('hrs,shd->rhd', weights, values, precision=HIGH).reshape(query_rows.shape[0], inner)
    return low_back(product(low(low_back(mixed)), weight_vo[:, inner:].T))

def feed_forward(rows, weight_in, weight_out):
    gate = low_back(product(rows, weight_in[0]))
    up_proj = low_back(product(rows, weight_in[1]))
    hidden = low(jax.nn.gelu(gate, approximate=True) * up_proj)
    return low_back(product(hidden, weight_out))

def group_forward(params, enc_rows, dec_rows, count, enc_valid, dec_valid, enc_buckets, dec_buckets):
    gains, tables, attn_qk, attn_vo, ff_in, ff_out = params
    enc_place = jnp.arange(ENC_TOK, dtype=jnp.int32)
    dec_place = jnp.arange(DEC_TOK, dtype=jnp.int32)
    enc_item = enc_place // (ENC_TOK // count)
    dec_item = dec_place // (DEC_TOK // count)
    enc_live = enc_valid == 1
    dec_live = dec_valid == 1
    enc_allowed = (enc_item[:, None] == enc_item[None, :]) & enc_live[None, :]
    self_allowed = (dec_item[:, None] == dec_item[None, :]) & dec_live[None, :] & (dec_place[None, :] <= dec_place[:, None])
    cross_allowed = (dec_item[:, None] == enc_item[None, :]) & enc_live[None, :]
    enc_index = enc_buckets[enc_place[None, :] - enc_place[:, None] + (ENC_TOK - 1)]
    dec_index = dec_buckets[jnp.maximum(dec_place[:, None] - dec_place[None, :], 0)]
    enc_bias = jnp.transpose(tables[0][enc_index], (2, 0, 1))
    self_bias = jnp.transpose(tables[1][dec_index], (2, 0, 1))
    normed = low(norm_gain(enc_rows, gains[0]))
    enc_mid = enc_rows + attention(normed, normed, attn_qk[0], attn_vo[0], enc_bias, enc_allowed)
    enc_end = enc_mid + feed_forward(low(norm_gain(enc_mid, gains[1])), ff_in[0], ff_out[0])
    memory = low(norm_gain(enc_end, gains[2]))
    normed = low(norm_gain(dec_rows, gains[3]))
    dec_one = dec_rows + attention(normed, normed, attn_qk[1], attn_vo[1], self_bias, self_allowed)
    normed = low(norm_gain(dec_one, gains[4]))
    dec_two = dec_one + attention(normed, memory, attn_qk[2], attn_vo[2], 0.0, cross_allowed)
    return dec_two + feed_forward(low(norm_gain(dec_two, gains[5])), ff_in[1], ff_out[1])

def add_pair(first, second):
    return first + second

def reference(enc_x, dec_x, dec_cot, item_count, enc_mask, dec_mask, enc_buckets, dec_buckets, gains, tables, attn_qk, attn_vo, ff_in, ff_out):
    params = (gains.astype(jnp.float32), tables.astype(jnp.float32), attn_qk.astype(jnp.float32), attn_vo.astype(jnp.float32), ff_in.astype(jnp.float32), ff_out.astype(jnp.float32))
    groups = (enc_x.astype(jnp.float32).reshape(N_DP, ENC_TOK, D), dec_x.astype(jnp.float32).reshape(N_DP, DEC_TOK, D), dec_cot.astype(jnp.float32).reshape(N_DP, DEC_TOK, D), item_count, enc_mask.reshape(N_DP, ENC_TOK), dec_mask.reshape(N_DP, DEC_TOK))

    def one_group(totals, group):
        enc_rows, dec_rows, cotangent, count, enc_valid, dec_valid = group

        def forward(weights, enc_in, dec_in):
            return group_forward(weights, enc_in, dec_in, count, enc_valid, dec_valid, enc_buckets, dec_buckets)
        output, pullback = jax.vjp(forward, params, enc_rows, dec_rows)
        grad_params, grad_enc, grad_dec = pullback(cotangent)
        totals = jax.tree.map(add_pair, totals, grad_params)
        return (totals, (output.astype(jnp.bfloat16), grad_enc, grad_dec))
    zeros = jax.tree.map(jnp.zeros_like, params)
    totals, stacked = lax.scan(one_group, zeros, groups)
    outputs, grad_enc, grad_dec = stacked
    return (outputs.reshape(N_DP * DEC_TOK, D), grad_enc.reshape(N_DP * ENC_TOK, D), grad_dec.reshape(N_DP * DEC_TOK, D), totals[0], totals[1], totals[2], totals[3], totals[4], totals[5])
```

```python
import jax
import jax.numpy as jnp
from jax import lax
from jax.sharding import PartitionSpec as P

HEADS = 6
HEAD = 64
INNER = HEADS * HEAD
BUCKETS = 32
EPSILON = 1e-06
MASKED = -1000000000.0
HIGH = lax.Precision.HIGHEST


def norm_gain(rows, gain):
    return rows * lax.rsqrt(jnp.mean(rows * rows, axis=-1, keepdims=True) + EPSILON) * gain


def norm_back(rows, gain, grad_rows):
    unused, pullback = jax.vjp(norm_gain, rows, gain)
    return pullback(grad_rows)


def ff_act(gate, up_proj):
    return jax.nn.gelu(gate, approximate=True) * up_proj


def to_low(value):
    return value.astype(jnp.bfloat16)


def product(left, right):
    return jnp.dot(left, right, preferred_element_type=jnp.float32)


def product_over_rows(left, right):
    return lax.dot_general(
        left, right, (((0,), (0,)), ((), ())), preferred_element_type=jnp.float32
    )


def product_over_cols(left, right):
    return lax.dot_general(
        left, right, (((1,), (1,)), ((), ())), preferred_element_type=jnp.float32
    )


def gather_t(rows):
    return lax.all_gather(rows, "tensor", axis=0, tiled=True)


def scatter_t(rows):
    return lax.psum_scatter(to_low(rows), "tensor", scatter_dimension=0, tiled=True).astype(
        jnp.float32
    )


def offset_bias(buckets, table):
    onehot = (buckets[:, None] == jnp.arange(BUCKETS)[None, :]).astype(jnp.float32)
    return (jnp.dot(onehot, table, precision=HIGH).T, onehot)


def toeplitz(offset_terms, start, block, columns):
    period = 2 * columns
    wrapped = jnp.concatenate(
        [
            offset_terms[:, columns - 1 :],
            jnp.zeros((HEADS, 1), jnp.float32),
            offset_terms[:, : columns - 1],
        ],
        axis=1,
    )
    doubled = jnp.concatenate([wrapped, wrapped], axis=1)
    shift = (period - start % period) % period
    rolled = lax.dynamic_slice_in_dim(doubled, shift, period, 1)
    tiled = jnp.tile(rolled, (1, block))[:, : block * (period - 1)]
    return tiled.reshape(HEADS, block, period - 1)[:, :, :columns]


def dec_spread(offset_terms, start, block, columns):
    whole = jnp.concatenate(
        [offset_terms[:, ::-1], jnp.broadcast_to(offset_terms[:, :1], (HEADS, columns - 1))], axis=1
    )
    return toeplitz(whole, start, block, columns)


def heads_of(matrix):
    return matrix.reshape(matrix.shape[0], HEADS, HEAD)


def attend(queries, key_values, bias, allowed):
    key_heads = heads_of(key_values[:, :INNER])
    value_heads = heads_of(key_values[:, INNER:])
    raw = jnp.einsum(
        "rhd,shd->hrs", heads_of(queries), key_heads, preferred_element_type=jnp.float32
    )
    if bias is not None:
        raw = raw + bias
    scores = jnp.where(allowed[None], raw, MASKED)
    weights = jax.nn.softmax(scores, axis=-1)
    mixed = jnp.einsum(
        "hrs,shd->rhd", to_low(weights), value_heads, preferred_element_type=jnp.float32
    )
    return to_low(mixed.reshape(queries.shape[0], INNER)), weights


def attend_back(queries, key_values, weights, grad_out):
    key_heads = heads_of(key_values[:, :INNER])
    value_heads = heads_of(key_values[:, INNER:])
    grad_heads = heads_of(grad_out)
    grad_weights = jnp.einsum(
        "rhd,shd->hrs", grad_heads, value_heads, preferred_element_type=jnp.float32
    )
    weighted = jnp.sum(weights * grad_weights, axis=-1, keepdims=True)
    grad_scores = to_low(weights * (grad_weights - weighted))
    grad_query = jnp.einsum(
        "hrs,shd->rhd", grad_scores, key_heads, preferred_element_type=jnp.float32
    )
    grad_keys = jnp.einsum(
        "hrs,rhd->shd", grad_scores, heads_of(queries), preferred_element_type=jnp.float32
    )
    grad_values = jnp.einsum(
        "hrs,rhd->shd", to_low(weights), grad_heads, preferred_element_type=jnp.float32
    )
    total = key_values.shape[0]
    grad_kv = jnp.concatenate(
        [grad_keys.reshape(total, INNER), grad_values.reshape(total, INNER)], axis=1
    )
    return to_low(grad_query.reshape(queries.shape[0], INNER)), grad_kv, grad_scores


def pair_of(rows, place, size):
    split = rows.reshape(rows.shape[0], size // 2, 2, rows.shape[1] // size)
    return lax.dynamic_index_in_dim(split, place, 2, keepdims=False).reshape(
        rows.shape[0], rows.shape[1] // 2
    )


def dp_sum(left, right):
    size = lax.axis_size("dp")
    place = lax.axis_index("dp")
    block = left.shape[1] // size
    low_bit = place % 2
    send = to_low(product_over_rows(pair_of(left, 1 - low_bit, size), right))
    keep = product_over_rows(pair_of(left, low_bit, size), right)
    other = lax.ppermute(send, "dp", [(i, i ^ 1) for i in range(size)])
    current = (keep + other).reshape(size // 2, block, right.shape[1])
    bit = 2
    while bit < size:
        current = current.reshape(current.shape[0] // 2, 2, block, right.shape[1])
        here = (place // bit) % 2
        mine = lax.dynamic_index_in_dim(current, here, 1, keepdims=False)
        send = to_low(lax.dynamic_index_in_dim(current, 1 - here, 1, keepdims=False))
        other = lax.ppermute(send, "dp", [(i, i ^ bit) for i in range(size)])
        current = mine + other
        bit *= 2
    return current.reshape(block, right.shape[1])


def ff_forward(rows_full, weight_in, weight_out):
    gate = product(rows_full, weight_in[0])
    up_proj = product(rows_full, weight_in[1])
    hidden = to_low(ff_act(gate, up_proj))
    return (product(hidden, weight_out), (gate, up_proj, hidden))


def ff_back(grad_full, saved, weight_in, weight_out):
    gate, up_proj, hidden = saved
    grad_hidden = product_over_cols(grad_full, weight_out)
    unused, pullback = jax.vjp(ff_act, gate, up_proj)
    grad_gate, grad_up = pullback(grad_hidden)
    grad_gate = to_low(grad_gate)
    grad_up = to_low(grad_up)
    grad_rows = product_over_cols(grad_gate, weight_in[0]) + product_over_cols(
        grad_up, weight_in[1]
    )
    return (grad_rows, grad_gate, grad_up)


def to_owner(pieces):
    stacked = jnp.stack(pieces)
    out = lax.all_to_all(stacked, "tensor", 0, 0, tiled=True)
    return out.reshape(out.shape[0] * out.shape[1], out.shape[2])


def on_device(
    enc_x, dec_x, dec_cot, item_count, enc_mask, dec_mask, enc_buckets, dec_buckets,
    gains, tables, attn_qk, attn_vo, ff_in, ff_out,
):
    tensor_id = lax.axis_index("tensor")
    enc_total, dec_total = enc_mask.shape[0], dec_mask.shape[0]
    enc_own, dec_own = enc_x.shape[0], dec_x.shape[0]
    count = item_count[0]
    enc_place = tensor_id * enc_own + jnp.arange(enc_own)
    dec_place = tensor_id * dec_own + jnp.arange(dec_own)
    enc_item = jnp.arange(enc_total) // (enc_total // count)
    dec_item = jnp.arange(dec_total) // (dec_total // count)
    enc_item_own = enc_place // (enc_total // count)
    dec_item_own = dec_place // (dec_total // count)
    enc_live = enc_mask == 1
    dec_live = dec_mask == 1
    enc_allowed = (enc_item_own[:, None] == enc_item[None, :]) & enc_live[None, :]
    self_allowed = (
        (dec_item_own[:, None] == dec_item[None, :])
        & dec_live[None, :]
        & (jnp.arange(dec_total)[None, :] <= dec_place[:, None])
    )
    cross_allowed = (dec_item_own[:, None] == enc_item[None, :]) & enc_live[None, :]
    enc_terms, enc_onehot = offset_bias(enc_buckets, tables[0])
    self_terms, self_onehot = offset_bias(dec_buckets, tables[1])

    def enc_bias_of(terms):
        return toeplitz(terms, tensor_id * enc_own, enc_own, enc_total)

    def self_bias_of(terms):
        return dec_spread(terms, tensor_id * dec_own, dec_own, dec_total)

    enc_bias, enc_bias_back = jax.vjp(enc_bias_of, enc_terms)
    self_bias, self_bias_back = jax.vjp(self_bias_of, self_terms)

    def project(rows, a):
        return to_low(product(rows, attn_qk[a][:, :INNER]))

    def project_kv(rows, a):
        return jnp.concatenate(
            [
                to_low(product(rows, attn_qk[a][:, INNER:])),
                to_low(product(rows, attn_vo[a][:, :INNER])),
            ],
            axis=1,
        )

    def out_weight(a):
        return attn_vo[a][:, INNER:]

    enc_start = enc_x.astype(jnp.float32)
    enc_h0 = to_low(norm_gain(enc_start, gains[0]))
    enc_q = project(enc_h0, 0)
    enc_kv = gather_t(project_kv(enc_h0, 0))
    enc_o, enc_p = attend(enc_q, enc_kv, enc_bias, enc_allowed)
    enc_mid = enc_start + product_over_cols(enc_o, out_weight(0))
    enc_h1 = gather_t(to_low(norm_gain(enc_mid, gains[1])))
    partial_value, enc_ff_saved = ff_forward(enc_h1, ff_in[0], ff_out[0])
    enc_end = enc_mid + scatter_t(partial_value)
    memory = to_low(norm_gain(enc_end, gains[2]))
    cross_kv = gather_t(project_kv(memory, 2))

    dec_start = dec_x.astype(jnp.float32)
    dec_hs = to_low(norm_gain(dec_start, gains[3]))
    self_q = project(dec_hs, 1)
    self_kv = gather_t(project_kv(dec_hs, 1))
    self_o, self_p = attend(self_q, self_kv, self_bias, self_allowed)
    dec_one = dec_start + product_over_cols(self_o, out_weight(1))
    dec_hc = to_low(norm_gain(dec_one, gains[4]))
    cross_q = project(dec_hc, 2)
    cross_o, cross_p = attend(cross_q, cross_kv, None, cross_allowed)
    dec_two = dec_one + product_over_cols(cross_o, out_weight(2))
    dec_hf = gather_t(to_low(norm_gain(dec_two, gains[5])))
    partial_value, dec_ff_saved = ff_forward(dec_hf, ff_in[1], ff_out[1])
    dec_out = (dec_two + scatter_t(partial_value)).astype(jnp.bfloat16)

    residual = dec_cot.astype(jnp.float32)
    dec_gy = gather_t(dec_cot)
    grad_rows, dec_gg, dec_gu = ff_back(dec_gy, dec_ff_saved, ff_in[1], ff_out[1])
    grad_rows, gain_five = norm_back(dec_two, gains[5], scatter_t(grad_rows))
    residual = residual + grad_rows
    cross_gy = to_low(residual)
    grad_o = to_low(product(cross_gy, out_weight(2)))
    cross_gq, grad_kv, unused = attend_back(cross_q, cross_kv, cross_p, grad_o)
    cross_gkv = to_low(scatter_t(grad_kv))
    grad_rows, gain_four = norm_back(
        dec_one, gains[4], product_over_cols(cross_gq, attn_qk[2][:, :INNER])
    )
    residual = residual + grad_rows

    def kv_back(grad_kv, a):
        return product_over_cols(grad_kv[:, :INNER], attn_qk[a][:, INNER:]) + product_over_cols(
            grad_kv[:, INNER:], attn_vo[a][:, :INNER]
        )

    memory_grad = kv_back(cross_gkv, 2)
    self_gy = to_low(residual)
    grad_o = to_low(product(self_gy, out_weight(1)))
    self_gq, grad_kv, self_gs = attend_back(self_q, self_kv, self_p, grad_o)
    self_gkv = to_low(scatter_t(grad_kv))
    grad_rows, gain_three = norm_back(
        dec_start,
        gains[3],
        product_over_cols(self_gq, attn_qk[1][:, :INNER]) + kv_back(self_gkv, 1),
    )
    dec_grad = residual + grad_rows

    residual, gain_two = norm_back(enc_end, gains[2], memory_grad)
    enc_gy = gather_t(to_low(residual))
    grad_rows, enc_gg, enc_gu = ff_back(enc_gy, enc_ff_saved, ff_in[0], ff_out[0])
    grad_rows, gain_one = norm_back(enc_mid, gains[1], scatter_t(grad_rows))
    residual = residual + grad_rows
    enc_ay = to_low(residual)
    grad_o = to_low(product(enc_ay, out_weight(0)))
    enc_gq, grad_kv, enc_gs = attend_back(enc_q, enc_kv, enc_p, grad_o)
    enc_gkv = to_low(scatter_t(grad_kv))
    grad_rows, gain_zero = norm_back(
        enc_start,
        gains[0],
        product_over_cols(enc_gq, attn_qk[0][:, :INNER]) + kv_back(enc_gkv, 0),
    )
    enc_grad = residual + grad_rows

    def attn_weights(query_rows, key_rows, grad_y, grad_q, grad_kv, mixed):
        rows = query_rows.shape[0]
        more = key_rows.shape[0] - rows

        def fill(value):
            return jnp.pad(value, ((0, more), (0, 0))) if more else value

        left = to_owner([fill(query_rows), key_rows, key_rows, fill(grad_y)])
        right = to_owner([fill(grad_q), grad_kv[:, :INNER], grad_kv[:, INNER:], fill(mixed)])
        return dp_sum(left, right)

    dec_ff = [
        dp_sum(dec_hf, dec_gg),
        dp_sum(dec_hf, dec_gu),
        dp_sum(dec_gy, dec_ff_saved[2]).T,
    ]
    cross_w = attn_weights(dec_hc, memory, cross_gy, cross_gq, cross_gkv, cross_o)
    self_w = attn_weights(dec_hs, dec_hs, self_gy, self_gq, self_gkv, self_o)
    enc_ff = [
        dp_sum(enc_h1, enc_gg),
        dp_sum(enc_h1, enc_gu),
        dp_sum(enc_gy, enc_ff_saved[2]).T,
    ]
    enc_w = attn_weights(enc_h0, enc_h0, enc_ay, enc_gq, enc_gkv, enc_o)
    ffin_sum = jnp.stack([jnp.stack(enc_ff[:2]), jnp.stack(dec_ff[:2])])
    ffout_sum = jnp.stack([enc_ff[2], dec_ff[2]])
    attn_all = lax.all_gather(
        to_low(jnp.stack([enc_w, self_w, cross_w])), "tensor", axis=2, tiled=True
    ).astype(jnp.float32)
    qk_sum = attn_all[:, :, : 2 * INNER]
    vo_sum = attn_all[:, :, 2 * INNER :]

    enc_offsets = enc_bias_back(enc_gs.astype(jnp.float32))[0]
    self_offsets = self_bias_back(self_gs.astype(jnp.float32))[0]
    tables_local = jnp.stack(
        [
            jnp.dot(enc_onehot.T, enc_offsets.T, precision=HIGH),
            jnp.dot(self_onehot.T, self_offsets.T, precision=HIGH),
        ]
    )
    gains_local = jnp.stack([gain_zero, gain_one, gain_two, gain_three, gain_four, gain_five])
    gains_sum, tables_sum = lax.psum((gains_local, tables_local), ("dp", "tensor"))
    return (dec_out, enc_grad, dec_grad, gains_sum, tables_sum, qk_sum, vo_sum, ffin_sum, ffout_sum)


def solution(mesh):
    rows = P(("dp", "tensor"), None)
    return jax.shard_map(
        on_device,
        mesh=mesh,
        in_specs=(
            rows, rows, rows, P("dp"), P("dp"), P("dp"), P(), P(), P(), P(), P(), P(),
            P(None, None, None, "tensor"), P(None, "tensor", None),
        ),
        out_specs=(
            rows, rows, rows, P(), P(), P(None, "dp", None), P(None, "dp", None),
            P(None, None, "dp", "tensor"), P(None, "tensor", "dp"),
        ),
        check_vma=False,
    )
```

```python
import functools

import jax
import jax.numpy as jnp
from jax import lax
from jax.experimental import pallas as pl
from jax.experimental.pallas import tpu as pltpu
from jax.sharding import PartitionSpec as P

HEADS = 6
HEAD = 64
INNER = HEADS * HEAD
PAIRS = HEADS // 2
PAIR = 2 * HEAD
BUCKETS = 32
EPSILON = 1e-06
MASKED = -1000000000.0
HIGH = lax.Precision.HIGHEST
F32 = jnp.float32
LOW = jnp.bfloat16
DEC_PAD = 32
VMEM_BYTES = 60 * 1024 * 1024
ROOT = 0.7978845608028654
CUBE = 0.044715


def to_low(value):
    return value.astype(LOW)


def dot(left, right):
    return jnp.dot(left, right, preferred_element_type=F32)


def dot_first(left, right):
    return lax.dot_general(left, right, (((0,), (0,)), ((), ())), preferred_element_type=F32)


def dot_last(left, right):
    return lax.dot_general(left, right, (((1,), (1,)), ((), ())), preferred_element_type=F32)


def norm_gain(rows, gain):
    return rows * lax.rsqrt(jnp.mean(rows * rows, axis=-1, keepdims=True) + EPSILON) * gain


def norm_back(rows, gain, grad_rows):
    scale = lax.rsqrt(jnp.mean(rows * rows, axis=-1, keepdims=True) + EPSILON)
    normed = rows * scale
    scaled = grad_rows * gain
    inner = jnp.mean(scaled * normed, axis=-1, keepdims=True)
    grad_gain = jnp.sum(grad_rows * normed, axis=0, keepdims=True)
    return scale * (scaled - normed * inner), grad_gain


def act_parts(gate, up_proj):
    square = gate * gate
    curve = jnp.tanh(ROOT * gate * (1.0 + CUBE * square))
    half = 0.5 * (1.0 + curve)
    slope = half + 0.5 * gate * (1.0 - curve * curve) * (ROOT * (1.0 + 3.0 * CUBE * square))
    return gate * half, up_proj * slope


def tiles(width, step=256):
    return [(start, min(start + step, width)) for start in range(0, width, step)]


class Peers:
    def __init__(self, send_sem, recv_sem):
        dp, tensor = lax.axis_index("dp"), lax.axis_index("tensor")
        chip, core = lax.div(tensor, 2), lax.rem(tensor, 2)
        self.dp = dp
        self.own = tensor
        self.sib = chip * 2 + (1 - core)
        self.far = (1 - chip) * 2 + core
        self.diag = (1 - chip) * 2 + (1 - core)
        self.send_sem, self.recv_sem = send_sem, recv_sem
        self.used = 0
        self.copies = []

    def greet(self):
        barrier = pltpu.get_barrier_semaphore()
        for peer in (self.sib, self.far):
            pl.semaphore_signal(
                barrier, inc=1, device_id=(self.dp, peer), device_id_type=pl.DeviceIdType.MESH
            )
        pl.semaphore_wait(barrier, 2)

    def send(self, source, target, peer):
        place = self.used
        self.used += 1
        copy = pltpu.make_async_remote_copy(
            src_ref=source,
            dst_ref=target,
            send_sem=self.send_sem.at[place],
            recv_sem=self.recv_sem.at[place],
            device_id=(self.dp, peer),
            device_id_type=pl.DeviceIdType.MESH,
        )
        copy.start()
        self.copies.append(copy)
        return copy

    def finish(self):
        for copy in self.copies:
            copy.wait_send()


class Gather:
    def __init__(self, peers, buf, near):
        self.peers, self.buf = peers, buf
        if near:
            self.slots = (0, 1, 2, 2, 3)
        else:
            self.slots = (peers.own, peers.own, peers.own, peers.far, peers.far)

    def start(self):
        own, at_sib, at_far, unused, unused = self.slots
        self.to_far = self.peers.send(self.buf.at[own], self.buf.at[at_far], self.peers.far)
        self.to_sib = self.peers.send(self.buf.at[own], self.buf.at[at_sib], self.peers.sib)

    def wait_near(self):
        self.to_sib.wait_recv()

    def relay(self):
        unused, unused, unused, far, far_at_sib = self.slots
        self.to_far.wait_recv()
        self.relayed = self.peers.send(
            self.buf.at[far], self.buf.at[far_at_sib], self.peers.sib
        )

    def wait_far(self):
        self.relayed.wait_recv()


def attend(queries, kv, bias_of, allowed, weights_out, mixed_out):
    rows = queries.shape[0]
    total = kv.shape[0] * kv.shape[1]
    first = lax.broadcasted_iota(jnp.int32, (rows, PAIR), 1) < HEAD
    for pair in range(PAIRS):
        lanes = slice(pair * PAIR, (pair + 1) * PAIR)
        keys = kv[:, :, lanes].reshape(total, PAIR)
        values = kv[:, :, INNER + pair * PAIR : INNER + (pair + 1) * PAIR].reshape(total, PAIR)
        both = queries[:, lanes].astype(F32)
        mixed = []
        for half in range(2):
            head = 2 * pair + half
            here = to_low(jnp.where(first if half == 0 else ~first, both, 0.0))
            scores = dot_last(here, keys)
            if bias_of is not None:
                scores = scores + bias_of(head)
            scores = jnp.where(allowed, scores, MASKED)
            shifted = jnp.exp(scores - jnp.max(scores, axis=-1, keepdims=True))
            weights = shifted / jnp.sum(shifted, axis=-1, keepdims=True)
            weights_out[head] = weights
            mixed.append(dot(to_low(weights), values))
        mixed_out[:, lanes] = to_low(jnp.where(first, mixed[0], mixed[1]))


def attend_back(queries, kv, weights_in, grad_out, grad_q_out, grad_kv_out, grad_s_out):
    rows = queries.shape[0]
    total = kv.shape[0] * kv.shape[1]
    block = kv.shape[1]
    first = lax.broadcasted_iota(jnp.int32, (rows, PAIR), 1) < HEAD
    first_key = lax.broadcasted_iota(jnp.int32, (total, PAIR), 1) < HEAD
    for pair in range(PAIRS):
        lanes = slice(pair * PAIR, (pair + 1) * PAIR)
        value_lanes = slice(INNER + pair * PAIR, INNER + (pair + 1) * PAIR)
        keys = kv[:, :, lanes].reshape(total, PAIR)
        values = kv[:, :, value_lanes].reshape(total, PAIR)
        query = queries[:, lanes]
        grad = grad_out[:, lanes]
        grad_wide = grad.astype(F32)
        grad_q, grad_k, grad_v = [], [], []
        for half in range(2):
            head = 2 * pair + half
            here = to_low(jnp.where(first if half == 0 else ~first, grad_wide, 0.0))
            weights = weights_in[head]
            grad_weights = dot_last(here, values)
            weighted = jnp.sum(weights * grad_weights, axis=-1, keepdims=True)
            grad_scores = to_low(weights * (grad_weights - weighted))
            if grad_s_out is not None:
                grad_s_out[head] = grad_scores
            grad_q.append(dot(grad_scores, keys))
            grad_k.append(dot_first(grad_scores, query))
            grad_v.append(dot_first(to_low(weights), grad))
        grad_q_out[:, lanes] = to_low(jnp.where(first, grad_q[0], grad_q[1]))
        grad_kv_out[:, :, lanes] = jnp.where(first_key, grad_k[0], grad_k[1]).reshape(
            4, block, PAIR
        )
        grad_kv_out[:, :, value_lanes] = jnp.where(first_key, grad_v[0], grad_v[1]).reshape(
            4, block, PAIR
        )


class Loads:
    def __init__(self, sems):
        self.sems, self.used = sems, 0

    def start(self, source, target):
        copy = pltpu.make_async_copy(source, target, self.sems.at[self.used])
        self.used += 1
        copy.start()
        return copy


def project_kv(rows, wqk, wvo, target):
    target[:, :INNER] = to_low(dot(rows, wqk[:, INNER:]))
    target[:, INNER:] = to_low(dot(rows, wvo[:, :INNER]))


def ff_up(rows, w_in, gelu_out, slope_out, hidden_out, slots):
    count, block = slots.stop - slots.start, gelu_out.shape[1]
    for low, high in tiles(gelu_out.shape[2]):
        gate = dot(rows, w_in[0, :, low:high])
        up_proj = dot(rows, w_in[1, :, low:high])
        gelu, slope = act_parts(gate, up_proj)
        shape = (count, block, high - low)
        gelu_out[slots, :, low:high] = gelu.reshape(shape)
        slope_out[slots, :, low:high] = slope.reshape(shape)
        hidden_out[slots, :, low:high] = to_low(gelu * up_proj).reshape(shape)


def reduce_far(peers, diag_part, far_part, send, recv):
    width = send.shape[2]
    for low, high in tiles(width):
        send[0, :, low:high] = to_low(diag_part(low, high))
    first = peers.send(send.at[0], recv.at[0], peers.sib)
    first.wait_recv()
    for low, high in tiles(width):
        send[2, :, low:high] = to_low(
            far_part(low, high) + recv[0, :, low:high].astype(F32)
        )
    return peers.send(send.at[2], recv.at[2], peers.far)


def ka_kernel(
    enc_x, dec_x, dec_cot, gains, enc_terms, enc_code, enc_item, self_mask, self_bias, dec_item,
    qk_all, vo_all, fi_all, fo_all,
    h0, enc_q, enc_kv, enc_p, enc_o, enc_mid, h1, enc_gelu, enc_slope, enc_hidden, enc_end, memory,
    cross_kv, hs, self_q, self_kv, self_p, self_o, dec_one, hc, cross_q, cross_p, cross_o, dec_two,
    hf, dec_gy, dec_gg, dec_gu, dec_hidden,
    wqk, wvo, wfi, wfo, part, send, recv, dec_gelu, dec_slope, send_sem, recv_sem, load_sem,
):
    peers = Peers(send_sem, recv_sem)
    loads = Loads(load_sem)
    get_qk, get_vo, get_fi, get_fo = {}, {}, {}, {}
    for a in (0, 1):
        get_qk[a] = loads.start(qk_all.at[a], wqk.at[a])
        get_vo[a] = loads.start(vo_all.at[a], wvo.at[a])
    get_fi[0] = loads.start(fi_all.at[0], wfi.at[0])
    get_fo[0] = loads.start(fo_all.at[0], wfo.at[0])
    get_qk[2] = loads.start(qk_all.at[2], wqk.at[2])
    get_vo[2] = loads.start(vo_all.at[2], wvo.at[2])
    get_fi[1] = loads.start(fi_all.at[1], wfi.at[1])
    get_fo[1] = loads.start(fo_all.at[1], wfo.at[1])
    peers.greet()

    normed = to_low(norm_gain(enc_x[...].astype(F32), gains[0:1]))
    h0[...] = normed
    get_qk[0].wait()
    get_vo[0].wait()
    project_kv(normed, wqk.at[0], wvo.at[0], enc_kv.at[peers.own])
    enc_gather = Gather(peers, enc_kv, False)
    enc_gather.start()
    normed_dec = to_low(norm_gain(dec_x[...].astype(F32), gains[3:4]))
    hs[...] = normed_dec
    get_qk[1].wait()
    get_vo[1].wait()
    project_kv(normed_dec, wqk.at[1], wvo.at[1], self_kv.at[peers.own])
    self_gather = Gather(peers, self_kv, False)
    self_gather.start()
    dec_gy[0] = dec_cot[...]
    gy_gather = Gather(peers, dec_gy, True)
    gy_gather.start()
    enc_q[...] = to_low(dot(normed, wqk[0, :, :INNER]))
    self_q[...] = to_low(dot(normed_dec, wqk[1, :, :INNER]))

    enc_gather.wait_near()
    enc_gather.relay()
    enc_allowed = enc_item[...] == enc_code[...]

    def enc_bias(head):
        own_rows, period = h0.shape[0], enc_terms.shape[1]
        spread = jnp.broadcast_to(enc_terms[head : head + 1, :], (own_rows, period))
        rolled = pltpu.roll(spread, 0, 1, stride=1, stride_axis=0)
        return rolled[:, : period // 2]

    enc_gather.wait_far()
    attend(enc_q[...], enc_kv, enc_bias, enc_allowed, enc_p, enc_o)
    for low, high in tiles(enc_mid.shape[1]):
        enc_mid[:, low:high] = enc_x[:, low:high].astype(F32) + dot_last(
            enc_o[...], wvo[0, low:high, INNER:]
        )
    h1[0] = to_low(norm_gain(enc_mid[...], gains[1:2]))
    h1_gather = Gather(peers, h1, True)
    h1_gather.start()

    self_gather.wait_near()
    self_gather.relay()
    gy_gather.wait_near()
    gy_gather.relay()
    self_gather.wait_far()
    gy_gather.wait_far()
    attend(
        self_q[...], self_kv, lambda head: self_bias[head], self_mask[...] > 0.5, self_p, self_o
    )
    for low, high in tiles(dec_one.shape[1]):
        dec_one[:, low:high] = dec_x[:, low:high].astype(F32) + dot_last(
            self_o[...], wvo[1, low:high, INNER:]
        )
    normed_dec = to_low(norm_gain(dec_one[...], gains[4:5]))
    hc[...] = normed_dec

    h1_gather.wait_near()
    get_fi[0].wait()
    get_fo[0].wait()
    block, width = h1.shape[1], h1.shape[2]

    def both(buf, slots):
        return buf[slots].reshape((slots.stop - slots.start) * block, buf.shape[2])

    near, away = slice(0, 2), slice(2, 4)
    ff_up(both(h1, near), wfi.at[0], enc_gelu, enc_slope, enc_hidden, near)
    h1_gather.relay()
    h1_gather.wait_far()
    ff_up(both(h1, away), wfi.at[0], enc_gelu, enc_slope, enc_hidden, away)
    hidden = both(enc_hidden, away)
    for low, high in tiles(width):
        value = dot_last(hidden, wfo[0, low:high, :])
        part[:, low:high] = value[:block]
        send[0, :, low:high] = to_low(value[block:])
    first = peers.send(send.at[0], recv.at[0], peers.sib)
    get_qk[2].wait()
    get_vo[2].wait()
    cross_q[...] = to_low(dot(hc[...], wqk[2, :, :INNER]))
    first.wait_recv()
    send[2] = to_low(part[...] + recv[0].astype(F32))
    second = peers.send(send.at[2], recv.at[2], peers.far)
    hidden = both(enc_hidden, near)
    for low, high in tiles(width):
        value = dot_last(hidden, wfo[0, low:high, :])
        part[:, low:high] = value[:block] + enc_mid[:, low:high]
        send[1, :, low:high] = to_low(value[block:])
    third = peers.send(send.at[1], recv.at[1], peers.sib)
    third.wait_recv()
    part[...] = part[...] + recv[1].astype(F32)
    second.wait_recv()
    ended = part[...] + recv[2].astype(F32)
    enc_end[...] = ended
    normed = to_low(norm_gain(ended, gains[2:3]))
    memory[...] = normed

    project_kv(normed, wqk.at[2], wvo.at[2], cross_kv.at[peers.own])
    cross_gather = Gather(peers, cross_kv, False)
    cross_gather.start()
    get_fi[1].wait()
    get_fo[1].wait()
    cross_allowed = dec_item[...] == enc_code[...]
    cross_gather.wait_near()
    cross_gather.relay()
    cross_gather.wait_far()
    attend(cross_q[...], cross_kv, None, cross_allowed, cross_p, cross_o)
    for low, high in tiles(dec_two.shape[1]):
        dec_two[:, low:high] = dec_one[:, low:high] + dot_last(
            cross_o[...], wvo[2, low:high, INNER:]
        )
    hf[0] = to_low(norm_gain(dec_two[...], gains[5:6]))
    hf_gather = Gather(peers, hf, True)
    hf_gather.start()

    rows = hf.shape[0] * hf.shape[1]
    hf_gather.wait_near()
    hf_gather.relay()
    grad_y = dec_gy[...].reshape(rows, width)
    hf_gather.wait_far()
    ff_up(hf[...].reshape(rows, width), wfi.at[1], dec_gelu, dec_slope, dec_hidden, slice(0, 4))
    for low, high in tiles(dec_gelu.shape[2]):
        grad_h = dot(grad_y, wfo[1, :, low:high]).reshape(4, hf.shape[1], high - low)
        dec_gg[:, :, low:high] = to_low(grad_h * dec_slope[:, :, low:high])
        dec_gu[:, :, low:high] = to_low(grad_h * dec_gelu[:, :, low:high])
    peers.finish()


def ka_call(enc_x, dec_x, dec_cot, gains, enc_terms, enc_code, enc_item, self_mask, self_bias,
            dec_item, attn_qk, attn_vo, ff_in, ff_out):
    rows, width = enc_x.shape
    dec_rows = dec_x.shape[0]
    units = ff_in.shape[3]
    total = enc_code.shape[1]
    kv_width = 2 * INNER
    shape = jax.ShapeDtypeStruct
    outs = [
        shape((rows, width), LOW), shape((rows, INNER), LOW), shape((4, rows, kv_width), LOW),
        shape((HEADS, rows, total), F32), shape((rows, INNER), LOW), shape((rows, width), F32),
        shape((4, rows, width), LOW), shape((4, rows, units), F32), shape((4, rows, units), F32),
        shape((4, rows, units), LOW), shape((rows, width), F32), shape((rows, width), LOW),
        shape((4, rows, kv_width), LOW),
        shape((dec_rows, width), LOW), shape((dec_rows, INNER), LOW),
        shape((4, dec_rows, kv_width), LOW), shape((HEADS, dec_rows, 4 * dec_rows), F32),
        shape((dec_rows, INNER), LOW), shape((dec_rows, width), F32),
        shape((dec_rows, width), LOW), shape((dec_rows, INNER), LOW),
        shape((HEADS, dec_rows, total), F32), shape((dec_rows, INNER), LOW),
        shape((dec_rows, width), F32),
        shape((4, dec_rows, width), LOW), shape((4, dec_rows, width), LOW),
        shape((4, dec_rows, units), LOW), shape((4, dec_rows, units), LOW),
        shape((4, dec_rows, units), LOW),
    ]
    vmem = pl.BlockSpec(memory_space=pltpu.VMEM)
    hbm = pl.BlockSpec(memory_space=pltpu.HBM)
    copies = 3 * 6 + 3
    return pl.pallas_call(
        ka_kernel,
        out_shape=outs,
        in_specs=[vmem] * 10 + [hbm] * 4,
        out_specs=[vmem] * len(outs),
        scratch_shapes=[
            pltpu.VMEM(attn_qk.shape, LOW), pltpu.VMEM(attn_vo.shape, LOW),
            pltpu.VMEM(ff_in.shape, LOW), pltpu.VMEM(ff_out.shape, LOW),
            pltpu.VMEM((rows, width), F32), pltpu.VMEM((3, rows, width), LOW),
            pltpu.VMEM((3, rows, width), LOW), pltpu.VMEM((4, dec_rows, units), F32),
            pltpu.VMEM((4, dec_rows, units), F32),
            pltpu.SemaphoreType.DMA((copies,)), pltpu.SemaphoreType.DMA((copies,)),
            pltpu.SemaphoreType.DMA((10,)),
        ],
        compiler_params=pltpu.CompilerParams(
            collective_id=0, has_side_effects=True, vmem_limit_bytes=VMEM_BYTES
        ),
        name="forward_chain",
    )(enc_x, dec_x, dec_cot, gains, enc_terms, enc_code, enc_item, self_mask, self_bias, dec_item,
      attn_qk, attn_vo, ff_in, ff_out)


def pad_rows(value, rows=DEC_PAD):
    return jnp.pad(value, ((0, rows - value.shape[0]), (0, 0)))


def prepare(item_count, enc_mask, dec_mask, enc_buckets, dec_buckets, tables, enc_own, dec_own):
    tensor_id = lax.axis_index("tensor")
    enc_total, dec_total = enc_mask.shape[0], dec_mask.shape[0]
    count = item_count[0]
    enc_len, dec_len = enc_total // count, dec_total // count
    enc_code = jnp.where(enc_mask == 1, jnp.arange(enc_total) // enc_len, -1)
    enc_item = (tensor_id * enc_own + jnp.arange(enc_own)) // enc_len
    slot = jnp.arange(4 * DEC_PAD)
    inside = slot % DEC_PAD
    place = slot // DEC_PAD * dec_own + inside
    real = inside < dec_own
    row = jnp.arange(DEC_PAD)
    row_real = row < dec_own
    row_place = tensor_id * dec_own + row
    dec_live = jnp.pad(dec_mask.reshape(4, dec_own), ((0, 0), (0, DEC_PAD - dec_own))).reshape(-1)
    key_item = jnp.where(real & (dec_live == 1), place // dec_len, -1)
    dec_item = jnp.where(row_real, row_place // dec_len, -2)
    self_mask = (
        (dec_item[:, None] == key_item[None, :]) & (place[None, :] <= row_place[:, None])
    ).astype(F32)
    onehot = (enc_buckets[:, None] == jnp.arange(BUCKETS)[None, :]).astype(F32)
    terms = jnp.dot(tables[0].T, onehot.T, precision=HIGH)
    terms = jnp.pad(terms, ((0, 2), (0, 1)))
    period = 2 * enc_total
    doubled = jnp.concatenate([terms, terms], axis=1)
    shift = (enc_total - 1 - tensor_id * enc_own + period) % period
    enc_terms = lax.dynamic_slice_in_dim(doubled, shift, period, 1)
    far_back = jnp.clip(row_place[:, None] - place[None, :], 0, dec_total - 1)
    far_back = (far_back[None] == jnp.arange(dec_total)[:, None, None]).astype(F32)
    far_back = far_back.reshape(dec_total, -1)
    dec_onehot = (dec_buckets[:, None] == jnp.arange(BUCKETS)[None, :]).astype(F32)
    dec_terms = jnp.dot(tables[1].T, dec_onehot.T, precision=HIGH)
    self_bias = jnp.dot(dec_terms, far_back, precision=HIGH).reshape(
        HEADS, DEC_PAD, 4 * DEC_PAD
    )
    return (
        enc_terms, enc_code.astype(F32)[None, :], enc_item.astype(F32)[:, None], self_mask,
        self_bias, dec_item.astype(F32)[:, None],
    ), (onehot, dec_onehot, far_back)


def kv_back(grad_kv, wqk, wvo, low, high):
    return dot_last(grad_kv[:, :INNER], wqk[low:high, INNER:]) + dot_last(
        grad_kv[:, INNER:], wvo[low:high, :INNER]
    )


class SumBlocks:
    def __init__(self, peers, buf, send, recv):
        self.peers, self.buf, self.send, self.recv = peers, buf, send, recv
        send[0] = to_low(buf[peers.diag])
        send[1] = to_low(buf[peers.sib])
        self.first = peers.send(send.at[0], recv.at[0], peers.sib)
        self.third = peers.send(send.at[1], recv.at[1], peers.sib)

    def cross(self):
        peers = self.peers
        self.first.wait_recv()
        self.send[2] = to_low(self.buf[peers.far] + self.recv[0].astype(F32))
        self.second = peers.send(self.send.at[2], self.recv.at[2], peers.far)

    def result(self):
        self.third.wait_recv()
        value = self.buf[self.peers.own] + self.recv[1].astype(F32)
        self.second.wait_recv()
        return value + self.recv[2].astype(F32)


class SumNear:
    def __init__(self, peers, part_of, block, total, send, recv):
        self.peers, self.total, self.send, self.recv = peers, total, send, recv
        for low, high in tiles(send.shape[2]):
            value = part_of(low, high)
            total[0, :, low:high] = value[:block]
            send[1, :, low:high] = to_low(value[block : 2 * block])
            total[1, :, low:high] = value[2 * block : 3 * block]
            send[0, :, low:high] = to_low(value[3 * block :])
        self.first = peers.send(send.at[0], recv.at[0], peers.sib)
        self.third = peers.send(send.at[1], recv.at[1], peers.sib)

    def cross(self):
        self.first.wait_recv()
        self.send[2] = to_low(self.total[1] + self.recv[0].astype(F32))
        self.second = self.peers.send(self.send.at[2], self.recv.at[2], self.peers.far)

    def result(self):
        self.third.wait_recv()
        value = self.total[0] + self.recv[1].astype(F32)
        self.second.wait_recv()
        return value + self.recv[2].astype(F32)


def kb_kernel(
    dec_gg, dec_gu, dec_hidden, dec_cot, dec_two, dec_one, gains, cross_q, cross_kv, cross_p,
    enc_end, enc_gelu, enc_slope, qk_all, vo_all, fi_all, fo_all,
    dec_out, cross_gy, cross_gq, cross_gkv, dec_one_grad, enc_end_grad, enc_gy, enc_gg, enc_gu,
    gains_grad,
    wqk, wvo, wfi, wfo, grad_kv, kv_send, kv_recv, row_total, row_send, row_recv, out_total,
    out_send, out_recv, send_sem, recv_sem, load_sem,
):
    peers = Peers(send_sem, recv_sem)
    loads = Loads(load_sem)
    get_fi = loads.start(fi_all.at[1], wfi)
    get_vo = loads.start(vo_all.at[2], wvo)
    get_qk = loads.start(qk_all.at[2], wqk)
    get_fo1 = loads.start(fo_all.at[1], wfo.at[1])
    get_fo0 = loads.start(fo_all.at[0], wfo.at[0])
    peers.greet()
    width = dec_two.shape[1]
    block = dec_two.shape[0]
    units = dec_gg.shape[2]
    gains_grad[...] = jnp.zeros_like(gains_grad)

    get_fi.wait()
    gate, up_proj = dec_gg[...].reshape(4 * block, units), dec_gu[...].reshape(4 * block, units)

    def grad_rows_part(low, high):
        return dot_last(gate, wfi[0, low:high, :]) + dot_last(up_proj, wfi[1, low:high, :])

    grad_rows = SumNear(peers, grad_rows_part, block, row_total, row_send, row_recv)
    grad_rows.cross()
    get_vo.wait()
    get_qk.wait()
    value, gain_row = norm_back(dec_two[...], gains[5:6], grad_rows.result())
    gains_grad[5:6] = gain_row
    residual = dec_cot[...].astype(F32) + value
    grad_y = to_low(residual)
    cross_gy[...] = grad_y

    grad_out = to_low(dot(grad_y, wvo[:, INNER:]))
    attend_back(cross_q[...], cross_kv, cross_p, grad_out, cross_gq, grad_kv, None)
    kv_sum = SumBlocks(peers, grad_kv, kv_send, kv_recv)
    kv_sum.cross()
    for low, high in tiles(width):
        row_total[0, :, low:high] = dot_last(cross_gq[...], wqk[low:high, :INNER])
    value, gain_row = norm_back(dec_one[...], gains[4:5], row_total[0])
    gains_grad[4:5] = gain_row
    dec_one_grad[...] = residual + value
    own_kv = to_low(kv_sum.result())
    cross_gkv[...] = own_kv
    for low, high in tiles(width):
        enc_end_grad[:, low:high] = kv_back(own_kv, wqk, wvo, low, high)
    value, gain_row = norm_back(enc_end[...], gains[2:3], enc_end_grad[...])
    gains_grad[2:3] = gain_row
    enc_end_grad[...] = value
    enc_gy[0] = to_low(value)
    gy_gather = Gather(peers, enc_gy, True)
    gy_gather.start()

    get_fo1.wait()
    hidden = dec_hidden[...].reshape(4 * block, units)
    out_sum = SumNear(
        peers, lambda low, high: dot_last(hidden, wfo[1, low:high, :]), block, out_total,
        out_send, out_recv,
    )

    get_fo0.wait()
    rows = enc_gy.shape[1]

    def gate_grads(slots):
        grad_y = enc_gy[slots].reshape(2 * rows, width)
        for low, high in tiles(units):
            grad_h = dot(grad_y, wfo[0, :, low:high]).reshape(2, rows, high - low)
            enc_gg[slots, :, low:high] = to_low(grad_h * enc_slope[slots, :, low:high])
            enc_gu[slots, :, low:high] = to_low(grad_h * enc_gelu[slots, :, low:high])

    gy_gather.wait_near()
    gate_grads(slice(0, 2))
    gy_gather.relay()
    out_sum.cross()
    gy_gather.wait_far()
    gate_grads(slice(2, 4))
    dec_out[...] = to_low(dec_two[...] + out_sum.result())
    peers.finish()


def kb_call(dec_gg, dec_gu, dec_hidden, dec_cot, dec_two, dec_one, gains, cross_q, cross_kv,
            cross_p, enc_end, enc_gelu, enc_slope, attn_qk, attn_vo, ff_in, ff_out):
    rows, width = enc_end.shape
    dec_rows = dec_two.shape[0]
    units = ff_in.shape[3]
    kv_width = 2 * INNER
    shape = jax.ShapeDtypeStruct
    outs = [
        shape((dec_rows, width), LOW), shape((dec_rows, width), LOW),
        shape((dec_rows, INNER), LOW), shape((rows, kv_width), LOW), shape((dec_rows, width), F32),
        shape((rows, width), F32), shape((4, rows, width), LOW), shape((4, rows, units), LOW),
        shape((4, rows, units), LOW), shape((8, width), F32),
    ]
    vmem = pl.BlockSpec(memory_space=pltpu.VMEM)
    hbm = pl.BlockSpec(memory_space=pltpu.HBM)
    copies = 3 * 3 + 3
    return pl.pallas_call(
        kb_kernel,
        out_shape=outs,
        in_specs=[vmem] * 13 + [hbm] * 4,
        out_specs=[vmem] * len(outs),
        scratch_shapes=[
            pltpu.VMEM(attn_qk.shape[1:], LOW), pltpu.VMEM(attn_vo.shape[1:], LOW),
            pltpu.VMEM(ff_in.shape[1:], LOW), pltpu.VMEM(ff_out.shape, LOW),
            pltpu.VMEM((4, rows, kv_width), F32), pltpu.VMEM((3, rows, kv_width), LOW),
            pltpu.VMEM((3, rows, kv_width), LOW), pltpu.VMEM((2, dec_rows, width), F32),
            pltpu.VMEM((3, dec_rows, width), LOW), pltpu.VMEM((3, dec_rows, width), LOW),
            pltpu.VMEM((2, dec_rows, width), F32), pltpu.VMEM((3, dec_rows, width), LOW),
            pltpu.VMEM((3, dec_rows, width), LOW),
            pltpu.SemaphoreType.DMA((copies,)), pltpu.SemaphoreType.DMA((copies,)),
            pltpu.SemaphoreType.DMA((5,)),
        ],
        compiler_params=pltpu.CompilerParams(
            collective_id=1, has_side_effects=True, vmem_limit_bytes=VMEM_BYTES
        ),
        name="middle_chain",
    )(dec_gg, dec_gu, dec_hidden, dec_cot, dec_two, dec_one, gains, cross_q, cross_kv, cross_p,
      enc_end, enc_gelu, enc_slope, attn_qk, attn_vo, ff_in, ff_out)


def kc_kernel(
    enc_gg, enc_gu, enc_end_grad, enc_mid, enc_x, gains, enc_q, enc_kv, enc_p, dec_one_grad, dec_x,
    self_q, self_kv, self_p, qk_all, vo_all, fi_all,
    enc_grad, enc_ay, enc_gq, enc_gkv, enc_offsets, dec_grad, self_gy, self_gq, self_gkv, self_gs,
    gains_grad,
    wqk, wvo, wfi, enc_gs, part, send, recv, enc_gkv_full, kv_send, kv_recv, self_gkv_full,
    self_send, self_recv, send_sem, recv_sem, load_sem,
):
    peers = Peers(send_sem, recv_sem)
    loads = Loads(load_sem)
    get_fi = loads.start(fi_all.at[0], wfi)
    get_vo1 = loads.start(vo_all.at[1], wvo.at[1])
    get_qk1 = loads.start(qk_all.at[1], wqk.at[1])
    get_vo0 = loads.start(vo_all.at[0], wvo.at[0])
    get_qk0 = loads.start(qk_all.at[0], wqk.at[0])
    peers.greet()
    rows, width = enc_mid.shape
    units = enc_gg.shape[2]
    gains_grad[...] = jnp.zeros_like(gains_grad)

    get_fi.wait()

    def grad_part(slots, low, high):
        gate = enc_gg[slots].reshape(2 * rows, units)
        up_proj = enc_gu[slots].reshape(2 * rows, units)
        return dot_last(gate, wfi[0, low:high, :]) + dot_last(up_proj, wfi[1, low:high, :])

    for low, high in tiles(width):
        value = grad_part(slice(2, 4), low, high)
        part[:, low:high] = value[:rows]
        send[0, :, low:high] = to_low(value[rows:])
    first = peers.send(send.at[0], recv.at[0], peers.sib)
    get_vo1.wait()
    residual_dec = dec_one_grad[...]
    grad_y = to_low(residual_dec)
    self_gy[...] = grad_y
    grad_out_dec = to_low(dot(grad_y, wvo[1, :, INNER:]))
    first.wait_recv()
    send[2] = to_low(part[...] + recv[0].astype(F32))
    second = peers.send(send.at[2], recv.at[2], peers.far)
    for low, high in tiles(width):
        value = grad_part(slice(0, 2), low, high)
        part[:, low:high] = value[:rows]
        send[1, :, low:high] = to_low(value[rows:])
    third = peers.send(send.at[1], recv.at[1], peers.sib)

    attend_back(self_q[...], self_kv, self_p, grad_out_dec, self_gq, self_gkv_full, self_gs)
    self_sum = SumBlocks(peers, self_gkv_full, self_send, self_recv)
    self_sum.cross()

    third.wait_recv()
    part[...] = part[...] + recv[1].astype(F32)
    second.wait_recv()
    get_vo0.wait()
    value, gain_row = norm_back(enc_mid[...], gains[1:2], part[...] + recv[2].astype(F32))
    gains_grad[1:2] = gain_row
    residual = enc_end_grad[...] + value
    grad_y = to_low(residual)
    enc_ay[...] = grad_y
    enc_grad[...] = residual

    grad_out = to_low(dot(grad_y, wvo[0, :, INNER:]))
    attend_back(enc_q[...], enc_kv, enc_p, grad_out, enc_gq, enc_gkv_full, enc_gs)
    enc_sum = SumBlocks(peers, enc_gkv_full, kv_send, kv_recv)
    get_qk0.wait()
    for low, high in tiles(width):
        part[:, low:high] = dot_last(enc_gq[...], wqk[0, low:high, :INNER])
    enc_sum.cross()

    get_qk1.wait()
    own_kv = to_low(self_sum.result())
    self_gkv[...] = own_kv
    for low, high in tiles(width):
        dec_grad[:, low:high] = dot_last(self_gq[...], wqk[1, low:high, :INNER]) + kv_back(
            own_kv, wqk.at[1], wvo.at[1], low, high
        )
    value, gain_row = norm_back(dec_x[...].astype(F32), gains[3:4], dec_grad[...])
    gains_grad[3:4] = gain_row
    dec_grad[...] = residual_dec + value

    turn = lax.broadcasted_iota(jnp.int32, (rows, rows), 0) + lax.broadcasted_iota(
        jnp.int32, (rows, rows), 1
    )
    turn = jnp.where(turn == rows - 1, 1.0, 0.0).astype(LOW)
    enc_offsets[...] = jnp.zeros_like(enc_offsets)
    for head in range(HEADS):
        turned = dot(turn, enc_gs[head])
        spread = jnp.concatenate([turned, jnp.zeros((rows, rows), F32)], axis=1)
        spread = pltpu.roll(spread, 0, 1, stride=1, stride_axis=0)
        enc_offsets[head : head + 1, :] = jnp.sum(spread, axis=0, keepdims=True)

    own_kv = to_low(enc_sum.result())
    enc_gkv[...] = own_kv
    for low, high in tiles(width):
        part[:, low:high] += kv_back(own_kv, wqk.at[0], wvo.at[0], low, high)
    value, gain_row = norm_back(enc_x[...].astype(F32), gains[0:1], part[...])
    gains_grad[0:1] = gain_row
    enc_grad[...] += value
    peers.finish()


def kc_call(enc_gg, enc_gu, enc_end_grad, enc_mid, enc_x, gains, enc_q, enc_kv, enc_p,
            dec_one_grad, dec_x, self_q, self_kv, self_p, attn_qk, attn_vo, ff_in):
    rows, width = enc_x.shape
    dec_rows = dec_x.shape[0]
    units = ff_in.shape[3]
    kv_width = 2 * INNER
    total = 4 * rows
    shape = jax.ShapeDtypeStruct
    outs = [
        shape((rows, width), F32), shape((rows, width), LOW), shape((rows, INNER), LOW),
        shape((rows, kv_width), LOW), shape((8, total + rows), F32),
        shape((dec_rows, width), F32), shape((dec_rows, width), LOW),
        shape((dec_rows, INNER), LOW), shape((dec_rows, kv_width), LOW),
        shape((HEADS, dec_rows, 4 * dec_rows), LOW), shape((8, width), F32),
    ]
    vmem = pl.BlockSpec(memory_space=pltpu.VMEM)
    hbm = pl.BlockSpec(memory_space=pltpu.HBM)
    copies = 3 * 3
    return pl.pallas_call(
        kc_kernel,
        out_shape=outs,
        in_specs=[vmem] * 14 + [hbm] * 3,
        out_specs=[vmem] * len(outs),
        scratch_shapes=[
            pltpu.VMEM((2,) + attn_qk.shape[1:], LOW), pltpu.VMEM((2,) + attn_vo.shape[1:], LOW),
            pltpu.VMEM(ff_in.shape[1:], LOW), pltpu.VMEM((HEADS, rows, total), LOW),
            pltpu.VMEM((rows, width), F32), pltpu.VMEM((3, rows, width), LOW),
            pltpu.VMEM((3, rows, width), LOW),
            pltpu.VMEM((4, rows, kv_width), F32), pltpu.VMEM((3, rows, kv_width), LOW),
            pltpu.VMEM((3, rows, kv_width), LOW),
            pltpu.VMEM((4, dec_rows, kv_width), F32), pltpu.VMEM((3, dec_rows, kv_width), LOW),
            pltpu.VMEM((3, dec_rows, kv_width), LOW),
            pltpu.SemaphoreType.DMA((copies,)), pltpu.SemaphoreType.DMA((copies,)),
            pltpu.SemaphoreType.DMA((5,)),
        ],
        compiler_params=pltpu.CompilerParams(
            collective_id=2, has_side_effects=True, vmem_limit_bytes=VMEM_BYTES
        ),
        name="last_chain",
    )(enc_gg, enc_gu, enc_end_grad, enc_mid, enc_x, gains, enc_q, enc_kv, enc_p, dec_one_grad,
      dec_x, self_q, self_kv, self_p, attn_qk, attn_vo, ff_in)


def pair_of(rows, place, size):
    split = rows.reshape(rows.shape[0], size // 2, 2, rows.shape[1] // size)
    return lax.dynamic_index_in_dim(split, place, 2, keepdims=False).reshape(
        rows.shape[0], rows.shape[1] // 2
    )


def dp_sum(left, right):
    size = lax.axis_size("dp")
    place = lax.axis_index("dp")
    block = left.shape[1] // size
    low_bit = place % 2
    send = to_low(dot_first(pair_of(left, 1 - low_bit, size), right))
    keep = dot_first(pair_of(left, low_bit, size), right)
    other = lax.ppermute(send, "dp", [(i, i ^ 1) for i in range(size)])
    current = (keep + other).reshape(size // 2, block, right.shape[1])
    bit = 2
    while bit < size:
        current = current.reshape(current.shape[0] // 2, 2, block, right.shape[1])
        here = (place // bit) % 2
        mine = lax.dynamic_index_in_dim(current, here, 1, keepdims=False)
        send = to_low(lax.dynamic_index_in_dim(current, 1 - here, 1, keepdims=False))
        other = lax.ppermute(send, "dp", [(i, i ^ bit) for i in range(size)])
        current = mine + other
        bit *= 2
    return current.reshape(block, right.shape[1])


def to_owner(pieces):
    out = lax.all_to_all(jnp.stack(pieces), "tensor", 0, 0, tiled=True)
    return out.reshape(out.shape[0] * out.shape[1], out.shape[2])


def attn_weights(query_rows, key_rows, grad_y, grad_q, grad_kv, mixed):
    more = key_rows.shape[0] - query_rows.shape[0]

    def fill(value):
        return jnp.pad(value, ((0, more), (0, 0))) if more else value

    left = to_owner([fill(query_rows), key_rows, key_rows, fill(grad_y)])
    right = to_owner([fill(grad_q), grad_kv[:, :INNER], grad_kv[:, INNER:], fill(mixed)])
    return dp_sum(left, right)


def flat(blocks):
    return blocks.reshape(blocks.shape[0] * blocks.shape[1], blocks.shape[2])


def on_device(
    enc_x, dec_x, dec_cot, item_count, enc_mask, dec_mask, enc_buckets, dec_buckets,
    gains, tables, attn_qk, attn_vo, ff_in, ff_out,
):
    tensor_id = lax.axis_index("tensor")
    enc_own, dec_own = enc_x.shape[0], dec_x.shape[0]
    enc_total = enc_mask.shape[0]
    small, (onehot, dec_onehot, far_back) = prepare(
        item_count, enc_mask, dec_mask, enc_buckets, dec_buckets, tables, enc_own, dec_own
    )
    ff_out_t = jnp.swapaxes(ff_out, 1, 2)
    dec_x, dec_cot = pad_rows(dec_x), pad_rows(dec_cot)
    (
        h0, enc_q, enc_kv, enc_p, enc_o, enc_mid, h1, enc_gelu, enc_slope, enc_hidden, enc_end,
        memory, cross_kv, hs, self_q, self_kv, self_p, self_o, dec_one, hc, cross_q, cross_p,
        cross_o, dec_two, hf, dec_gy, dec_gg, dec_gu, dec_hidden,
    ) = ka_call(enc_x, dec_x, dec_cot, gains, *small, attn_qk, attn_vo, ff_in, ff_out_t)
    dec_ff = [
        dp_sum(flat(hf), flat(dec_gg)),
        dp_sum(flat(hf), flat(dec_gu)),
        dp_sum(flat(dec_gy), flat(dec_hidden)).T,
    ]
    (
        dec_out, cross_gy, cross_gq, cross_gkv, dec_one_grad, enc_end_grad, enc_gy, enc_gg, enc_gu,
        gains_b,
    ) = kb_call(
        dec_gg, dec_gu, dec_hidden, dec_cot, dec_two, dec_one, gains, cross_q, cross_kv, cross_p,
        enc_end, enc_gelu, enc_slope, attn_qk, attn_vo, ff_in, ff_out_t,
    )
    enc_ff = [
        dp_sum(flat(h1), flat(enc_gg)),
        dp_sum(flat(h1), flat(enc_gu)),
        dp_sum(flat(enc_gy), flat(enc_hidden)).T,
    ]
    cross_w = attn_weights(hc, memory, cross_gy, cross_gq, cross_gkv, cross_o)
    (
        enc_grad, enc_ay, enc_gq, enc_gkv, enc_offsets, dec_grad, self_gy, self_gq, self_gkv,
        self_gs, gains_c,
    ) = kc_call(
        enc_gg, enc_gu, enc_end_grad, enc_mid, enc_x, gains, enc_q, enc_kv, enc_p, dec_one_grad,
        dec_x, self_q, self_kv, self_p, attn_qk, attn_vo, ff_in,
    )
    self_w = attn_weights(hs, hs, self_gy, self_gq, self_gkv, self_o)
    enc_w = attn_weights(h0, h0, enc_ay, enc_gq, enc_gkv, enc_o)
    ffin_sum = jnp.stack([jnp.stack(enc_ff[:2]), jnp.stack(dec_ff[:2])])
    ffout_sum = jnp.stack([enc_ff[2], dec_ff[2]])
    attn_all = lax.all_gather(
        to_low(jnp.stack([enc_w, self_w, cross_w])), "tensor", axis=2, tiled=True
    ).astype(F32)
    qk_sum = attn_all[:, :, : 2 * INNER]
    vo_sum = attn_all[:, :, 2 * INNER :]

    padded = jnp.pad(enc_offsets, ((0, 0), (enc_total - enc_own, enc_total)))
    placed = lax.dynamic_slice_in_dim(padded, tensor_id * enc_own, 2 * enc_total - 1, 1)
    enc_table = jnp.dot(placed[:HEADS], onehot, precision=HIGH).T
    self_table = jnp.dot(
        lax.dot_general(
            self_gs.reshape(HEADS, -1).astype(F32), far_back, (((1,), (1,)), ((), ())),
            precision=HIGH,
        ),
        dec_onehot,
        precision=HIGH,
    ).T
    tables_local = jnp.stack([enc_table, self_table])
    gains_sum, tables_sum = lax.psum(((gains_b + gains_c)[:6], tables_local), ("dp", "tensor"))
    return (
        dec_out[:dec_own], enc_grad, dec_grad[:dec_own], gains_sum, tables_sum, qk_sum, vo_sum,
        ffin_sum, ffout_sum,
    )


def solution(mesh):
    rows = P(("dp", "tensor"), None)
    return jax.shard_map(
        on_device,
        mesh=mesh,
        in_specs=(
            rows, rows, rows, P("dp"), P("dp"), P("dp"), P(), P(), P(), P(), P(), P(),
            P(None, None, None, "tensor"), P(None, "tensor", None),
        ),
        out_specs=(
            rows, rows, rows, P(), P(), P(None, "dp", None), P(None, "dp", None),
            P(None, None, "dp", "tensor"), P(None, "tensor", "dp"),
        ),
        check_vma=False,
    )
```

```python
import functools

import jax
import jax.numpy as jnp
from jax import lax
from jax.experimental import pallas as pl
from jax.experimental.pallas import tpu as pltpu
from jax.sharding import PartitionSpec as P

HEADS = 6
HEAD = 64
INNER = HEADS * HEAD
PAIRS = HEADS // 2
PAIR = 2 * HEAD
BUCKETS = 32
EPSILON = 1e-06
MASKED = -1000000000.0
HIGH = lax.Precision.HIGHEST
F32 = jnp.float32
LOW = jnp.bfloat16
DEC_PAD = 32
VMEM_BYTES = 60 * 1024 * 1024
ROOT = 0.7978845608028654
CUBE = 0.044715


def to_low(value):
    return value.astype(LOW)


def dot(left, right):
    return jnp.dot(left, right, preferred_element_type=F32)


def dot_first(left, right):
    return lax.dot_general(left, right, (((0,), (0,)), ((), ())), preferred_element_type=F32)


def dot_last(left, right):
    return lax.dot_general(left, right, (((1,), (1,)), ((), ())), preferred_element_type=F32)


def norm_gain(rows, gain):
    return rows * lax.rsqrt(jnp.mean(rows * rows, axis=-1, keepdims=True) + EPSILON) * gain


def norm_back(rows, gain, grad_rows):
    scale = lax.rsqrt(jnp.mean(rows * rows, axis=-1, keepdims=True) + EPSILON)
    normed = rows * scale
    scaled = grad_rows * gain
    inner = jnp.mean(scaled * normed, axis=-1, keepdims=True)
    grad_gain = jnp.sum(grad_rows * normed, axis=0, keepdims=True)
    return scale * (scaled - normed * inner), grad_gain


def act_parts(gate, up_proj):
    square = gate * gate
    curve = jnp.tanh(ROOT * gate * (1.0 + CUBE * square))
    half = 0.5 * (1.0 + curve)
    slope = half + 0.5 * gate * (1.0 - curve * curve) * (ROOT * (1.0 + 3.0 * CUBE * square))
    return gate * half, up_proj * slope


def tiles(width, step=256):
    return [(start, min(start + step, width)) for start in range(0, width, step)]


class Peers:
    def __init__(self, send_sem, recv_sem):
        dp, tensor = lax.axis_index("dp"), lax.axis_index("tensor")
        chip, core = lax.div(tensor, 2), lax.rem(tensor, 2)
        self.dp = dp
        self.own = tensor
        self.sib = chip * 2 + (1 - core)
        self.far = (1 - chip) * 2 + core
        self.diag = (1 - chip) * 2 + (1 - core)
        self.send_sem, self.recv_sem = send_sem, recv_sem
        self.used = 0
        self.copies = []

    def bit(self, place):
        return lax.rem(lax.div(self.dp, 2**place), 2)

    def across(self, place):
        return (self.dp + (1 - 2 * self.bit(place)) * 2**place, self.own)

    def device(self, peer):
        return peer if isinstance(peer, tuple) else (self.dp, peer)

    def greet(self, more=()):
        barrier = pltpu.get_barrier_semaphore()
        for peer in (self.sib, self.far) + tuple(more):
            pl.semaphore_signal(
                barrier, inc=1, device_id=self.device(peer), device_id_type=pl.DeviceIdType.MESH
            )
        pl.semaphore_wait(barrier, 2 + len(more))

    def send(self, source, target, peer):
        place = self.used
        self.used += 1
        copy = pltpu.make_async_remote_copy(
            src_ref=source,
            dst_ref=target,
            send_sem=self.send_sem.at[place],
            recv_sem=self.recv_sem.at[place],
            device_id=self.device(peer),
            device_id_type=pl.DeviceIdType.MESH,
        )
        copy.start()
        self.copies.append(copy)
        return copy

    def finish(self):
        for copy in self.copies:
            copy.wait_send()


class Gather:
    def __init__(self, peers, buf, near):
        self.peers, self.buf = peers, buf
        if near:
            self.slots = (0, 1, 2, 2, 3)
        else:
            self.slots = (peers.own, peers.own, peers.own, peers.far, peers.far)

    def start(self):
        own, at_sib, at_far, unused, unused = self.slots
        self.to_far = self.peers.send(self.buf.at[own], self.buf.at[at_far], self.peers.far)
        self.to_sib = self.peers.send(self.buf.at[own], self.buf.at[at_sib], self.peers.sib)

    def wait_near(self):
        self.to_sib.wait_recv()

    def relay(self):
        unused, unused, unused, far, far_at_sib = self.slots
        self.to_far.wait_recv()
        self.relayed = self.peers.send(
            self.buf.at[far], self.buf.at[far_at_sib], self.peers.sib
        )

    def wait_far(self):
        self.relayed.wait_recv()


def attend(queries, kv, bias_of, allowed, weights_out, mixed_out):
    rows = queries.shape[0]
    total = kv.shape[0] * kv.shape[1]
    first = lax.broadcasted_iota(jnp.int32, (rows, PAIR), 1) < HEAD
    for pair in range(PAIRS):
        lanes = slice(pair * PAIR, (pair + 1) * PAIR)
        keys = kv[:, :, lanes].reshape(total, PAIR)
        values = kv[:, :, INNER + pair * PAIR : INNER + (pair + 1) * PAIR].reshape(total, PAIR)
        both = queries[:, lanes].astype(F32)
        mixed = []
        for half in range(2):
            head = 2 * pair + half
            here = to_low(jnp.where(first if half == 0 else ~first, both, 0.0))
            scores = dot_last(here, keys)
            if bias_of is not None:
                scores = scores + bias_of(head)
            scores = jnp.where(allowed, scores, MASKED)
            shifted = jnp.exp(scores - jnp.max(scores, axis=-1, keepdims=True))
            weights = shifted / jnp.sum(shifted, axis=-1, keepdims=True)
            weights_out[head] = weights
            mixed.append(dot(to_low(weights), values))
        mixed_out[:, lanes] = to_low(jnp.where(first, mixed[0], mixed[1]))


def attend_back(queries, kv, weights_in, grad_out, grad_q_out, grad_kv_out, grad_s_out):
    rows = queries.shape[0]
    total = kv.shape[0] * kv.shape[1]
    block = kv.shape[1]
    first = lax.broadcasted_iota(jnp.int32, (rows, PAIR), 1) < HEAD
    first_key = lax.broadcasted_iota(jnp.int32, (total, PAIR), 1) < HEAD
    for pair in range(PAIRS):
        lanes = slice(pair * PAIR, (pair + 1) * PAIR)
        value_lanes = slice(INNER + pair * PAIR, INNER + (pair + 1) * PAIR)
        keys = kv[:, :, lanes].reshape(total, PAIR)
        values = kv[:, :, value_lanes].reshape(total, PAIR)
        query = queries[:, lanes]
        grad = grad_out[:, lanes]
        grad_wide = grad.astype(F32)
        grad_q, grad_k, grad_v = [], [], []
        for half in range(2):
            head = 2 * pair + half
            here = to_low(jnp.where(first if half == 0 else ~first, grad_wide, 0.0))
            weights = weights_in[head]
            grad_weights = dot_last(here, values)
            weighted = jnp.sum(weights * grad_weights, axis=-1, keepdims=True)
            grad_scores = to_low(weights * (grad_weights - weighted))
            if grad_s_out is not None:
                grad_s_out[head] = grad_scores
            grad_q.append(dot(grad_scores, keys))
            grad_k.append(dot_first(grad_scores, query))
            grad_v.append(dot_first(to_low(weights), grad))
        grad_q_out[:, lanes] = to_low(jnp.where(first, grad_q[0], grad_q[1]))
        grad_kv_out[:, :, lanes] = jnp.where(first_key, grad_k[0], grad_k[1]).reshape(
            4, block, PAIR
        )
        grad_kv_out[:, :, value_lanes] = jnp.where(first_key, grad_v[0], grad_v[1]).reshape(
            4, block, PAIR
        )


class Exchange:
    def __init__(self, peers, whole, rows):
        partner = peers.across(0)
        self.rows = [
            (peers.send(own.at[0], other.at[0], partner), Gather(peers, other, True))
            for own, other in rows
        ]
        self.whole = [peers.send(own, other, partner) for own, other in whole]

    def spread(self):
        for copy, gather in self.rows:
            copy.wait_recv()
            gather.start()

    def relay(self):
        for unused, gather in self.rows:
            gather.wait_near()
            gather.relay()

    def finish(self):
        for unused, gather in self.rows:
            gather.wait_far()
        for copy in self.whole:
            copy.wait_recv()


class Loads:
    def __init__(self, sems):
        self.sems, self.used = sems, 0

    def start(self, source, target):
        copy = pltpu.make_async_copy(source, target, self.sems.at[self.used])
        self.used += 1
        copy.start()
        return copy


def project_kv(rows, wqk, wvo, target):
    target[:, :INNER] = to_low(dot(rows, wqk[:, INNER:]))
    target[:, INNER:] = to_low(dot(rows, wvo[:, :INNER]))


def ff_up(rows, w_in, gelu_out, slope_out, hidden_out, slots):
    count, block = slots.stop - slots.start, gelu_out.shape[1]
    for low, high in tiles(gelu_out.shape[2]):
        gate = dot(rows, w_in[0, :, low:high])
        up_proj = dot(rows, w_in[1, :, low:high])
        gelu, slope = act_parts(gate, up_proj)
        shape = (count, block, high - low)
        gelu_out[slots, :, low:high] = gelu.reshape(shape)
        slope_out[slots, :, low:high] = slope.reshape(shape)
        hidden_out[slots, :, low:high] = to_low(gelu * up_proj).reshape(shape)


def reduce_far(peers, diag_part, far_part, send, recv):
    width = send.shape[2]
    for low, high in tiles(width):
        send[0, :, low:high] = to_low(diag_part(low, high))
    first = peers.send(send.at[0], recv.at[0], peers.sib)
    first.wait_recv()
    for low, high in tiles(width):
        send[2, :, low:high] = to_low(
            far_part(low, high) + recv[0, :, low:high].astype(F32)
        )
    return peers.send(send.at[2], recv.at[2], peers.far)


def ka_kernel(
    enc_x, dec_x, dec_cot, gains, enc_terms, enc_code, enc_item, self_mask, self_bias, dec_item,
    qk_all, vo_all, fi_all, fo_all,
    h0, enc_q, enc_kv, enc_p, enc_o, enc_mid, h1, enc_gelu, enc_slope, enc_hidden, enc_end, memory,
    cross_kv, hs, self_q, self_kv, self_p, self_o, dec_one, hc, cross_q, cross_p, cross_o, dec_two,
    hf, dec_gy, dec_gg, dec_gu, dec_hidden,
    wqk, wvo, wfi, wfo, part, send, recv, dec_gelu, dec_slope, send_sem, recv_sem, load_sem,
):
    peers = Peers(send_sem, recv_sem)
    loads = Loads(load_sem)
    get_qk, get_vo, get_fi, get_fo = {}, {}, {}, {}
    for a in (0, 1):
        get_qk[a] = loads.start(qk_all.at[a], wqk.at[a])
        get_vo[a] = loads.start(vo_all.at[a], wvo.at[a])
    get_fi[0] = loads.start(fi_all.at[0], wfi.at[0])
    get_fo[0] = loads.start(fo_all.at[0], wfo.at[0])
    get_qk[2] = loads.start(qk_all.at[2], wqk.at[2])
    get_vo[2] = loads.start(vo_all.at[2], wvo.at[2])
    get_fi[1] = loads.start(fi_all.at[1], wfi.at[1])
    get_fo[1] = loads.start(fo_all.at[1], wfo.at[1])
    peers.greet()

    normed = to_low(norm_gain(enc_x[...].astype(F32), gains[0:1]))
    h0[...] = normed
    get_qk[0].wait()
    get_vo[0].wait()
    project_kv(normed, wqk.at[0], wvo.at[0], enc_kv.at[peers.own])
    enc_gather = Gather(peers, enc_kv, False)
    enc_gather.start()
    normed_dec = to_low(norm_gain(dec_x[...].astype(F32), gains[3:4]))
    hs[...] = normed_dec
    get_qk[1].wait()
    get_vo[1].wait()
    project_kv(normed_dec, wqk.at[1], wvo.at[1], self_kv.at[peers.own])
    self_gather = Gather(peers, self_kv, False)
    self_gather.start()
    dec_gy[0] = dec_cot[...]
    gy_gather = Gather(peers, dec_gy, True)
    gy_gather.start()
    enc_q[...] = to_low(dot(normed, wqk[0, :, :INNER]))
    self_q[...] = to_low(dot(normed_dec, wqk[1, :, :INNER]))

    enc_gather.wait_near()
    enc_gather.relay()
    enc_allowed = enc_item[...] == enc_code[...]

    def enc_bias(head):
        own_rows, period = h0.shape[0], enc_terms.shape[1]
        spread = jnp.broadcast_to(enc_terms[head : head + 1, :], (own_rows, period))
        rolled = pltpu.roll(spread, 0, 1, stride=1, stride_axis=0)
        return rolled[:, : period // 2]

    enc_gather.wait_far()
    attend(enc_q[...], enc_kv, enc_bias, enc_allowed, enc_p, enc_o)
    for low, high in tiles(enc_mid.shape[1]):
        enc_mid[:, low:high] = enc_x[:, low:high].astype(F32) + dot_last(
            enc_o[...], wvo[0, low:high, INNER:]
        )
    h1[0] = to_low(norm_gain(enc_mid[...], gains[1:2]))
    h1_gather = Gather(peers, h1, True)
    h1_gather.start()

    self_gather.wait_near()
    self_gather.relay()
    gy_gather.wait_near()
    gy_gather.relay()
    self_gather.wait_far()
    gy_gather.wait_far()
    attend(
        self_q[...], self_kv, lambda head: self_bias[head], self_mask[...] > 0.5, self_p, self_o
    )
    for low, high in tiles(dec_one.shape[1]):
        dec_one[:, low:high] = dec_x[:, low:high].astype(F32) + dot_last(
            self_o[...], wvo[1, low:high, INNER:]
        )
    normed_dec = to_low(norm_gain(dec_one[...], gains[4:5]))
    hc[...] = normed_dec

    h1_gather.wait_near()
    get_fi[0].wait()
    get_fo[0].wait()
    block, width = h1.shape[1], h1.shape[2]

    def both(buf, slots):
        return buf[slots].reshape((slots.stop - slots.start) * block, buf.shape[2])

    near, away = slice(0, 2), slice(2, 4)
    ff_up(both(h1, near), wfi.at[0], enc_gelu, enc_slope, enc_hidden, near)
    h1_gather.relay()
    h1_gather.wait_far()
    ff_up(both(h1, away), wfi.at[0], enc_gelu, enc_slope, enc_hidden, away)
    hidden = both(enc_hidden, away)
    for low, high in tiles(width):
        value = dot_last(hidden, wfo[0, low:high, :])
        part[:, low:high] = value[:block]
        send[0, :, low:high] = to_low(value[block:])
    first = peers.send(send.at[0], recv.at[0], peers.sib)
    get_qk[2].wait()
    get_vo[2].wait()
    cross_q[...] = to_low(dot(hc[...], wqk[2, :, :INNER]))
    first.wait_recv()
    send[2] = to_low(part[...] + recv[0].astype(F32))
    second = peers.send(send.at[2], recv.at[2], peers.far)
    hidden = both(enc_hidden, near)
    for low, high in tiles(width):
        value = dot_last(hidden, wfo[0, low:high, :])
        part[:, low:high] = value[:block] + enc_mid[:, low:high]
        send[1, :, low:high] = to_low(value[block:])
    third = peers.send(send.at[1], recv.at[1], peers.sib)
    third.wait_recv()
    part[...] = part[...] + recv[1].astype(F32)
    second.wait_recv()
    ended = part[...] + recv[2].astype(F32)
    enc_end[...] = ended
    normed = to_low(norm_gain(ended, gains[2:3]))
    memory[...] = normed

    project_kv(normed, wqk.at[2], wvo.at[2], cross_kv.at[peers.own])
    cross_gather = Gather(peers, cross_kv, False)
    cross_gather.start()
    get_fi[1].wait()
    get_fo[1].wait()
    cross_allowed = dec_item[...] == enc_code[...]
    cross_gather.wait_near()
    cross_gather.relay()
    cross_gather.wait_far()
    attend(cross_q[...], cross_kv, None, cross_allowed, cross_p, cross_o)
    for low, high in tiles(dec_two.shape[1]):
        dec_two[:, low:high] = dec_one[:, low:high] + dot_last(
            cross_o[...], wvo[2, low:high, INNER:]
        )
    hf[0] = to_low(norm_gain(dec_two[...], gains[5:6]))
    hf_gather = Gather(peers, hf, True)
    hf_gather.start()

    rows = hf.shape[0] * hf.shape[1]
    hf_gather.wait_near()
    hf_gather.relay()
    grad_y = dec_gy[...].reshape(rows, width)
    hf_gather.wait_far()
    ff_up(hf[...].reshape(rows, width), wfi.at[1], dec_gelu, dec_slope, dec_hidden, slice(0, 4))
    for low, high in tiles(dec_gelu.shape[2]):
        grad_h = dot(grad_y, wfo[1, :, low:high]).reshape(4, hf.shape[1], high - low)
        dec_gg[:, :, low:high] = to_low(grad_h * dec_slope[:, :, low:high])
        dec_gu[:, :, low:high] = to_low(grad_h * dec_gelu[:, :, low:high])
    peers.finish()


def ka_call(enc_x, dec_x, dec_cot, gains, enc_terms, enc_code, enc_item, self_mask, self_bias,
            dec_item, attn_qk, attn_vo, ff_in, ff_out):
    rows, width = enc_x.shape
    dec_rows = dec_x.shape[0]
    units = ff_in.shape[3]
    total = enc_code.shape[1]
    kv_width = 2 * INNER
    shape = jax.ShapeDtypeStruct
    outs = [
        shape((rows, width), LOW), shape((rows, INNER), LOW), shape((4, rows, kv_width), LOW),
        shape((HEADS, rows, total), F32), shape((rows, INNER), LOW), shape((rows, width), F32),
        shape((4, rows, width), LOW), shape((4, rows, units), F32), shape((4, rows, units), F32),
        shape((4, rows, units), LOW), shape((rows, width), F32), shape((rows, width), LOW),
        shape((4, rows, kv_width), LOW),
        shape((dec_rows, width), LOW), shape((dec_rows, INNER), LOW),
        shape((4, dec_rows, kv_width), LOW), shape((HEADS, dec_rows, 4 * dec_rows), F32),
        shape((dec_rows, INNER), LOW), shape((dec_rows, width), F32),
        shape((dec_rows, width), LOW), shape((dec_rows, INNER), LOW),
        shape((HEADS, dec_rows, total), F32), shape((dec_rows, INNER), LOW),
        shape((dec_rows, width), F32),
        shape((4, dec_rows, width), LOW), shape((4, dec_rows, width), LOW),
        shape((4, dec_rows, units), LOW), shape((4, dec_rows, units), LOW),
        shape((4, dec_rows, units), LOW),
    ]
    vmem = pl.BlockSpec(memory_space=pltpu.VMEM)
    hbm = pl.BlockSpec(memory_space=pltpu.HBM)
    copies = 3 * 6 + 3
    return pl.pallas_call(
        ka_kernel,
        out_shape=outs,
        in_specs=[vmem] * 10 + [hbm] * 4,
        out_specs=[vmem] * len(outs),
        scratch_shapes=[
            pltpu.VMEM(attn_qk.shape, LOW), pltpu.VMEM(attn_vo.shape, LOW),
            pltpu.VMEM(ff_in.shape, LOW), pltpu.VMEM(ff_out.shape, LOW),
            pltpu.VMEM((rows, width), F32), pltpu.VMEM((3, rows, width), LOW),
            pltpu.VMEM((3, rows, width), LOW), pltpu.VMEM((4, dec_rows, units), F32),
            pltpu.VMEM((4, dec_rows, units), F32),
            pltpu.SemaphoreType.DMA((copies,)), pltpu.SemaphoreType.DMA((copies,)),
            pltpu.SemaphoreType.DMA((10,)),
        ],
        compiler_params=pltpu.CompilerParams(
            collective_id=0, has_side_effects=True, vmem_limit_bytes=VMEM_BYTES
        ),
        name="forward_chain",
    )(enc_x, dec_x, dec_cot, gains, enc_terms, enc_code, enc_item, self_mask, self_bias, dec_item,
      attn_qk, attn_vo, ff_in, ff_out)


def pad_rows(value, rows=DEC_PAD):
    return jnp.pad(value, ((0, rows - value.shape[0]), (0, 0)))


def prepare(item_count, enc_mask, dec_mask, enc_buckets, dec_buckets, tables, enc_own, dec_own):
    tensor_id = lax.axis_index("tensor")
    enc_total, dec_total = enc_mask.shape[0], dec_mask.shape[0]
    count = item_count[0]
    enc_len, dec_len = enc_total // count, dec_total // count
    enc_code = jnp.where(enc_mask == 1, jnp.arange(enc_total) // enc_len, -1)
    enc_item = (tensor_id * enc_own + jnp.arange(enc_own)) // enc_len
    slot = jnp.arange(4 * DEC_PAD)
    inside = slot % DEC_PAD
    place = slot // DEC_PAD * dec_own + inside
    real = inside < dec_own
    row = jnp.arange(DEC_PAD)
    row_real = row < dec_own
    row_place = tensor_id * dec_own + row
    dec_live = jnp.pad(dec_mask.reshape(4, dec_own), ((0, 0), (0, DEC_PAD - dec_own))).reshape(-1)
    key_item = jnp.where(real & (dec_live == 1), place // dec_len, -1)
    dec_item = jnp.where(row_real, row_place // dec_len, -2)
    self_mask = (
        (dec_item[:, None] == key_item[None, :]) & (place[None, :] <= row_place[:, None])
    ).astype(F32)
    onehot = (enc_buckets[:, None] == jnp.arange(BUCKETS)[None, :]).astype(F32)
    terms = jnp.dot(tables[0].T, onehot.T, precision=HIGH)
    terms = jnp.pad(terms, ((0, 2), (0, 1)))
    period = 2 * enc_total
    doubled = jnp.concatenate([terms, terms], axis=1)
    shift = (enc_total - 1 - tensor_id * enc_own + period) % period
    enc_terms = lax.dynamic_slice_in_dim(doubled, shift, period, 1)
    far_back = jnp.clip(row_place[:, None] - place[None, :], 0, dec_total - 1)
    far_back = (far_back[None] == jnp.arange(dec_total)[:, None, None]).astype(F32)
    far_back = far_back.reshape(dec_total, -1)
    dec_onehot = (dec_buckets[:, None] == jnp.arange(BUCKETS)[None, :]).astype(F32)
    dec_terms = jnp.dot(tables[1].T, dec_onehot.T, precision=HIGH)
    self_bias = jnp.dot(dec_terms, far_back, precision=HIGH).reshape(
        HEADS, DEC_PAD, 4 * DEC_PAD
    )
    return (
        enc_terms, enc_code.astype(F32)[None, :], enc_item.astype(F32)[:, None], self_mask,
        self_bias, dec_item.astype(F32)[:, None],
    ), (onehot, dec_onehot, far_back)


def kv_back(grad_kv, wqk, wvo, low, high):
    return dot_last(grad_kv[:, :INNER], wqk[low:high, INNER:]) + dot_last(
        grad_kv[:, INNER:], wvo[low:high, :INNER]
    )


class SumBlocks:
    def __init__(self, peers, buf, send, recv):
        self.peers, self.buf, self.send, self.recv = peers, buf, send, recv
        send[0] = to_low(buf[peers.diag])
        send[1] = to_low(buf[peers.sib])
        self.first = peers.send(send.at[0], recv.at[0], peers.sib)
        self.third = peers.send(send.at[1], recv.at[1], peers.sib)

    def cross(self):
        peers = self.peers
        self.first.wait_recv()
        self.send[2] = to_low(self.buf[peers.far] + self.recv[0].astype(F32))
        self.second = peers.send(self.send.at[2], self.recv.at[2], peers.far)

    def result(self):
        self.third.wait_recv()
        value = self.buf[self.peers.own] + self.recv[1].astype(F32)
        self.second.wait_recv()
        return value + self.recv[2].astype(F32)


class SumNear:
    def __init__(self, peers, part_of, block, total, send, recv):
        self.peers, self.total, self.send, self.recv = peers, total, send, recv
        for low, high in tiles(send.shape[2]):
            value = part_of(low, high)
            total[0, :, low:high] = value[:block]
            send[1, :, low:high] = to_low(value[block : 2 * block])
            total[1, :, low:high] = value[2 * block : 3 * block]
            send[0, :, low:high] = to_low(value[3 * block :])
        self.first = peers.send(send.at[0], recv.at[0], peers.sib)
        self.third = peers.send(send.at[1], recv.at[1], peers.sib)

    def cross(self):
        self.first.wait_recv()
        self.send[2] = to_low(self.total[1] + self.recv[0].astype(F32))
        self.second = self.peers.send(self.send.at[2], self.recv.at[2], self.peers.far)

    def result(self):
        self.third.wait_recv()
        value = self.total[0] + self.recv[1].astype(F32)
        self.second.wait_recv()
        return value + self.recv[2].astype(F32)


def kb_kernel(
    dec_gg, dec_gu, dec_hidden, dec_cot, dec_two, dec_one, gains, cross_q, cross_kv, cross_p,
    enc_end, enc_gelu, enc_slope, qk_all, vo_all, fi_all, fo_all, hf, dec_gy, h1, enc_hidden,
    dec_out, cross_gy, cross_gq, cross_gkv, dec_one_grad, enc_end_grad, enc_gy, enc_gg, enc_gu,
    gains_grad, x_dec_gg, x_dec_gu, x_dec_hidden, x_hf, x_dec_gy, x_h1, x_enc_hidden,
    wqk, wvo, wfi, wfo, grad_kv, kv_send, kv_recv, row_total, row_send, row_recv, out_total,
    out_send, out_recv, send_sem, recv_sem, load_sem,
):
    peers = Peers(send_sem, recv_sem)
    loads = Loads(load_sem)
    get_fi = loads.start(fi_all.at[1], wfi)
    get_vo = loads.start(vo_all.at[2], wvo)
    get_qk = loads.start(qk_all.at[2], wqk)
    get_fo1 = loads.start(fo_all.at[1], wfo.at[1])
    get_fo0 = loads.start(fo_all.at[0], wfo.at[0])
    peers.greet([peers.across(0)])
    exchange = Exchange(
        peers,
        [(dec_gg, x_dec_gg), (dec_gu, x_dec_gu), (dec_hidden, x_dec_hidden),
         (enc_hidden, x_enc_hidden)],
        [(hf, x_hf), (dec_gy, x_dec_gy), (h1, x_h1)],
    )
    width = dec_two.shape[1]
    block = dec_two.shape[0]
    units = dec_gg.shape[2]
    gains_grad[...] = jnp.zeros_like(gains_grad)

    get_fi.wait()
    gate, up_proj = dec_gg[...].reshape(4 * block, units), dec_gu[...].reshape(4 * block, units)

    def grad_rows_part(low, high):
        return dot_last(gate, wfi[0, low:high, :]) + dot_last(up_proj, wfi[1, low:high, :])

    grad_rows = SumNear(peers, grad_rows_part, block, row_total, row_send, row_recv)
    grad_rows.cross()
    get_vo.wait()
    get_qk.wait()
    value, gain_row = norm_back(dec_two[...], gains[5:6], grad_rows.result())
    gains_grad[5:6] = gain_row
    residual = dec_cot[...].astype(F32) + value
    grad_y = to_low(residual)
    cross_gy[...] = grad_y

    grad_out = to_low(dot(grad_y, wvo[:, INNER:]))
    attend_back(cross_q[...], cross_kv, cross_p, grad_out, cross_gq, grad_kv, None)
    kv_sum = SumBlocks(peers, grad_kv, kv_send, kv_recv)
    kv_sum.cross()
    for low, high in tiles(width):
        row_total[0, :, low:high] = dot_last(cross_gq[...], wqk[low:high, :INNER])
    value, gain_row = norm_back(dec_one[...], gains[4:5], row_total[0])
    gains_grad[4:5] = gain_row
    dec_one_grad[...] = residual + value
    own_kv = to_low(kv_sum.result())
    cross_gkv[...] = own_kv
    for low, high in tiles(width):
        enc_end_grad[:, low:high] = kv_back(own_kv, wqk, wvo, low, high)
    value, gain_row = norm_back(enc_end[...], gains[2:3], enc_end_grad[...])
    gains_grad[2:3] = gain_row
    enc_end_grad[...] = value
    enc_gy[0] = to_low(value)
    gy_gather = Gather(peers, enc_gy, True)
    gy_gather.start()

    get_fo1.wait()
    hidden = dec_hidden[...].reshape(4 * block, units)
    out_sum = SumNear(
        peers, lambda low, high: dot_last(hidden, wfo[1, low:high, :]), block, out_total,
        out_send, out_recv,
    )

    exchange.spread()
    get_fo0.wait()
    rows = enc_gy.shape[1]

    def gate_grads(slots):
        grad_y = enc_gy[slots].reshape(2 * rows, width)
        for low, high in tiles(units):
            grad_h = dot(grad_y, wfo[0, :, low:high]).reshape(2, rows, high - low)
            enc_gg[slots, :, low:high] = to_low(grad_h * enc_slope[slots, :, low:high])
            enc_gu[slots, :, low:high] = to_low(grad_h * enc_gelu[slots, :, low:high])

    gy_gather.wait_near()
    gate_grads(slice(0, 2))
    gy_gather.relay()
    out_sum.cross()
    gy_gather.wait_far()
    gate_grads(slice(2, 4))
    exchange.relay()
    dec_out[...] = to_low(dec_two[...] + out_sum.result())
    exchange.finish()
    peers.finish()


def kb_call(dec_gg, dec_gu, dec_hidden, dec_cot, dec_two, dec_one, gains, cross_q, cross_kv,
            cross_p, enc_end, enc_gelu, enc_slope, attn_qk, attn_vo, ff_in, ff_out, hf, dec_gy, h1,
            enc_hidden):
    rows, width = enc_end.shape
    dec_rows = dec_two.shape[0]
    units = ff_in.shape[3]
    kv_width = 2 * INNER
    shape = jax.ShapeDtypeStruct
    outs = [
        shape((dec_rows, width), LOW), shape((dec_rows, width), LOW),
        shape((dec_rows, INNER), LOW), shape((rows, kv_width), LOW), shape((dec_rows, width), F32),
        shape((rows, width), F32), shape((4, rows, width), LOW), shape((4, rows, units), LOW),
        shape((4, rows, units), LOW), shape((8, width), F32),
    ]
    traded = [shape(value.shape, LOW) for value in (dec_gg, dec_gu, dec_hidden, hf, dec_gy, h1,
                                                    enc_hidden)]
    vmem = pl.BlockSpec(memory_space=pltpu.VMEM)
    hbm = pl.BlockSpec(memory_space=pltpu.HBM)
    copies = 3 * 3 + 3 + len(traded) + 9
    return pl.pallas_call(
        kb_kernel,
        out_shape=outs + traded,
        in_specs=[vmem] * 13 + [hbm] * 8,
        out_specs=[vmem] * len(outs) + [hbm] * len(traded),
        scratch_shapes=[
            pltpu.VMEM(attn_qk.shape[1:], LOW), pltpu.VMEM(attn_vo.shape[1:], LOW),
            pltpu.VMEM(ff_in.shape[1:], LOW), pltpu.VMEM(ff_out.shape, LOW),
            pltpu.VMEM((4, rows, kv_width), F32), pltpu.VMEM((3, rows, kv_width), LOW),
            pltpu.VMEM((3, rows, kv_width), LOW), pltpu.VMEM((2, dec_rows, width), F32),
            pltpu.VMEM((3, dec_rows, width), LOW), pltpu.VMEM((3, dec_rows, width), LOW),
            pltpu.VMEM((2, dec_rows, width), F32), pltpu.VMEM((3, dec_rows, width), LOW),
            pltpu.VMEM((3, dec_rows, width), LOW),
            pltpu.SemaphoreType.DMA((copies,)), pltpu.SemaphoreType.DMA((copies,)),
            pltpu.SemaphoreType.DMA((5,)),
        ],
        compiler_params=pltpu.CompilerParams(
            collective_id=1, has_side_effects=True, vmem_limit_bytes=VMEM_BYTES
        ),
        name="middle_chain",
    )(dec_gg, dec_gu, dec_hidden, dec_cot, dec_two, dec_one, gains, cross_q, cross_kv, cross_p,
      enc_end, enc_gelu, enc_slope, attn_qk, attn_vo, ff_in, ff_out, hf, dec_gy, h1, enc_hidden)


def kc_kernel(
    enc_gg, enc_gu, enc_end_grad, enc_mid, enc_x, gains, enc_q, enc_kv, enc_p, dec_one_grad, dec_x,
    self_q, self_kv, self_p, qk_all, vo_all, fi_all, enc_gy,
    enc_grad, enc_ay, enc_gq, enc_gkv, enc_offsets, dec_grad, self_gy, self_gq, self_gkv, self_gs,
    gains_grad, x_enc_gg, x_enc_gu, x_enc_gy,
    wqk, wvo, wfi, enc_gs, part, send, recv, enc_gkv_full, kv_send, kv_recv, self_gkv_full,
    self_send, self_recv, send_sem, recv_sem, load_sem,
):
    peers = Peers(send_sem, recv_sem)
    loads = Loads(load_sem)
    get_fi = loads.start(fi_all.at[0], wfi)
    get_vo1 = loads.start(vo_all.at[1], wvo.at[1])
    get_qk1 = loads.start(qk_all.at[1], wqk.at[1])
    get_vo0 = loads.start(vo_all.at[0], wvo.at[0])
    get_qk0 = loads.start(qk_all.at[0], wqk.at[0])
    peers.greet([peers.across(0)])
    exchange = Exchange(peers, [(enc_gg, x_enc_gg), (enc_gu, x_enc_gu)], [(enc_gy, x_enc_gy)])
    rows, width = enc_mid.shape
    units = enc_gg.shape[2]
    gains_grad[...] = jnp.zeros_like(gains_grad)

    get_fi.wait()

    def grad_part(slots, low, high):
        gate = enc_gg[slots].reshape(2 * rows, units)
        up_proj = enc_gu[slots].reshape(2 * rows, units)
        return dot_last(gate, wfi[0, low:high, :]) + dot_last(up_proj, wfi[1, low:high, :])

    for low, high in tiles(width):
        value = grad_part(slice(2, 4), low, high)
        part[:, low:high] = value[:rows]
        send[0, :, low:high] = to_low(value[rows:])
    first = peers.send(send.at[0], recv.at[0], peers.sib)
    get_vo1.wait()
    residual_dec = dec_one_grad[...]
    grad_y = to_low(residual_dec)
    self_gy[...] = grad_y
    grad_out_dec = to_low(dot(grad_y, wvo[1, :, INNER:]))
    first.wait_recv()
    send[2] = to_low(part[...] + recv[0].astype(F32))
    second = peers.send(send.at[2], recv.at[2], peers.far)
    for low, high in tiles(width):
        value = grad_part(slice(0, 2), low, high)
        part[:, low:high] = value[:rows]
        send[1, :, low:high] = to_low(value[rows:])
    third = peers.send(send.at[1], recv.at[1], peers.sib)

    attend_back(self_q[...], self_kv, self_p, grad_out_dec, self_gq, self_gkv_full, self_gs)
    self_sum = SumBlocks(peers, self_gkv_full, self_send, self_recv)
    self_sum.cross()

    third.wait_recv()
    part[...] = part[...] + recv[1].astype(F32)
    second.wait_recv()
    get_vo0.wait()
    value, gain_row = norm_back(enc_mid[...], gains[1:2], part[...] + recv[2].astype(F32))
    gains_grad[1:2] = gain_row
    residual = enc_end_grad[...] + value
    grad_y = to_low(residual)
    enc_ay[...] = grad_y
    enc_grad[...] = residual

    exchange.spread()
    grad_out = to_low(dot(grad_y, wvo[0, :, INNER:]))
    attend_back(enc_q[...], enc_kv, enc_p, grad_out, enc_gq, enc_gkv_full, enc_gs)
    enc_sum = SumBlocks(peers, enc_gkv_full, kv_send, kv_recv)
    get_qk0.wait()
    for low, high in tiles(width):
        part[:, low:high] = dot_last(enc_gq[...], wqk[0, low:high, :INNER])
    enc_sum.cross()

    get_qk1.wait()
    own_kv = to_low(self_sum.result())
    self_gkv[...] = own_kv
    for low, high in tiles(width):
        dec_grad[:, low:high] = dot_last(self_gq[...], wqk[1, low:high, :INNER]) + kv_back(
            own_kv, wqk.at[1], wvo.at[1], low, high
        )
    value, gain_row = norm_back(dec_x[...].astype(F32), gains[3:4], dec_grad[...])
    gains_grad[3:4] = gain_row
    dec_grad[...] = residual_dec + value

    turn = lax.broadcasted_iota(jnp.int32, (rows, rows), 0) + lax.broadcasted_iota(
        jnp.int32, (rows, rows), 1
    )
    turn = jnp.where(turn == rows - 1, 1.0, 0.0).astype(LOW)
    enc_offsets[...] = jnp.zeros_like(enc_offsets)
    for head in range(HEADS):
        turned = dot(turn, enc_gs[head])
        spread = jnp.concatenate([turned, jnp.zeros((rows, rows), F32)], axis=1)
        spread = pltpu.roll(spread, 0, 1, stride=1, stride_axis=0)
        enc_offsets[head : head + 1, :] = jnp.sum(spread, axis=0, keepdims=True)

    exchange.relay()
    own_kv = to_low(enc_sum.result())
    enc_gkv[...] = own_kv
    for low, high in tiles(width):
        part[:, low:high] += kv_back(own_kv, wqk.at[0], wvo.at[0], low, high)
    value, gain_row = norm_back(enc_x[...].astype(F32), gains[0:1], part[...])
    gains_grad[0:1] = gain_row
    enc_grad[...] += value
    exchange.finish()
    peers.finish()


def kc_call(enc_gg, enc_gu, enc_end_grad, enc_mid, enc_x, gains, enc_q, enc_kv, enc_p,
            dec_one_grad, dec_x, self_q, self_kv, self_p, attn_qk, attn_vo, ff_in, enc_gy):
    rows, width = enc_x.shape
    dec_rows = dec_x.shape[0]
    units = ff_in.shape[3]
    kv_width = 2 * INNER
    total = 4 * rows
    shape = jax.ShapeDtypeStruct
    outs = [
        shape((rows, width), F32), shape((rows, width), LOW), shape((rows, INNER), LOW),
        shape((rows, kv_width), LOW), shape((8, total + rows), F32),
        shape((dec_rows, width), F32), shape((dec_rows, width), LOW),
        shape((dec_rows, INNER), LOW), shape((dec_rows, kv_width), LOW),
        shape((HEADS, dec_rows, 4 * dec_rows), LOW), shape((8, width), F32),
    ]
    traded = [shape(value.shape, LOW) for value in (enc_gg, enc_gu, enc_gy)]
    vmem = pl.BlockSpec(memory_space=pltpu.VMEM)
    hbm = pl.BlockSpec(memory_space=pltpu.HBM)
    copies = 3 * 3 + len(traded) + 3
    return pl.pallas_call(
        kc_kernel,
        out_shape=outs + traded,
        in_specs=[vmem] * 14 + [hbm] * 4,
        out_specs=[vmem] * len(outs) + [hbm] * len(traded),
        scratch_shapes=[
            pltpu.VMEM((2,) + attn_qk.shape[1:], LOW), pltpu.VMEM((2,) + attn_vo.shape[1:], LOW),
            pltpu.VMEM(ff_in.shape[1:], LOW), pltpu.VMEM((HEADS, rows, total), LOW),
            pltpu.VMEM((rows, width), F32), pltpu.VMEM((3, rows, width), LOW),
            pltpu.VMEM((3, rows, width), LOW),
            pltpu.VMEM((4, rows, kv_width), F32), pltpu.VMEM((3, rows, kv_width), LOW),
            pltpu.VMEM((3, rows, kv_width), LOW),
            pltpu.VMEM((4, dec_rows, kv_width), F32), pltpu.VMEM((3, dec_rows, kv_width), LOW),
            pltpu.VMEM((3, dec_rows, kv_width), LOW),
            pltpu.SemaphoreType.DMA((copies,)), pltpu.SemaphoreType.DMA((copies,)),
            pltpu.SemaphoreType.DMA((5,)),
        ],
        compiler_params=pltpu.CompilerParams(
            collective_id=2, has_side_effects=True, vmem_limit_bytes=VMEM_BYTES
        ),
        name="last_chain",
    )(enc_gg, enc_gu, enc_end_grad, enc_mid, enc_x, gains, enc_q, enc_kv, enc_p, dec_one_grad,
      dec_x, self_q, self_kv, self_p, attn_qk, attn_vo, ff_in, enc_gy)


CHUNK = 256
LAG = 2


class Reduce:
    def __init__(self, peers, places, product, columns, total, send, recv, slot, finish, ships):
        self.ships = ships
        self.peers, self.places, self.product, self.columns = peers, places, product, columns
        self.total, self.send, self.recv, self.slot, self.done = total, send, recv, slot, finish
        self.steps = len(places) + 1

    def buffers(self, step):
        lanes = pl.ds(0, self.columns)
        return (
            self.send[step].at[self.slot % self.send[step].shape[0], :, lanes],
            self.recv[step].at[self.slot, :, lanes],
        )

    def ship(self, step, value, place):
        source, target = self.buffers(step)
        key = (id(self.send), step, self.slot % self.send[step].shape[0])
        if key in self.ships:
            self.ships[key].wait_send()
            self.peers.copies = [c for c in self.peers.copies if c is not self.ships[key]]
        source[...] = to_low(value)
        self.copy = self.peers.send(source, target, self.peers.across(place))
        self.ships[key] = self.copy

    def run(self, step):
        lanes = pl.ds(0, self.columns)
        if step == 0:
            here = self.peers.bit(self.places[0])
            self.ship(0, self.product(1 - here), self.places[0])
            self.height = self.send[0].shape[1]
            self.start = 0
            self.total[: self.height, lanes] = self.product(here)
            return
        self.copy.wait_recv()
        arrived = self.buffers(step - 1)[1]
        if step == self.steps - 1:
            rows = pl.ds(self.start, self.height)
            self.done(self.total[rows, lanes] + arrived[...].astype(F32))
            return
        self.height //= 2
        place = self.places[step]
        here = self.peers.bit(place)
        away = pl.multiple_of(self.start + (1 - here) * self.height, 16)
        kept = pl.multiple_of(self.start + here * self.height, 16)
        from_away = pl.multiple_of((1 - here) * self.height, 16)
        from_kept = pl.multiple_of(here * self.height, 16)
        self.ship(
            step,
            self.total[pl.ds(away, self.height), lanes]
            + arrived[pl.ds(from_away, self.height), :].astype(F32),
            place,
        )
        self.total[pl.ds(kept, self.height), lanes] += arrived[
            pl.ds(from_kept, self.height), :
        ].astype(F32)
        self.start = kept


class Spread:
    def __init__(self, peers, partners, total, recv):
        self.peers, self.partners, self.total, self.recv = peers, partners, total, recv
        self.steps = len(partners) + 1

    def run(self, step):
        if step:
            self.copy.wait_recv()
            self.total[step] = self.total[step - 1] + self.recv[step - 1]
        if step < len(self.partners):
            self.copy = self.peers.send(
                self.total.at[step], self.recv.at[step], self.partners[step]
            )


def to_owners(peers, sources, target, rows_of):
    sends = []
    for peer in (peers.far, peers.diag, peers.sib):
        place = peers.used
        peers.used += 1
        for role in range(4):
            rows = rows_of[role]

            def copy(role=role, rows=rows, place=place, peer=peer):
                return pltpu.make_async_remote_copy(
                    src_ref=sources[role],
                    dst_ref=target.at[peers.own, pl.ds(0, rows)],
                    send_sem=peers.send_sem.at[place],
                    recv_sem=peers.recv_sem.at[place],
                    device_id=peers.device(peer),
                    device_id_type=pl.DeviceIdType.MESH,
                )

            @pl.when(peer == role)
            def _(copy=copy):
                copy().start()

            sends.append((peer, role, copy))
    return sends


def owners_recv(peers, sends):
    for unused, role, copy in sends:

        @pl.when(peers.own == role)
        def _(copy=copy):
            copy().wait_recv()


def owners_sent(peers, sends):
    for peer, role, copy in sends:

        @pl.when(peer == role)
        def _(copy=copy):
            copy().wait_send()


def kd_kernel(
    select, small, enc_gg, enc_gu, enc_hidden, x_enc_gg, x_enc_gu, x_enc_hidden,
    dec_gg, dec_gu, dec_hidden, x_dec_gg, x_dec_gu, x_dec_hidden,
    hf, x_hf, dec_gy, x_dec_gy,
    h0, enc_ay, enc_gq, enc_gk, enc_gv, enc_o, hs, self_gy, self_gq, self_gk, self_gv, self_o,
    hc, memory, cross_gy, cross_gq, cross_gk, cross_gv, cross_o,
    h1, x_h1, enc_gy, x_enc_gy,
    ffin, ffout, attn, small_out,
    stage, chosen, chosen_attn, left_enc, left_cross, left_self, right_enc, right_cross, right_self,
    total, attn_total, small_total, small_recv, attn_mine, *rest,
    block, steps,
):
    ff_steps, attn_steps = steps - 1, steps
    ff_send, ff_recv = rest[:ff_steps], rest[ff_steps : 2 * ff_steps]
    rest = rest[2 * ff_steps :]
    at_send, at_recv = rest[:attn_steps], rest[attn_steps : 2 * attn_steps]
    send_sem, recv_sem, load_sem, own_sem = rest[2 * attn_steps :]
    peers = Peers(send_sem, recv_sem)
    loads = Loads(load_sem)

    def fetch(sources):
        return [
            loads.start(source, stage.at[pl.ds(4 * part, 4)])
            for part, source in enumerate(sources)
        ]

    fetched = [fetch((h1, x_h1))]
    for buf in (left_cross, right_cross):
        buf[...] = jnp.zeros_like(buf)
    partners = [peers.across(place) for place in range(steps)]
    peers.greet([peers.diag] + partners)

    dec_rows, enc_rows = hs.shape[0], h0.shape[0]
    owned = []
    kinds = (
        ((h0, h0, h0, enc_ay), (enc_gq, enc_gk, enc_gv, enc_o), left_enc, right_enc,
         (enc_rows,) * 4),
        ((hs, hs, hs, self_gy), (self_gq, self_gk, self_gv, self_o), left_self, right_self,
         (dec_rows,) * 4),
        ((hc, memory, memory, cross_gy), (cross_gq, cross_gk, cross_gv, cross_o), left_cross,
         right_cross, (dec_rows, enc_rows, enc_rows, dec_rows)),
    )
    spread = Spread(
        peers, [peers.sib, peers.far] + partners, small_total, small_recv
    )
    small_total[0] = small[...]
    spread.run(0)
    for lefts, rights, left, right, rows_of in kinds:
        owned.append(
            (to_owners(peers, lefts, left, rows_of), to_owners(peers, rights, right, rows_of))
        )
        for role in range(4):

            @pl.when(peers.own == role)
            def _(role=role, lefts=lefts, rights=rights, left=left, right=right, rows_of=rows_of):
                for source, target, sem in ((lefts, left, 0), (rights, right, 1)):
                    copy = pltpu.make_async_copy(
                        source[role], target.at[peers.own, pl.ds(0, rows_of[role])],
                        own_sem.at[sem],
                    )
                    copy.start()
                    copy.wait()

    width = h0.shape[1]
    units = enc_gg.shape[2]
    items = []
    ships = {}

    def flat(value):
        return value.reshape(value.shape[0] * value.shape[1], value.shape[2])

    def choose(target, source, rows):
        def run():
            for low, high in tiles(rows, 256):
                target[:, :, low:high] = to_low(
                    dot_last(select[peers.bit(0)], source(low, high))
                ).reshape(2, target.shape[1], high - low)

        return run

    def product_of(left, rows, parts, low, high):
        def run(half):
            value = None
            for part, right in enumerate(parts):
                here = dot(left[half, :, part * rows : (part + 1) * rows],
                           flat(right[:, :, low:high]))
                value = here if value is None else value + here
            return value

        return run

    def finish_in(layer, kind, low, high):
        def run(value):
            ffin[layer, kind, :, low:high] = value[:block]

        return run

    def finish_out(layer, low, high):
        def run(value):
            ffout[layer, :, low:high] = value[:block]

        return run

    count = 0
    ring = total.shape[0]

    def wait_fetch():
        for copy in fetched.pop():
            copy.wait()

    def fetch_next():
        fetched.append(fetch((enc_gy, x_enc_gy)))

    def staged(low, high):
        return flat(stage[...])[low:high]

    def both(own, other):
        def source(low, high):
            return jnp.concatenate([flat(own[...]), flat(other[...])], axis=0)[low:high]

        return source

    enc_total, dec_total = 4 * enc_rows, 4 * dec_rows
    groups = (
        (0, staged, wait_fetch, enc_total, fetch_next,
         ((0, (enc_gg, x_enc_gg)), (1, (enc_gu, x_enc_gu)))),
        (0, staged, wait_fetch, enc_total, None, ((2, (enc_hidden, x_enc_hidden)),)),
        (1, both(hf, x_hf), None, dec_total, None,
         ((0, (dec_gg, x_dec_gg)), (1, (dec_gu, x_dec_gu)))),
        (1, both(dec_gy, x_dec_gy), None, dec_total, None,
         ((2, (dec_hidden, x_dec_hidden)),)),
    )
    for layer, source, before, rows, after, products in groups:
        left = chosen
        prepare_left = choose(left, source, 2 * rows)
        for kind, parts in products:
            for low, high in tiles(units, CHUNK):
                item = Reduce(
                    peers, list(range(1, steps)), product_of(left, rows, parts, low, high),
                    high - low, total.at[count % ring], ff_send, ff_recv, count,
                    finish_in(layer, kind, low, high) if kind < 2
                    else finish_out(layer, low, high), ships,
                )
                item.before = [before, prepare_left, after] if prepare_left is not None else []
                prepare_left = None
                items.append(item)
                count += 1

    for a, (lefts, rights, left, right, rows_of) in enumerate(kinds):
        rows = left.shape[0] * left.shape[1]

        def before(a=a, left=left, rows=rows):
            for sends in owned[a]:
                owners_recv(peers, sends)
            for half in range(2):
                for low, high in tiles(rows, 256):
                    chosen_attn[half, :, low:high] = to_low(
                        dot_last(select[half], flat(left[...])[low:high])
                    )

        for place, (low, high) in enumerate(tiles(INNER, CHUNK)):

            def product(half, right=right, rows=rows, low=low, high=high):
                return dot(chosen_attn[half, :, :rows], flat(right[:, :, low:high]))

            def finish(value, a=a, low=low, high=high):
                attn_mine[a, :, low:high] = to_low(value)

            slot = 2 * a + place
            item = Reduce(
                peers, list(range(steps)), product, high - low,
                attn_total.at[slot % attn_total.shape[0]], at_send, at_recv, slot, finish, ships,
            )
            item.before = [before] if place == 0 else []
            items.append(item)

    lag = LAG
    last = max(place + lag * (item.steps - 1) for place, item in enumerate(items))
    for now in range(last + 1):
        for place, item in reversed(list(enumerate(items))):
            step, odd = divmod(now - place, lag)
            if odd == 0 and 0 < step < item.steps:
                item.run(step)
        if now < len(items):
            for action in items[now].before:
                if action is not None:
                    action()
            items[now].run(0)
        if now % 2 == 1 and now // 2 + 1 < spread.steps:
            spread.run(now // 2 + 1)
    small_out[...] = small_total[spread.steps - 1]
    attn[peers.own] = attn_mine[...]
    gather = Gather(peers, attn, False)
    gather.start()
    gather.wait_near()
    gather.relay()
    gather.wait_far()
    for pair in owned:
        for sends in pair:
            owners_sent(peers, sends)
    peers.finish()


def kd_call(size, block, padded, select, small, arrays, streamed):
    enc_gg, hf, h0, hs = arrays[0], arrays[12], arrays[16], arrays[22]
    width, units = h0.shape[1], enc_gg.shape[2]
    enc_rows, dec_rows = h0.shape[0], hs.shape[0]
    steps = size.bit_length() - 1
    shape = jax.ShapeDtypeStruct
    outs = [
        shape((2, 2, block, units), F32), shape((2, block, units), F32),
        shape((4, 3, padded, INNER), LOW), shape(small.shape, F32),
    ]
    vmem = pl.BlockSpec(memory_space=pltpu.VMEM)
    hbm = pl.BlockSpec(memory_space=pltpu.HBM)
    half = size * padded // 2
    ff_items = 6 * len(tiles(units, CHUNK))
    at_items = 3 * len(tiles(INNER, CHUNK))
    ff_heights = [half >> (step + 1) for step in range(steps - 1)]
    at_heights = [half >> step for step in range(steps)]

    def bufs(items, heights):
        return [pltpu.VMEM((items, height, CHUNK), LOW) for height in heights]

    copies = ff_items * (steps - 1) + at_items * steps + 3 * 6 + (2 + steps) + 3
    lag_slots = LAG * (steps - 1) + 1
    return pl.pallas_call(
        functools.partial(kd_kernel, block=block, steps=steps),
        out_shape=outs,
        in_specs=[vmem] * (2 + 16) + [hbm] * (len(arrays) - 16 + len(streamed)),
        out_specs=[vmem] * len(outs),
        scratch_shapes=[
            pltpu.VMEM((8, enc_rows, width), LOW),
            pltpu.VMEM((2, half // 2, 8 * enc_rows), LOW),
            pltpu.VMEM((2, half, 4 * enc_rows), LOW),
            pltpu.VMEM((4, enc_rows, width), LOW), pltpu.VMEM((4, enc_rows, width), LOW),
            pltpu.VMEM((4, dec_rows, width), LOW),
            pltpu.VMEM((4, enc_rows, INNER), LOW), pltpu.VMEM((4, enc_rows, INNER), LOW),
            pltpu.VMEM((4, dec_rows, INNER), LOW),
            pltpu.VMEM((lag_slots, half // 2, CHUNK), F32),
            pltpu.VMEM((at_items, half, CHUNK), F32),
            pltpu.VMEM((3 + steps,) + small.shape, F32),
            pltpu.VMEM((2 + steps,) + small.shape, F32),
            pltpu.VMEM((3, padded, INNER), LOW),
            *bufs(4, ff_heights), *bufs(ff_items, ff_heights), *bufs(2, at_heights),
            *bufs(at_items, at_heights),
            pltpu.SemaphoreType.DMA((copies,)), pltpu.SemaphoreType.DMA((copies,)),
            pltpu.SemaphoreType.DMA((4,)), pltpu.SemaphoreType.DMA((2,)),
        ],
        compiler_params=pltpu.CompilerParams(
            collective_id=3, has_side_effects=True, vmem_limit_bytes=62 * 1024 * 1024
        ),
        name="weight_sums",
    )(select, small, *arrays, *streamed)


def block_choice(size, block, padded, width):
    bits = size.bit_length() - 1
    columns = []
    for place in range(size):
        owner = sum(((place >> (bits - 1 - bit)) & 1) << bit for bit in range(bits))
        columns += [owner * block + inside if inside < block else -1 for inside in range(padded)]
    columns = jnp.asarray(columns, jnp.int32)
    select = (columns[:, None] == jnp.arange(width)[None, :]).astype(LOW)
    return select.reshape(2, size * padded // 2, width)


def on_device(
    enc_x, dec_x, dec_cot, item_count, enc_mask, dec_mask, enc_buckets, dec_buckets,
    gains, tables, attn_qk, attn_vo, ff_in, ff_out,
):
    tensor_id = lax.axis_index("tensor")
    size = lax.axis_size("dp")
    enc_own, dec_own = enc_x.shape[0], dec_x.shape[0]
    width = enc_x.shape[1]
    enc_total = enc_mask.shape[0]
    block = width // size
    padded = (block + 15) // 16 * 16
    small, (onehot, dec_onehot, far_back) = prepare(
        item_count, enc_mask, dec_mask, enc_buckets, dec_buckets, tables, enc_own, dec_own
    )
    select = block_choice(size, block, padded, width)
    ff_out_t = jnp.swapaxes(ff_out, 1, 2)
    dec_x, dec_cot = pad_rows(dec_x), pad_rows(dec_cot)
    (
        h0, enc_q, enc_kv, enc_p, enc_o, enc_mid, h1, enc_gelu, enc_slope, enc_hidden, enc_end,
        memory, cross_kv, hs, self_q, self_kv, self_p, self_o, dec_one, hc, cross_q, cross_p,
        cross_o, dec_two, hf, dec_gy, dec_gg, dec_gu, dec_hidden,
    ) = ka_call(enc_x, dec_x, dec_cot, gains, *small, attn_qk, attn_vo, ff_in, ff_out_t)
    (
        dec_out, cross_gy, cross_gq, cross_gkv, dec_one_grad, enc_end_grad, enc_gy, enc_gg, enc_gu,
        gains_b, x_dec_gg, x_dec_gu, x_dec_hidden, x_hf, x_dec_gy, x_h1, x_enc_hidden,
    ) = kb_call(
        dec_gg, dec_gu, dec_hidden, dec_cot, dec_two, dec_one, gains, cross_q, cross_kv, cross_p,
        enc_end, enc_gelu, enc_slope, attn_qk, attn_vo, ff_in, ff_out_t, hf, dec_gy, h1, enc_hidden,
    )
    (
        enc_grad, enc_ay, enc_gq, enc_gkv, enc_offsets, dec_grad, self_gy, self_gq, self_gkv,
        self_gs, gains_c, x_enc_gg, x_enc_gu, x_enc_gy,
    ) = kc_call(
        enc_gg, enc_gu, enc_end_grad, enc_mid, enc_x, gains, enc_q, enc_kv, enc_p, dec_one_grad,
        dec_x, self_q, self_kv, self_p, attn_qk, attn_vo, ff_in, enc_gy,
    )

    spread = jnp.pad(enc_offsets, ((0, 0), (enc_total - enc_own, enc_total)))
    placed = lax.dynamic_slice_in_dim(spread, tensor_id * enc_own, 2 * enc_total - 1, 1)
    enc_table = jnp.dot(placed[:HEADS], onehot, precision=HIGH).T
    self_table = jnp.dot(
        lax.dot_general(
            self_gs.reshape(HEADS, -1).astype(F32), far_back, (((1,), (1,)), ((), ())),
            precision=HIGH,
        ),
        dec_onehot,
        precision=HIGH,
    ).T
    table_row = jnp.concatenate([enc_table.reshape(-1), self_table.reshape(-1)])
    table_row = jnp.pad(table_row, (0, width - table_row.shape[0]))
    row = jnp.arange(8)[:, None]
    small_sums = jnp.where(row == 6, table_row[None, :], gains_b + gains_c)

    ffin_sum, ffout_sum, attn, sums = kd_call(
        size, block, padded, select, small_sums,
        [
            enc_gg, enc_gu, enc_hidden, x_enc_gg, x_enc_gu, x_enc_hidden,
            dec_gg, dec_gu, dec_hidden, x_dec_gg, x_dec_gu, x_dec_hidden,
            hf, x_hf, dec_gy, x_dec_gy,
            h0, enc_ay, enc_gq, enc_gkv[:, :INNER], enc_gkv[:, INNER:], enc_o,
            hs, self_gy, self_gq, self_gkv[:, :INNER], self_gkv[:, INNER:], self_o,
            hc, memory, cross_gy, cross_gq, cross_gkv[:, :INNER], cross_gkv[:, INNER:], cross_o,
        ],
        [h1, x_h1, enc_gy, x_enc_gy],
    )
    ffout_sum = jnp.swapaxes(ffout_sum, 1, 2)
    attn = attn[:, :, :block].astype(F32)
    qk_sum = jnp.concatenate([attn[0], attn[1]], axis=2)
    vo_sum = jnp.concatenate([attn[2], attn[3]], axis=2)
    gains_sum = sums[:6]
    tables_sum = sums[6, : tables.size].reshape(tables.shape)
    return (
        dec_out[:dec_own], enc_grad, dec_grad[:dec_own], gains_sum, tables_sum, qk_sum, vo_sum,
        ffin_sum, ffout_sum,
    )


def solution(mesh):
    rows = P(("dp", "tensor"), None)
    return jax.shard_map(
        on_device,
        mesh=mesh,
        in_specs=(
            rows, rows, rows, P("dp"), P("dp"), P("dp"), P(), P(), P(), P(), P(), P(),
            P(None, None, None, "tensor"), P(None, "tensor", None),
        ),
        out_specs=(
            rows, rows, rows, P(), P(), P(None, "dp", None), P(None, "dp", None),
            P(None, None, "dp", "tensor"), P(None, "tensor", "dp"),
        ),
        check_vma=False,
    )
```

```python
import functools

import jax
import jax.numpy as jnp
from jax import lax
from jax.experimental import pallas as pl
from jax.experimental.pallas import tpu as pltpu
from jax.sharding import PartitionSpec as P

HEADS = 6
HEAD = 64
INNER = HEADS * HEAD
PAIRS = HEADS // 2
PAIR = 2 * HEAD
BUCKETS = 32
EPSILON = 1e-06
MASKED = -1000000000.0
HIGH = lax.Precision.HIGHEST
F32 = jnp.float32
LOW = jnp.bfloat16
DEC_PAD = 32
VMEM_BYTES = 60 * 1024 * 1024
ROOT = 0.7978845608028654
CUBE = 0.044715


def to_low(value):
    return value.astype(LOW)


def dot(left, right):
    return jnp.dot(left, right, preferred_element_type=F32)


def dot_first(left, right):
    return lax.dot_general(left, right, (((0,), (0,)), ((), ())), preferred_element_type=F32)


def dot_last(left, right):
    return lax.dot_general(left, right, (((1,), (1,)), ((), ())), preferred_element_type=F32)


def norm_gain(rows, gain):
    return rows * lax.rsqrt(jnp.mean(rows * rows, axis=-1, keepdims=True) + EPSILON) * gain


def norm_back(rows, gain, grad_rows):
    scale = lax.rsqrt(jnp.mean(rows * rows, axis=-1, keepdims=True) + EPSILON)
    normed = rows * scale
    scaled = grad_rows * gain
    inner = jnp.mean(scaled * normed, axis=-1, keepdims=True)
    grad_gain = jnp.sum(grad_rows * normed, axis=0, keepdims=True)
    return scale * (scaled - normed * inner), grad_gain


def act_parts(gate, up_proj):
    square = gate * gate
    curve = jnp.tanh(ROOT * gate * (1.0 + CUBE * square))
    half = 0.5 * (1.0 + curve)
    slope = half + 0.5 * gate * (1.0 - curve * curve) * (ROOT * (1.0 + 3.0 * CUBE * square))
    return gate * half, up_proj * slope


def tiles(width, step=256):
    return [(start, min(start + step, width)) for start in range(0, width, step)]


class Peers:
    def __init__(self, send_sem, recv_sem):
        dp, tensor = lax.axis_index("dp"), lax.axis_index("tensor")
        chip, core = lax.div(tensor, 2), lax.rem(tensor, 2)
        self.dp = dp
        self.own = tensor
        self.sib = chip * 2 + (1 - core)
        self.far = (1 - chip) * 2 + core
        self.diag = (1 - chip) * 2 + (1 - core)
        self.send_sem, self.recv_sem = send_sem, recv_sem
        self.used = 0
        self.copies = []

    def bit(self, place):
        return lax.rem(lax.div(self.dp, 2**place), 2)

    def across(self, place):
        return (self.dp + (1 - 2 * self.bit(place)) * 2**place, self.own)

    def device(self, peer):
        return peer if isinstance(peer, tuple) else (self.dp, peer)

    def greet(self, more=()):
        barrier = pltpu.get_barrier_semaphore()
        for peer in (self.sib, self.far) + tuple(more):
            pl.semaphore_signal(
                barrier, inc=1, device_id=self.device(peer), device_id_type=pl.DeviceIdType.MESH
            )
        pl.semaphore_wait(barrier, 2 + len(more))

    def send(self, source, target, peer):
        place = self.used
        self.used += 1
        assert place < self.send_sem.shape[0]
        copy = pltpu.make_async_remote_copy(
            src_ref=source,
            dst_ref=target,
            send_sem=self.send_sem.at[place],
            recv_sem=self.recv_sem.at[place],
            device_id=self.device(peer),
            device_id_type=pl.DeviceIdType.MESH,
        )
        copy.start()
        self.copies.append(copy)
        return copy

    def finish(self):
        for copy in self.copies:
            copy.wait_send()


class Gather:
    def __init__(self, peers, buf, near):
        self.peers, self.buf = peers, buf
        if near:
            self.slots = (0, 1, 2, 2, 3)
        else:
            self.slots = (peers.own, peers.own, peers.own, peers.far, peers.far)

    def start(self):
        own, at_sib, at_far, unused, unused = self.slots
        self.to_far = self.peers.send(self.buf.at[own], self.buf.at[at_far], self.peers.far)
        self.to_sib = self.peers.send(self.buf.at[own], self.buf.at[at_sib], self.peers.sib)

    def wait_near(self):
        self.to_sib.wait_recv()

    def relay(self):
        unused, unused, unused, far, far_at_sib = self.slots
        self.to_far.wait_recv()
        self.relayed = self.peers.send(
            self.buf.at[far], self.buf.at[far_at_sib], self.peers.sib
        )

    def wait_far(self):
        self.relayed.wait_recv()


def attend(queries, kv, bias_of, allowed, weights_out, mixed_out):
    rows = queries.shape[0]
    total = kv.shape[0] * kv.shape[1]
    first = lax.broadcasted_iota(jnp.int32, (rows, PAIR), 1) < HEAD
    for pair in range(PAIRS):
        lanes = slice(pair * PAIR, (pair + 1) * PAIR)
        keys = kv[:, :, lanes].reshape(total, PAIR)
        values = kv[:, :, INNER + pair * PAIR : INNER + (pair + 1) * PAIR].reshape(total, PAIR)
        both = queries[:, lanes].astype(F32)
        mixed = []
        for half in range(2):
            head = 2 * pair + half
            here = to_low(jnp.where(first if half == 0 else ~first, both, 0.0))
            scores = dot_last(here, keys)
            if bias_of is not None:
                scores = scores + bias_of(head)
            scores = jnp.where(allowed, scores, MASKED)
            shifted = jnp.exp(scores - jnp.max(scores, axis=-1, keepdims=True))
            weights = shifted / jnp.sum(shifted, axis=-1, keepdims=True)
            weights_out[head] = weights
            mixed.append(dot(to_low(weights), values))
        mixed_out[:, lanes] = to_low(jnp.where(first, mixed[0], mixed[1]))


def attend_back(queries, kv, weights_in, grad_out, grad_q_out, grad_kv_out, grad_s_out):
    rows = queries.shape[0]
    total = kv.shape[0] * kv.shape[1]
    block = kv.shape[1]
    first = lax.broadcasted_iota(jnp.int32, (rows, PAIR), 1) < HEAD
    first_key = lax.broadcasted_iota(jnp.int32, (total, PAIR), 1) < HEAD
    for pair in range(PAIRS):
        lanes = slice(pair * PAIR, (pair + 1) * PAIR)
        value_lanes = slice(INNER + pair * PAIR, INNER + (pair + 1) * PAIR)
        keys = kv[:, :, lanes].reshape(total, PAIR)
        values = kv[:, :, value_lanes].reshape(total, PAIR)
        query = queries[:, lanes]
        grad = grad_out[:, lanes]
        grad_wide = grad.astype(F32)
        grad_q, grad_k, grad_v = [], [], []
        for half in range(2):
            head = 2 * pair + half
            here = to_low(jnp.where(first if half == 0 else ~first, grad_wide, 0.0))
            weights = weights_in[head]
            grad_weights = dot_last(here, values)
            weighted = jnp.sum(weights * grad_weights, axis=-1, keepdims=True)
            grad_scores = to_low(weights * (grad_weights - weighted))
            if grad_s_out is not None:
                grad_s_out[head] = grad_scores
            grad_q.append(dot(grad_scores, keys))
            grad_k.append(dot_first(grad_scores, query))
            grad_v.append(dot_first(to_low(weights), grad))
        grad_q_out[:, lanes] = to_low(jnp.where(first, grad_q[0], grad_q[1]))
        grad_kv_out[:, :, lanes] = jnp.where(first_key, grad_k[0], grad_k[1]).reshape(
            4, block, PAIR
        )
        grad_kv_out[:, :, value_lanes] = jnp.where(first_key, grad_v[0], grad_v[1]).reshape(
            4, block, PAIR
        )


class Exchange:
    def __init__(self, peers, whole, rows, place=0):
        partner = peers.across(place)
        self.rows = [
            (peers.send(own.at[0], other.at[0], partner), Gather(peers, other, True))
            for own, other in rows
        ]
        self.whole = [peers.send(own, other, partner) for own, other in whole]

    def spread(self):
        for copy, gather in self.rows:
            copy.wait_recv()
            gather.start()

    def relay(self):
        for unused, gather in self.rows:
            gather.wait_near()
            gather.relay()

    def finish_rows(self):
        for unused, gather in self.rows:
            gather.wait_far()

    def finish_first(self):
        self.whole.pop(0).wait_recv()

    def finish_whole(self):
        for copy in self.whole:
            copy.wait_recv()
        self.whole = []


class Loads:
    def __init__(self, sems):
        self.sems, self.used = sems, 0

    def start(self, source, target):
        copy = pltpu.make_async_copy(source, target, self.sems.at[self.used])
        self.used += 1
        copy.start()
        return copy


def wait_all(copies):
    for copy in copies:
        copy.wait()
    copies.clear()


def project_kv(rows, wqk, wvo, target):
    target[:, :INNER] = to_low(dot(rows, wqk[:, INNER:]))
    target[:, INNER:] = to_low(dot(rows, wvo[:, :INNER]))


def ff_up(rows, w_in, gelu_out, slope_out, hidden_out, slots):
    count, block = slots.stop - slots.start, gelu_out.shape[1]
    for low, high in tiles(gelu_out.shape[2]):
        gate = dot(rows, w_in[0, :, low:high])
        up_proj = dot(rows, w_in[1, :, low:high])
        gelu, slope = act_parts(gate, up_proj)
        shape = (count, block, high - low)
        gelu_out[slots, :, low:high] = gelu.reshape(shape)
        slope_out[slots, :, low:high] = slope.reshape(shape)
        hidden_out[slots, :, low:high] = to_low(gelu * up_proj).reshape(shape)


def reduce_far(peers, diag_part, far_part, send, recv):
    width = send.shape[2]
    for low, high in tiles(width):
        send[0, :, low:high] = to_low(diag_part(low, high))
    first = peers.send(send.at[0], recv.at[0], peers.sib)
    first.wait_recv()
    for low, high in tiles(width):
        send[2, :, low:high] = to_low(
            far_part(low, high) + recv[0, :, low:high].astype(F32)
        )
    return peers.send(send.at[2], recv.at[2], peers.far)


def ka_kernel(
    enc_x, dec_x, dec_cot, gains, enc_terms, enc_code, enc_item, self_mask, self_bias, dec_item,
    qk_all, vo_all, fi_all, fo_all,
    h0, enc_q, enc_kv, enc_p, enc_o, enc_mid, h1, enc_gelu, enc_slope, enc_hidden, enc_end, memory,
    cross_kv, hs, self_q, self_kv, self_p, self_o, dec_one, hc, cross_q, cross_p, cross_o, dec_two,
    hf, dec_gy, dec_gg, dec_gu, dec_hidden,
    wqk, wvo, wfi, wfo, part, send, recv, dec_gelu, dec_slope, send_sem, recv_sem, load_sem,
):
    peers = Peers(send_sem, recv_sem)
    loads = Loads(load_sem)
    get_qk, get_vo, get_fi, get_fo = {}, {}, {}, {}
    for a in (0, 1):
        get_qk[a] = loads.start(qk_all.at[a], wqk.at[a])
        get_vo[a] = loads.start(vo_all.at[a], wvo.at[a])
    get_fi[0] = loads.start(fi_all.at[0], wfi.at[0])
    get_fo[0] = loads.start(fo_all.at[0], wfo.at[0])
    get_qk[2] = loads.start(qk_all.at[2], wqk.at[2])
    get_vo[2] = loads.start(vo_all.at[2], wvo.at[2])
    get_fi[1] = loads.start(fi_all.at[1], wfi.at[1])
    get_fo[1] = loads.start(fo_all.at[1], wfo.at[1])
    peers.greet()

    normed = to_low(norm_gain(enc_x[...].astype(F32), gains[0:1]))
    h0[...] = normed
    get_qk[0].wait()
    get_vo[0].wait()
    project_kv(normed, wqk.at[0], wvo.at[0], enc_kv.at[peers.own])
    enc_gather = Gather(peers, enc_kv, False)
    enc_gather.start()
    normed_dec = to_low(norm_gain(dec_x[...].astype(F32), gains[3:4]))
    hs[...] = normed_dec
    get_qk[1].wait()
    get_vo[1].wait()
    project_kv(normed_dec, wqk.at[1], wvo.at[1], self_kv.at[peers.own])
    self_gather = Gather(peers, self_kv, False)
    self_gather.start()
    dec_gy[0] = dec_cot[...]
    gy_gather = Gather(peers, dec_gy, True)
    gy_gather.start()
    enc_q[...] = to_low(dot(normed, wqk[0, :, :INNER]))
    self_q[...] = to_low(dot(normed_dec, wqk[1, :, :INNER]))

    enc_gather.wait_near()
    enc_gather.relay()
    enc_allowed = enc_item[...] == enc_code[...]

    def enc_bias(head):
        own_rows, period = h0.shape[0], enc_terms.shape[1]
        spread = jnp.broadcast_to(enc_terms[head : head + 1, :], (own_rows, period))
        rolled = pltpu.roll(spread, 0, 1, stride=1, stride_axis=0)
        return rolled[:, : period // 2]

    enc_gather.wait_far()
    attend(enc_q[...], enc_kv, enc_bias, enc_allowed, enc_p, enc_o)
    for low, high in tiles(enc_mid.shape[1]):
        enc_mid[:, low:high] = enc_x[:, low:high].astype(F32) + dot_last(
            enc_o[...], wvo[0, low:high, INNER:]
        )
    h1[0] = to_low(norm_gain(enc_mid[...], gains[1:2]))
    h1_gather = Gather(peers, h1, True)
    h1_gather.start()

    self_gather.wait_near()
    self_gather.relay()
    gy_gather.wait_near()
    gy_gather.relay()
    self_gather.wait_far()
    gy_gather.wait_far()
    attend(
        self_q[...], self_kv, lambda head: self_bias[head], self_mask[...] > 0.5, self_p, self_o
    )
    for low, high in tiles(dec_one.shape[1]):
        dec_one[:, low:high] = dec_x[:, low:high].astype(F32) + dot_last(
            self_o[...], wvo[1, low:high, INNER:]
        )
    normed_dec = to_low(norm_gain(dec_one[...], gains[4:5]))
    hc[...] = normed_dec

    h1_gather.wait_near()
    get_fi[0].wait()
    get_fo[0].wait()
    block, width = h1.shape[1], h1.shape[2]

    def both(buf, slots):
        return buf[slots].reshape((slots.stop - slots.start) * block, buf.shape[2])

    near, away = slice(0, 2), slice(2, 4)
    ff_up(both(h1, near), wfi.at[0], enc_gelu, enc_slope, enc_hidden, near)
    h1_gather.relay()
    h1_gather.wait_far()
    ff_up(both(h1, away), wfi.at[0], enc_gelu, enc_slope, enc_hidden, away)
    hidden = both(enc_hidden, away)
    for low, high in tiles(width):
        value = dot_last(hidden, wfo[0, low:high, :])
        part[:, low:high] = value[:block]
        send[0, :, low:high] = to_low(value[block:])
    first = peers.send(send.at[0], recv.at[0], peers.sib)
    get_qk[2].wait()
    get_vo[2].wait()
    cross_q[...] = to_low(dot(hc[...], wqk[2, :, :INNER]))
    first.wait_recv()
    send[2] = to_low(part[...] + recv[0].astype(F32))
    second = peers.send(send.at[2], recv.at[2], peers.far)
    hidden = both(enc_hidden, near)
    for low, high in tiles(width):
        value = dot_last(hidden, wfo[0, low:high, :])
        part[:, low:high] = value[:block] + enc_mid[:, low:high]
        send[1, :, low:high] = to_low(value[block:])
    third = peers.send(send.at[1], recv.at[1], peers.sib)
    third.wait_recv()
    part[...] = part[...] + recv[1].astype(F32)
    second.wait_recv()
    ended = part[...] + recv[2].astype(F32)
    enc_end[...] = ended
    normed = to_low(norm_gain(ended, gains[2:3]))
    memory[...] = normed

    project_kv(normed, wqk.at[2], wvo.at[2], cross_kv.at[peers.own])
    cross_gather = Gather(peers, cross_kv, False)
    cross_gather.start()
    get_fi[1].wait()
    get_fo[1].wait()
    cross_allowed = dec_item[...] == enc_code[...]
    cross_gather.wait_near()
    cross_gather.relay()
    cross_gather.wait_far()
    attend(cross_q[...], cross_kv, None, cross_allowed, cross_p, cross_o)
    for low, high in tiles(dec_two.shape[1]):
        dec_two[:, low:high] = dec_one[:, low:high] + dot_last(
            cross_o[...], wvo[2, low:high, INNER:]
        )
    hf[0] = to_low(norm_gain(dec_two[...], gains[5:6]))
    hf_gather = Gather(peers, hf, True)
    hf_gather.start()

    rows = hf.shape[0] * hf.shape[1]
    hf_gather.wait_near()
    hf_gather.relay()
    grad_y = dec_gy[...].reshape(rows, width)
    hf_gather.wait_far()
    ff_up(hf[...].reshape(rows, width), wfi.at[1], dec_gelu, dec_slope, dec_hidden, slice(0, 4))
    for low, high in tiles(dec_gelu.shape[2]):
        grad_h = dot(grad_y, wfo[1, :, low:high]).reshape(4, hf.shape[1], high - low)
        dec_gg[:, :, low:high] = to_low(grad_h * dec_slope[:, :, low:high])
        dec_gu[:, :, low:high] = to_low(grad_h * dec_gelu[:, :, low:high])
    peers.finish()


def ka_call(enc_x, dec_x, dec_cot, gains, enc_terms, enc_code, enc_item, self_mask, self_bias,
            dec_item, attn_qk, attn_vo, ff_in, ff_out):
    rows, width = enc_x.shape
    dec_rows = dec_x.shape[0]
    units = ff_in.shape[3]
    total = enc_code.shape[1]
    kv_width = 2 * INNER
    shape = jax.ShapeDtypeStruct
    outs = [
        shape((rows, width), LOW), shape((rows, INNER), LOW), shape((4, rows, kv_width), LOW),
        shape((HEADS, rows, total), F32), shape((rows, INNER), LOW), shape((rows, width), F32),
        shape((4, rows, width), LOW), shape((4, rows, units), F32), shape((4, rows, units), F32),
        shape((4, rows, units), LOW), shape((rows, width), F32), shape((rows, width), LOW),
        shape((4, rows, kv_width), LOW),
        shape((dec_rows, width), LOW), shape((dec_rows, INNER), LOW),
        shape((4, dec_rows, kv_width), LOW), shape((HEADS, dec_rows, 4 * dec_rows), F32),
        shape((dec_rows, INNER), LOW), shape((dec_rows, width), F32),
        shape((dec_rows, width), LOW), shape((dec_rows, INNER), LOW),
        shape((HEADS, dec_rows, total), F32), shape((dec_rows, INNER), LOW),
        shape((dec_rows, width), F32),
        shape((4, dec_rows, width), LOW), shape((4, dec_rows, width), LOW),
        shape((4, dec_rows, units), LOW), shape((4, dec_rows, units), LOW),
        shape((4, dec_rows, units), LOW),
    ]
    vmem = pl.BlockSpec(memory_space=pltpu.VMEM)
    hbm = pl.BlockSpec(memory_space=pltpu.HBM)
    copies = 3 * 6 + 3
    return pl.pallas_call(
        ka_kernel,
        out_shape=outs,
        in_specs=[vmem] * 10 + [hbm] * 4,
        out_specs=[vmem] * len(outs),
        scratch_shapes=[
            pltpu.VMEM(attn_qk.shape, LOW), pltpu.VMEM(attn_vo.shape, LOW),
            pltpu.VMEM(ff_in.shape, LOW), pltpu.VMEM(ff_out.shape, LOW),
            pltpu.VMEM((rows, width), F32), pltpu.VMEM((3, rows, width), LOW),
            pltpu.VMEM((3, rows, width), LOW), pltpu.VMEM((4, dec_rows, units), F32),
            pltpu.VMEM((4, dec_rows, units), F32),
            pltpu.SemaphoreType.DMA((copies,)), pltpu.SemaphoreType.DMA((copies,)),
            pltpu.SemaphoreType.DMA((10,)),
        ],
        compiler_params=pltpu.CompilerParams(
            collective_id=0, has_side_effects=True, vmem_limit_bytes=VMEM_BYTES
        ),
        name="forward_chain",
    )(enc_x, dec_x, dec_cot, gains, enc_terms, enc_code, enc_item, self_mask, self_bias, dec_item,
      attn_qk, attn_vo, ff_in, ff_out)


def pad_rows(value, rows=DEC_PAD):
    return jnp.pad(value, ((0, rows - value.shape[0]), (0, 0)))


def prepare(item_count, enc_mask, dec_mask, enc_buckets, dec_buckets, tables, enc_own, dec_own):
    tensor_id = lax.axis_index("tensor")
    enc_total, dec_total = enc_mask.shape[0], dec_mask.shape[0]
    count = item_count[0]
    enc_len, dec_len = enc_total // count, dec_total // count
    enc_code = jnp.where(enc_mask == 1, jnp.arange(enc_total) // enc_len, -1)
    enc_item = (tensor_id * enc_own + jnp.arange(enc_own)) // enc_len
    slot = jnp.arange(4 * DEC_PAD)
    inside = slot % DEC_PAD
    place = slot // DEC_PAD * dec_own + inside
    real = inside < dec_own
    row = jnp.arange(DEC_PAD)
    row_real = row < dec_own
    row_place = tensor_id * dec_own + row
    dec_live = jnp.pad(dec_mask.reshape(4, dec_own), ((0, 0), (0, DEC_PAD - dec_own))).reshape(-1)
    key_item = jnp.where(real & (dec_live == 1), place // dec_len, -1)
    dec_item = jnp.where(row_real, row_place // dec_len, -2)
    self_mask = (
        (dec_item[:, None] == key_item[None, :]) & (place[None, :] <= row_place[:, None])
    ).astype(F32)
    onehot = (enc_buckets[:, None] == jnp.arange(BUCKETS)[None, :]).astype(F32)
    terms = jnp.dot(tables[0].T, onehot.T, precision=HIGH)
    terms = jnp.pad(terms, ((0, 2), (0, 1)))
    period = 2 * enc_total
    doubled = jnp.concatenate([terms, terms], axis=1)
    shift = (enc_total - 1 - tensor_id * enc_own + period) % period
    enc_terms = lax.dynamic_slice_in_dim(doubled, shift, period, 1)
    far_back = jnp.clip(row_place[:, None] - place[None, :], 0, dec_total - 1)
    far_back = (far_back[None] == jnp.arange(dec_total)[:, None, None]).astype(F32)
    far_back = far_back.reshape(dec_total, -1)
    dec_onehot = (dec_buckets[:, None] == jnp.arange(BUCKETS)[None, :]).astype(F32)
    dec_terms = jnp.dot(tables[1].T, dec_onehot.T, precision=HIGH)
    self_bias = jnp.dot(dec_terms, far_back, precision=HIGH).reshape(
        HEADS, DEC_PAD, 4 * DEC_PAD
    )
    spots = jnp.pad(onehot, ((0, 1), (0, 0)))
    enc_spots = lax.dynamic_slice_in_dim(
        spots, enc_total - enc_own - tensor_id * enc_own, enc_total + enc_own, 0
    )
    self_bucket = jnp.dot(
        dec_buckets.astype(F32)[None, :], far_back, precision=HIGH
    ).reshape(DEC_PAD, 4 * DEC_PAD)
    return (
        enc_terms, enc_code.astype(F32)[None, :], enc_item.astype(F32)[:, None], self_mask,
        self_bias, dec_item.astype(F32)[:, None],
    ), (enc_spots, self_bucket)


CHUNK = 256
RING = 4


def lag_of(steps):
    return 2 if steps <= 3 else 1


class Reduce:
    def __init__(self, peers, places, product, columns, total, send, recv, slot, finish, ships):
        self.ships = ships
        self.peers, self.places, self.product, self.columns = peers, places, product, columns
        self.total, self.send, self.recv, self.slot, self.done = total, send, recv, slot, finish
        self.steps = len(places) + 1

    def buffers(self, step):
        lanes = pl.ds(0, self.columns)
        return (
            self.send[step].at[self.slot % self.send[step].shape[0], :, lanes],
            self.recv[step].at[self.slot, :, lanes],
        )

    def ship(self, step, value, place):
        source, target = self.buffers(step)
        key = (id(self.send), step, self.slot % self.send[step].shape[0])
        if key in self.ships:
            self.ships[key].wait_send()
            self.peers.copies = [c for c in self.peers.copies if c is not self.ships[key]]
        source[...] = to_low(value)
        self.copy = self.peers.send(source, target, self.peers.across(place))
        self.ships[key] = self.copy

    def run(self, step):
        lanes = pl.ds(0, self.columns)
        if step == 0:
            here = self.peers.bit(self.places[0])
            self.ship(0, self.product(1 - here), self.places[0])
            self.height = self.send[0].shape[1]
            self.start = 0
            self.total[: self.height, lanes] = self.product(here)
            return
        self.copy.wait_recv()
        arrived = self.buffers(step - 1)[1]
        if step == self.steps - 1:
            rows = pl.ds(self.start, self.height)
            self.done(self.total[rows, lanes] + arrived[...].astype(F32))
            return
        self.height //= 2
        place = self.places[step]
        here = self.peers.bit(place)
        away = pl.multiple_of(self.start + (1 - here) * self.height, 16)
        kept = pl.multiple_of(self.start + here * self.height, 16)
        from_away = pl.multiple_of((1 - here) * self.height, 16)
        from_kept = pl.multiple_of(here * self.height, 16)
        self.ship(
            step,
            self.total[pl.ds(away, self.height), lanes]
            + arrived[pl.ds(from_away, self.height), :].astype(F32),
            place,
        )
        self.total[pl.ds(kept, self.height), lanes] += arrived[
            pl.ds(from_kept, self.height), :
        ].astype(F32)
        self.start = kept


class Stream:
    def __init__(self, items, lag):
        self.items, self.lag, self.now = items, lag, 0
        self.last = max(place + lag * (item.steps - 1) for place, item in enumerate(items))

    def pump(self, ticks=1):
        for unused in range(ticks):
            now = self.now
            if now > self.last:
                return
            self.now += 1
            for place, item in reversed(list(enumerate(self.items))):
                step, odd = divmod(now - place, self.lag)
                if odd == 0 and 0 < step < item.steps:
                    item.run(step)
            if now < len(self.items):
                for action in self.items[now].before:
                    if action is not None:
                        action()
                self.items[now].run(0)

    def drain(self):
        self.pump(self.last + 1 - self.now)


def flat(value):
    return value.reshape(value.shape[0] * value.shape[1], value.shape[2])


def choose_rows(select, rows, chosen, start):
    for low, high in tiles(rows.shape[0]):
        chosen[:, :, start + low : start + high] = to_low(
            dot_last(select[...], rows[low:high])
        ).reshape(2, chosen.shape[1], high - low)


class Products:
    def __init__(self, peers, select, first, steps, chosen, total, *buffers):
        self.peers, self.select, self.chosen, self.total = peers, select, chosen, total
        self.places = list(range(first, steps))
        self.send, self.recv = buffers[: steps - first], buffers[steps - first :]
        self.items, self.ships = [], {}

    def choose(self, lefts, before):
        def run():
            if before is not None:
                before()
            rows = lefts[0].shape[0] * lefts[0].shape[1]
            for part, left in enumerate(lefts):
                choose_rows(self.select, flat(left[...]), self.chosen, part * rows)

        return run

    def add(self, lefts, rights, out, before=None, ready=()):
        actions = [] if lefts is None else [self.choose(lefts, before)]
        for kind, parts in enumerate(rights):
            rows = parts[0].shape[0] * parts[0].shape[1]
            if ready:
                actions.append(ready[kind])
            for low, high in tiles(parts[0].shape[2], CHUNK):

                def product(half, parts=parts, low=low, high=high):
                    value = None
                    for part, right in enumerate(parts):
                        here = dot(
                            self.chosen[half, :, part * rows : (part + 1) * rows],
                            flat(right[:, :, low:high]),
                        )
                        value = here if value is None else value + here
                    return value

                def finish(value, kind=kind, low=low, high=high):
                    out[kind, :, low:high] = value[: out.shape[1]]

                count = len(self.items)
                item = Reduce(
                    self.peers, self.places, product, high - low,
                    self.total.at[count % self.total.shape[0]], self.send, self.recv, count,
                    finish, self.ships,
                )
                item.before, actions = actions, []
                self.items.append(item)


def product_scratch(size, padded, rows, items, first):
    chosen = size * padded >> first
    steps = size.bit_length() - 1
    heights = [chosen >> (step + 1) for step in range(steps - first)]
    return [
        pltpu.VMEM((2, chosen // 2, rows), LOW),
        pltpu.VMEM((lag_of(steps) * (steps - first) + 1, chosen // 2, CHUNK), F32),
        *[pltpu.VMEM((RING, height, CHUNK), LOW) for height in heights],
        *[pltpu.VMEM((items, height, CHUNK), LOW) for height in heights],
    ]


def to_owners(peers, sources, target, rows_of, own_sem):
    sends = []
    for peer in (peers.far, peers.diag, peers.sib):
        place = peers.used
        peers.used += 1
        for role in range(4):
            rows = rows_of[role]

            def copy(role=role, rows=rows, place=place, peer=peer):
                return pltpu.make_async_remote_copy(
                    src_ref=sources[role],
                    dst_ref=target.at[peers.own, pl.ds(0, rows)],
                    send_sem=peers.send_sem.at[place],
                    recv_sem=peers.recv_sem.at[place],
                    device_id=peers.device(peer),
                    device_id_type=pl.DeviceIdType.MESH,
                )

            @pl.when(peer == role)
            def _(copy=copy):
                copy().start()

            sends.append((peer, role, copy))
    for role in range(4):

        def keep(role=role):
            return pltpu.make_async_copy(
                sources[role], target.at[peers.own, pl.ds(0, rows_of[role])], own_sem
            )

        @pl.when(peers.own == role)
        def _(keep=keep):
            keep().start()

        sends.append((None, role, keep))
    return sends


def owners_done(peers, sends):
    for peer, role, copy in sends:

        @pl.when(peers.own == role)
        def _(copy=copy, peer=peer):
            copy().wait() if peer is None else copy().wait_recv()

        if peer is not None:

            @pl.when(peer == role)
            def _(copy=copy):
                copy().wait_send()


def kv_back(grad_kv, wqk, wvo, low, high):
    return dot_last(grad_kv[:, :INNER], wqk[low:high, INNER:]) + dot_last(
        grad_kv[:, INNER:], wvo[low:high, :INNER]
    )


class SumBlocks:
    def __init__(self, peers, buf, send, recv):
        self.peers, self.buf, self.send, self.recv = peers, buf, send, recv
        send[0] = to_low(buf[peers.diag])
        send[1] = to_low(buf[peers.sib])
        self.first = peers.send(send.at[0], recv.at[0], peers.sib)
        self.third = peers.send(send.at[1], recv.at[1], peers.sib)

    def cross(self):
        peers = self.peers
        self.first.wait_recv()
        self.send[2] = to_low(self.buf[peers.far] + self.recv[0].astype(F32))
        self.second = peers.send(self.send.at[2], self.recv.at[2], peers.far)

    def result(self):
        self.third.wait_recv()
        value = self.buf[self.peers.own] + self.recv[1].astype(F32)
        self.second.wait_recv()
        return value + self.recv[2].astype(F32)


class SumNear:
    def __init__(self, peers, part_of, block, total, send, recv):
        self.peers, self.total, self.send, self.recv = peers, total, send, recv
        for low, high in tiles(send.shape[2]):
            value = part_of(low, high)
            total[0, :, low:high] = value[:block]
            send[1, :, low:high] = to_low(value[block : 2 * block])
            total[1, :, low:high] = value[2 * block : 3 * block]
            send[0, :, low:high] = to_low(value[3 * block :])
        self.first = peers.send(send.at[0], recv.at[0], peers.sib)
        self.third = peers.send(send.at[1], recv.at[1], peers.sib)

    def cross(self):
        self.first.wait_recv()
        self.send[2] = to_low(self.total[1] + self.recv[0].astype(F32))
        self.second = self.peers.send(self.send.at[2], self.recv.at[2], self.peers.far)

    def result(self):
        self.third.wait_recv()
        value = self.total[0] + self.recv[1].astype(F32)
        self.second.wait_recv()
        return value + self.recv[2].astype(F32)


def kb_kernel(
    dec_gg, dec_gu, dec_hidden, dec_cot, dec_two, dec_one, gains, cross_q, hf,
    qk_all, vo_all, fi_all, fo_all, dec_gy, h1, enc_hidden, cross_kv_all, cross_p_all, enc_end_all,
    enc_gelu_all, enc_slope_all, select_all,
    dec_out, cross_gy, cross_gq, cross_gk, cross_gv, dec_one_grad, enc_end_grad, enc_gy, enc_gg, enc_gu,
    gains_grad, dec_ffin, x_dec_hidden, z_dec_hidden, zx_dec_hidden, x_dec_gy, z_dec_gy, zx_dec_gy,
    x_h1, x_enc_hidden,
    wqk, wvo, wfi, wfo, grad_kv, kv_send, kv_recv, row_total, row_send, row_recv, out_total,
    out_send, out_recv, x_dec_gg, z_dec_gg, zx_dec_gg, x_dec_gu, z_dec_gu, zx_dec_gu, x_hf, z_hf,
    zx_hf, cross_kv, cross_p, enc_end, enc_gelu, enc_slope, select, *rest,
    steps,
):
    scratch, (send_sem, recv_sem, load_sem) = rest[:-3], rest[-3:]
    peers = Peers(send_sem, recv_sem)
    loads = Loads(load_sem)
    get_fi = loads.start(fi_all.at[1], wfi)
    get_cross = [
        loads.start(vo_all.at[2], wvo), loads.start(cross_kv_all, cross_kv),
        loads.start(cross_p_all, cross_p), loads.start(qk_all.at[2], wqk),
        loads.start(enc_end_all, enc_end),
    ]
    get_fo1 = loads.start(fo_all.at[1], wfo.at[1])
    get_up = [
        loads.start(fo_all.at[0], wfo.at[0]), loads.start(enc_gelu_all, enc_gelu),
        loads.start(enc_slope_all, enc_slope),
    ]
    quarter = select.shape[0]
    get_select = loads.start(
        select_all.at[
            peers.bit(0), pl.ds(pl.multiple_of(peers.bit(1) * quarter, 16), quarter)
        ],
        select,
    )
    peers.greet([peers.across(place) for place in range(steps)])
    by_x = Exchange(peers, [(dec_gg, x_dec_gg), (dec_gu, x_dec_gu)], [(hf, x_hf)])
    by_z = Exchange(peers, [(dec_gg, z_dec_gg), (dec_gu, z_dec_gu)], [(hf, z_hf)], 1)
    later = [Exchange(peers, [], [(h1, x_h1)])]
    passed = []

    def pass_on():
        by_x.spread()
        by_z.spread()
        by_x.finish_whole()
        passed.append(
            Exchange(peers, [(x_dec_gg, zx_dec_gg), (x_dec_gu, zx_dec_gu)], [(x_hf, zx_hf)], 1)
        )
        later.append(
            Exchange(
                peers, [(dec_hidden, x_dec_hidden)] + enc_part(0, 2), [(dec_gy, x_dec_gy)]
            )
        )
        later[0].spread()

    def enc_part(low, high):
        return [(enc_hidden.at[slot], x_enc_hidden.at[slot]) for slot in range(low, high)]

    def pass_later():
        later[1].spread()
        later[1].finish_first()
        later.append(Exchange(peers, enc_part(2, 4), []))
        later.append(Exchange(peers, [(dec_hidden, z_dec_hidden)], [(dec_gy, z_dec_gy)], 1))
        later.append(
            Exchange(peers, [(x_dec_hidden, zx_dec_hidden)], [(x_dec_gy, zx_dec_gy)], 1)
        )

    def arrived():
        get_select.wait()
        for exchange in (by_x, by_z, passed[0]):
            exchange.finish_rows()
            exchange.finish_whole()

    products = Products(peers, select, 2, steps, *scratch)
    products.add(
        [hf, x_hf, z_hf, zx_hf],
        [(dec_gg, x_dec_gg, z_dec_gg, zx_dec_gg), (dec_gu, x_dec_gu, z_dec_gu, zx_dec_gu)],
        dec_ffin, before=arrived,
    )
    stream = Stream(products.items, lag_of(steps))
    width = dec_two.shape[1]
    block = dec_two.shape[0]
    units = dec_gg.shape[2]
    gains_grad[...] = jnp.zeros_like(gains_grad)

    get_fi.wait()
    gate, up_proj = dec_gg[...].reshape(4 * block, units), dec_gu[...].reshape(4 * block, units)

    def grad_rows_part(low, high):
        return dot_last(gate, wfi[0, low:high, :]) + dot_last(up_proj, wfi[1, low:high, :])

    grad_rows = SumNear(peers, grad_rows_part, block, row_total, row_send, row_recv)
    grad_rows.cross()
    wait_all(get_cross)
    value, gain_row = norm_back(dec_two[...], gains[5:6], grad_rows.result())
    gains_grad[5:6] = gain_row
    residual = dec_cot[...].astype(F32) + value
    grad_y = to_low(residual)
    cross_gy[...] = grad_y

    grad_out = to_low(dot(grad_y, wvo[:, INNER:]))
    attend_back(cross_q[...], cross_kv, cross_p, grad_out, cross_gq, grad_kv, None)
    kv_sum = SumBlocks(peers, grad_kv, kv_send, kv_recv)
    kv_sum.cross()
    pass_on()
    for low, high in tiles(width):
        row_total[0, :, low:high] = dot_last(cross_gq[...], wqk[low:high, :INNER])
    value, gain_row = norm_back(dec_one[...], gains[4:5], row_total[0])
    gains_grad[4:5] = gain_row
    dec_one_grad[...] = residual + value
    by_x.relay()
    by_z.relay()
    own_kv = to_low(kv_sum.result())
    cross_gk[...] = own_kv[:, :INNER]
    cross_gv[...] = own_kv[:, INNER:]
    for low, high in tiles(width):
        enc_end_grad[:, low:high] = kv_back(own_kv, wqk, wvo, low, high)
    value, gain_row = norm_back(enc_end[...], gains[2:3], enc_end_grad[...])
    gains_grad[2:3] = gain_row
    enc_end_grad[...] = value
    enc_gy[0] = to_low(value)
    gy_gather = Gather(peers, enc_gy, True)
    gy_gather.start()

    get_fo1.wait()
    hidden = dec_hidden[...].reshape(4 * block, units)
    out_sum = SumNear(
        peers, lambda low, high: dot_last(hidden, wfo[1, low:high, :]), block, out_total,
        out_send, out_recv,
    )

    passed[0].spread()
    pass_later()
    wait_all(get_up)
    rows = enc_gy.shape[1]

    def gate_grads(slots):
        grad_y = enc_gy[slots].reshape(2 * rows, width)
        for low, high in tiles(units):
            grad_h = dot(grad_y, wfo[0, :, low:high]).reshape(2, rows, high - low)
            enc_gg[slots, :, low:high] = to_low(grad_h * enc_slope[slots, :, low:high])
            enc_gu[slots, :, low:high] = to_low(grad_h * enc_gelu[slots, :, low:high])

    gy_gather.wait_near()
    gate_grads(slice(0, 2))
    gy_gather.relay()
    passed[0].relay()
    stream.pump(3)
    out_sum.cross()
    gy_gather.wait_far()
    gate_grads(slice(2, 4))
    stream.pump(2)
    for exchange in later[2:]:
        exchange.spread()
    stream.pump(2)
    for exchange in later:
        exchange.relay()
    dec_out[...] = to_low(dec_two[...] + out_sum.result())
    stream.drain()
    for exchange in later:
        exchange.finish_rows()
        exchange.finish_whole()
    peers.finish()


def kb_call(dec_gg, dec_gu, dec_hidden, dec_cot, dec_two, dec_one, gains, cross_q, cross_kv,
            cross_p, enc_end, enc_gelu, enc_slope, attn_qk, attn_vo, ff_in, ff_out, hf, dec_gy, h1,
            enc_hidden, select, size, block, padded):
    rows, width = enc_end.shape
    dec_rows = dec_two.shape[0]
    units = ff_in.shape[3]
    kv_width = 2 * INNER
    shape = jax.ShapeDtypeStruct
    outs = [
        shape((dec_rows, width), LOW), shape((dec_rows, width), LOW),
        shape((dec_rows, INNER), LOW), shape((rows, INNER), LOW), shape((rows, INNER), LOW),
        shape((dec_rows, width), F32), shape((rows, width), F32), shape((4, rows, width), LOW), shape((4, rows, units), LOW),
        shape((4, rows, units), LOW), shape((8, width), F32), shape((2, block, units), F32),
    ]
    traded = [
        shape(value.shape, LOW)
        for value in (dec_hidden,) * 3 + (dec_gy,) * 3 + (h1, enc_hidden)
    ]
    steps = size.bit_length() - 1
    items = 2 * len(tiles(units, CHUNK))
    vmem = pl.BlockSpec(memory_space=pltpu.VMEM)
    hbm = pl.BlockSpec(memory_space=pltpu.HBM)
    copies = 3 * 3 + 3 + 41 + items * (steps - 2)
    return pl.pallas_call(
        functools.partial(kb_kernel, steps=steps),
        out_shape=outs + traded,
        in_specs=[vmem] * 9 + [hbm] * 13,
        out_specs=[vmem] * len(outs) + [hbm] * len(traded),
        scratch_shapes=[
            pltpu.VMEM(attn_qk.shape[1:], LOW), pltpu.VMEM(attn_vo.shape[1:], LOW),
            pltpu.VMEM(ff_in.shape[1:], LOW), pltpu.VMEM(ff_out.shape, LOW),
            pltpu.VMEM((4, rows, kv_width), F32), pltpu.VMEM((3, rows, kv_width), LOW),
            pltpu.VMEM((3, rows, kv_width), LOW), pltpu.VMEM((2, dec_rows, width), F32),
            pltpu.VMEM((3, dec_rows, width), LOW), pltpu.VMEM((3, dec_rows, width), LOW),
            pltpu.VMEM((2, dec_rows, width), F32), pltpu.VMEM((3, dec_rows, width), LOW),
            pltpu.VMEM((3, dec_rows, width), LOW),
            *[pltpu.VMEM(dec_gg.shape, LOW)] * 6, *[pltpu.VMEM(hf.shape, LOW)] * 3,
            pltpu.VMEM(cross_kv.shape, LOW), pltpu.VMEM(cross_p.shape, F32),
            pltpu.VMEM(enc_end.shape, F32), pltpu.VMEM(enc_gelu.shape, F32),
            pltpu.VMEM(enc_slope.shape, F32), pltpu.VMEM((size * padded // 4, width), LOW),
            *product_scratch(size, padded, 4 * 4 * dec_rows, items, 2),
            pltpu.SemaphoreType.DMA((copies,)), pltpu.SemaphoreType.DMA((copies,)),
            pltpu.SemaphoreType.DMA((11,)),
        ],
        compiler_params=pltpu.CompilerParams(
            collective_id=1, has_side_effects=True, vmem_limit_bytes=VMEM_BYTES
        ),
        name="middle_chain",
    )(dec_gg, dec_gu, dec_hidden, dec_cot, dec_two, dec_one, gains, cross_q, hf,
      attn_qk, attn_vo, ff_in, ff_out, dec_gy, h1, enc_hidden, cross_kv, cross_p, enc_end,
      enc_gelu, enc_slope, select)


def kc_kernel(
    enc_gg, enc_gu, gains, gains_mid, enc_q, dec_one_grad, dec_x, self_q, self_kv, self_p,
    enc_spots, self_bucket,
    qk_all, vo_all, fi_all, enc_end_grad_all, enc_mid_all, enc_x_all, enc_kv_all, enc_p_all,
    enc_gy_all, dec_gy_all, x_dec_gy_all, z_dec_gy_all, zx_dec_gy_all, dec_hidden_all,
    x_dec_hidden_all, z_dec_hidden_all, zx_dec_hidden_all, enc_hidden_all, x_enc_hidden_all,
    select_all, h1_all, x_h1_all, hs, hc, memory, cross_gy, cross_gq, cross_gk, cross_gv,
    cross_o,
    enc_grad, enc_ay, enc_gq, enc_gk, enc_gv, dec_grad, self_gy, self_gq, self_gk, self_gv,
    small, ffout, chosen_h1, left_cross, right_cross, left_self, x_enc_gg, x_enc_gu,
    wqk, wvo, wfi, enc_gs, self_gs, part, send, recv, enc_gkv_full, kv_send, kv_recv,
    self_gkv_full, self_send, self_recv, x_enc_gy, enc_end_grad, enc_mid, enc_x, enc_kv, enc_p,
    enc_gy, dec_gys, dec_hiddens, enc_hidden, x_enc_hidden, select, stage, *rest,
    steps,
):
    dec_scratch, enc_scratch = rest[: 2 * steps - 2], rest[2 * steps - 2 : -4]
    send_sem, recv_sem, load_sem, own_sem = rest[-4:]
    peers = Peers(send_sem, recv_sem)
    loads = Loads(load_sem)
    get_fi = loads.start(fi_all.at[0], wfi)
    get_vo1 = loads.start(vo_all.at[1], wvo.at[1])
    get_select = loads.start(select_all.at[peers.bit(0)], select)
    get_dec = [
        loads.start(source, target.at[place])
        for sources, target in (
            ((dec_gy_all, x_dec_gy_all, z_dec_gy_all, zx_dec_gy_all), dec_gys),
            ((dec_hidden_all, x_dec_hidden_all, z_dec_hidden_all, zx_dec_hidden_all), dec_hiddens),
        )
        for place, source in enumerate(sources)
    ]
    get_mid = [
        loads.start(enc_mid_all, enc_mid), loads.start(enc_end_grad_all, enc_end_grad),
        loads.start(vo_all.at[0], wvo.at[0]), loads.start(enc_kv_all, enc_kv),
        loads.start(enc_p_all, enc_p),
    ]
    get_out = [
        loads.start(enc_gy_all, enc_gy), loads.start(enc_hidden_all, enc_hidden),
        loads.start(x_enc_hidden_all, x_enc_hidden),
    ]
    get_last = [
        loads.start(qk_all.at[0], wqk.at[0]), loads.start(qk_all.at[1], wqk.at[1]),
        loads.start(enc_x_all, enc_x),
    ]
    for buf in (left_cross, right_cross):
        buf[...] = jnp.zeros_like(buf)
    peers.greet([peers.diag] + [peers.across(place) for place in range(steps)])
    exchange = Exchange(
        peers, [(enc_gg, x_enc_gg), (enc_gu, x_enc_gu)], [(enc_gy_all, x_enc_gy)]
    )
    dec_rows, enc_rows = hs.shape[0], memory.shape[0]
    short = (dec_rows,) * 4
    mixed = (dec_rows, enc_rows, enc_rows, dec_rows)
    owned = [
        to_owners(peers, (hc, memory, memory, cross_gy), left_cross, mixed, own_sem.at[0]),
        to_owners(
            peers, (cross_gq, cross_gk, cross_gv, cross_o), right_cross, mixed, own_sem.at[1]
        ),
    ]

    def arrived():
        wait_all(get_out)
        exchange.relay()
        exchange.finish_rows()

    def ready():
        get_select.wait()
        wait_all(get_dec)

    quarter = select.shape[0] // 2
    dec_select = select.at[pl.ds(pl.multiple_of(peers.bit(1) * quarter, 16), quarter)]
    dec_products = Products(peers, dec_select, 2, steps, *dec_scratch)
    dec_products.add(
        [dec_gys.at[place] for place in range(4)], [[dec_hiddens.at[place] for place in range(4)]],
        ffout.at[pl.ds(1, 1)], before=ready,
    )
    enc_products = Products(peers, select, 1, steps, *enc_scratch)
    enc_products.add(
        [enc_gy, x_enc_gy], [(enc_hidden, x_enc_hidden)], ffout.at[pl.ds(0, 1)], before=arrived
    )
    stream = Stream(dec_products.items + enc_products.items, lag_of(steps))
    staged = []

    def fetch_rows(place):
        source = (h1_all, x_h1_all)[place // 4]
        staged.append(loads.start(source.at[place % 4], stage.at[place % 2]))

    def choose_next(place):
        staged.pop(0).wait()
        choose_rows(select, stage[place % 2], chosen_h1, place * enc_rows)
        if place + 2 < 8:
            fetch_rows(place + 2)

    rows, width = enc_mid.shape
    units = enc_gg.shape[2]
    small[...] = jnp.zeros_like(small)
    small[:8] = gains_mid[...]

    get_fi.wait()

    def grad_part(slots, low, high):
        gate = enc_gg[slots].reshape(2 * rows, units)
        up_proj = enc_gu[slots].reshape(2 * rows, units)
        return dot_last(gate, wfi[0, low:high, :]) + dot_last(up_proj, wfi[1, low:high, :])

    for low, high in tiles(width):
        value = grad_part(slice(2, 4), low, high)
        part[:, low:high] = value[:rows]
        send[0, :, low:high] = to_low(value[rows:])
    for place in range(2):
        fetch_rows(place)
    first = peers.send(send.at[0], recv.at[0], peers.sib)
    stream.pump(1)
    get_vo1.wait()
    residual_dec = dec_one_grad[...]
    grad_y = to_low(residual_dec)
    self_gy[...] = grad_y
    owned.append(to_owners(peers, (hs, hs, hs, self_gy), left_self, short, own_sem.at[2]))
    grad_out_dec = to_low(dot(grad_y, wvo[1, :, INNER:]))
    exchange.spread()
    first.wait_recv()
    send[2] = to_low(part[...] + recv[0].astype(F32))
    second = peers.send(send.at[2], recv.at[2], peers.far)
    for low, high in tiles(width):
        value = grad_part(slice(0, 2), low, high)
        part[:, low:high] = value[:rows]
        send[1, :, low:high] = to_low(value[rows:])
    third = peers.send(send.at[1], recv.at[1], peers.sib)

    stream.pump(1)
    attend_back(self_q[...], self_kv, self_p, grad_out_dec, self_gq, self_gkv_full, self_gs)
    self_sum = SumBlocks(peers, self_gkv_full, self_send, self_recv)
    self_sum.cross()

    stream.pump(1)
    for place in range(3):
        choose_next(place)

    columns = []
    for bucket in range(BUCKETS):
        here = jnp.where(self_bucket[...] == bucket, 1.0, 0.0)
        sums = jnp.sum(self_gs[...].astype(F32) * here[None], axis=1)
        columns.append(jnp.sum(sums, axis=1, keepdims=True))
    self_table = jnp.concatenate(columns, axis=1)

    stream.pump(1)
    third.wait_recv()
    part[...] = part[...] + recv[1].astype(F32)
    second.wait_recv()
    wait_all(get_mid)
    value, gain_row = norm_back(enc_mid[...], gains[1:2], part[...] + recv[2].astype(F32))
    small[1:2] = gain_row
    residual = enc_end_grad[...] + value
    grad_y = to_low(residual)
    enc_ay[...] = grad_y
    enc_grad[...] = residual

    grad_out = to_low(dot(grad_y, wvo[0, :, INNER:]))
    attend_back(enc_q[...], enc_kv, enc_p, grad_out, enc_gq, enc_gkv_full, enc_gs)
    enc_sum = SumBlocks(peers, enc_gkv_full, kv_send, kv_recv)
    stream.pump(2)
    wait_all(get_last)
    for low, high in tiles(width):
        part[:, low:high] = dot_last(enc_gq[...], wqk[0, low:high, :INNER])
    enc_sum.cross()

    stream.pump(1)
    choose_next(3)
    own_kv = to_low(self_sum.result())
    self_gk[...] = own_kv[:, :INNER]
    self_gv[...] = own_kv[:, INNER:]
    for low, high in tiles(width):
        dec_grad[:, low:high] = dot_last(self_gq[...], wqk[1, low:high, :INNER]) + kv_back(
            own_kv, wqk.at[1], wvo.at[1], low, high
        )
    value, gain_row = norm_back(dec_x[...].astype(F32), gains[3:4], dec_grad[...])
    small[3:4] = gain_row
    dec_grad[...] = residual_dec + value

    turn = lax.broadcasted_iota(jnp.int32, (rows, rows), 0) + lax.broadcasted_iota(
        jnp.int32, (rows, rows), 1
    )
    turn = jnp.where(turn == rows - 1, 1.0, 0.0).astype(LOW)
    offsets = []
    for head in range(HEADS):
        turned = dot(turn, enc_gs[head])
        spread = jnp.concatenate([turned, jnp.zeros((rows, rows), F32)], axis=1)
        spread = pltpu.roll(spread, 0, 1, stride=1, stride_axis=0)
        offsets.append(jnp.sum(spread, axis=0, keepdims=True))
    enc_table = jnp.dot(
        jnp.concatenate(offsets + [jnp.zeros((2, offsets[0].shape[1]), F32)], axis=0),
        enc_spots[...], precision=HIGH, preferred_element_type=F32,
    )
    small[8:, :BUCKETS] = enc_table
    small[8 : 8 + HEADS, PAIR : PAIR + BUCKETS] = self_table

    stream.pump(2)
    own_kv = to_low(enc_sum.result())
    enc_gk[...] = own_kv[:, :INNER]
    enc_gv[...] = own_kv[:, INNER:]
    for low, high in tiles(width):
        part[:, low:high] += kv_back(own_kv, wqk.at[0], wvo.at[0], low, high)
    value, gain_row = norm_back(enc_x[...].astype(F32), gains[0:1], part[...])
    small[0:1] = gain_row
    enc_grad[...] += value
    for place in range(4, 8):
        stream.pump(1)
        choose_next(place)
    stream.drain()
    exchange.finish_whole()
    for sends in owned:
        owners_done(peers, sends)
    peers.finish()


def kc_call(size, block, padded, near, streamed):
    enc_gg, dec_x = near[0], near[6]
    attn_qk, attn_vo, ff_in = streamed[:3]
    rows, width = streamed[4].shape
    dec_rows = dec_x.shape[0]
    units = ff_in.shape[3]
    kv_width = 2 * INNER
    total = 4 * rows
    half = size * padded // 2
    steps = size.bit_length() - 1
    items = len(tiles(units, CHUNK))
    shape = jax.ShapeDtypeStruct
    outs = [
        shape((rows, width), F32), shape((rows, width), LOW), shape((rows, INNER), LOW),
        shape((rows, INNER), LOW), shape((rows, INNER), LOW),
        shape((dec_rows, width), F32), shape((dec_rows, width), LOW),
        shape((dec_rows, INNER), LOW), shape((dec_rows, INNER), LOW),
        shape((dec_rows, INNER), LOW),
        shape((16, width), F32), shape((2, block, units), F32),
        shape((2, half // 2, 2 * total), LOW), shape((4, rows, width), LOW),
        shape((4, rows, INNER), LOW),
    ]
    apart = [
        shape((4, dec_rows, width), LOW),
        shape(enc_gg.shape, LOW), shape(enc_gg.shape, LOW),
    ]
    vmem = pl.BlockSpec(memory_space=pltpu.VMEM)
    hbm = pl.BlockSpec(memory_space=pltpu.HBM)
    copies = 3 * 3 + 3 + 3 + 3 * 3 + items * (2 * steps - 3)
    return pl.pallas_call(
        functools.partial(kc_kernel, steps=steps),
        out_shape=outs + apart,
        in_specs=[vmem] * len(near) + [hbm] * len(streamed),
        out_specs=[vmem] * len(outs) + [hbm] * len(apart),
        scratch_shapes=[
            pltpu.VMEM((2,) + attn_qk.shape[1:], LOW), pltpu.VMEM((2,) + attn_vo.shape[1:], LOW),
            pltpu.VMEM(ff_in.shape[1:], LOW), pltpu.VMEM((HEADS, rows, total), LOW),
            pltpu.VMEM((HEADS, dec_rows, 4 * dec_rows), LOW),
            pltpu.VMEM((rows, width), F32), pltpu.VMEM((3, rows, width), LOW),
            pltpu.VMEM((3, rows, width), LOW),
            pltpu.VMEM((4, rows, kv_width), F32), pltpu.VMEM((3, rows, kv_width), LOW),
            pltpu.VMEM((3, rows, kv_width), LOW),
            pltpu.VMEM((4, dec_rows, kv_width), F32), pltpu.VMEM((3, dec_rows, kv_width), LOW),
            pltpu.VMEM((3, dec_rows, kv_width), LOW), pltpu.VMEM((4, rows, width), LOW),
            pltpu.VMEM((rows, width), F32), pltpu.VMEM((rows, width), F32),
            pltpu.VMEM((rows, width), LOW), pltpu.VMEM((4, rows, kv_width), LOW),
            pltpu.VMEM((HEADS, rows, total), F32), pltpu.VMEM((4, rows, width), LOW),
            pltpu.VMEM((4, 4, dec_rows, width), LOW), pltpu.VMEM((4, 4, dec_rows, units), LOW),
            pltpu.VMEM((4, rows, units), LOW), pltpu.VMEM((4, rows, units), LOW),
            pltpu.VMEM((half, width), LOW), pltpu.VMEM((2, rows, width), LOW),
            *product_scratch(size, padded, 4 * 4 * dec_rows, items, 2),
            *product_scratch(size, padded, 2 * total, items, 1),
            pltpu.SemaphoreType.DMA((copies,)), pltpu.SemaphoreType.DMA((copies,)),
            pltpu.SemaphoreType.DMA((3 + 8 + 5 + 3 + 3 + 8,)), pltpu.SemaphoreType.DMA((3,)),
        ],
        compiler_params=pltpu.CompilerParams(
            collective_id=2, has_side_effects=True, vmem_limit_bytes=62 * 1024 * 1024
        ),
        name="last_chain",
    )(*near, *streamed)
class Spread:
    def __init__(self, peers, partners, total, recv):
        self.peers, self.partners, self.total, self.recv = peers, partners, total, recv
        self.steps = len(partners) + 1

    def run(self, step):
        if step:
            self.copy.wait_recv()
            self.total[step] = self.total[step - 1] + self.recv[step - 1]
        if step < len(self.partners):
            self.copy = self.peers.send(
                self.total.at[step], self.recv.at[step], self.partners[step]
            )


def kd_kernel(
    small,
    chosen_h1, enc_gg_all, x_enc_gg_all, enc_gu_all, x_enc_gu_all, select_all,
    left_cross_all, right_cross_all, left_self_all, h0, enc_ay,
    enc_gq, enc_gk, enc_gv, enc_o, self_gq, self_gk, self_gv, self_o, dec_ffin,
    ffin, qk, vo, small_out,
    enc_ffin, enc_gg, x_enc_gg, enc_gu, x_enc_gu, select, chosen_attn, left_enc, left_cross,
    left_self, right_enc, right_cross, right_self, attn_total, attn, small_total, small_recv,
    *rest,
    block, steps,
):
    scratch, rest = rest[: 2 * steps], rest[2 * steps :]
    at_send, at_recv = rest[:steps], rest[steps : 2 * steps]
    send_sem, recv_sem, load_sem, own_sem = rest[2 * steps :]
    peers = Peers(send_sem, recv_sem)
    loads = Loads(load_sem)
    get_gate = [
        loads.start(chosen_h1, scratch[0]), loads.start(enc_gg_all, enc_gg),
        loads.start(x_enc_gg_all, x_enc_gg),
    ]
    get_cross = [
        loads.start(select_all, select), loads.start(left_cross_all, left_cross),
        loads.start(right_cross_all, right_cross),
    ]
    get_up = [loads.start(enc_gu_all, enc_gu), loads.start(x_enc_gu_all, x_enc_gu)]
    get_self = [loads.start(left_self_all, left_self)]
    passed = loads.start(dec_ffin, ffin.at[1])
    partners = [peers.across(place) for place in range(steps)]
    peers.greet([peers.diag] + partners)
    dec_rows, enc_rows = self_gq.shape[0], enc_gq.shape[0]
    own_self = to_owners(
        peers, (self_gq, self_gk, self_gv, self_o), right_self, (dec_rows,) * 4, own_sem.at[0]
    )
    own_enc = to_owners(
        peers, (enc_gq, enc_gk, enc_gv, enc_o), right_enc, (enc_rows,) * 4, own_sem.at[1]
    )
    own_left = to_owners(peers, (h0, h0, h0, enc_ay), left_enc, (enc_rows,) * 4, own_sem.at[3])
    spread = Spread(peers, [peers.sib, peers.far] + partners, small_total, small_recv)
    small_total[0] = small[...]
    spread.run(0)

    products = Products(peers, None, 1, steps, *scratch)
    products.add(
        None, [(enc_gg, x_enc_gg), (enc_gu, x_enc_gu)], enc_ffin,
        ready=(lambda: wait_all(get_gate), lambda: wait_all(get_up)),
    )

    def wait_self():
        wait_all(get_self)
        owners_done(peers, own_self)

    def wait_enc():
        owners_done(peers, own_enc)
        owners_done(peers, own_left)

    kinds = (
        (2, left_cross, right_cross, lambda: wait_all(get_cross)),
        (1, left_self, right_self, wait_self), (0, left_enc, right_enc, wait_enc),
    )
    attn_items, gathers = [], []
    for a, left, right, arrived in kinds:
        rows = left.shape[0] * left.shape[1]

        def before(left=left, arrived=arrived):
            arrived()
            for half in range(2):
                for low, high in tiles(left.shape[0] * left.shape[1]):
                    chosen_attn[half, :, low:high] = to_low(
                        dot_last(select[half], flat(left[...])[low:high])
                    )

        for place, (low, high) in enumerate(tiles(INNER, CHUNK)):

            def product(half, right=right, rows=rows, low=low, high=high):
                return dot(chosen_attn[half, :, :rows], flat(right[:, :, low:high]))

            def finish(value, a=a, low=low, high=high, last=high == INNER):
                attn[a, peers.own, :, low:high] = to_low(value)
                if last:
                    gathers.append((a, Gather(peers, attn.at[a], False)))
                    gathers[-1][1].start()

            slot = len(attn_items)
            item = Reduce(
                peers, list(range(steps)), product, high - low, attn_total.at[slot], at_send,
                at_recv, slot, finish, products.ships,
            )
            item.before = [before] if place == 0 else []
            attn_items.append(item)

    items = []
    for place in range(max(len(products.items), len(attn_items) + 2)):
        if 2 <= place < len(attn_items) + 2:
            items.append(attn_items[place - 2])
        if place < len(products.items):
            items.append(products.items[place])
    stream = Stream(items, lag_of(steps))
    while stream.now <= stream.last:
        stream.pump()
        if stream.now % 2 == 0 and stream.now // 2 < spread.steps:
            spread.run(stream.now // 2)
    small_out[...] = small_total[spread.steps - 1]
    left = pltpu.make_async_copy(enc_ffin, ffin.at[0], own_sem.at[2])
    left.start()
    for a, gather in gathers:
        gather.wait_near()
        gather.relay()
    for a, gather in gathers:
        gather.wait_far()
        for place, out in enumerate((qk, qk, vo, vo)):
            lanes = slice(place % 2 * INNER, (place % 2 + 1) * INNER)
            out[a, :, lanes] = attn[a, place, :, :].astype(F32)[:block]
    left.wait()
    passed.wait()
    peers.finish()


def kd_call(size, block, padded, width, small, streamed):
    gate, self_q = streamed[1], streamed[15]
    units, enc_rows, dec_rows = gate.shape[2], gate.shape[1], self_q.shape[0]
    steps = size.bit_length() - 1
    shape = jax.ShapeDtypeStruct
    outs = [
        shape((2, 2, block, units), F32), shape((3, block, 2 * INNER), F32),
        shape((3, block, 2 * INNER), F32), shape(small.shape, F32),
    ]
    vmem = pl.BlockSpec(memory_space=pltpu.VMEM)
    hbm = pl.BlockSpec(memory_space=pltpu.HBM)
    half = size * padded // 2
    ff_items = 2 * len(tiles(units, CHUNK))
    at_items = 3 * len(tiles(INNER, CHUNK))
    at_heights = [half >> step for step in range(steps)]

    def bufs(items, heights):
        return [pltpu.VMEM((items, height, CHUNK), LOW) for height in heights]

    copies = ff_items * (steps - 1) + at_items * steps + 3 * 3 + (2 + steps) + 9
    return pl.pallas_call(
        functools.partial(kd_kernel, block=block, steps=steps),
        out_shape=outs,
        in_specs=[vmem] + [hbm] * len(streamed),
        out_specs=[hbm] + [vmem] * 3,
        scratch_shapes=[
            pltpu.VMEM((2, block, units), F32),
            *[pltpu.VMEM(gate.shape, LOW)] * 4,
            pltpu.VMEM((2, half, width), LOW),
            pltpu.VMEM((2, half, 4 * enc_rows), LOW),
            pltpu.VMEM((4, enc_rows, width), LOW), pltpu.VMEM((4, enc_rows, width), LOW),
            pltpu.VMEM((4, dec_rows, width), LOW),
            pltpu.VMEM((4, enc_rows, INNER), LOW), pltpu.VMEM((4, enc_rows, INNER), LOW),
            pltpu.VMEM((4, dec_rows, INNER), LOW),
            pltpu.VMEM((at_items, half, CHUNK), F32),
            pltpu.VMEM((3, 4, padded, INNER), LOW),
            pltpu.VMEM((3 + steps,) + small.shape, F32),
            pltpu.VMEM((2 + steps,) + small.shape, F32),
            *product_scratch(size, padded, 8 * enc_rows, ff_items, 1),
            *bufs(2, at_heights), *bufs(at_items, at_heights),
            pltpu.SemaphoreType.DMA((copies,)), pltpu.SemaphoreType.DMA((copies,)),
            pltpu.SemaphoreType.DMA((10,)), pltpu.SemaphoreType.DMA((4,)),
        ],
        compiler_params=pltpu.CompilerParams(
            collective_id=3, has_side_effects=True, vmem_limit_bytes=62 * 1024 * 1024
        ),
        name="weight_sums",
    )(small, *streamed)


def block_choice(size, block, padded, width):
    bits = size.bit_length() - 1
    columns = []
    for place in range(size):
        owner = sum(((place >> (bits - 1 - bit)) & 1) << bit for bit in range(bits))
        columns += [owner * block + inside if inside < block else -1 for inside in range(padded)]
    columns = jnp.asarray(columns, jnp.int32)
    select = (columns[:, None] == jnp.arange(width)[None, :]).astype(LOW)
    return select.reshape(2, size * padded // 2, width)


def on_device(
    enc_x, dec_x, dec_cot, item_count, enc_mask, dec_mask, enc_buckets, dec_buckets,
    gains, tables, attn_qk, attn_vo, ff_in, ff_out,
):
    tensor_id = lax.axis_index("tensor")
    size = lax.axis_size("dp")
    enc_own, dec_own = enc_x.shape[0], dec_x.shape[0]
    width = enc_x.shape[1]
    block = width // size
    padded = (block + 15) // 16 * 16
    small, (enc_spots, self_bucket) = prepare(
        item_count, enc_mask, dec_mask, enc_buckets, dec_buckets, tables, enc_own, dec_own
    )
    select = block_choice(size, block, padded, width)
    ff_out_t = jnp.swapaxes(ff_out, 1, 2)
    dec_x, dec_cot = pad_rows(dec_x), pad_rows(dec_cot)
    (
        h0, enc_q, enc_kv, enc_p, enc_o, enc_mid, h1, enc_gelu, enc_slope, enc_hidden, enc_end,
        memory, cross_kv, hs, self_q, self_kv, self_p, self_o, dec_one, hc, cross_q, cross_p,
        cross_o, dec_two, hf, dec_gy, dec_gg, dec_gu, dec_hidden,
    ) = ka_call(enc_x, dec_x, dec_cot, gains, *small, attn_qk, attn_vo, ff_in, ff_out_t)
    (
        dec_out, cross_gy, cross_gq, cross_gk, cross_gv, dec_one_grad, enc_end_grad, enc_gy,
        enc_gg, enc_gu, gains_mid, dec_ffin, x_dec_hidden, z_dec_hidden, zx_dec_hidden, x_dec_gy,
        z_dec_gy, zx_dec_gy, x_h1, x_enc_hidden,
    ) = kb_call(
        dec_gg, dec_gu, dec_hidden, dec_cot, dec_two, dec_one, gains, cross_q, cross_kv, cross_p,
        enc_end, enc_gelu, enc_slope, attn_qk, attn_vo, ff_in, ff_out_t, hf, dec_gy, h1, enc_hidden,
        select, size, block, padded,
    )
    (
        enc_grad, enc_ay, enc_gq, enc_gk, enc_gv, dec_grad, self_gy, self_gq, self_gk, self_gv,
        sums, ffout_sum, chosen_h1, left_cross, right_cross, left_self, x_enc_gg,
        x_enc_gu,
    ) = kc_call(
        size, block, padded,
        [
            enc_gg, enc_gu, gains, gains_mid, enc_q, dec_one_grad, dec_x, self_q, self_kv, self_p,
            enc_spots, self_bucket,
        ],
        [
            attn_qk, attn_vo, ff_in, enc_end_grad, enc_mid, enc_x, enc_kv, enc_p, enc_gy, dec_gy,
            x_dec_gy, z_dec_gy, zx_dec_gy, dec_hidden, x_dec_hidden, z_dec_hidden, zx_dec_hidden,
            enc_hidden, x_enc_hidden, select, h1, x_h1, hs, hc, memory, cross_gy, cross_gq,
            cross_gk, cross_gv, cross_o,
        ],
    )
    ffin_sum, qk_sum, vo_sum, sums = kd_call(
        size, block, padded, width, sums,
        [
            chosen_h1, enc_gg, x_enc_gg, enc_gu, x_enc_gu, select, left_cross, right_cross,
            left_self, h0, enc_ay, enc_gq, enc_gk, enc_gv, enc_o, self_gq, self_gk, self_gv, self_o,
            dec_ffin,
        ],
    )
    ffout_sum = jnp.swapaxes(ffout_sum, 1, 2)
    table_rows = sums[8 : 8 + HEADS]
    tables_sum = jnp.stack(
        [table_rows[:, :BUCKETS].T, table_rows[:, PAIR : PAIR + BUCKETS].T]
    )
    return (
        dec_out[:dec_own], enc_grad, dec_grad[:dec_own], sums[:6], tables_sum, qk_sum, vo_sum,
        ffin_sum, ffout_sum,
    )


def solution(mesh):
    rows = P(("dp", "tensor"), None)
    return jax.shard_map(
        on_device,
        mesh=mesh,
        in_specs=(
            rows, rows, rows, P("dp"), P("dp"), P("dp"), P(), P(), P(), P(), P(), P(),
            P(None, None, None, "tensor"), P(None, "tensor", None),
        ),
        out_specs=(
            rows, rows, rows, P(), P(), P(None, "dp", None), P(None, "dp", None),
            P(None, None, "dp", "tensor"), P(None, "tensor", "dp"),
        ),
        check_vma=False,
    )
```

```python
import functools

import jax
import jax.numpy as jnp
from jax import lax
from jax.experimental import pallas as pl
from jax.experimental.pallas import tpu as pltpu
from jax.sharding import PartitionSpec as P

HEADS = 6
HEAD = 64
INNER = HEADS * HEAD
PAIRS = HEADS // 2
PAIR = 2 * HEAD
BUCKETS = 32
EPSILON = 1e-06
MASKED = -1000000000.0
HIGH = lax.Precision.HIGHEST
F32 = jnp.float32
LOW = jnp.bfloat16
DEC_PAD = 32
VMEM_BYTES = 60 * 1024 * 1024
ROOT = 0.7978845608028654
CUBE = 0.044715


def to_low(value):
    return value.astype(LOW)


def dot(left, right):
    return jnp.dot(left, right, preferred_element_type=F32)


def dot_first(left, right):
    return lax.dot_general(left, right, (((0,), (0,)), ((), ())), preferred_element_type=F32)


def dot_last(left, right):
    return lax.dot_general(left, right, (((1,), (1,)), ((), ())), preferred_element_type=F32)


def norm_gain(rows, gain):
    return rows * lax.rsqrt(jnp.mean(rows * rows, axis=-1, keepdims=True) + EPSILON) * gain


def norm_back(rows, gain, grad_rows):
    scale = lax.rsqrt(jnp.mean(rows * rows, axis=-1, keepdims=True) + EPSILON)
    normed = rows * scale
    scaled = grad_rows * gain
    inner = jnp.mean(scaled * normed, axis=-1, keepdims=True)
    grad_gain = jnp.sum(grad_rows * normed, axis=0, keepdims=True)
    return scale * (scaled - normed * inner), grad_gain


def act_parts(gate, up_proj):
    square = gate * gate
    curve = jnp.tanh(ROOT * gate * (1.0 + CUBE * square))
    half = 0.5 * (1.0 + curve)
    slope = half + 0.5 * gate * (1.0 - curve * curve) * (ROOT * (1.0 + 3.0 * CUBE * square))
    return gate * half, up_proj * slope


def tiles(width, step=256):
    return [(start, min(start + step, width)) for start in range(0, width, step)]


class Peers:
    def __init__(self, send_sem, recv_sem):
        dp, tensor = lax.axis_index("dp"), lax.axis_index("tensor")
        chip, core = lax.div(tensor, 2), lax.rem(tensor, 2)
        self.dp = dp
        self.own = tensor
        self.sib = chip * 2 + (1 - core)
        self.far = (1 - chip) * 2 + core
        self.diag = (1 - chip) * 2 + (1 - core)
        self.send_sem, self.recv_sem = send_sem, recv_sem
        self.used = 0
        self.copies = []

    def bit(self, place):
        return lax.rem(lax.div(self.dp, 2**place), 2)

    def across(self, place):
        return (self.dp + (1 - 2 * self.bit(place)) * 2**place, self.own)

    def device(self, peer):
        return peer if isinstance(peer, tuple) else (self.dp, peer)

    def greet(self, more=()):
        barrier = pltpu.get_barrier_semaphore()
        for peer in (self.sib, self.far) + tuple(more):
            pl.semaphore_signal(
                barrier, inc=1, device_id=self.device(peer), device_id_type=pl.DeviceIdType.MESH
            )
        pl.semaphore_wait(barrier, 2 + len(more))

    def send(self, source, target, peer):
        place = self.used
        self.used += 1
        assert place < self.send_sem.shape[0]
        copy = pltpu.make_async_remote_copy(
            src_ref=source,
            dst_ref=target,
            send_sem=self.send_sem.at[place],
            recv_sem=self.recv_sem.at[place],
            device_id=self.device(peer),
            device_id_type=pl.DeviceIdType.MESH,
        )
        copy.start()
        self.copies.append(copy)
        return copy

    def finish(self):
        for copy in self.copies:
            copy.wait_send()


class Gather:
    def __init__(self, peers, buf, near, source=None):
        self.peers, self.buf, self.source = peers, buf, source
        if near:
            self.slots = (0, 1, 2, 2, 3)
        else:
            self.slots = (peers.own, peers.own, peers.own, peers.far, peers.far)

    def start(self):
        own, at_sib, at_far, unused, unused = self.slots
        source = self.buf.at[own] if self.source is None else self.source
        self.to_far = self.peers.send(source, self.buf.at[at_far], self.peers.far)
        self.to_sib = self.peers.send(source, self.buf.at[at_sib], self.peers.sib)

    def wait_near(self):
        self.to_sib.wait_recv()

    def relay(self):
        unused, unused, unused, far, far_at_sib = self.slots
        self.to_far.wait_recv()
        self.relayed = self.peers.send(
            self.buf.at[far], self.buf.at[far_at_sib], self.peers.sib
        )

    def wait_far(self):
        self.relayed.wait_recv()


def attend(queries, kv, bias_of, allowed, weights_out, mixed_out):
    rows = queries.shape[0]
    total = kv.shape[0] * kv.shape[1]
    first = lax.broadcasted_iota(jnp.int32, (rows, PAIR), 1) < HEAD
    for pair in range(PAIRS):
        lanes = slice(pair * PAIR, (pair + 1) * PAIR)
        keys = kv[:, :, lanes].reshape(total, PAIR)
        values = kv[:, :, INNER + pair * PAIR : INNER + (pair + 1) * PAIR].reshape(total, PAIR)
        both = queries[:, lanes].astype(F32)
        mixed = []
        for half in range(2):
            head = 2 * pair + half
            here = to_low(jnp.where(first if half == 0 else ~first, both, 0.0))
            scores = dot_last(here, keys)
            if bias_of is not None:
                scores = scores + bias_of(head)
            scores = jnp.where(allowed, scores, MASKED)
            shifted = jnp.exp(scores - jnp.max(scores, axis=-1, keepdims=True))
            weights = shifted / jnp.sum(shifted, axis=-1, keepdims=True)
            weights_out[head] = weights
            mixed.append(dot(to_low(weights), values))
        mixed_out[:, lanes] = to_low(jnp.where(first, mixed[0], mixed[1]))


def attend_back(queries, kv, weights_in, grad_out, grad_q_out, grad_kv_out, grad_s_out):
    rows = queries.shape[0]
    total = kv.shape[0] * kv.shape[1]
    block = kv.shape[1]
    first = lax.broadcasted_iota(jnp.int32, (rows, PAIR), 1) < HEAD
    first_key = lax.broadcasted_iota(jnp.int32, (total, PAIR), 1) < HEAD
    for pair in range(PAIRS):
        lanes = slice(pair * PAIR, (pair + 1) * PAIR)
        value_lanes = slice(INNER + pair * PAIR, INNER + (pair + 1) * PAIR)
        keys = kv[:, :, lanes].reshape(total, PAIR)
        values = kv[:, :, value_lanes].reshape(total, PAIR)
        query = queries[:, lanes]
        grad = grad_out[:, lanes]
        grad_wide = grad.astype(F32)
        grad_q, grad_k, grad_v = [], [], []
        for half in range(2):
            head = 2 * pair + half
            here = to_low(jnp.where(first if half == 0 else ~first, grad_wide, 0.0))
            weights = weights_in[head]
            grad_weights = dot_last(here, values)
            weighted = jnp.sum(weights * grad_weights, axis=-1, keepdims=True)
            grad_scores = to_low(weights * (grad_weights - weighted))
            if grad_s_out is not None:
                grad_s_out[head] = grad_scores
            grad_q.append(dot(grad_scores, keys))
            grad_k.append(dot_first(grad_scores, query))
            grad_v.append(dot_first(to_low(weights), grad))
        grad_q_out[:, lanes] = to_low(jnp.where(first, grad_q[0], grad_q[1]))
        grad_kv_out[:, :, lanes] = jnp.where(first_key, grad_k[0], grad_k[1]).reshape(
            4, block, PAIR
        )
        grad_kv_out[:, :, value_lanes] = jnp.where(first_key, grad_v[0], grad_v[1]).reshape(
            4, block, PAIR
        )


class Exchange:
    def __init__(self, peers, whole, rows, place=0):
        partner = peers.across(place)
        self.rows = [
            (peers.send(own.at[0], other.at[0], partner), Gather(peers, other, True))
            for own, other in rows
        ]
        self.whole = [peers.send(own, other, partner) for own, other in whole]

    def spread(self):
        for copy, gather in self.rows:
            copy.wait_recv()
            gather.start()

    def relay(self):
        for unused, gather in self.rows:
            gather.wait_near()
            gather.relay()

    def finish_rows(self):
        for unused, gather in self.rows:
            gather.wait_far()

    def finish_first(self):
        self.whole.pop(0).wait_recv()

    def finish_whole(self):
        for copy in self.whole:
            copy.wait_recv()
        self.whole = []


class Loads:
    def __init__(self, sems):
        self.sems, self.used = sems, 0

    def start(self, source, target):
        copy = pltpu.make_async_copy(source, target, self.sems.at[self.used])
        self.used += 1
        copy.start()
        return copy


def wait_all(copies):
    for copy in copies:
        copy.wait()
    copies.clear()


def project_kv(rows, wqk, wvo, target):
    target[:, :INNER] = to_low(dot(rows, wqk[:, INNER:]))
    target[:, INNER:] = to_low(dot(rows, wvo[:, :INNER]))


def ff_up(rows, w_in, gelu_out, slope_out, hidden_out, slots):
    count, block = slots.stop - slots.start, gelu_out.shape[1]
    for low, high in tiles(gelu_out.shape[2]):
        gate = dot(rows, w_in[0, :, low:high])
        up_proj = dot(rows, w_in[1, :, low:high])
        gelu, slope = act_parts(gate, up_proj)
        shape = (count, block, high - low)
        gelu_out[slots, :, low:high] = gelu.reshape(shape)
        slope_out[slots, :, low:high] = slope.reshape(shape)
        hidden_out[slots, :, low:high] = to_low(gelu * up_proj).reshape(shape)


def reduce_far(peers, diag_part, far_part, send, recv):
    width = send.shape[2]
    for low, high in tiles(width):
        send[0, :, low:high] = to_low(diag_part(low, high))
    first = peers.send(send.at[0], recv.at[0], peers.sib)
    first.wait_recv()
    for low, high in tiles(width):
        send[2, :, low:high] = to_low(
            far_part(low, high) + recv[0, :, low:high].astype(F32)
        )
    return peers.send(send.at[2], recv.at[2], peers.far)


def ka_kernel(
    enc_x, dec_x_short, dec_cot_short, gains, enc_terms, self_bias, item_count, enc_mask, dec_mask,
    qk_all, vo_all, fi_all, fo_all,
    h0, enc_q, enc_kv, enc_p, enc_o, enc_mid, h1, enc_gelu, enc_slope, enc_hidden, enc_end, memory,
    cross_kv, hs, self_q, self_kv, self_p, self_o, dec_one, hc, cross_q, cross_p, cross_o, dec_two,
    hf, dec_gy, dec_gg, dec_gu, dec_hidden, dec_x, dec_cot,
    x_h1, x_enc_hidden,
    wqk, wvo, wfi, wfo, part, send, recv, dec_gelu, dec_slope, send_sem, recv_sem, load_sem,
):
    peers = Peers(send_sem, recv_sem)
    loads = Loads(load_sem)
    get_qk, get_vo, get_fi, get_fo = {}, {}, {}, {}
    for a in (0, 1):
        get_qk[a] = loads.start(qk_all.at[a], wqk.at[a])
        get_vo[a] = loads.start(vo_all.at[a], wvo.at[a])
    get_fi[0] = loads.start(fi_all.at[0], wfi.at[0])
    get_fo[0] = loads.start(fo_all.at[0], wfo.at[0])
    get_qk[2] = loads.start(qk_all.at[2], wqk.at[2])
    get_vo[2] = loads.start(vo_all.at[2], wvo.at[2])
    get_fi[1] = loads.start(fi_all.at[1], wfi.at[1])
    get_fo[1] = loads.start(fo_all.at[1], wfo.at[1])
    peers.greet([peers.across(0)])

    enc_rows, dec_rows, real_rows = enc_x.shape[0], dec_x.shape[0], dec_x_short.shape[0]
    enc_total, dec_total = 4 * enc_rows, 4 * real_rows

    def item_of(place, total):
        scaled = place * item_count[...]
        return sum((scaled >= part * total).astype(jnp.int32) for part in (1, 2, 3))

    def counted(rows, columns, axis):
        return lax.broadcasted_iota(jnp.int32, (rows, columns), axis)

    enc_code = jnp.where(enc_mask[...] == 1, item_of(counted(1, enc_total, 1), enc_total), -1)
    enc_item = item_of(counted(enc_rows, 1, 0) + peers.own * enc_rows, enc_total)
    slot = counted(1, 4 * dec_rows, 1)
    inside = lax.rem(slot, dec_rows)
    key_place = lax.div(slot, dec_rows) * real_rows + inside
    key_item = jnp.where(
        (inside < real_rows) & (dec_mask[...] == 1), item_of(key_place, dec_total), -1
    )
    row = counted(dec_rows, 1, 0)
    row_place = row + peers.own * real_rows
    dec_item = jnp.where(row < real_rows, item_of(row_place, dec_total), -2)
    self_allowed = (dec_item == key_item) & (key_place <= row_place)

    fill = jnp.zeros((dec_rows - real_rows, dec_x.shape[1]), F32)
    for short, padded in ((dec_x_short, dec_x), (dec_cot_short, dec_cot)):
        padded[...] = to_low(jnp.concatenate([short[...].astype(F32), fill], axis=0))

    normed = to_low(norm_gain(enc_x[...].astype(F32), gains[0:1]))
    h0[...] = normed
    get_qk[0].wait()
    get_vo[0].wait()
    project_kv(normed, wqk.at[0], wvo.at[0], enc_kv.at[peers.own])
    enc_gather = Gather(peers, enc_kv, False)
    enc_gather.start()
    normed_dec = to_low(norm_gain(dec_x[...].astype(F32), gains[3:4]))
    hs[...] = normed_dec
    get_qk[1].wait()
    get_vo[1].wait()
    project_kv(normed_dec, wqk.at[1], wvo.at[1], self_kv.at[peers.own])
    self_gather = Gather(peers, self_kv, False)
    self_gather.start()
    dec_gy[0] = dec_cot[...]
    gy_gather = Gather(peers, dec_gy, True)
    gy_gather.start()
    enc_q[...] = to_low(dot(normed, wqk[0, :, :INNER]))
    self_q[...] = to_low(dot(normed_dec, wqk[1, :, :INNER]))

    enc_gather.wait_near()
    enc_gather.relay()
    enc_allowed = enc_item == enc_code

    def enc_bias(head):
        own_rows, period = h0.shape[0], enc_terms.shape[1]
        spread = jnp.broadcast_to(enc_terms[head : head + 1, :], (own_rows, period))
        rolled = pltpu.roll(spread, 0, 1, stride=1, stride_axis=0)
        return rolled[:, : period // 2]

    enc_gather.wait_far()
    attend(enc_q[...], enc_kv, enc_bias, enc_allowed, enc_p, enc_o)
    for low, high in tiles(enc_mid.shape[1]):
        enc_mid[:, low:high] = enc_x[:, low:high].astype(F32) + dot_last(
            enc_o[...], wvo[0, low:high, INNER:]
        )
    h1[0] = to_low(norm_gain(enc_mid[...], gains[1:2]))
    h1_gather = Gather(peers, h1, True)
    h1_gather.start()
    exchanges = [Exchange(peers, [(h1.at[0], x_h1)], [])]

    def hidden_part(low, high):
        return [(enc_hidden.at[slot], x_enc_hidden.at[slot]) for slot in range(low, high)]

    self_gather.wait_near()
    self_gather.relay()
    gy_gather.wait_near()
    gy_gather.relay()
    self_gather.wait_far()
    gy_gather.wait_far()
    attend(
        self_q[...], self_kv, lambda head: self_bias[head], self_allowed, self_p, self_o
    )
    for low, high in tiles(dec_one.shape[1]):
        dec_one[:, low:high] = dec_x[:, low:high].astype(F32) + dot_last(
            self_o[...], wvo[1, low:high, INNER:]
        )
    normed_dec = to_low(norm_gain(dec_one[...], gains[4:5]))
    hc[...] = normed_dec

    h1_gather.wait_near()
    get_fi[0].wait()
    get_fo[0].wait()
    block, width = h1.shape[1], h1.shape[2]

    def both(buf, slots):
        return buf[slots].reshape((slots.stop - slots.start) * block, buf.shape[2])

    near, away = slice(0, 2), slice(2, 4)
    ff_up(both(h1, near), wfi.at[0], enc_gelu, enc_slope, enc_hidden, near)
    exchanges.append(Exchange(peers, hidden_part(0, 2), []))
    h1_gather.relay()
    h1_gather.wait_far()
    ff_up(both(h1, away), wfi.at[0], enc_gelu, enc_slope, enc_hidden, away)
    hidden = both(enc_hidden, away)
    for low, high in tiles(width):
        value = dot_last(hidden, wfo[0, low:high, :])
        part[:, low:high] = value[:block]
        send[0, :, low:high] = to_low(value[block:])
    first = peers.send(send.at[0], recv.at[0], peers.sib)
    exchanges.append(Exchange(peers, hidden_part(2, 4), []))
    get_qk[2].wait()
    get_vo[2].wait()
    cross_q[...] = to_low(dot(hc[...], wqk[2, :, :INNER]))
    first.wait_recv()
    send[2] = to_low(part[...] + recv[0].astype(F32))
    second = peers.send(send.at[2], recv.at[2], peers.far)
    hidden = both(enc_hidden, near)
    for low, high in tiles(width):
        value = dot_last(hidden, wfo[0, low:high, :])
        part[:, low:high] = value[:block] + enc_mid[:, low:high]
        send[1, :, low:high] = to_low(value[block:])
    third = peers.send(send.at[1], recv.at[1], peers.sib)
    third.wait_recv()
    part[...] = part[...] + recv[1].astype(F32)
    second.wait_recv()
    ended = part[...] + recv[2].astype(F32)
    enc_end[...] = ended
    normed = to_low(norm_gain(ended, gains[2:3]))
    memory[...] = normed

    project_kv(normed, wqk.at[2], wvo.at[2], cross_kv.at[peers.own])
    cross_gather = Gather(peers, cross_kv, False)
    cross_gather.start()
    get_fi[1].wait()
    get_fo[1].wait()
    cross_allowed = dec_item == enc_code
    cross_gather.wait_near()
    cross_gather.relay()
    cross_gather.wait_far()
    attend(cross_q[...], cross_kv, None, cross_allowed, cross_p, cross_o)
    for low, high in tiles(dec_two.shape[1]):
        dec_two[:, low:high] = dec_one[:, low:high] + dot_last(
            cross_o[...], wvo[2, low:high, INNER:]
        )
    hf[0] = to_low(norm_gain(dec_two[...], gains[5:6]))
    hf_gather = Gather(peers, hf, True)
    hf_gather.start()

    rows = hf.shape[0] * hf.shape[1]
    hf_gather.wait_near()
    hf_gather.relay()
    grad_y = dec_gy[...].reshape(rows, width)
    hf_gather.wait_far()
    ff_up(hf[...].reshape(rows, width), wfi.at[1], dec_gelu, dec_slope, dec_hidden, slice(0, 4))
    for low, high in tiles(dec_gelu.shape[2]):
        grad_h = dot(grad_y, wfo[1, :, low:high]).reshape(4, hf.shape[1], high - low)
        dec_gg[:, :, low:high] = to_low(grad_h * dec_slope[:, :, low:high])
        dec_gu[:, :, low:high] = to_low(grad_h * dec_gelu[:, :, low:high])
    for exchange in exchanges:
        exchange.finish_whole()
    peers.finish()


def ka_call(enc_x, dec_x, dec_cot, gains, enc_terms, self_bias, item_count, enc_mask, dec_mask, attn_qk, attn_vo, ff_in, ff_out):
    rows, width = enc_x.shape
    dec_rows = DEC_PAD
    units = ff_in.shape[3]
    total = enc_mask.shape[1]
    kv_width = 2 * INNER
    shape = jax.ShapeDtypeStruct
    outs = [
        shape((rows, width), LOW), shape((rows, INNER), LOW), shape((4, rows, kv_width), LOW),
        shape((HEADS, rows, total), F32), shape((rows, INNER), LOW), shape((rows, width), F32),
        shape((4, rows, width), LOW), shape((4, rows, units), F32), shape((4, rows, units), F32),
        shape((4, rows, units), LOW), shape((rows, width), F32), shape((rows, width), LOW),
        shape((4, rows, kv_width), LOW),
        shape((dec_rows, width), LOW), shape((dec_rows, INNER), LOW),
        shape((4, dec_rows, kv_width), LOW), shape((HEADS, dec_rows, 4 * dec_rows), F32),
        shape((dec_rows, INNER), LOW), shape((dec_rows, width), F32),
        shape((dec_rows, width), LOW), shape((dec_rows, INNER), LOW),
        shape((HEADS, dec_rows, total), F32), shape((dec_rows, INNER), LOW),
        shape((dec_rows, width), F32),
        shape((4, dec_rows, width), LOW), shape((4, dec_rows, width), LOW),
        shape((4, dec_rows, units), LOW), shape((4, dec_rows, units), LOW),
        shape((4, dec_rows, units), LOW), shape((dec_rows, width), LOW),
        shape((dec_rows, width), LOW),
    ]
    traded = [shape((rows, width), LOW), shape((4, rows, units), LOW)]
    vmem = pl.BlockSpec(memory_space=pltpu.VMEM)
    hbm = pl.BlockSpec(memory_space=pltpu.HBM)
    copies = 3 * 6 + 3 + 1 + 4
    return pl.pallas_call(
        ka_kernel,
        out_shape=outs + traded,
        in_specs=[vmem] * 9 + [hbm] * 4,
        out_specs=[vmem] * len(outs) + [hbm] * len(traded),
        scratch_shapes=[
            pltpu.VMEM(attn_qk.shape, LOW), pltpu.VMEM(attn_vo.shape, LOW),
            pltpu.VMEM(ff_in.shape, LOW), pltpu.VMEM(ff_out.shape, LOW),
            pltpu.VMEM((rows, width), F32), pltpu.VMEM((3, rows, width), LOW),
            pltpu.VMEM((3, rows, width), LOW), pltpu.VMEM((4, dec_rows, units), F32),
            pltpu.VMEM((4, dec_rows, units), F32),
            pltpu.SemaphoreType.DMA((copies,)), pltpu.SemaphoreType.DMA((copies,)),
            pltpu.SemaphoreType.DMA((10,)),
        ],
        compiler_params=pltpu.CompilerParams(
            collective_id=0, has_side_effects=True, vmem_limit_bytes=VMEM_BYTES
        ),
        name="forward_chain",
    )(enc_x, dec_x, dec_cot, gains, enc_terms, self_bias, item_count, enc_mask, dec_mask,
      attn_qk, attn_vo, ff_in, ff_out)


def prepare(item_count, enc_mask, dec_mask, enc_buckets, dec_buckets, tables, enc_own, dec_own):
    tensor_id = lax.axis_index("tensor")
    enc_total, dec_total = enc_mask.shape[0], dec_mask.shape[0]
    slot = jnp.arange(4 * DEC_PAD)
    place = slot // DEC_PAD * dec_own + slot % DEC_PAD
    row_place = tensor_id * dec_own + jnp.arange(DEC_PAD)
    dec_live = jnp.pad(dec_mask.reshape(4, dec_own), ((0, 0), (0, DEC_PAD - dec_own)))
    onehot = (enc_buckets[:, None] == jnp.arange(BUCKETS)[None, :]).astype(F32)
    terms = jnp.dot(tables[0].T, onehot.T, precision=HIGH)
    terms = jnp.pad(terms, ((0, 2), (0, 1)))
    period = 2 * enc_total
    doubled = jnp.concatenate([terms, terms], axis=1)
    shift = (enc_total - 1 - tensor_id * enc_own + period) % period
    enc_terms = lax.dynamic_slice_in_dim(doubled, shift, period, 1)
    far_back = jnp.clip(row_place[:, None] - place[None, :], 0, dec_total - 1)
    far_back = (far_back[None] == jnp.arange(dec_total)[:, None, None]).astype(F32)
    far_back = far_back.reshape(dec_total, -1)
    dec_onehot = (dec_buckets[:, None] == jnp.arange(BUCKETS)[None, :]).astype(F32)
    dec_terms = jnp.dot(tables[1].T, dec_onehot.T, precision=HIGH)
    self_bias = jnp.dot(dec_terms, far_back, precision=HIGH).reshape(
        HEADS, DEC_PAD, 4 * DEC_PAD
    )
    spots = jnp.pad(onehot, ((0, 1), (0, 0)))
    enc_spots = lax.dynamic_slice_in_dim(
        spots, enc_total - enc_own - tensor_id * enc_own, enc_total + enc_own, 0
    )
    self_bucket = jnp.dot(
        dec_buckets.astype(F32)[None, :], far_back, precision=HIGH
    ).reshape(DEC_PAD, 4 * DEC_PAD)
    return (
        enc_terms, self_bias, item_count.reshape(1, 1), enc_mask.reshape(1, enc_total),
        dec_live.reshape(1, 4 * DEC_PAD),
    ), (enc_spots, self_bucket)


CHUNK = 256
RING = 4


def lag_of(steps):
    return 2 if steps <= 3 else 1


class Reduce:
    def __init__(self, peers, places, product, columns, total, send, recv, slot, finish, ships):
        self.ships = ships
        self.peers, self.places, self.product, self.columns = peers, places, product, columns
        self.total, self.send, self.recv, self.slot, self.done = total, send, recv, slot, finish
        self.steps = len(places) + 1

    def buffers(self, step):
        lanes = pl.ds(0, self.columns)
        return (
            self.send[step].at[self.slot % self.send[step].shape[0], :, lanes],
            self.recv[step].at[self.slot, :, lanes],
        )

    def ship(self, step, value, place):
        source, target = self.buffers(step)
        key = (id(self.send), step, self.slot % self.send[step].shape[0])
        if key in self.ships:
            self.ships[key].wait_send()
            self.peers.copies = [c for c in self.peers.copies if c is not self.ships[key]]
        source[...] = to_low(value)
        self.copy = self.peers.send(source, target, self.peers.across(place))
        self.ships[key] = self.copy

    def run(self, step):
        lanes = pl.ds(0, self.columns)
        if step == 0:
            here = self.peers.bit(self.places[0])
            self.ship(0, self.product(1 - here), self.places[0])
            self.height = self.send[0].shape[1]
            self.start = 0
            self.total[: self.height, lanes] = self.product(here)
            return
        self.copy.wait_recv()
        arrived = self.buffers(step - 1)[1]
        if step == self.steps - 1:
            rows = pl.ds(self.start, self.height)
            self.done(self.total[rows, lanes] + arrived[...].astype(F32))
            return
        self.height //= 2
        place = self.places[step]
        here = self.peers.bit(place)
        away = pl.multiple_of(self.start + (1 - here) * self.height, 16)
        kept = pl.multiple_of(self.start + here * self.height, 16)
        from_away = pl.multiple_of((1 - here) * self.height, 16)
        from_kept = pl.multiple_of(here * self.height, 16)
        self.ship(
            step,
            self.total[pl.ds(away, self.height), lanes]
            + arrived[pl.ds(from_away, self.height), :].astype(F32),
            place,
        )
        self.total[pl.ds(kept, self.height), lanes] += arrived[
            pl.ds(from_kept, self.height), :
        ].astype(F32)
        self.start = kept


class Stream:
    def __init__(self, items, lag):
        self.items, self.lag, self.now = items, lag, 0
        self.last = max(place + lag * (item.steps - 1) for place, item in enumerate(items))

    def pump(self, ticks=1):
        for unused in range(ticks):
            now = self.now
            if now > self.last:
                return
            self.now += 1
            for place, item in reversed(list(enumerate(self.items))):
                step, odd = divmod(now - place, self.lag)
                if odd == 0 and 0 < step < item.steps:
                    item.run(step)
            if now < len(self.items):
                for action in self.items[now].before:
                    if action is not None:
                        action()
                self.items[now].run(0)

    def drain(self):
        self.pump(self.last + 1 - self.now)


def flat(value):
    return value.reshape(value.shape[0] * value.shape[1], value.shape[2])


def choose_rows(peers, layout, first, rows, chosen, start):
    size, block, padded = layout
    bits = size.bit_length() - 1
    width = rows.shape[1]
    for known in range(2**first):

        def run(known=known):
            for half in range(2):
                for place in range(chosen.shape[1] // padded):
                    owner = known + (half << first)
                    for bit in range(first + 1, bits):
                        owner += ((place >> (bits - 1 - bit)) & 1) << bit
                    left = owner * block // 128 * 128
                    right = min(-(-(owner + 1) * block // 128) * 128, width)
                    inside = lax.broadcasted_iota(jnp.int32, (padded, right - left), 0)
                    lane = lax.broadcasted_iota(jnp.int32, (padded, right - left), 1)
                    picked = (lane - inside == owner * block - left) & (inside < block)
                    pick = to_low(jnp.where(picked, 1.0, 0.0))
                    for low, high in tiles(rows.shape[0]):
                        chosen[
                            half, place * padded : (place + 1) * padded,
                            start + low : start + high,
                        ] = to_low(dot_last(pick, rows[low:high, left:right]))

        if first:
            same = peers.bit(0) == known % 2
            for bit in range(1, first):
                same = same & (peers.bit(bit) == (known >> bit) % 2)
            pl.when(same)(run)
        else:
            run()


class Products:
    def __init__(self, peers, layout, first, steps, chosen, total, *buffers):
        self.peers, self.layout, self.first = peers, layout, first
        self.chosen, self.total = chosen, total
        self.places = list(range(first, steps))
        self.send, self.recv = buffers[: steps - first], buffers[steps - first :]
        self.items, self.ships = [], {}

    def choose(self, lefts, before):
        def run():
            if before is not None:
                before()
            rows = lefts[0].shape[0] * lefts[0].shape[1]
            for part, left in enumerate(lefts):
                choose_rows(
                    self.peers, self.layout, self.first, flat(left[...]), self.chosen, part * rows
                )

        return run

    def add(self, lefts, rights, out, before=None, ready=()):
        actions = [] if lefts is None else [self.choose(lefts, before)]
        for kind, parts in enumerate(rights):
            rows = parts[0].shape[0] * parts[0].shape[1]
            if ready:
                actions.append(ready[kind])
            for low, high in tiles(parts[0].shape[2], CHUNK):

                def product(half, parts=parts, low=low, high=high):
                    value = None
                    for part, right in enumerate(parts):
                        here = dot(
                            self.chosen[half, :, part * rows : (part + 1) * rows],
                            flat(right[:, :, low:high]),
                        )
                        value = here if value is None else value + here
                    return value

                def finish(value, kind=kind, low=low, high=high):
                    out[kind, :, low:high] = value[: out.shape[1]]

                count = len(self.items)
                item = Reduce(
                    self.peers, self.places, product, high - low,
                    self.total.at[count % self.total.shape[0]], self.send, self.recv, count,
                    finish, self.ships,
                )
                item.before, actions = actions, []
                self.items.append(item)


def product_scratch(size, padded, rows, items, first):
    chosen = size * padded >> first
    steps = size.bit_length() - 1
    heights = [chosen >> (step + 1) for step in range(steps - first)]
    return [
        pltpu.VMEM((2, chosen // 2, rows), LOW),
        pltpu.VMEM((lag_of(steps) * (steps - first) + 1, chosen // 2, CHUNK), F32),
        *[pltpu.VMEM((RING, height, CHUNK), LOW) for height in heights],
        *[pltpu.VMEM((items, height, CHUNK), LOW) for height in heights],
    ]


def to_owners(peers, sources, target, rows_of, own_sem):
    sends = []
    for peer in (peers.far, peers.diag, peers.sib):
        place = peers.used
        peers.used += 1
        for role in range(4):
            rows = rows_of[role]

            def copy(role=role, rows=rows, place=place, peer=peer):
                return pltpu.make_async_remote_copy(
                    src_ref=sources[role],
                    dst_ref=target.at[peers.own, pl.ds(0, rows)],
                    send_sem=peers.send_sem.at[place],
                    recv_sem=peers.recv_sem.at[place],
                    device_id=peers.device(peer),
                    device_id_type=pl.DeviceIdType.MESH,
                )

            @pl.when(peer == role)
            def _(copy=copy):
                copy().start()

            sends.append((peer, role, copy))
    for role in range(4):

        def keep(role=role):
            return pltpu.make_async_copy(
                sources[role], target.at[peers.own, pl.ds(0, rows_of[role])], own_sem
            )

        @pl.when(peers.own == role)
        def _(keep=keep):
            keep().start()

        sends.append((None, role, keep))
    return sends


def owners_done(peers, sends):
    for peer, role, copy in sends:

        @pl.when(peers.own == role)
        def _(copy=copy, peer=peer):
            copy().wait() if peer is None else copy().wait_recv()

        if peer is not None:

            @pl.when(peer == role)
            def _(copy=copy):
                copy().wait_send()


def kv_back(grad_kv, wqk, wvo, low, high):
    return dot_last(grad_kv[:, :INNER], wqk[low:high, INNER:]) + dot_last(
        grad_kv[:, INNER:], wvo[low:high, :INNER]
    )


class SumBlocks:
    def __init__(self, peers, buf, send, recv):
        self.peers, self.buf, self.send, self.recv = peers, buf, send, recv
        send[0] = to_low(buf[peers.diag])
        send[1] = to_low(buf[peers.sib])
        self.first = peers.send(send.at[0], recv.at[0], peers.sib)
        self.third = peers.send(send.at[1], recv.at[1], peers.sib)

    def cross(self):
        peers = self.peers
        self.first.wait_recv()
        self.send[2] = to_low(self.buf[peers.far] + self.recv[0].astype(F32))
        self.second = peers.send(self.send.at[2], self.recv.at[2], peers.far)

    def result(self):
        self.third.wait_recv()
        value = self.buf[self.peers.own] + self.recv[1].astype(F32)
        self.second.wait_recv()
        return value + self.recv[2].astype(F32)


class SumNear:
    def __init__(self, peers, part_of, block, total, send, recv):
        self.peers, self.total, self.send, self.recv = peers, total, send, recv
        for low, high in tiles(send.shape[2]):
            value = part_of(low, high)
            total[0, :, low:high] = value[:block]
            send[1, :, low:high] = to_low(value[block : 2 * block])
            total[1, :, low:high] = value[2 * block : 3 * block]
            send[0, :, low:high] = to_low(value[3 * block :])
        self.first = peers.send(send.at[0], recv.at[0], peers.sib)
        self.third = peers.send(send.at[1], recv.at[1], peers.sib)

    def cross(self):
        self.first.wait_recv()
        self.send[2] = to_low(self.total[1] + self.recv[0].astype(F32))
        self.second = self.peers.send(self.send.at[2], self.recv.at[2], self.peers.far)

    def result(self):
        self.third.wait_recv()
        value = self.total[0] + self.recv[1].astype(F32)
        self.second.wait_recv()
        return value + self.recv[2].astype(F32)


def kb_kernel(
    dec_gg, dec_gu, dec_hidden, dec_cot, dec_two, dec_one, gains, cross_q, hf,
    qk_all, vo_all, fi_all, fo_all, dec_gy, cross_kv_all, cross_p_all, enc_end_all,
    enc_gelu_all, enc_slope_all,
    dec_out, cross_gy, cross_gq, cross_gk, cross_gv, dec_one_grad, enc_end_grad, enc_gy, enc_gg, enc_gu,
    gains_grad, dec_gate, x_dec_hidden, x_dec_gy, x_dec_gu, x_hf,
    wqk, wvo, wfi, wfo, grad_kv, kv_send, kv_recv, row_total, row_send, row_recv, out_total,
    out_send, out_recv, x_dec_gg, cross_kv, cross_p, enc_end, enc_gelu, enc_slope,
    *rest,
    layout, steps,
):
    scratch, (send_sem, recv_sem, load_sem) = rest[:-3], rest[-3:]
    peers = Peers(send_sem, recv_sem)
    loads = Loads(load_sem)
    get_fi = loads.start(fi_all.at[1], wfi)
    get_cross = [
        loads.start(vo_all.at[2], wvo), loads.start(cross_kv_all, cross_kv),
        loads.start(cross_p_all, cross_p), loads.start(qk_all.at[2], wqk),
        loads.start(enc_end_all, enc_end),
    ]
    get_fo1 = loads.start(fo_all.at[1], wfo.at[1])
    get_up = [
        loads.start(fo_all.at[0], wfo.at[0]), loads.start(enc_gelu_all, enc_gelu),
        loads.start(enc_slope_all, enc_slope),
    ]
    peers.greet([peers.across(place) for place in range(steps)])
    first = Exchange(peers, [(dec_gg, x_dec_gg)], [(hf, x_hf)])
    later = [
        Exchange(
            peers, [(dec_gu, x_dec_gu), (dec_hidden, x_dec_hidden)], [(dec_gy, x_dec_gy)]
        )
    ]

    def arrived():
        first.finish_rows()
        first.finish_whole()

    products = Products(peers, layout, 1, steps, *scratch)
    products.add(
        [hf, x_hf], [(dec_gg, x_dec_gg)], dec_gate, before=arrived
    )
    stream = Stream(products.items, lag_of(steps))
    width = dec_two.shape[1]
    block = dec_two.shape[0]
    units = dec_gg.shape[2]
    gains_grad[...] = jnp.zeros_like(gains_grad)

    get_fi.wait()
    gate, up_proj = dec_gg[...].reshape(4 * block, units), dec_gu[...].reshape(4 * block, units)

    def grad_rows_part(low, high):
        return dot_last(gate, wfi[0, low:high, :]) + dot_last(up_proj, wfi[1, low:high, :])

    grad_rows = SumNear(peers, grad_rows_part, block, row_total, row_send, row_recv)
    grad_rows.cross()
    wait_all(get_cross)
    first.spread()
    value, gain_row = norm_back(dec_two[...], gains[5:6], grad_rows.result())
    gains_grad[5:6] = gain_row
    residual = dec_cot[...].astype(F32) + value
    grad_y = to_low(residual)
    cross_gy[...] = grad_y

    grad_out = to_low(dot(grad_y, wvo[:, INNER:]))
    first.relay()
    stream.pump(1)
    attend_back(cross_q[...], cross_kv, cross_p, grad_out, cross_gq, grad_kv, None)
    kv_sum = SumBlocks(peers, grad_kv, kv_send, kv_recv)
    kv_sum.cross()
    stream.pump(1)
    for low, high in tiles(width):
        row_total[0, :, low:high] = dot_last(cross_gq[...], wqk[low:high, :INNER])
    value, gain_row = norm_back(dec_one[...], gains[4:5], row_total[0])
    gains_grad[4:5] = gain_row
    dec_one_grad[...] = residual + value
    stream.pump(1)
    own_kv = to_low(kv_sum.result())
    cross_gk[...] = own_kv[:, :INNER]
    cross_gv[...] = own_kv[:, INNER:]
    for low, high in tiles(width):
        enc_end_grad[:, low:high] = kv_back(own_kv, wqk, wvo, low, high)
    value, gain_row = norm_back(enc_end[...], gains[2:3], enc_end_grad[...])
    gains_grad[2:3] = gain_row
    enc_end_grad[...] = value
    enc_gy[0] = to_low(value)
    gy_gather = Gather(peers, enc_gy, True)
    gy_gather.start()

    get_fo1.wait()
    hidden = dec_hidden[...].reshape(4 * block, units)
    out_sum = SumNear(
        peers, lambda low, high: dot_last(hidden, wfo[1, low:high, :]), block, out_total,
        out_send, out_recv,
    )

    stream.pump(1)
    for exchange in later:
        exchange.spread()
    wait_all(get_up)
    rows = enc_gy.shape[1]

    def gate_grads(slots):
        grad_y = enc_gy[slots].reshape(2 * rows, width)
        for low, high in tiles(units):
            grad_h = dot(grad_y, wfo[0, :, low:high]).reshape(2, rows, high - low)
            enc_gg[slots, :, low:high] = to_low(grad_h * enc_slope[slots, :, low:high])
            enc_gu[slots, :, low:high] = to_low(grad_h * enc_gelu[slots, :, low:high])

    gy_gather.wait_near()
    stream.pump(1)
    gate_grads(slice(0, 2))
    gy_gather.relay()
    out_sum.cross()
    stream.pump(1)
    gy_gather.wait_far()
    gate_grads(slice(2, 4))
    stream.pump(1)
    for exchange in later:
        exchange.relay()
    stream.pump(1)
    dec_out[...] = to_low(dec_two[...] + out_sum.result())
    stream.drain()
    for exchange in later:
        exchange.finish_rows()
        exchange.finish_whole()
    peers.finish()


def kb_call(dec_gg, dec_gu, dec_hidden, dec_cot, dec_two, dec_one, gains, cross_q, cross_kv,
            cross_p, enc_end, enc_gelu, enc_slope, attn_qk, attn_vo, ff_in, ff_out, hf, dec_gy,
            size, block, padded):
    rows, width = enc_end.shape
    dec_rows = dec_two.shape[0]
    units = ff_in.shape[3]
    kv_width = 2 * INNER
    shape = jax.ShapeDtypeStruct
    outs = [
        shape((dec_rows, width), LOW), shape((dec_rows, width), LOW),
        shape((dec_rows, INNER), LOW), shape((rows, INNER), LOW), shape((rows, INNER), LOW),
        shape((dec_rows, width), F32), shape((rows, width), F32), shape((4, rows, width), LOW), shape((4, rows, units), LOW),
        shape((4, rows, units), LOW), shape((8, width), F32), shape((1, block, units), F32),
    ]
    traded = [
        shape(value.shape, LOW)
        for value in (dec_hidden, dec_gy, dec_gu, hf)
    ]
    steps = size.bit_length() - 1
    items = len(tiles(units, CHUNK))
    vmem = pl.BlockSpec(memory_space=pltpu.VMEM)
    hbm = pl.BlockSpec(memory_space=pltpu.HBM)
    copies = 3 * 3 + 3 + 5 + 6 + items * (steps - 1)
    return pl.pallas_call(
        functools.partial(kb_kernel, layout=(size, block, padded), steps=steps),
        out_shape=outs + traded,
        in_specs=[vmem] * 9 + [hbm] * 10,
        out_specs=[vmem] * len(outs) + [hbm] * (len(traded) - 1) + [vmem],
        scratch_shapes=[
            pltpu.VMEM(attn_qk.shape[1:], LOW), pltpu.VMEM(attn_vo.shape[1:], LOW),
            pltpu.VMEM(ff_in.shape[1:], LOW), pltpu.VMEM(ff_out.shape, LOW),
            pltpu.VMEM((4, rows, kv_width), F32), pltpu.VMEM((3, rows, kv_width), LOW),
            pltpu.VMEM((3, rows, kv_width), LOW), pltpu.VMEM((2, dec_rows, width), F32),
            pltpu.VMEM((3, dec_rows, width), LOW), pltpu.VMEM((3, dec_rows, width), LOW),
            pltpu.VMEM((2, dec_rows, width), F32), pltpu.VMEM((3, dec_rows, width), LOW),
            pltpu.VMEM((3, dec_rows, width), LOW),
            pltpu.VMEM(dec_gg.shape, LOW),
            pltpu.VMEM(cross_kv.shape, LOW), pltpu.VMEM(cross_p.shape, F32),
            pltpu.VMEM(enc_end.shape, F32), pltpu.VMEM(enc_gelu.shape, F32),
            pltpu.VMEM(enc_slope.shape, F32),
            *product_scratch(size, padded, 2 * 4 * dec_rows, items, 1),
            pltpu.SemaphoreType.DMA((copies,)), pltpu.SemaphoreType.DMA((copies,)),
            pltpu.SemaphoreType.DMA((10,)),
        ],
        compiler_params=pltpu.CompilerParams(
            collective_id=1, has_side_effects=True, vmem_limit_bytes=VMEM_BYTES
        ),
        name="middle_chain",
    )(dec_gg, dec_gu, dec_hidden, dec_cot, dec_two, dec_one, gains, cross_q, hf,
      attn_qk, attn_vo, ff_in, ff_out, dec_gy, cross_kv, cross_p, enc_end,
      enc_gelu, enc_slope)


def kc_kernel(
    enc_gg, enc_gu, gains, gains_mid, enc_q, dec_one_grad, dec_x, self_q, self_kv, self_p,
    enc_spots, self_bucket,
    qk_all, vo_all, fi_all, enc_end_grad_all, enc_mid_all, enc_x_all, enc_kv_all, enc_p_all,
    enc_gy_all, hf_all, x_hf_all, dec_gu_all, x_dec_gu_all, dec_gy_all, x_dec_gy_all,
    dec_hidden_all, x_dec_hidden_all, enc_hidden_all,
    x_enc_hidden_all, h1_all, x_h1_rows, hs, hc, memory, cross_gy, cross_gq, cross_gk, cross_gv,
    cross_o,
    enc_grad, enc_ay, enc_gq, enc_gk, enc_gv, dec_grad, self_gy, self_gq, self_gk, self_gv,
    small, ffout, dec_up, chosen_h1, left_cross, right_cross, left_self, x_enc_gg, x_enc_gu, x_h1,
    wqk, wvo, wfi, enc_gs, self_gs, part, send, recv, enc_gkv_full, kv_send, kv_recv,
    self_gkv_full, self_send, self_recv, x_enc_gy, enc_end_grad, enc_mid, enc_x, enc_kv, enc_p,
    enc_gy, hfs, dec_gus, dec_gys, dec_hiddens, enc_hidden, x_enc_hidden, stage, *rest,
    layout, steps,
):
    dec_scratch, enc_scratch = rest[: 2 * steps], rest[2 * steps : -4]
    send_sem, recv_sem, load_sem, own_sem = rest[-4:]
    peers = Peers(send_sem, recv_sem)
    loads = Loads(load_sem)
    get_dec = [
        loads.start(source, target.at[place])
        for sources, target in (
            ((hf_all, x_hf_all), hfs), ((dec_gu_all, x_dec_gu_all), dec_gus),
            ((dec_gy_all, x_dec_gy_all), dec_gys), ((dec_hidden_all, x_dec_hidden_all), dec_hiddens),
        )
        for place, source in enumerate(sources)
    ]
    get_fi = loads.start(fi_all.at[0], wfi)
    get_vo1 = loads.start(vo_all.at[1], wvo.at[1])
    get_mid = [
        loads.start(enc_mid_all, enc_mid), loads.start(enc_end_grad_all, enc_end_grad),
        loads.start(vo_all.at[0], wvo.at[0]), loads.start(enc_kv_all, enc_kv),
        loads.start(enc_p_all, enc_p),
    ]
    get_out = [
        loads.start(enc_gy_all, enc_gy), loads.start(enc_hidden_all, enc_hidden),
        loads.start(x_enc_hidden_all, x_enc_hidden),
    ]
    get_last = [
        loads.start(qk_all.at[0], wqk.at[0]), loads.start(qk_all.at[1], wqk.at[1]),
        loads.start(enc_x_all, enc_x),
    ]
    for buf in (left_cross, right_cross):
        buf[...] = jnp.zeros_like(buf)
    peers.greet([peers.diag] + [peers.across(place) for place in range(steps)])
    exchange = Exchange(
        peers, [(enc_gg, x_enc_gg), (enc_gu, x_enc_gu)], [(enc_gy_all, x_enc_gy)]
    )
    dec_rows, enc_rows = hs.shape[0], memory.shape[0]
    short = (dec_rows,) * 4
    mixed = (dec_rows, enc_rows, enc_rows, dec_rows)
    owned = [
        to_owners(peers, (hc, memory, memory, cross_gy), left_cross, mixed, own_sem.at[0]),
        to_owners(
            peers, (cross_gq, cross_gk, cross_gv, cross_o), right_cross, mixed, own_sem.at[1]
        ),
    ]

    h1_gather = Gather(peers, x_h1, True, x_h1_rows)

    def arrived():
        wait_all(get_out)
        exchange.relay()
        exchange.finish_rows()

    def ready():
        wait_all(get_dec)

    dec_products = Products(peers, layout, 1, steps, *dec_scratch)
    dec_products.add(
        [hfs.at[place] for place in range(2)], [[dec_gus.at[place] for place in range(2)]], dec_up,
        before=ready,
    )
    dec_products.add(
        [dec_gys.at[place] for place in range(2)], [[dec_hiddens.at[place] for place in range(2)]],
        ffout.at[pl.ds(1, 1)],
    )
    enc_products = Products(peers, layout, 1, steps, *enc_scratch)
    enc_products.add(
        [enc_gy, x_enc_gy], [(enc_hidden, x_enc_hidden)], ffout.at[pl.ds(0, 1)], before=arrived
    )
    stream = Stream(dec_products.items + enc_products.items, lag_of(steps))
    staged = []

    def fetch_rows(place):
        if place == 5:
            h1_gather.wait_near()
            h1_gather.relay()
        if place == 7:
            h1_gather.wait_far()
        source = x_h1_rows if place == 4 else (h1_all, x_h1)[place // 4].at[place % 4]
        staged.append(loads.start(source, stage.at[place % 2]))

    def choose_next(place):
        staged.pop(0).wait()
        choose_rows(peers, layout, 1, stage[place % 2], chosen_h1, place * enc_rows)
        if place + 2 < 8:
            fetch_rows(place + 2)

    rows, width = enc_mid.shape
    units = enc_gg.shape[2]
    small[...] = jnp.zeros_like(small)
    small[:8] = gains_mid[...]

    stream.pump(2)
    get_fi.wait()

    def grad_part(slots, low, high):
        gate = enc_gg[slots].reshape(2 * rows, units)
        up_proj = enc_gu[slots].reshape(2 * rows, units)
        return dot_last(gate, wfi[0, low:high, :]) + dot_last(up_proj, wfi[1, low:high, :])

    for low, high in tiles(width):
        value = grad_part(slice(2, 4), low, high)
        part[:, low:high] = value[:rows]
        send[0, :, low:high] = to_low(value[rows:])
    for place in range(2):
        fetch_rows(place)
    first = peers.send(send.at[0], recv.at[0], peers.sib)
    stream.pump(1)
    get_vo1.wait()
    residual_dec = dec_one_grad[...]
    grad_y = to_low(residual_dec)
    self_gy[...] = grad_y
    owned.append(to_owners(peers, (hs, hs, hs, self_gy), left_self, short, own_sem.at[2]))
    grad_out_dec = to_low(dot(grad_y, wvo[1, :, INNER:]))
    exchange.spread()
    first.wait_recv()
    send[2] = to_low(part[...] + recv[0].astype(F32))
    second = peers.send(send.at[2], recv.at[2], peers.far)
    for low, high in tiles(width):
        value = grad_part(slice(0, 2), low, high)
        part[:, low:high] = value[:rows]
        send[1, :, low:high] = to_low(value[rows:])
    third = peers.send(send.at[1], recv.at[1], peers.sib)

    stream.pump(1)
    attend_back(self_q[...], self_kv, self_p, grad_out_dec, self_gq, self_gkv_full, self_gs)
    self_sum = SumBlocks(peers, self_gkv_full, self_send, self_recv)
    self_sum.cross()

    stream.pump(1)
    for place in range(3):
        choose_next(place)

    columns = []
    for bucket in range(BUCKETS):
        here = jnp.where(self_bucket[...] == bucket, 1.0, 0.0)
        sums = jnp.sum(self_gs[...].astype(F32) * here[None], axis=1)
        columns.append(jnp.sum(sums, axis=1, keepdims=True))
    self_table = jnp.concatenate(columns, axis=1)

    stream.pump(1)
    third.wait_recv()
    part[...] = part[...] + recv[1].astype(F32)
    second.wait_recv()
    wait_all(get_mid)
    value, gain_row = norm_back(enc_mid[...], gains[1:2], part[...] + recv[2].astype(F32))
    small[1:2] = gain_row
    residual = enc_end_grad[...] + value
    grad_y = to_low(residual)
    enc_ay[...] = grad_y
    enc_grad[...] = residual

    h1_gather.start()
    grad_out = to_low(dot(grad_y, wvo[0, :, INNER:]))
    attend_back(enc_q[...], enc_kv, enc_p, grad_out, enc_gq, enc_gkv_full, enc_gs)
    enc_sum = SumBlocks(peers, enc_gkv_full, kv_send, kv_recv)
    stream.pump(2)
    wait_all(get_last)
    for low, high in tiles(width):
        part[:, low:high] = dot_last(enc_gq[...], wqk[0, low:high, :INNER])
    enc_sum.cross()

    stream.pump(1)
    choose_next(3)
    own_kv = to_low(self_sum.result())
    self_gk[...] = own_kv[:, :INNER]
    self_gv[...] = own_kv[:, INNER:]
    for low, high in tiles(width):
        dec_grad[:, low:high] = dot_last(self_gq[...], wqk[1, low:high, :INNER]) + kv_back(
            own_kv, wqk.at[1], wvo.at[1], low, high
        )
    value, gain_row = norm_back(dec_x[...].astype(F32), gains[3:4], dec_grad[...])
    small[3:4] = gain_row
    dec_grad[...] = residual_dec + value

    turn = lax.broadcasted_iota(jnp.int32, (rows, rows), 0) + lax.broadcasted_iota(
        jnp.int32, (rows, rows), 1
    )
    turn = jnp.where(turn == rows - 1, 1.0, 0.0).astype(LOW)
    offsets = []
    for head in range(HEADS):
        turned = dot(turn, enc_gs[head])
        spread = jnp.concatenate([turned, jnp.zeros((rows, rows), F32)], axis=1)
        spread = pltpu.roll(spread, 0, 1, stride=1, stride_axis=0)
        offsets.append(jnp.sum(spread, axis=0, keepdims=True))
    enc_table = jnp.dot(
        jnp.concatenate(offsets + [jnp.zeros((2, offsets[0].shape[1]), F32)], axis=0),
        enc_spots[...], precision=HIGH, preferred_element_type=F32,
    )
    small[8:, :BUCKETS] = enc_table
    small[8 : 8 + HEADS, PAIR : PAIR + BUCKETS] = self_table

    stream.pump(2)
    own_kv = to_low(enc_sum.result())
    enc_gk[...] = own_kv[:, :INNER]
    enc_gv[...] = own_kv[:, INNER:]
    for low, high in tiles(width):
        part[:, low:high] += kv_back(own_kv, wqk.at[0], wvo.at[0], low, high)
    value, gain_row = norm_back(enc_x[...].astype(F32), gains[0:1], part[...])
    small[0:1] = gain_row
    enc_grad[...] += value
    for place in range(4, 8):
        stream.pump(1)
        choose_next(place)
    stream.drain()
    exchange.finish_whole()
    for sends in owned:
        owners_done(peers, sends)
    peers.finish()


def kc_call(size, block, padded, near, streamed):
    enc_gg, dec_x = near[0], near[6]
    attn_qk, attn_vo, ff_in = streamed[:3]
    rows, width = streamed[4].shape
    dec_rows = dec_x.shape[0]
    units = ff_in.shape[3]
    kv_width = 2 * INNER
    total = 4 * rows
    half = size * padded // 2
    steps = size.bit_length() - 1
    items = len(tiles(units, CHUNK))
    shape = jax.ShapeDtypeStruct
    outs = [
        shape((rows, width), F32), shape((rows, width), LOW), shape((rows, INNER), LOW),
        shape((rows, INNER), LOW), shape((rows, INNER), LOW),
        shape((dec_rows, width), F32), shape((dec_rows, width), LOW),
        shape((dec_rows, INNER), LOW), shape((dec_rows, INNER), LOW),
        shape((dec_rows, INNER), LOW),
        shape((16, width), F32), shape((2, block, units), F32), shape((1, block, units), F32),
        shape((2, half // 2, 2 * total), LOW), shape((4, rows, width), LOW),
        shape((4, rows, INNER), LOW),
    ]
    apart = [
        shape((4, dec_rows, width), LOW),
        shape(enc_gg.shape, LOW), shape(enc_gg.shape, LOW), shape((4, rows, width), LOW),
    ]
    vmem = pl.BlockSpec(memory_space=pltpu.VMEM)
    hbm = pl.BlockSpec(memory_space=pltpu.HBM)
    copies = 3 * 3 + 3 + 3 + 3 * 3 + 3 + 3 * items * (steps - 1)
    return pl.pallas_call(
        functools.partial(kc_kernel, layout=(size, block, padded), steps=steps),
        out_shape=outs + apart,
        in_specs=[vmem] * len(near) + [hbm] * len(streamed),
        out_specs=[vmem] * len(outs) + [hbm] * len(apart),
        scratch_shapes=[
            pltpu.VMEM((2,) + attn_qk.shape[1:], LOW), pltpu.VMEM((2,) + attn_vo.shape[1:], LOW),
            pltpu.VMEM(ff_in.shape[1:], LOW), pltpu.VMEM((HEADS, rows, total), LOW),
            pltpu.VMEM((HEADS, dec_rows, 4 * dec_rows), LOW),
            pltpu.VMEM((rows, width), F32), pltpu.VMEM((3, rows, width), LOW),
            pltpu.VMEM((3, rows, width), LOW),
            pltpu.VMEM((4, rows, kv_width), F32), pltpu.VMEM((3, rows, kv_width), LOW),
            pltpu.VMEM((3, rows, kv_width), LOW),
            pltpu.VMEM((4, dec_rows, kv_width), F32), pltpu.VMEM((3, dec_rows, kv_width), LOW),
            pltpu.VMEM((3, dec_rows, kv_width), LOW), pltpu.VMEM((4, rows, width), LOW),
            pltpu.VMEM((rows, width), F32), pltpu.VMEM((rows, width), F32),
            pltpu.VMEM((rows, width), LOW), pltpu.VMEM((4, rows, kv_width), LOW),
            pltpu.VMEM((HEADS, rows, total), F32), pltpu.VMEM((4, rows, width), LOW),
            *[pltpu.VMEM((2, 4, dec_rows, width), LOW), pltpu.VMEM((2, 4, dec_rows, units), LOW)] * 2,
            pltpu.VMEM((4, rows, units), LOW), pltpu.VMEM((4, rows, units), LOW),
            pltpu.VMEM((2, rows, width), LOW),
            *product_scratch(size, padded, 2 * 4 * dec_rows, 2 * items, 1),
            *product_scratch(size, padded, 2 * total, items, 1),
            pltpu.SemaphoreType.DMA((copies,)), pltpu.SemaphoreType.DMA((copies,)),
            pltpu.SemaphoreType.DMA((2 + 8 + 5 + 3 + 3 + 8,)), pltpu.SemaphoreType.DMA((3,)),
        ],
        compiler_params=pltpu.CompilerParams(
            collective_id=2, has_side_effects=True, vmem_limit_bytes=62 * 1024 * 1024
        ),
        name="last_chain",
    )(*near, *streamed)
class Spread:
    def __init__(self, peers, partners, total, recv):
        self.peers, self.partners, self.total, self.recv = peers, partners, total, recv
        self.steps = len(partners) + 1

    def run(self, step):
        if step:
            self.copy.wait_recv()
            self.total[step] = self.total[step - 1] + self.recv[step - 1]
        if step < len(self.partners):
            self.copy = self.peers.send(
                self.total.at[step], self.recv.at[step], self.partners[step]
            )


def kd_kernel(
    small,
    chosen_h1, enc_gg_all, x_enc_gg_all, enc_gu_all, x_enc_gu_all,
    left_cross_all, right_cross_all, left_self_all, h0, enc_ay,
    enc_gq, enc_gk, enc_gv, enc_o, self_gq, self_gk, self_gv, self_o, dec_gate,
    dec_up,
    ffin, qk, vo, small_out,
    enc_ffin, enc_gg, x_enc_gg, enc_gu, x_enc_gu, chosen_attn, left_enc, left_cross,
    left_self, right_enc, right_cross, right_self, attn_total, attn, small_total, small_recv,
    *rest,
    layout, steps,
):
    size, block, padded = layout
    scratch, rest = rest[: 2 * steps], rest[2 * steps :]
    at_send, at_recv = rest[:steps], rest[steps : 2 * steps]
    send_sem, recv_sem, load_sem, own_sem = rest[2 * steps :]
    peers = Peers(send_sem, recv_sem)
    loads = Loads(load_sem)
    get_gate = [
        loads.start(chosen_h1, scratch[0]), loads.start(enc_gg_all, enc_gg),
        loads.start(x_enc_gg_all, x_enc_gg),
    ]
    get_cross = [
        loads.start(left_cross_all, left_cross), loads.start(right_cross_all, right_cross),
    ]
    get_up = [loads.start(enc_gu_all, enc_gu), loads.start(x_enc_gu_all, x_enc_gu)]
    get_self = [loads.start(left_self_all, left_self)]
    passed = [
        loads.start(dec_gate, ffin.at[1, pl.ds(0, 1)]), loads.start(dec_up, ffin.at[1, pl.ds(1, 1)])
    ]
    partners = [peers.across(place) for place in range(steps)]
    peers.greet([peers.diag] + partners)
    dec_rows, enc_rows = self_gq.shape[0], enc_gq.shape[0]
    own_self = to_owners(
        peers, (self_gq, self_gk, self_gv, self_o), right_self, (dec_rows,) * 4, own_sem.at[0]
    )
    own_enc = to_owners(
        peers, (enc_gq, enc_gk, enc_gv, enc_o), right_enc, (enc_rows,) * 4, own_sem.at[1]
    )
    own_left = to_owners(peers, (h0, h0, h0, enc_ay), left_enc, (enc_rows,) * 4, own_sem.at[3])
    spread = Spread(peers, [peers.sib, peers.far] + partners, small_total, small_recv)
    small_total[0] = small[...]
    spread.run(0)

    products = Products(peers, layout, 1, steps, *scratch)
    products.add(
        None, [(enc_gg, x_enc_gg), (enc_gu, x_enc_gu)], enc_ffin,
        ready=(lambda: wait_all(get_gate), lambda: wait_all(get_up)),
    )

    def wait_self():
        wait_all(get_self)
        owners_done(peers, own_self)

    def wait_enc():
        owners_done(peers, own_enc)
        owners_done(peers, own_left)

    kinds = (
        (2, left_cross, right_cross, lambda: wait_all(get_cross)),
        (1, left_self, right_self, wait_self), (0, left_enc, right_enc, wait_enc),
    )
    attn_items, gathers = [], []
    for a, left, right, arrived in kinds:
        rows = left.shape[0] * left.shape[1]

        def before(left=left, right=right, arrived=arrived):
            arrived()
            if block % 8:
                choose_rows(peers, layout, 0, flat(left[...]), chosen_attn, 0)
                return
            for low, high in tiles(INNER, CHUNK):
                chosen_attn[:, low:high] = dot_first(flat(left[...]), flat(right[:, :, low:high]))

        for place, (low, high) in enumerate(tiles(INNER, CHUNK)):

            def product(half, right=right, rows=rows, low=low, high=high):
                if block % 8:
                    return dot(chosen_attn[half, :, :rows], flat(right[:, :, low:high]))
                parts = []
                for place in range(size // 2):
                    owner = half
                    for bit in range(1, steps):
                        owner = owner + (((place >> (steps - 1 - bit)) & 1) << bit)
                    start = pl.multiple_of(owner * block, 8)
                    parts.append(chosen_attn[pl.ds(start, block), low:high])
                    if padded > block:
                        parts.append(jnp.zeros((padded - block, high - low), F32))
                return jnp.concatenate(parts, axis=0)

            def finish(value, a=a, low=low, high=high, last=high == INNER):
                attn[a, peers.own, :, low:high] = to_low(value)
                if last:
                    gathers.append((a, Gather(peers, attn.at[a], False)))
                    gathers[-1][1].start()

            slot = len(attn_items)
            item = Reduce(
                peers, list(range(steps)), product, high - low, attn_total.at[slot], at_send,
                at_recv, slot, finish, products.ships,
            )
            item.before = [before] if place == 0 else []
            attn_items.append(item)

    items = []
    for place in range(max(len(products.items), len(attn_items) + 2)):
        if 2 <= place < len(attn_items) + 2:
            items.append(attn_items[place - 2])
        if place < len(products.items):
            items.append(products.items[place])
    stream = Stream(items, lag_of(steps))
    while stream.now <= stream.last:
        stream.pump()
        if stream.now % 2 == 0 and stream.now // 2 < spread.steps:
            spread.run(stream.now // 2)
    small_out[...] = small_total[spread.steps - 1]
    left = pltpu.make_async_copy(enc_ffin, ffin.at[0], own_sem.at[2])
    left.start()
    for a, gather in gathers:
        gather.wait_near()
        gather.relay()
    for a, gather in gathers:
        gather.wait_far()
        for place, out in enumerate((qk, qk, vo, vo)):
            lanes = slice(place % 2 * INNER, (place % 2 + 1) * INNER)
            out[a, :, lanes] = attn[a, place, :, :].astype(F32)[:block]
    left.wait()
    wait_all(passed)
    peers.finish()


def kd_call(size, block, padded, width, small, streamed):
    gate, self_q = streamed[1], streamed[14]
    units, enc_rows, dec_rows = gate.shape[2], gate.shape[1], self_q.shape[0]
    steps = size.bit_length() - 1
    shape = jax.ShapeDtypeStruct
    outs = [
        shape((2, 2, block, units), F32), shape((3, block, 2 * INNER), F32),
        shape((3, block, 2 * INNER), F32), shape(small.shape, F32),
    ]
    vmem = pl.BlockSpec(memory_space=pltpu.VMEM)
    hbm = pl.BlockSpec(memory_space=pltpu.HBM)
    half = size * padded // 2
    ff_items = 2 * len(tiles(units, CHUNK))
    at_items = 3 * len(tiles(INNER, CHUNK))
    at_heights = [half >> step for step in range(steps)]

    def bufs(items, heights):
        return [pltpu.VMEM((items, height, CHUNK), LOW) for height in heights]

    copies = ff_items * (steps - 1) + at_items * steps + 3 * 3 + (2 + steps) + 9
    return pl.pallas_call(
        functools.partial(kd_kernel, layout=(size, block, padded), steps=steps),
        out_shape=outs,
        in_specs=[vmem] + [hbm] * len(streamed),
        out_specs=[hbm] + [vmem] * 3,
        scratch_shapes=[
            pltpu.VMEM((2, block, units), F32),
            *[pltpu.VMEM(gate.shape, LOW)] * 4,
            pltpu.VMEM((2, half, 4 * enc_rows), LOW) if block % 8 else pltpu.VMEM((width, INNER), F32),
            pltpu.VMEM((4, enc_rows, width), LOW), pltpu.VMEM((4, enc_rows, width), LOW),
            pltpu.VMEM((4, dec_rows, width), LOW),
            pltpu.VMEM((4, enc_rows, INNER), LOW), pltpu.VMEM((4, enc_rows, INNER), LOW),
            pltpu.VMEM((4, dec_rows, INNER), LOW),
            pltpu.VMEM((at_items, half, CHUNK), F32),
            pltpu.VMEM((3, 4, padded, INNER), LOW),
            pltpu.VMEM((3 + steps,) + small.shape, F32),
            pltpu.VMEM((2 + steps,) + small.shape, F32),
            *product_scratch(size, padded, 8 * enc_rows, ff_items, 1),
            *bufs(2, at_heights), *bufs(at_items, at_heights),
            pltpu.SemaphoreType.DMA((copies,)), pltpu.SemaphoreType.DMA((copies,)),
            pltpu.SemaphoreType.DMA((10,)), pltpu.SemaphoreType.DMA((4,)),
        ],
        compiler_params=pltpu.CompilerParams(
            collective_id=3, has_side_effects=True, vmem_limit_bytes=62 * 1024 * 1024
        ),
        name="weight_sums",
    )(small, *streamed)


def on_device(
    enc_x, dec_x, dec_cot, item_count, enc_mask, dec_mask, enc_buckets, dec_buckets,
    gains, tables, attn_qk, attn_vo, ff_in, ff_out,
):
    tensor_id = lax.axis_index("tensor")
    size = lax.axis_size("dp")
    enc_own, dec_own = enc_x.shape[0], dec_x.shape[0]
    width = enc_x.shape[1]
    block = width // size
    padded = (block + 15) // 16 * 16
    small, (enc_spots, self_bucket) = prepare(
        item_count, enc_mask, dec_mask, enc_buckets, dec_buckets, tables, enc_own, dec_own
    )
    ff_out_t = jnp.swapaxes(ff_out, 1, 2)
    (
        h0, enc_q, enc_kv, enc_p, enc_o, enc_mid, h1, enc_gelu, enc_slope, enc_hidden, enc_end,
        memory, cross_kv, hs, self_q, self_kv, self_p, self_o, dec_one, hc, cross_q, cross_p,
        cross_o, dec_two, hf, dec_gy, dec_gg, dec_gu, dec_hidden, dec_x, dec_cot,
        x_h1_rows, x_enc_hidden,
    ) = ka_call(enc_x, dec_x, dec_cot, gains, *small, attn_qk, attn_vo, ff_in, ff_out_t)
    (
        dec_out, cross_gy, cross_gq, cross_gk, cross_gv, dec_one_grad, enc_end_grad, enc_gy,
        enc_gg, enc_gu, gains_mid, dec_gate, x_dec_hidden, x_dec_gy, x_dec_gu, x_hf,
    ) = kb_call(
        dec_gg, dec_gu, dec_hidden, dec_cot, dec_two, dec_one, gains, cross_q, cross_kv, cross_p,
        enc_end, enc_gelu, enc_slope, attn_qk, attn_vo, ff_in, ff_out_t, hf, dec_gy,
        size, block, padded,
    )
    (
        enc_grad, enc_ay, enc_gq, enc_gk, enc_gv, dec_grad, self_gy, self_gq, self_gk, self_gv,
        sums, ffout_sum, dec_up, chosen_h1, left_cross, right_cross, left_self, x_enc_gg,
        x_enc_gu, unused,
    ) = kc_call(
        size, block, padded,
        [
            enc_gg, enc_gu, gains, gains_mid, enc_q, dec_one_grad, dec_x, self_q, self_kv, self_p,
            enc_spots, self_bucket,
        ],
        [
            attn_qk, attn_vo, ff_in, enc_end_grad, enc_mid, enc_x, enc_kv, enc_p, enc_gy, hf, x_hf,
            dec_gu, x_dec_gu, dec_gy, x_dec_gy, dec_hidden, x_dec_hidden, enc_hidden, x_enc_hidden, h1, x_h1_rows, hs, hc, memory, cross_gy, cross_gq,
            cross_gk, cross_gv, cross_o,
        ],
    )
    ffin_sum, qk_sum, vo_sum, sums = kd_call(
        size, block, padded, width, sums,
        [
            chosen_h1, enc_gg, x_enc_gg, enc_gu, x_enc_gu, left_cross, right_cross,
            left_self, h0, enc_ay, enc_gq, enc_gk, enc_gv, enc_o, self_gq, self_gk, self_gv, self_o,
            dec_gate, dec_up,
        ],
    )
    ffout_sum = jnp.swapaxes(ffout_sum, 1, 2)
    table_rows = sums[8 : 8 + HEADS]
    tables_sum = jnp.stack(
        [table_rows[:, :BUCKETS].T, table_rows[:, PAIR : PAIR + BUCKETS].T]
    )
    return (
        dec_out[:dec_own], enc_grad, dec_grad[:dec_own], sums[:6], tables_sum, qk_sum, vo_sum,
        ffin_sum, ffout_sum,
    )


def solution(mesh):
    rows = P(("dp", "tensor"), None)
    return jax.shard_map(
        on_device,
        mesh=mesh,
        in_specs=(
            rows, rows, rows, P("dp"), P("dp"), P("dp"), P(), P(), P(), P(), P(), P(),
            P(None, None, None, "tensor"), P(None, "tensor", None),
        ),
        out_specs=(
            rows, rows, rows, P(), P(), P(None, "dp", None), P(None, "dp", None),
            P(None, None, "dp", "tensor"), P(None, "tensor", "dp"),
        ),
        check_vma=False,
    )
```

```python
import functools

import jax
import jax.numpy as jnp
from jax import lax
from jax.experimental import pallas as pl
from jax.experimental.pallas import tpu as pltpu
from jax.sharding import PartitionSpec as P

HEADS = 6
HEAD = 64
INNER = HEADS * HEAD
PAIRS = HEADS // 2
PAIR = 2 * HEAD
BUCKETS = 32
EPSILON = 1e-06
MASKED = -1000000000.0
HIGH = lax.Precision.HIGHEST
F32 = jnp.float32
LOW = jnp.bfloat16
DEC_PAD = 32
VMEM_BYTES = 60 * 1024 * 1024
ROOT = 0.7978845608028654
CUBE = 0.044715


def to_low(value):
    return value.astype(LOW)


def dot(left, right):
    return jnp.dot(left, right, preferred_element_type=F32)


def dot_first(left, right):
    return lax.dot_general(left, right, (((0,), (0,)), ((), ())), preferred_element_type=F32)


def dot_last(left, right):
    return lax.dot_general(left, right, (((1,), (1,)), ((), ())), preferred_element_type=F32)


def norm_gain(rows, gain):
    return rows * lax.rsqrt(jnp.mean(rows * rows, axis=-1, keepdims=True) + EPSILON) * gain


def norm_back(rows, gain, grad_rows):
    scale = lax.rsqrt(jnp.mean(rows * rows, axis=-1, keepdims=True) + EPSILON)
    normed = rows * scale
    scaled = grad_rows * gain
    inner = jnp.mean(scaled * normed, axis=-1, keepdims=True)
    grad_gain = jnp.sum(grad_rows * normed, axis=0, keepdims=True)
    return scale * (scaled - normed * inner), grad_gain


def act_parts(gate, up_proj):
    square = gate * gate
    curve = jnp.tanh(ROOT * gate * (1.0 + CUBE * square))
    half = 0.5 * (1.0 + curve)
    slope = half + 0.5 * gate * (1.0 - curve * curve) * (ROOT * (1.0 + 3.0 * CUBE * square))
    return gate * half, up_proj * slope


def tiles(width, step=256):
    return [(start, min(start + step, width)) for start in range(0, width, step)]


class Peers:
    def __init__(self, send_sem, recv_sem):
        dp, tensor = lax.axis_index("dp"), lax.axis_index("tensor")
        chip, core = lax.div(tensor, 2), lax.rem(tensor, 2)
        self.dp = dp
        self.own = tensor
        self.sib = chip * 2 + (1 - core)
        self.far = (1 - chip) * 2 + core
        self.diag = (1 - chip) * 2 + (1 - core)
        self.send_sem, self.recv_sem = send_sem, recv_sem
        self.used = 0
        self.copies = []

    def bit(self, place):
        return lax.rem(lax.div(self.dp, 2**place), 2)

    def across(self, place):
        return (self.dp + (1 - 2 * self.bit(place)) * 2**place, self.own)

    def device(self, peer):
        return peer if isinstance(peer, tuple) else (self.dp, peer)

    def greet(self, more=()):
        barrier = pltpu.get_barrier_semaphore()
        for peer in (self.sib, self.far) + tuple(more):
            pl.semaphore_signal(
                barrier, inc=1, device_id=self.device(peer), device_id_type=pl.DeviceIdType.MESH
            )
        pl.semaphore_wait(barrier, 2 + len(more))

    def send(self, source, target, peer):
        place = self.used
        self.used += 1
        assert place < self.send_sem.shape[0]
        copy = pltpu.make_async_remote_copy(
            src_ref=source,
            dst_ref=target,
            send_sem=self.send_sem.at[place],
            recv_sem=self.recv_sem.at[place],
            device_id=self.device(peer),
            device_id_type=pl.DeviceIdType.MESH,
        )
        copy.start()
        self.copies.append(copy)
        return copy

    def finish(self):
        for copy in self.copies:
            copy.wait_send()


class Gather:
    def __init__(self, peers, buf, near, source=None):
        self.peers, self.buf, self.source = peers, buf, source
        if near:
            self.slots = (0, 1, 2, 2, 3)
        else:
            self.slots = (peers.own, peers.own, peers.own, peers.far, peers.far)

    def start(self):
        own, at_sib, at_far, unused, unused = self.slots
        source = self.buf.at[own] if self.source is None else self.source
        self.to_far = self.peers.send(source, self.buf.at[at_far], self.peers.far)
        self.to_sib = self.peers.send(source, self.buf.at[at_sib], self.peers.sib)

    def wait_near(self):
        self.to_sib.wait_recv()

    def relay(self):
        unused, unused, unused, far, far_at_sib = self.slots
        self.to_far.wait_recv()
        self.relayed = self.peers.send(
            self.buf.at[far], self.buf.at[far_at_sib], self.peers.sib
        )

    def wait_far(self):
        self.relayed.wait_recv()


def attend(queries, kv, bias_of, allowed, weights_out, mixed_out):
    rows = queries.shape[0]
    total = kv.shape[0] * kv.shape[1]
    first = lax.broadcasted_iota(jnp.int32, (rows, PAIR), 1) < HEAD
    for pair in range(PAIRS):
        lanes = slice(pair * PAIR, (pair + 1) * PAIR)
        keys = kv[:, :, lanes].reshape(total, PAIR)
        values = kv[:, :, INNER + pair * PAIR : INNER + (pair + 1) * PAIR].reshape(total, PAIR)
        both = queries[:, lanes].astype(F32)
        mixed = []
        for half in range(2):
            head = 2 * pair + half
            here = to_low(jnp.where(first if half == 0 else ~first, both, 0.0))
            scores = dot_last(here, keys)
            if bias_of is not None:
                scores = scores + bias_of(head)
            scores = jnp.where(allowed, scores, MASKED)
            shifted = jnp.exp(scores - jnp.max(scores, axis=-1, keepdims=True))
            weights = shifted / jnp.sum(shifted, axis=-1, keepdims=True)
            weights_out[head] = weights
            mixed.append(dot(to_low(weights), values))
        mixed_out[:, lanes] = to_low(jnp.where(first, mixed[0], mixed[1]))


def attend_back(queries, kv, weights_in, grad_out, grad_q_out, grad_kv_out, grad_s_out):
    rows = queries.shape[0]
    total = kv.shape[0] * kv.shape[1]
    block = kv.shape[1]
    first = lax.broadcasted_iota(jnp.int32, (rows, PAIR), 1) < HEAD
    first_key = lax.broadcasted_iota(jnp.int32, (total, PAIR), 1) < HEAD
    for pair in range(PAIRS):
        lanes = slice(pair * PAIR, (pair + 1) * PAIR)
        value_lanes = slice(INNER + pair * PAIR, INNER + (pair + 1) * PAIR)
        keys = kv[:, :, lanes].reshape(total, PAIR)
        values = kv[:, :, value_lanes].reshape(total, PAIR)
        query = queries[:, lanes]
        grad = grad_out[:, lanes]
        grad_wide = grad.astype(F32)
        grad_q, grad_k, grad_v = [], [], []
        for half in range(2):
            head = 2 * pair + half
            here = to_low(jnp.where(first if half == 0 else ~first, grad_wide, 0.0))
            weights = weights_in[head]
            grad_weights = dot_last(here, values)
            weighted = jnp.sum(weights * grad_weights, axis=-1, keepdims=True)
            grad_scores = to_low(weights * (grad_weights - weighted))
            if grad_s_out is not None:
                grad_s_out[head] = grad_scores
            grad_q.append(dot(grad_scores, keys))
            grad_k.append(dot_first(grad_scores, query))
            grad_v.append(dot_first(to_low(weights), grad))
        grad_q_out[:, lanes] = to_low(jnp.where(first, grad_q[0], grad_q[1]))
        grad_kv_out[:, :, lanes] = jnp.where(first_key, grad_k[0], grad_k[1]).reshape(
            4, block, PAIR
        )
        grad_kv_out[:, :, value_lanes] = jnp.where(first_key, grad_v[0], grad_v[1]).reshape(
            4, block, PAIR
        )


class Exchange:
    def __init__(self, peers, whole, rows, place=0):
        partner = peers.across(place)
        self.rows = [
            (peers.send(own.at[0], other.at[0], partner), Gather(peers, other, True))
            for own, other in rows
        ]
        self.whole = [peers.send(own, other, partner) for own, other in whole]

    def spread(self):
        for copy, gather in self.rows:
            copy.wait_recv()
            gather.start()

    def relay(self):
        for unused, gather in self.rows:
            gather.wait_near()
            gather.relay()

    def finish_rows(self):
        for unused, gather in self.rows:
            gather.wait_far()

    def finish_first(self):
        self.whole.pop(0).wait_recv()

    def finish_whole(self):
        for copy in self.whole:
            copy.wait_recv()
        self.whole = []


class Loads:
    def __init__(self, sems):
        self.sems, self.used = sems, 0

    def start(self, source, target):
        copy = pltpu.make_async_copy(source, target, self.sems.at[self.used])
        self.used += 1
        copy.start()
        return copy


def wait_all(copies):
    for copy in copies:
        copy.wait()
    copies.clear()


def project_kv(rows, wqk, wvo, target):
    target[:, :INNER] = to_low(dot(rows, wqk[:, INNER:]))
    target[:, INNER:] = to_low(dot(rows, wvo[:, :INNER]))


def ff_up(rows, w_in, gelu_out, slope_out, hidden_out, slots):
    count, block = slots.stop - slots.start, gelu_out.shape[1]
    for low, high in tiles(gelu_out.shape[2]):
        gate = dot(rows, w_in[0, :, low:high])
        up_proj = dot(rows, w_in[1, :, low:high])
        gelu, slope = act_parts(gate, up_proj)
        shape = (count, block, high - low)
        gelu_out[slots, :, low:high] = gelu.reshape(shape)
        slope_out[slots, :, low:high] = slope.reshape(shape)
        hidden_out[slots, :, low:high] = to_low(gelu * up_proj).reshape(shape)


def reduce_far(peers, diag_part, far_part, send, recv):
    width = send.shape[2]
    for low, high in tiles(width):
        send[0, :, low:high] = to_low(diag_part(low, high))
    first = peers.send(send.at[0], recv.at[0], peers.sib)
    first.wait_recv()
    for low, high in tiles(width):
        send[2, :, low:high] = to_low(
            far_part(low, high) + recv[0, :, low:high].astype(F32)
        )
    return peers.send(send.at[2], recv.at[2], peers.far)


def ka_kernel(
    enc_x, dec_x_short, dec_cot_short, gains, enc_terms, self_bias, item_count, enc_mask, dec_mask,
    qk_all, vo_all, fi_all, fo_all,
    h0, enc_q, enc_kv_out, enc_p_out, enc_o, enc_mid_out, h1_out, enc_gelu_out, enc_slope_out,
    enc_hidden_out, enc_end_out, memory, cross_kv_out, hs, self_q, self_kv, self_p, self_o,
    dec_one, hc, cross_q, cross_p, cross_o, dec_two, hf, dec_gy, dec_gg, dec_gu, dec_hidden,
    dec_x, dec_cot, x_h1, x_enc_hidden,
    wqk, wvo, wfi, wfo, part, send, recv, dec_gelu, dec_slope, dec_gh,
    enc_kv, enc_p, enc_mid, h1, enc_gelu, enc_slope, enc_hidden, enc_end, cross_kv,
    send_sem, recv_sem, load_sem, store_sem,
):
    peers = Peers(send_sem, recv_sem)
    loads, stores, stored = Loads(load_sem), Loads(store_sem), []
    get_qk, get_vo, get_fi, get_fo = {}, {}, {}, {}
    for a in (0, 1):
        get_qk[a] = loads.start(qk_all.at[a], wqk.at[a])
        get_vo[a] = loads.start(vo_all.at[a], wvo.at[a])
    get_fi[0] = loads.start(fi_all.at[0], wfi.at[0])
    get_fo[0] = loads.start(fo_all.at[0], wfo.at[0])
    get_qk[2] = loads.start(qk_all.at[2], wqk.at[2])
    get_vo[2] = loads.start(vo_all.at[2], wvo.at[2])
    get_fi[1] = loads.start(fi_all.at[1], wfi.at[1])
    get_fo[1] = loads.start(fo_all.at[1], wfo.at[1])
    peers.greet([peers.across(0)])

    enc_rows, dec_rows, real_rows = enc_x.shape[0], dec_x.shape[0], dec_x_short.shape[0]
    enc_total, dec_total = 4 * enc_rows, 4 * real_rows

    def item_of(place, total):
        scaled = place * item_count[...]
        return sum((scaled >= part * total).astype(jnp.int32) for part in (1, 2, 3))

    def counted(rows, columns, axis):
        return lax.broadcasted_iota(jnp.int32, (rows, columns), axis)

    enc_code = jnp.where(enc_mask[...] == 1, item_of(counted(1, enc_total, 1), enc_total), -1)
    enc_item = item_of(counted(enc_rows, 1, 0) + peers.own * enc_rows, enc_total)
    slot = counted(1, 4 * dec_rows, 1)
    inside = lax.rem(slot, dec_rows)
    key_place = lax.div(slot, dec_rows) * real_rows + inside
    key_item = jnp.where(
        (inside < real_rows) & (dec_mask[...] == 1), item_of(key_place, dec_total), -1
    )
    row = counted(dec_rows, 1, 0)
    row_place = row + peers.own * real_rows
    dec_item = jnp.where(row < real_rows, item_of(row_place, dec_total), -2)
    self_allowed = (dec_item == key_item) & (key_place <= row_place)

    fill = jnp.zeros((dec_rows - real_rows, dec_x.shape[1]), F32)
    for short, padded in ((dec_x_short, dec_x), (dec_cot_short, dec_cot)):
        padded[...] = to_low(jnp.concatenate([short[...].astype(F32), fill], axis=0))

    normed = to_low(norm_gain(enc_x[...].astype(F32), gains[0:1]))
    h0[...] = normed
    get_qk[0].wait()
    get_vo[0].wait()
    project_kv(normed, wqk.at[0], wvo.at[0], enc_kv.at[peers.own])
    enc_gather = Gather(peers, enc_kv, False)
    enc_gather.start()
    normed_dec = to_low(norm_gain(dec_x[...].astype(F32), gains[3:4]))
    hs[...] = normed_dec
    get_qk[1].wait()
    get_vo[1].wait()
    project_kv(normed_dec, wqk.at[1], wvo.at[1], self_kv.at[peers.own])
    self_gather = Gather(peers, self_kv, False)
    self_gather.start()
    dec_gy[0] = dec_cot[...]
    gy_gather = Gather(peers, dec_gy, True)
    gy_gather.start()
    enc_q[...] = to_low(dot(normed, wqk[0, :, :INNER]))
    self_q[...] = to_low(dot(normed_dec, wqk[1, :, :INNER]))

    enc_gather.wait_near()
    enc_gather.relay()
    enc_allowed = enc_item == enc_code

    def enc_bias(head):
        own_rows, period = h0.shape[0], enc_terms.shape[1]
        spread = jnp.broadcast_to(enc_terms[head : head + 1, :], (own_rows, period))
        rolled = pltpu.roll(spread, 0, 1, stride=1, stride_axis=0)
        return rolled[:, : period // 2]

    enc_gather.wait_far()
    attend(enc_q[...], enc_kv, enc_bias, enc_allowed, enc_p, enc_o)
    stored += [stores.start(enc_kv, enc_kv_out), stores.start(enc_p, enc_p_out)]
    for low, high in tiles(enc_mid.shape[1]):
        enc_mid[:, low:high] = enc_x[:, low:high].astype(F32) + dot_last(
            enc_o[...], wvo[0, low:high, INNER:]
        )
    h1[0] = to_low(norm_gain(enc_mid[...], gains[1:2]))
    h1_gather = Gather(peers, h1, True)
    h1_gather.start()
    exchanges = [Exchange(peers, [(h1.at[0], x_h1)], [])]

    def hidden_part(low, high):
        return [(enc_hidden.at[slot], x_enc_hidden.at[slot]) for slot in range(low, high)]

    self_gather.wait_near()
    self_gather.relay()
    gy_gather.wait_near()
    gy_gather.relay()
    self_gather.wait_far()
    gy_gather.wait_far()
    attend(
        self_q[...], self_kv, lambda head: self_bias[head], self_allowed, self_p, self_o
    )
    for low, high in tiles(dec_one.shape[1]):
        dec_one[:, low:high] = dec_x[:, low:high].astype(F32) + dot_last(
            self_o[...], wvo[1, low:high, INNER:]
        )
    normed_dec = to_low(norm_gain(dec_one[...], gains[4:5]))
    hc[...] = normed_dec

    h1_gather.wait_near()
    get_fi[0].wait()
    get_fo[0].wait()
    block, width = h1.shape[1], h1.shape[2]

    def both(buf, slots):
        return buf[slots].reshape((slots.stop - slots.start) * block, buf.shape[2])

    near, away = slice(0, 2), slice(2, 4)
    ff_up(both(h1, near), wfi.at[0], enc_gelu, enc_slope, enc_hidden, near)
    exchanges.append(Exchange(peers, hidden_part(0, 2), []))
    h1_gather.relay()
    h1_gather.wait_far()
    ff_up(both(h1, away), wfi.at[0], enc_gelu, enc_slope, enc_hidden, away)
    stored += [
        stores.start(h1, h1_out), stores.start(enc_gelu, enc_gelu_out),
        stores.start(enc_slope, enc_slope_out), stores.start(enc_hidden, enc_hidden_out),
        stores.start(enc_mid, enc_mid_out),
    ]
    hidden = both(enc_hidden, away)
    for low, high in tiles(width):
        value = dot_last(hidden, wfo[0, low:high, :])
        part[:, low:high] = value[:block]
        send[0, :, low:high] = to_low(value[block:])
    first = peers.send(send.at[0], recv.at[0], peers.sib)
    exchanges.append(Exchange(peers, hidden_part(2, 4), []))
    get_qk[2].wait()
    get_vo[2].wait()
    cross_q[...] = to_low(dot(hc[...], wqk[2, :, :INNER]))
    first.wait_recv()
    send[2] = to_low(part[...] + recv[0].astype(F32))
    second = peers.send(send.at[2], recv.at[2], peers.far)
    hidden = both(enc_hidden, near)
    for low, high in tiles(width):
        value = dot_last(hidden, wfo[0, low:high, :])
        part[:, low:high] = value[:block] + enc_mid[:, low:high]
        send[1, :, low:high] = to_low(value[block:])
    third = peers.send(send.at[1], recv.at[1], peers.sib)
    get_fi[1].wait()
    get_fo[1].wait()
    grad_y = dec_gy[...].reshape(4 * dec_rows, width)
    for low, high in tiles(dec_gh.shape[2]):
        dec_gh[:, :, low:high] = dot(grad_y, wfo[1, :, low:high]).reshape(4, dec_rows, high - low)
    third.wait_recv()
    part[...] = part[...] + recv[1].astype(F32)
    second.wait_recv()
    ended = part[...] + recv[2].astype(F32)
    enc_end[...] = ended
    stored.append(stores.start(enc_end, enc_end_out))
    normed = to_low(norm_gain(ended, gains[2:3]))
    memory[...] = normed

    project_kv(normed, wqk.at[2], wvo.at[2], cross_kv.at[peers.own])
    cross_gather = Gather(peers, cross_kv, False)
    cross_gather.start()
    cross_allowed = dec_item == enc_code
    cross_gather.wait_near()
    cross_gather.relay()
    cross_gather.wait_far()
    attend(cross_q[...], cross_kv, None, cross_allowed, cross_p, cross_o)
    stored.append(stores.start(cross_kv, cross_kv_out))
    for low, high in tiles(dec_two.shape[1]):
        dec_two[:, low:high] = dec_one[:, low:high] + dot_last(
            cross_o[...], wvo[2, low:high, INNER:]
        )
    hf[0] = to_low(norm_gain(dec_two[...], gains[5:6]))
    hf_gather = Gather(peers, hf, True)
    hf_gather.start()

    rows = hf.shape[0] * hf.shape[1]
    hf_gather.wait_near()
    hf_gather.relay()
    hf_gather.wait_far()
    ff_up(hf[...].reshape(rows, width), wfi.at[1], dec_gelu, dec_slope, dec_hidden, slice(0, 4))
    dec_gg[...] = to_low(dec_gh[...] * dec_slope[...])
    dec_gu[...] = to_low(dec_gh[...] * dec_gelu[...])
    for exchange in exchanges:
        exchange.finish_whole()
    wait_all(stored)
    peers.finish()


def ka_call(enc_x, dec_x, dec_cot, gains, enc_terms, self_bias, item_count, enc_mask, dec_mask, attn_qk, attn_vo, ff_in, ff_out):
    rows, width = enc_x.shape
    dec_rows = DEC_PAD
    units = ff_in.shape[3]
    total = enc_mask.shape[1]
    kv_width = 2 * INNER
    shape = jax.ShapeDtypeStruct
    outs = [
        shape((rows, width), LOW), shape((rows, INNER), LOW), shape((4, rows, kv_width), LOW),
        shape((HEADS, rows, total), F32), shape((rows, INNER), LOW), shape((rows, width), F32),
        shape((4, rows, width), LOW), shape((4, rows, units), F32), shape((4, rows, units), F32),
        shape((4, rows, units), LOW), shape((rows, width), F32), shape((rows, width), LOW),
        shape((4, rows, kv_width), LOW),
        shape((dec_rows, width), LOW), shape((dec_rows, INNER), LOW),
        shape((4, dec_rows, kv_width), LOW), shape((HEADS, dec_rows, 4 * dec_rows), F32),
        shape((dec_rows, INNER), LOW), shape((dec_rows, width), F32),
        shape((dec_rows, width), LOW), shape((dec_rows, INNER), LOW),
        shape((HEADS, dec_rows, total), F32), shape((dec_rows, INNER), LOW),
        shape((dec_rows, width), F32),
        shape((4, dec_rows, width), LOW), shape((4, dec_rows, width), LOW),
        shape((4, dec_rows, units), LOW), shape((4, dec_rows, units), LOW),
        shape((4, dec_rows, units), LOW), shape((dec_rows, width), LOW),
        shape((dec_rows, width), LOW),
    ]
    traded = [shape((rows, width), LOW), shape((4, rows, units), LOW)]
    vmem = pl.BlockSpec(memory_space=pltpu.VMEM)
    hbm = pl.BlockSpec(memory_space=pltpu.HBM)
    copies = 3 * 6 + 3 + 1 + 4
    apart = (2, 3, 5, 6, 7, 8, 9, 10, 12)
    return pl.pallas_call(
        ka_kernel,
        out_shape=outs + traded,
        in_specs=[vmem] * 9 + [hbm] * 4,
        out_specs=[hbm if place in apart else vmem for place in range(len(outs))]
        + [hbm] * len(traded),
        scratch_shapes=[
            pltpu.VMEM(attn_qk.shape, LOW), pltpu.VMEM(attn_vo.shape, LOW),
            pltpu.VMEM(ff_in.shape, LOW), pltpu.VMEM(ff_out.shape, LOW),
            pltpu.VMEM((rows, width), F32), pltpu.VMEM((3, rows, width), LOW),
            pltpu.VMEM((3, rows, width), LOW), pltpu.VMEM((4, dec_rows, units), F32),
            pltpu.VMEM((4, dec_rows, units), F32), pltpu.VMEM((4, dec_rows, units), F32),
            *[pltpu.VMEM(outs[place].shape, outs[place].dtype) for place in apart],
            pltpu.SemaphoreType.DMA((copies,)), pltpu.SemaphoreType.DMA((copies,)),
            pltpu.SemaphoreType.DMA((10,)), pltpu.SemaphoreType.DMA((len(apart),)),
        ],
        compiler_params=pltpu.CompilerParams(
            collective_id=0, has_side_effects=True, vmem_limit_bytes=VMEM_BYTES
        ),
        name="forward_chain",
    )(enc_x, dec_x, dec_cot, gains, enc_terms, self_bias, item_count, enc_mask, dec_mask,
      attn_qk, attn_vo, ff_in, ff_out)


def prepare(item_count, enc_mask, dec_mask, enc_buckets, dec_buckets, tables, enc_own, dec_own):
    tensor_id = lax.axis_index("tensor")
    enc_total, dec_total = enc_mask.shape[0], dec_mask.shape[0]
    slot = jnp.arange(4 * DEC_PAD)
    place = slot // DEC_PAD * dec_own + slot % DEC_PAD
    row_place = tensor_id * dec_own + jnp.arange(DEC_PAD)
    dec_live = jnp.pad(dec_mask.reshape(4, dec_own), ((0, 0), (0, DEC_PAD - dec_own)))
    onehot = (enc_buckets[:, None] == jnp.arange(BUCKETS)[None, :]).astype(F32)
    terms = jnp.dot(tables[0].T, onehot.T, precision=HIGH)
    terms = jnp.pad(terms, ((0, 2), (0, 1)))
    period = 2 * enc_total
    doubled = jnp.concatenate([terms, terms], axis=1)
    shift = (enc_total - 1 - tensor_id * enc_own + period) % period
    enc_terms = lax.dynamic_slice_in_dim(doubled, shift, period, 1)
    far_back = jnp.clip(row_place[:, None] - place[None, :], 0, dec_total - 1)
    far_back = (far_back[None] == jnp.arange(dec_total)[:, None, None]).astype(F32)
    far_back = far_back.reshape(dec_total, -1)
    dec_onehot = (dec_buckets[:, None] == jnp.arange(BUCKETS)[None, :]).astype(F32)
    dec_terms = jnp.dot(tables[1].T, dec_onehot.T, precision=HIGH)
    self_bias = jnp.dot(dec_terms, far_back, precision=HIGH).reshape(
        HEADS, DEC_PAD, 4 * DEC_PAD
    )
    spots = jnp.pad(onehot, ((0, 1), (0, 0)))
    enc_spots = lax.dynamic_slice_in_dim(
        spots, enc_total - enc_own - tensor_id * enc_own, enc_total + enc_own, 0
    )
    self_bucket = jnp.dot(
        dec_buckets.astype(F32)[None, :], far_back, precision=HIGH
    ).reshape(DEC_PAD, 4 * DEC_PAD)
    return (
        enc_terms, self_bias, item_count.reshape(1, 1), enc_mask.reshape(1, enc_total),
        dec_live.reshape(1, 4 * DEC_PAD),
    ), (enc_spots, self_bucket)


RING = 4


def chunk_of(size):
    return 512 if size <= 8 else 256


def lag_of(steps):
    return 2 if steps <= 3 else 1


class Reduce:
    def __init__(self, peers, places, product, columns, total, send, recv, slot, finish, ships):
        self.ships = ships
        self.peers, self.places, self.product, self.columns = peers, places, product, columns
        self.total, self.send, self.recv, self.slot, self.done = total, send, recv, slot, finish
        self.steps = len(places) + 1

    def buffers(self, step):
        lanes = pl.ds(0, self.columns)
        return (
            self.send[step].at[self.slot % self.send[step].shape[0], :, lanes],
            self.recv[step].at[self.slot, :, lanes],
        )

    def ship(self, step, value, place):
        source, target = self.buffers(step)
        key = (id(self.send), step, self.slot % self.send[step].shape[0])
        if key in self.ships:
            self.ships[key].wait_send()
            self.peers.copies = [c for c in self.peers.copies if c is not self.ships[key]]
        source[...] = to_low(value)
        self.copy = self.peers.send(source, target, self.peers.across(place))
        self.ships[key] = self.copy

    def run(self, step):
        lanes = pl.ds(0, self.columns)
        if step == 0:
            here = self.peers.bit(self.places[0])
            self.ship(0, self.product(1 - here), self.places[0])
            self.height = self.send[0].shape[1]
            self.start = 0
            self.total[: self.height, lanes] = self.product(here)
            return
        self.copy.wait_recv()
        arrived = self.buffers(step - 1)[1]
        if step == self.steps - 1:
            rows = pl.ds(self.start, self.height)
            self.done(self.total[rows, lanes] + arrived[...].astype(F32))
            return
        self.height //= 2
        place = self.places[step]
        here = self.peers.bit(place)
        away = pl.multiple_of(self.start + (1 - here) * self.height, 16)
        kept = pl.multiple_of(self.start + here * self.height, 16)
        from_away = pl.multiple_of((1 - here) * self.height, 16)
        from_kept = pl.multiple_of(here * self.height, 16)
        self.ship(
            step,
            self.total[pl.ds(away, self.height), lanes]
            + arrived[pl.ds(from_away, self.height), :].astype(F32),
            place,
        )
        self.total[pl.ds(kept, self.height), lanes] += arrived[
            pl.ds(from_kept, self.height), :
        ].astype(F32)
        self.start = kept


class Stream:
    def __init__(self, items, lag):
        self.items, self.lag, self.now = items, lag, 0
        self.last = max(place + lag * (item.steps - 1) for place, item in enumerate(items))

    def pump(self, ticks=1):
        for unused in range(ticks):
            now = self.now
            if now > self.last:
                return
            self.now += 1
            for place, item in reversed(list(enumerate(self.items))):
                step, odd = divmod(now - place, self.lag)
                if odd == 0 and 0 < step < item.steps:
                    item.run(step)
            if now < len(self.items):
                for action in self.items[now].before:
                    if action is not None:
                        action()
                self.items[now].run(0)

    def drain(self):
        self.pump(self.last + 1 - self.now)


def flat(value):
    return value.reshape(value.shape[0] * value.shape[1], value.shape[2])


def choose_rows(peers, layout, first, rows, chosen, start):
    size, block, padded = layout
    bits = size.bit_length() - 1
    width = rows.shape[1]
    for known in range(2**first):

        def run(known=known):
            for half in range(2):
                for place in range(chosen.shape[1] // padded):
                    owner = known + (half << first)
                    for bit in range(first + 1, bits):
                        owner += ((place >> (bits - 1 - bit)) & 1) << bit
                    left = owner * block // 128 * 128
                    right = min(-(-(owner + 1) * block // 128) * 128, width)
                    inside = lax.broadcasted_iota(jnp.int32, (padded, right - left), 0)
                    lane = lax.broadcasted_iota(jnp.int32, (padded, right - left), 1)
                    picked = (lane - inside == owner * block - left) & (inside < block)
                    pick = to_low(jnp.where(picked, 1.0, 0.0))
                    for low, high in tiles(rows.shape[0]):
                        chosen[
                            half, place * padded : (place + 1) * padded,
                            start + low : start + high,
                        ] = to_low(dot_last(pick, rows[low:high, left:right]))

        if first:
            same = peers.bit(0) == known % 2
            for bit in range(1, first):
                same = same & (peers.bit(bit) == (known >> bit) % 2)
            pl.when(same)(run)
        else:
            run()


class Products:
    def __init__(self, peers, layout, first, steps, chosen, total, *buffers):
        self.peers, self.layout, self.first = peers, layout, first
        self.chosen, self.total = chosen, total
        self.places = list(range(first, steps))
        self.send, self.recv = buffers[: steps - first], buffers[steps - first :]
        self.items, self.ships = [], {}

    def choose(self, lefts, before):
        def run():
            if before is not None:
                before()
            rows = lefts[0].shape[0] * lefts[0].shape[1]
            for part, left in enumerate(lefts):
                choose_rows(
                    self.peers, self.layout, self.first, flat(left[...]), self.chosen, part * rows
                )

        return run

    def add(self, lefts, rights, out, before=None, ready=()):
        actions = [] if lefts is None else [self.choose(lefts, before)]
        for kind, parts in enumerate(rights):
            rows = parts[0].shape[0] * parts[0].shape[1]
            if ready:
                actions.append(ready[kind])
            for low, high in tiles(parts[0].shape[2], self.total.shape[2]):

                def product(half, parts=parts, low=low, high=high):
                    value = None
                    for part, right in enumerate(parts):
                        here = dot(
                            self.chosen[half, :, part * rows : (part + 1) * rows],
                            flat(right[:, :, low:high]),
                        )
                        value = here if value is None else value + here
                    return value

                def finish(value, kind=kind, low=low, high=high):
                    out[kind, :, low:high] = value[: out.shape[1]]

                count = len(self.items)
                item = Reduce(
                    self.peers, self.places, product, high - low,
                    self.total.at[count % self.total.shape[0]], self.send, self.recv, count,
                    finish, self.ships,
                )
                item.before, actions = actions, []
                self.items.append(item)


def product_scratch(size, padded, rows, items, first, chunk):
    chosen = size * padded >> first
    steps = size.bit_length() - 1
    heights = [chosen >> (step + 1) for step in range(steps - first)]
    return [
        pltpu.VMEM((2, chosen // 2, rows), LOW),
        pltpu.VMEM((lag_of(steps) * (steps - first) + 1, chosen // 2, chunk), F32),
        *[pltpu.VMEM((RING, height, chunk), LOW) for height in heights],
        *[pltpu.VMEM((items, height, chunk), LOW) for height in heights],
    ]


def to_owners(peers, sources, target, rows_of, own_sem):
    sends = []
    for peer in (peers.far, peers.diag, peers.sib):
        place = peers.used
        peers.used += 1
        for role in range(4):
            rows = rows_of[role]

            def copy(role=role, rows=rows, place=place, peer=peer):
                return pltpu.make_async_remote_copy(
                    src_ref=sources[role],
                    dst_ref=target.at[peers.own, pl.ds(0, rows)],
                    send_sem=peers.send_sem.at[place],
                    recv_sem=peers.recv_sem.at[place],
                    device_id=peers.device(peer),
                    device_id_type=pl.DeviceIdType.MESH,
                )

            @pl.when(peer == role)
            def _(copy=copy):
                copy().start()

            sends.append((peer, role, copy))
    for role in range(4):

        def keep(role=role):
            return pltpu.make_async_copy(
                sources[role], target.at[peers.own, pl.ds(0, rows_of[role])], own_sem
            )

        @pl.when(peers.own == role)
        def _(keep=keep):
            keep().start()

        sends.append((None, role, keep))
    return sends


def owners_done(peers, sends):
    for peer, role, copy in sends:

        @pl.when(peers.own == role)
        def _(copy=copy, peer=peer):
            copy().wait() if peer is None else copy().wait_recv()

        if peer is not None:

            @pl.when(peer == role)
            def _(copy=copy):
                copy().wait_send()


def kv_back(grad_kv, wqk, wvo, low, high):
    return dot_last(grad_kv[:, :INNER], wqk[low:high, INNER:]) + dot_last(
        grad_kv[:, INNER:], wvo[low:high, :INNER]
    )


class SumBlocks:
    def __init__(self, peers, buf, send, recv):
        self.peers, self.buf, self.send, self.recv = peers, buf, send, recv
        send[0] = to_low(buf[peers.diag])
        send[1] = to_low(buf[peers.sib])
        self.first = peers.send(send.at[0], recv.at[0], peers.sib)
        self.third = peers.send(send.at[1], recv.at[1], peers.sib)

    def cross(self):
        peers = self.peers
        self.first.wait_recv()
        self.send[2] = to_low(self.buf[peers.far] + self.recv[0].astype(F32))
        self.second = peers.send(self.send.at[2], self.recv.at[2], peers.far)

    def result(self):
        self.third.wait_recv()
        value = self.buf[self.peers.own] + self.recv[1].astype(F32)
        self.second.wait_recv()
        return value + self.recv[2].astype(F32)


class SumNear:
    def __init__(self, peers, part_of, block, total, send, recv):
        self.peers, self.total, self.send, self.recv = peers, total, send, recv
        for low, high in tiles(send.shape[2]):
            value = part_of(low, high)
            total[0, :, low:high] = value[:block]
            send[1, :, low:high] = to_low(value[block : 2 * block])
            total[1, :, low:high] = value[2 * block : 3 * block]
            send[0, :, low:high] = to_low(value[3 * block :])
        self.first = peers.send(send.at[0], recv.at[0], peers.sib)
        self.third = peers.send(send.at[1], recv.at[1], peers.sib)

    def cross(self):
        self.first.wait_recv()
        self.send[2] = to_low(self.total[1] + self.recv[0].astype(F32))
        self.second = self.peers.send(self.send.at[2], self.recv.at[2], self.peers.far)

    def result(self):
        self.third.wait_recv()
        value = self.total[0] + self.recv[1].astype(F32)
        self.second.wait_recv()
        return value + self.recv[2].astype(F32)


def kb_kernel(
    dec_gg, dec_gu, dec_hidden, dec_cot, dec_two, dec_one, gains, cross_q, hf,
    qk_all, vo_all, fi_all, fo_all, dec_gy, cross_kv_all, cross_p_all, enc_end_all,
    enc_gelu_all, enc_slope_all,
    dec_out, cross_gy, cross_gq, cross_gk, cross_gv, dec_one_grad, enc_end_grad, enc_gy, enc_gg, enc_gu,
    gains_grad, dec_gate, x_dec_hidden, x_dec_gy, x_dec_gu, x_hf,
    wqk, wvo, wfi, wfo, grad_kv, kv_send, kv_recv, row_total, row_send, row_recv, out_total,
    out_send, out_recv, x_dec_gg, cross_kv, cross_p, enc_end, enc_gelu, enc_slope,
    *rest,
    layout, steps,
):
    scratch, (send_sem, recv_sem, load_sem) = rest[:-3], rest[-3:]
    peers = Peers(send_sem, recv_sem)
    loads = Loads(load_sem)
    get_fi = loads.start(fi_all.at[1], wfi)
    get_cross = [
        loads.start(vo_all.at[2], wvo), loads.start(cross_kv_all, cross_kv),
        loads.start(cross_p_all, cross_p), loads.start(qk_all.at[2], wqk),
        loads.start(enc_end_all, enc_end),
    ]
    get_fo1 = loads.start(fo_all.at[1], wfo.at[1])
    get_up = [
        loads.start(fo_all.at[0], wfo.at[0]), loads.start(enc_gelu_all, enc_gelu),
        loads.start(enc_slope_all, enc_slope),
    ]
    peers.greet([peers.across(place) for place in range(steps)])
    first = Exchange(peers, [(dec_gg, x_dec_gg)], [(hf, x_hf)])
    later = [
        Exchange(
            peers, [(dec_gu, x_dec_gu), (dec_hidden, x_dec_hidden)], [(dec_gy, x_dec_gy)]
        )
    ]

    def arrived():
        first.finish_rows()
        first.finish_whole()

    products = Products(peers, layout, 1, steps, *scratch)
    products.add(
        [hf, x_hf], [(dec_gg, x_dec_gg)], dec_gate, before=arrived
    )
    stream = Stream(products.items, lag_of(steps))
    width = dec_two.shape[1]
    block = dec_two.shape[0]
    units = dec_gg.shape[2]
    gains_grad[...] = jnp.zeros_like(gains_grad)

    get_fi.wait()
    gate, up_proj = dec_gg[...].reshape(4 * block, units), dec_gu[...].reshape(4 * block, units)

    def grad_rows_part(low, high):
        return dot_last(gate, wfi[0, low:high, :]) + dot_last(up_proj, wfi[1, low:high, :])

    grad_rows = SumNear(peers, grad_rows_part, block, row_total, row_send, row_recv)
    grad_rows.cross()
    wait_all(get_cross)
    first.spread()
    value, gain_row = norm_back(dec_two[...], gains[5:6], grad_rows.result())
    gains_grad[5:6] = gain_row
    residual = dec_cot[...].astype(F32) + value
    grad_y = to_low(residual)
    cross_gy[...] = grad_y

    grad_out = to_low(dot(grad_y, wvo[:, INNER:]))
    first.relay()
    stream.pump(1)
    attend_back(cross_q[...], cross_kv, cross_p, grad_out, cross_gq, grad_kv, None)
    kv_sum = SumBlocks(peers, grad_kv, kv_send, kv_recv)
    kv_sum.cross()
    stream.pump(1)
    for low, high in tiles(width):
        row_total[0, :, low:high] = dot_last(cross_gq[...], wqk[low:high, :INNER])
    value, gain_row = norm_back(dec_one[...], gains[4:5], row_total[0])
    gains_grad[4:5] = gain_row
    dec_one_grad[...] = residual + value
    stream.pump(1)
    own_kv = to_low(kv_sum.result())
    cross_gk[...] = own_kv[:, :INNER]
    cross_gv[...] = own_kv[:, INNER:]
    for low, high in tiles(width):
        enc_end_grad[:, low:high] = kv_back(own_kv, wqk, wvo, low, high)
    value, gain_row = norm_back(enc_end[...], gains[2:3], enc_end_grad[...])
    gains_grad[2:3] = gain_row
    enc_end_grad[...] = value
    enc_gy[0] = to_low(value)
    gy_gather = Gather(peers, enc_gy, True)
    gy_gather.start()

    get_fo1.wait()
    hidden = dec_hidden[...].reshape(4 * block, units)
    out_sum = SumNear(
        peers, lambda low, high: dot_last(hidden, wfo[1, low:high, :]), block, out_total,
        out_send, out_recv,
    )

    stream.pump(1)
    for exchange in later:
        exchange.spread()
    wait_all(get_up)
    rows = enc_gy.shape[1]

    def gate_grads(slots):
        grad_y = enc_gy[slots].reshape(2 * rows, width)
        for low, high in tiles(units):
            grad_h = dot(grad_y, wfo[0, :, low:high]).reshape(2, rows, high - low)
            enc_gg[slots, :, low:high] = to_low(grad_h * enc_slope[slots, :, low:high])
            enc_gu[slots, :, low:high] = to_low(grad_h * enc_gelu[slots, :, low:high])

    gy_gather.wait_near()
    stream.pump(1)
    gate_grads(slice(0, 2))
    gy_gather.relay()
    out_sum.cross()
    stream.pump(1)
    gy_gather.wait_far()
    gate_grads(slice(2, 4))
    stream.pump(1)
    for exchange in later:
        exchange.relay()
    stream.pump(1)
    dec_out[...] = to_low(dec_two[...] + out_sum.result())
    stream.drain()
    for exchange in later:
        exchange.finish_rows()
        exchange.finish_whole()
    peers.finish()


def kb_call(dec_gg, dec_gu, dec_hidden, dec_cot, dec_two, dec_one, gains, cross_q, cross_kv,
            cross_p, enc_end, enc_gelu, enc_slope, attn_qk, attn_vo, ff_in, ff_out, hf, dec_gy,
            size, block, padded):
    rows, width = enc_end.shape
    dec_rows = dec_two.shape[0]
    units = ff_in.shape[3]
    kv_width = 2 * INNER
    shape = jax.ShapeDtypeStruct
    outs = [
        shape((dec_rows, width), LOW), shape((dec_rows, width), LOW),
        shape((dec_rows, INNER), LOW), shape((rows, INNER), LOW), shape((rows, INNER), LOW),
        shape((dec_rows, width), F32), shape((rows, width), F32), shape((4, rows, width), LOW), shape((4, rows, units), LOW),
        shape((4, rows, units), LOW), shape((8, width), F32), shape((1, block, units), F32),
    ]
    traded = [
        shape(value.shape, LOW)
        for value in (dec_hidden, dec_gy, dec_gu, hf)
    ]
    steps = size.bit_length() - 1
    items = len(tiles(units, 256))
    vmem = pl.BlockSpec(memory_space=pltpu.VMEM)
    hbm = pl.BlockSpec(memory_space=pltpu.HBM)
    copies = 3 * 3 + 3 + 5 + 6 + items * (steps - 1)
    return pl.pallas_call(
        functools.partial(kb_kernel, layout=(size, block, padded), steps=steps),
        out_shape=outs + traded,
        in_specs=[vmem] * 9 + [hbm] * 10,
        out_specs=[vmem] * len(outs) + [hbm] * (len(traded) - 1) + [vmem],
        scratch_shapes=[
            pltpu.VMEM(attn_qk.shape[1:], LOW), pltpu.VMEM(attn_vo.shape[1:], LOW),
            pltpu.VMEM(ff_in.shape[1:], LOW), pltpu.VMEM(ff_out.shape, LOW),
            pltpu.VMEM((4, rows, kv_width), F32), pltpu.VMEM((3, rows, kv_width), LOW),
            pltpu.VMEM((3, rows, kv_width), LOW), pltpu.VMEM((2, dec_rows, width), F32),
            pltpu.VMEM((3, dec_rows, width), LOW), pltpu.VMEM((3, dec_rows, width), LOW),
            pltpu.VMEM((2, dec_rows, width), F32), pltpu.VMEM((3, dec_rows, width), LOW),
            pltpu.VMEM((3, dec_rows, width), LOW),
            pltpu.VMEM(dec_gg.shape, LOW),
            pltpu.VMEM(cross_kv.shape, LOW), pltpu.VMEM(cross_p.shape, F32),
            pltpu.VMEM(enc_end.shape, F32), pltpu.VMEM(enc_gelu.shape, F32),
            pltpu.VMEM(enc_slope.shape, F32),
            *product_scratch(size, padded, 2 * 4 * dec_rows, items, 1, 256),
            pltpu.SemaphoreType.DMA((copies,)), pltpu.SemaphoreType.DMA((copies,)),
            pltpu.SemaphoreType.DMA((10,)),
        ],
        compiler_params=pltpu.CompilerParams(
            collective_id=1, has_side_effects=True, vmem_limit_bytes=VMEM_BYTES
        ),
        name="middle_chain",
    )(dec_gg, dec_gu, dec_hidden, dec_cot, dec_two, dec_one, gains, cross_q, hf,
      attn_qk, attn_vo, ff_in, ff_out, dec_gy, cross_kv, cross_p, enc_end,
      enc_gelu, enc_slope)


def kc_kernel(
    enc_gg, enc_gu, gains, gains_mid, enc_q, dec_one_grad, dec_x, self_q, self_kv, self_p,
    enc_spots, self_bucket,
    qk_all, vo_all, fi_all, enc_end_grad_all, enc_mid_all, enc_x_all, enc_kv_all, enc_p_all,
    enc_gy_all, hf_all, x_hf_all, dec_gu_all, x_dec_gu_all, dec_gy_all, x_dec_gy_all,
    dec_hidden_all, x_dec_hidden_all, enc_hidden_all,
    x_enc_hidden_all, h1_all, x_h1_rows, hs, hc, memory, cross_gy, cross_gq, cross_gk, cross_gv,
    cross_o,
    enc_grad, enc_ay, enc_gq, enc_gk, enc_gv, dec_grad, self_gy, self_gq, self_gk, self_gv,
    small, ffout, dec_up, chosen_h1, left_cross, right_cross, left_self, x_enc_gg, x_enc_gu, x_h1,
    wqk, wvo, wfi, enc_gs, self_gs, part, send, recv, enc_gkv_full, kv_send, kv_recv,
    self_gkv_full, self_send, self_recv, x_enc_gy, enc_end_grad, enc_mid, enc_x, enc_kv, enc_p,
    enc_gy, hfs, dec_gus, dec_gys, dec_hiddens, enc_hidden, x_enc_hidden, stage, *rest,
    layout, steps,
):
    dec_scratch, enc_scratch = rest[: 2 * steps], rest[2 * steps : -4]
    send_sem, recv_sem, load_sem, own_sem = rest[-4:]
    peers = Peers(send_sem, recv_sem)
    loads = Loads(load_sem)
    get_dec = [
        loads.start(source, target.at[place])
        for sources, target in (
            ((hf_all, x_hf_all), hfs), ((dec_gu_all, x_dec_gu_all), dec_gus),
            ((dec_gy_all, x_dec_gy_all), dec_gys), ((dec_hidden_all, x_dec_hidden_all), dec_hiddens),
        )
        for place, source in enumerate(sources)
    ]
    get_fi = loads.start(fi_all.at[0], wfi)
    get_vo1 = loads.start(vo_all.at[1], wvo.at[1])
    get_mid = [
        loads.start(enc_mid_all, enc_mid), loads.start(enc_end_grad_all, enc_end_grad),
        loads.start(vo_all.at[0], wvo.at[0]), loads.start(enc_kv_all, enc_kv),
        loads.start(enc_p_all, enc_p),
    ]
    get_out = [
        loads.start(enc_gy_all, enc_gy), loads.start(enc_hidden_all, enc_hidden),
        loads.start(x_enc_hidden_all, x_enc_hidden),
    ]
    get_last = [
        loads.start(qk_all.at[0], wqk.at[0]), loads.start(qk_all.at[1], wqk.at[1]),
        loads.start(enc_x_all, enc_x),
    ]
    for buf in (left_cross, right_cross):
        buf[...] = jnp.zeros_like(buf)
    peers.greet([peers.diag] + [peers.across(place) for place in range(steps)])
    exchange = Exchange(
        peers, [(enc_gg, x_enc_gg), (enc_gu, x_enc_gu)], [(enc_gy_all, x_enc_gy)]
    )
    dec_rows, enc_rows = hs.shape[0], memory.shape[0]
    short = (dec_rows,) * 4
    mixed = (dec_rows, enc_rows, enc_rows, dec_rows)
    owned = [
        to_owners(peers, (hc, memory, memory, cross_gy), left_cross, mixed, own_sem.at[0]),
        to_owners(
            peers, (cross_gq, cross_gk, cross_gv, cross_o), right_cross, mixed, own_sem.at[1]
        ),
    ]

    h1_gather = Gather(peers, x_h1, True, x_h1_rows)

    def arrived():
        wait_all(get_out)
        exchange.relay()
        exchange.finish_rows()

    def ready():
        wait_all(get_dec)

    dec_products = Products(peers, layout, 1, steps, *dec_scratch)
    dec_products.add(
        [hfs.at[place] for place in range(2)], [[dec_gus.at[place] for place in range(2)]], dec_up,
        before=ready,
    )
    dec_products.add(
        [dec_gys.at[place] for place in range(2)], [[dec_hiddens.at[place] for place in range(2)]],
        ffout.at[pl.ds(1, 1)],
    )
    enc_products = Products(peers, layout, 1, steps, *enc_scratch)
    enc_products.add(
        [enc_gy, x_enc_gy], [(enc_hidden, x_enc_hidden)], ffout.at[pl.ds(0, 1)], before=arrived
    )
    stream = Stream(dec_products.items + enc_products.items, lag_of(steps))
    staged = []

    def fetch_rows(place):
        if place == 5:
            h1_gather.wait_near()
            h1_gather.relay()
        if place == 7:
            h1_gather.wait_far()
        source = x_h1_rows if place == 4 else (h1_all, x_h1)[place // 4].at[place % 4]
        staged.append(loads.start(source, stage.at[place % 2]))

    def choose_next(place):
        staged.pop(0).wait()
        choose_rows(peers, layout, 1, stage[place % 2], chosen_h1, place * enc_rows)
        if place + 2 < 8:
            fetch_rows(place + 2)

    rows, width = enc_mid.shape
    units = enc_gg.shape[2]
    small[...] = jnp.zeros_like(small)
    small[:8] = gains_mid[...]

    stream.pump(2)
    get_fi.wait()

    def grad_part(slots, low, high):
        gate = enc_gg[slots].reshape(2 * rows, units)
        up_proj = enc_gu[slots].reshape(2 * rows, units)
        return dot_last(gate, wfi[0, low:high, :]) + dot_last(up_proj, wfi[1, low:high, :])

    for low, high in tiles(width):
        value = grad_part(slice(2, 4), low, high)
        part[:, low:high] = value[:rows]
        send[0, :, low:high] = to_low(value[rows:])
    for place in range(2):
        fetch_rows(place)
    first = peers.send(send.at[0], recv.at[0], peers.sib)
    stream.pump(1)
    get_vo1.wait()
    residual_dec = dec_one_grad[...]
    grad_y = to_low(residual_dec)
    self_gy[...] = grad_y
    owned.append(to_owners(peers, (hs, hs, hs, self_gy), left_self, short, own_sem.at[2]))
    grad_out_dec = to_low(dot(grad_y, wvo[1, :, INNER:]))
    exchange.spread()
    first.wait_recv()
    send[2] = to_low(part[...] + recv[0].astype(F32))
    second = peers.send(send.at[2], recv.at[2], peers.far)
    for low, high in tiles(width):
        value = grad_part(slice(0, 2), low, high)
        part[:, low:high] = value[:rows]
        send[1, :, low:high] = to_low(value[rows:])
    third = peers.send(send.at[1], recv.at[1], peers.sib)

    stream.pump(1)
    attend_back(self_q[...], self_kv, self_p, grad_out_dec, self_gq, self_gkv_full, self_gs)
    self_sum = SumBlocks(peers, self_gkv_full, self_send, self_recv)
    self_sum.cross()

    stream.pump(1)
    for place in range(3):
        choose_next(place)

    columns = []
    for bucket in range(BUCKETS):
        here = jnp.where(self_bucket[...] == bucket, 1.0, 0.0)
        sums = jnp.sum(self_gs[...].astype(F32) * here[None], axis=1)
        columns.append(jnp.sum(sums, axis=1, keepdims=True))
    self_table = jnp.concatenate(columns, axis=1)

    stream.pump(1)
    third.wait_recv()
    part[...] = part[...] + recv[1].astype(F32)
    second.wait_recv()
    wait_all(get_mid)
    value, gain_row = norm_back(enc_mid[...], gains[1:2], part[...] + recv[2].astype(F32))
    small[1:2] = gain_row
    residual = enc_end_grad[...] + value
    grad_y = to_low(residual)
    enc_ay[...] = grad_y
    enc_grad[...] = residual

    h1_gather.start()
    grad_out = to_low(dot(grad_y, wvo[0, :, INNER:]))
    attend_back(enc_q[...], enc_kv, enc_p, grad_out, enc_gq, enc_gkv_full, enc_gs)
    enc_sum = SumBlocks(peers, enc_gkv_full, kv_send, kv_recv)
    stream.pump(2)
    wait_all(get_last)
    for low, high in tiles(width):
        part[:, low:high] = dot_last(enc_gq[...], wqk[0, low:high, :INNER])
    enc_sum.cross()

    stream.pump(1)
    choose_next(3)
    own_kv = to_low(self_sum.result())
    self_gk[...] = own_kv[:, :INNER]
    self_gv[...] = own_kv[:, INNER:]
    for low, high in tiles(width):
        dec_grad[:, low:high] = dot_last(self_gq[...], wqk[1, low:high, :INNER]) + kv_back(
            own_kv, wqk.at[1], wvo.at[1], low, high
        )
    value, gain_row = norm_back(dec_x[...].astype(F32), gains[3:4], dec_grad[...])
    small[3:4] = gain_row
    dec_grad[...] = residual_dec + value

    turn = lax.broadcasted_iota(jnp.int32, (rows, rows), 0) + lax.broadcasted_iota(
        jnp.int32, (rows, rows), 1
    )
    turn = jnp.where(turn == rows - 1, 1.0, 0.0).astype(LOW)
    offsets = []
    for head in range(HEADS):
        turned = dot(turn, enc_gs[head])
        spread = jnp.concatenate([turned, jnp.zeros((rows, rows), F32)], axis=1)
        spread = pltpu.roll(spread, 0, 1, stride=1, stride_axis=0)
        offsets.append(jnp.sum(spread, axis=0, keepdims=True))
    enc_table = jnp.dot(
        jnp.concatenate(offsets + [jnp.zeros((2, offsets[0].shape[1]), F32)], axis=0),
        enc_spots[...], precision=HIGH, preferred_element_type=F32,
    )
    small[8:, :BUCKETS] = enc_table
    small[8 : 8 + HEADS, PAIR : PAIR + BUCKETS] = self_table

    stream.pump(2)
    own_kv = to_low(enc_sum.result())
    enc_gk[...] = own_kv[:, :INNER]
    enc_gv[...] = own_kv[:, INNER:]
    for low, high in tiles(width):
        part[:, low:high] += kv_back(own_kv, wqk.at[0], wvo.at[0], low, high)
    value, gain_row = norm_back(enc_x[...].astype(F32), gains[0:1], part[...])
    small[0:1] = gain_row
    enc_grad[...] += value
    for place in range(4, 8):
        stream.pump(1)
        choose_next(place)
    stream.drain()
    exchange.finish_whole()
    for sends in owned:
        owners_done(peers, sends)
    peers.finish()


def kc_call(size, block, padded, near, streamed):
    enc_gg, dec_x = near[0], near[6]
    attn_qk, attn_vo, ff_in = streamed[:3]
    rows, width = streamed[4].shape
    dec_rows = dec_x.shape[0]
    units = ff_in.shape[3]
    kv_width = 2 * INNER
    total = 4 * rows
    half = size * padded // 2
    steps = size.bit_length() - 1
    items = len(tiles(units, chunk_of(size)))
    shape = jax.ShapeDtypeStruct
    outs = [
        shape((rows, width), F32), shape((rows, width), LOW), shape((rows, INNER), LOW),
        shape((rows, INNER), LOW), shape((rows, INNER), LOW),
        shape((dec_rows, width), F32), shape((dec_rows, width), LOW),
        shape((dec_rows, INNER), LOW), shape((dec_rows, INNER), LOW),
        shape((dec_rows, INNER), LOW),
        shape((16, width), F32), shape((2, block, units), F32), shape((1, block, units), F32),
        shape((2, half // 2, 2 * total), LOW), shape((4, rows, width), LOW),
        shape((4, rows, INNER), LOW),
    ]
    apart = [
        shape((4, dec_rows, width), LOW),
        shape(enc_gg.shape, LOW), shape(enc_gg.shape, LOW), shape((4, rows, width), LOW),
    ]
    vmem = pl.BlockSpec(memory_space=pltpu.VMEM)
    hbm = pl.BlockSpec(memory_space=pltpu.HBM)
    copies = 3 * 3 + 3 + 3 + 3 * 3 + 3 + 3 * items * (steps - 1)
    return pl.pallas_call(
        functools.partial(kc_kernel, layout=(size, block, padded), steps=steps),
        out_shape=outs + apart,
        in_specs=[vmem] * len(near) + [hbm] * len(streamed),
        out_specs=[vmem] * len(outs) + [hbm] * len(apart),
        scratch_shapes=[
            pltpu.VMEM((2,) + attn_qk.shape[1:], LOW), pltpu.VMEM((2,) + attn_vo.shape[1:], LOW),
            pltpu.VMEM(ff_in.shape[1:], LOW), pltpu.VMEM((HEADS, rows, total), LOW),
            pltpu.VMEM((HEADS, dec_rows, 4 * dec_rows), LOW),
            pltpu.VMEM((rows, width), F32), pltpu.VMEM((3, rows, width), LOW),
            pltpu.VMEM((3, rows, width), LOW),
            pltpu.VMEM((4, rows, kv_width), F32), pltpu.VMEM((3, rows, kv_width), LOW),
            pltpu.VMEM((3, rows, kv_width), LOW),
            pltpu.VMEM((4, dec_rows, kv_width), F32), pltpu.VMEM((3, dec_rows, kv_width), LOW),
            pltpu.VMEM((3, dec_rows, kv_width), LOW), pltpu.VMEM((4, rows, width), LOW),
            pltpu.VMEM((rows, width), F32), pltpu.VMEM((rows, width), F32),
            pltpu.VMEM((rows, width), LOW), pltpu.VMEM((4, rows, kv_width), LOW),
            pltpu.VMEM((HEADS, rows, total), F32), pltpu.VMEM((4, rows, width), LOW),
            *[pltpu.VMEM((2, 4, dec_rows, width), LOW), pltpu.VMEM((2, 4, dec_rows, units), LOW)] * 2,
            pltpu.VMEM((4, rows, units), LOW), pltpu.VMEM((4, rows, units), LOW),
            pltpu.VMEM((2, rows, width), LOW),
            *product_scratch(size, padded, 2 * 4 * dec_rows, 2 * items, 1, chunk_of(size)),
            *product_scratch(size, padded, 2 * total, items, 1, chunk_of(size)),
            pltpu.SemaphoreType.DMA((copies,)), pltpu.SemaphoreType.DMA((copies,)),
            pltpu.SemaphoreType.DMA((2 + 8 + 5 + 3 + 3 + 8,)), pltpu.SemaphoreType.DMA((3,)),
        ],
        compiler_params=pltpu.CompilerParams(
            collective_id=2, has_side_effects=True, vmem_limit_bytes=62 * 1024 * 1024
        ),
        name="last_chain",
    )(*near, *streamed)
class Spread:
    def __init__(self, peers, partners, total, recv):
        self.peers, self.partners, self.total, self.recv = peers, partners, total, recv
        self.steps = len(partners) + 1

    def run(self, step):
        if step:
            self.copy.wait_recv()
            self.total[step] = self.total[step - 1] + self.recv[step - 1]
        if step < len(self.partners):
            self.copy = self.peers.send(
                self.total.at[step], self.recv.at[step], self.partners[step]
            )


def kd_kernel(
    small,
    chosen_h1, enc_gg_all, x_enc_gg_all, enc_gu_all, x_enc_gu_all,
    left_cross_all, right_cross_all, left_self_all, h0, enc_ay,
    enc_gq, enc_gk, enc_gv, enc_o, self_gq, self_gk, self_gv, self_o, dec_gate,
    dec_up,
    ffin, qk, vo, small_out,
    enc_ffin, enc_gg, x_enc_gg, enc_gu, x_enc_gu, chosen_attn, left_enc, left_cross,
    left_self, right_enc, right_cross, right_self, attn_total, attn, small_total, small_recv,
    *rest,
    layout, steps,
):
    size, block, padded = layout
    scratch, rest = rest[: 2 * steps], rest[2 * steps :]
    at_send, at_recv = rest[:steps], rest[steps : 2 * steps]
    send_sem, recv_sem, load_sem, own_sem = rest[2 * steps :]
    peers = Peers(send_sem, recv_sem)
    loads = Loads(load_sem)
    get_gate = [
        loads.start(chosen_h1, scratch[0]), loads.start(enc_gg_all, enc_gg),
        loads.start(x_enc_gg_all, x_enc_gg),
    ]
    get_cross = [
        loads.start(left_cross_all, left_cross), loads.start(right_cross_all, right_cross),
    ]
    get_up = [loads.start(enc_gu_all, enc_gu), loads.start(x_enc_gu_all, x_enc_gu)]
    get_self = [loads.start(left_self_all, left_self)]
    passed = [
        loads.start(dec_gate, ffin.at[1, pl.ds(0, 1)]), loads.start(dec_up, ffin.at[1, pl.ds(1, 1)])
    ]
    partners = [peers.across(place) for place in range(steps)]
    peers.greet([peers.diag] + partners)
    dec_rows, enc_rows = self_gq.shape[0], enc_gq.shape[0]
    own_self = to_owners(
        peers, (self_gq, self_gk, self_gv, self_o), right_self, (dec_rows,) * 4, own_sem.at[0]
    )
    own_enc = to_owners(
        peers, (enc_gq, enc_gk, enc_gv, enc_o), right_enc, (enc_rows,) * 4, own_sem.at[1]
    )
    own_left = to_owners(peers, (h0, h0, h0, enc_ay), left_enc, (enc_rows,) * 4, own_sem.at[3])
    spread = Spread(peers, [peers.sib, peers.far] + partners, small_total, small_recv)
    small_total[0] = small[...]
    spread.run(0)

    products = Products(peers, layout, 1, steps, *scratch)
    products.add(
        None, [(enc_gg, x_enc_gg), (enc_gu, x_enc_gu)], enc_ffin,
        ready=(lambda: wait_all(get_gate), lambda: wait_all(get_up)),
    )

    def wait_self():
        wait_all(get_self)
        owners_done(peers, own_self)

    def wait_enc():
        owners_done(peers, own_enc)
        owners_done(peers, own_left)

    kinds = (
        (2, left_cross, right_cross, lambda: wait_all(get_cross)),
        (1, left_self, right_self, wait_self), (0, left_enc, right_enc, wait_enc),
    )
    attn_items, gathers = [], []
    for a, left, right, arrived in kinds:
        rows = left.shape[0] * left.shape[1]

        def before(left=left, right=right, arrived=arrived):
            arrived()
            if block % 8:
                choose_rows(peers, layout, 0, flat(left[...]), chosen_attn, 0)
                return
            for low, high in tiles(INNER, chunk_of(size)):
                chosen_attn[:, low:high] = dot_first(flat(left[...]), flat(right[:, :, low:high]))

        for place, (low, high) in enumerate(tiles(INNER, chunk_of(size))):

            def product(half, right=right, rows=rows, low=low, high=high):
                if block % 8:
                    return dot(chosen_attn[half, :, :rows], flat(right[:, :, low:high]))
                parts = []
                for place in range(size // 2):
                    owner = half
                    for bit in range(1, steps):
                        owner = owner + (((place >> (steps - 1 - bit)) & 1) << bit)
                    start = pl.multiple_of(owner * block, 8)
                    parts.append(chosen_attn[pl.ds(start, block), low:high])
                    if padded > block:
                        parts.append(jnp.zeros((padded - block, high - low), F32))
                return jnp.concatenate(parts, axis=0)

            def finish(value, a=a, low=low, high=high, last=high == INNER):
                attn[a, peers.own, :, low:high] = to_low(value)
                if last:
                    gathers.append((a, Gather(peers, attn.at[a], False)))
                    gathers[-1][1].start()

            slot = len(attn_items)
            item = Reduce(
                peers, list(range(steps)), product, high - low, attn_total.at[slot], at_send,
                at_recv, slot, finish, products.ships,
            )
            item.before = [before] if place == 0 else []
            attn_items.append(item)

    items = []
    for place in range(max(len(products.items), len(attn_items) + 2)):
        if 2 <= place < len(attn_items) + 2:
            items.append(attn_items[place - 2])
        if place < len(products.items):
            items.append(products.items[place])
    stream = Stream(items, lag_of(steps))
    spreading = []

    def settle(relay, write):
        for entry in spreading:
            a, gather, begun, relayed = entry
            if not relayed and stream.now - begun >= relay:
                gather.wait_near()
                gather.relay()
                entry[3] = True
        for entry in list(spreading):
            a, gather, begun, relayed = entry
            if relayed and stream.now - begun >= write:
                gather.wait_far()
                for place, out in enumerate((qk, qk, vo, vo)):
                    lanes = slice(place % 2 * INNER, (place % 2 + 1) * INNER)
                    out[a, :, lanes] = attn[a, place, :, :].astype(F32)[:block]
                spreading.remove(entry)

    while stream.now <= stream.last:
        stream.pump()
        spreading += [[a, gather, stream.now, False] for a, gather in gathers]
        gathers.clear()
        settle(1, 2)
        if stream.now < 2 * spread.steps:
            if stream.now % 2 == 0:
                spread.run(stream.now // 2)
    for step in range(1, spread.steps):
        if 2 * step > stream.last + 1:
            spread.run(step)
    small_out[...] = small_total[spread.steps - 1]
    left = pltpu.make_async_copy(enc_ffin, ffin.at[0], own_sem.at[2])
    left.start()
    settle(0, 0)
    settle(0, 0)
    left.wait()
    wait_all(passed)
    peers.finish()


def kd_call(size, block, padded, width, small, streamed):
    gate, self_q = streamed[1], streamed[14]
    units, enc_rows, dec_rows = gate.shape[2], gate.shape[1], self_q.shape[0]
    steps = size.bit_length() - 1
    shape = jax.ShapeDtypeStruct
    outs = [
        shape((2, 2, block, units), F32), shape((3, block, 2 * INNER), F32),
        shape((3, block, 2 * INNER), F32), shape(small.shape, F32),
    ]
    vmem = pl.BlockSpec(memory_space=pltpu.VMEM)
    hbm = pl.BlockSpec(memory_space=pltpu.HBM)
    half = size * padded // 2
    ff_items = 2 * len(tiles(units, chunk_of(size)))
    at_items = 3 * len(tiles(INNER, chunk_of(size)))
    at_heights = [half >> step for step in range(steps)]

    def bufs(items, heights):
        return [pltpu.VMEM((items, height, chunk_of(size)), LOW) for height in heights]

    copies = ff_items * (steps - 1) + at_items * steps + 3 * 3 + (2 + steps) + 9
    return pl.pallas_call(
        functools.partial(kd_kernel, layout=(size, block, padded), steps=steps),
        out_shape=outs,
        in_specs=[vmem] + [hbm] * len(streamed),
        out_specs=[hbm] + [vmem] * 3,
        scratch_shapes=[
            pltpu.VMEM((2, block, units), F32),
            *[pltpu.VMEM(gate.shape, LOW)] * 4,
            pltpu.VMEM((2, half, 4 * enc_rows), LOW) if block % 8 else pltpu.VMEM((width, INNER), F32),
            pltpu.VMEM((4, enc_rows, width), LOW), pltpu.VMEM((4, enc_rows, width), LOW),
            pltpu.VMEM((4, dec_rows, width), LOW),
            pltpu.VMEM((4, enc_rows, INNER), LOW), pltpu.VMEM((4, enc_rows, INNER), LOW),
            pltpu.VMEM((4, dec_rows, INNER), LOW),
            pltpu.VMEM((at_items, half, chunk_of(size)), F32),
            pltpu.VMEM((3, 4, padded, INNER), LOW),
            pltpu.VMEM((3 + steps,) + small.shape, F32),
            pltpu.VMEM((2 + steps,) + small.shape, F32),
            *product_scratch(size, padded, 8 * enc_rows, ff_items, 1, chunk_of(size)),
            *bufs(2, at_heights), *bufs(at_items, at_heights),
            pltpu.SemaphoreType.DMA((copies,)), pltpu.SemaphoreType.DMA((copies,)),
            pltpu.SemaphoreType.DMA((10,)), pltpu.SemaphoreType.DMA((4,)),
        ],
        compiler_params=pltpu.CompilerParams(
            collective_id=3, has_side_effects=True, vmem_limit_bytes=62 * 1024 * 1024
        ),
        name="weight_sums",
    )(small, *streamed)


def on_device(
    enc_x, dec_x, dec_cot, item_count, enc_mask, dec_mask, enc_buckets, dec_buckets,
    gains, tables, attn_qk, attn_vo, ff_in, ff_out,
):
    tensor_id = lax.axis_index("tensor")
    size = lax.axis_size("dp")
    enc_own, dec_own = enc_x.shape[0], dec_x.shape[0]
    width = enc_x.shape[1]
    block = width // size
    padded = (block + 15) // 16 * 16
    small, (enc_spots, self_bucket) = prepare(
        item_count, enc_mask, dec_mask, enc_buckets, dec_buckets, tables, enc_own, dec_own
    )
    ff_out_t = jnp.swapaxes(ff_out, 1, 2)
    (
        h0, enc_q, enc_kv, enc_p, enc_o, enc_mid, h1, enc_gelu, enc_slope, enc_hidden, enc_end,
        memory, cross_kv, hs, self_q, self_kv, self_p, self_o, dec_one, hc, cross_q, cross_p,
        cross_o, dec_two, hf, dec_gy, dec_gg, dec_gu, dec_hidden, dec_x, dec_cot,
        x_h1_rows, x_enc_hidden,
    ) = ka_call(enc_x, dec_x, dec_cot, gains, *small, attn_qk, attn_vo, ff_in, ff_out_t)
    (
        dec_out, cross_gy, cross_gq, cross_gk, cross_gv, dec_one_grad, enc_end_grad, enc_gy,
        enc_gg, enc_gu, gains_mid, dec_gate, x_dec_hidden, x_dec_gy, x_dec_gu, x_hf,
    ) = kb_call(
        dec_gg, dec_gu, dec_hidden, dec_cot, dec_two, dec_one, gains, cross_q, cross_kv, cross_p,
        enc_end, enc_gelu, enc_slope, attn_qk, attn_vo, ff_in, ff_out_t, hf, dec_gy,
        size, block, padded,
    )
    (
        enc_grad, enc_ay, enc_gq, enc_gk, enc_gv, dec_grad, self_gy, self_gq, self_gk, self_gv,
        sums, ffout_sum, dec_up, chosen_h1, left_cross, right_cross, left_self, x_enc_gg,
        x_enc_gu, unused,
    ) = kc_call(
        size, block, padded,
        [
            enc_gg, enc_gu, gains, gains_mid, enc_q, dec_one_grad, dec_x, self_q, self_kv, self_p,
            enc_spots, self_bucket,
        ],
        [
            attn_qk, attn_vo, ff_in, enc_end_grad, enc_mid, enc_x, enc_kv, enc_p, enc_gy, hf, x_hf,
            dec_gu, x_dec_gu, dec_gy, x_dec_gy, dec_hidden, x_dec_hidden, enc_hidden, x_enc_hidden, h1, x_h1_rows, hs, hc, memory, cross_gy, cross_gq,
            cross_gk, cross_gv, cross_o,
        ],
    )
    ffin_sum, qk_sum, vo_sum, sums = kd_call(
        size, block, padded, width, sums,
        [
            chosen_h1, enc_gg, x_enc_gg, enc_gu, x_enc_gu, left_cross, right_cross,
            left_self, h0, enc_ay, enc_gq, enc_gk, enc_gv, enc_o, self_gq, self_gk, self_gv, self_o,
            dec_gate, dec_up,
        ],
    )
    ffout_sum = jnp.swapaxes(ffout_sum, 1, 2)
    table_rows = sums[8 : 8 + HEADS]
    tables_sum = jnp.stack(
        [table_rows[:, :BUCKETS].T, table_rows[:, PAIR : PAIR + BUCKETS].T]
    )
    return (
        dec_out[:dec_own], enc_grad, dec_grad[:dec_own], sums[:6], tables_sum, qk_sum, vo_sum,
        ffin_sum, ffout_sum,
    )


def solution(mesh):
    rows = P(("dp", "tensor"), None)
    return jax.shard_map(
        on_device,
        mesh=mesh,
        in_specs=(
            rows, rows, rows, P("dp"), P("dp"), P("dp"), P(), P(), P(), P(), P(), P(),
            P(None, None, None, "tensor"), P(None, "tensor", None),
        ),
        out_specs=(
            rows, rows, rows, P(), P(), P(None, "dp", None), P(None, "dp", None),
            P(None, None, "dp", "tensor"), P(None, "tensor", "dp"),
        ),
        check_vma=False,
    )
```

```python
import functools

import jax
import jax.numpy as jnp
from jax import lax
from jax.experimental import pallas as pl
from jax.experimental.pallas import tpu as pltpu
from jax.sharding import PartitionSpec as P

HEADS = 6
HEAD = 64
INNER = HEADS * HEAD
PAIRS = HEADS // 2
PAIR = 2 * HEAD
BUCKETS = 32
EPSILON = 1e-06
MASKED = -1000000000.0
HIGH = lax.Precision.HIGHEST
F32 = jnp.float32
LOW = jnp.bfloat16
DEC_PAD = 32
VMEM_BYTES = 60 * 1024 * 1024
ROOT = 0.7978845608028654
CUBE = 0.044715


def to_low(value):
    return value.astype(LOW)


def dot(left, right):
    return jnp.dot(left, right, preferred_element_type=F32)


def dot_first(left, right):
    return lax.dot_general(left, right, (((0,), (0,)), ((), ())), preferred_element_type=F32)


def dot_last(left, right):
    return lax.dot_general(left, right, (((1,), (1,)), ((), ())), preferred_element_type=F32)


def norm_gain(rows, gain):
    return rows * lax.rsqrt(jnp.mean(rows * rows, axis=-1, keepdims=True) + EPSILON) * gain


def norm_back(rows, gain, grad_rows):
    scale = lax.rsqrt(jnp.mean(rows * rows, axis=-1, keepdims=True) + EPSILON)
    normed = rows * scale
    scaled = grad_rows * gain
    inner = jnp.mean(scaled * normed, axis=-1, keepdims=True)
    grad_gain = jnp.sum(grad_rows * normed, axis=0, keepdims=True)
    return scale * (scaled - normed * inner), grad_gain


def act_parts(gate, up_proj):
    square = gate * gate
    curve = jnp.tanh(ROOT * gate * (1.0 + CUBE * square))
    half = 0.5 * (1.0 + curve)
    slope = half + 0.5 * gate * (1.0 - curve * curve) * (ROOT * (1.0 + 3.0 * CUBE * square))
    return gate * half, up_proj * slope


def tiles(width, step=256):
    return [(start, min(start + step, width)) for start in range(0, width, step)]


class Peers:
    def __init__(self, send_sem, recv_sem):
        dp, tensor = lax.axis_index("dp"), lax.axis_index("tensor")
        chip, core = lax.div(tensor, 2), lax.rem(tensor, 2)
        self.dp = dp
        self.own = tensor
        self.sib = chip * 2 + (1 - core)
        self.far = (1 - chip) * 2 + core
        self.diag = (1 - chip) * 2 + (1 - core)
        self.send_sem, self.recv_sem = send_sem, recv_sem
        self.used = 0
        self.copies = []

    def bit(self, place):
        return lax.rem(lax.div(self.dp, 2**place), 2)

    def across(self, place):
        return (self.dp + (1 - 2 * self.bit(place)) * 2**place, self.own)

    def device(self, peer):
        return peer if isinstance(peer, tuple) else (self.dp, peer)

    def greet(self, more=()):
        barrier = pltpu.get_barrier_semaphore()
        for peer in (self.sib, self.far) + tuple(more):
            pl.semaphore_signal(
                barrier, inc=1, device_id=self.device(peer), device_id_type=pl.DeviceIdType.MESH
            )
        pl.semaphore_wait(barrier, 2 + len(more))

    def send(self, source, target, peer):
        place = self.used
        self.used += 1
        assert place < self.send_sem.shape[0]
        copy = pltpu.make_async_remote_copy(
            src_ref=source,
            dst_ref=target,
            send_sem=self.send_sem.at[place],
            recv_sem=self.recv_sem.at[place],
            device_id=self.device(peer),
            device_id_type=pl.DeviceIdType.MESH,
        )
        copy.start()
        self.copies.append(copy)
        return copy

    def finish(self):
        for copy in self.copies:
            copy.wait_send()


class Gather:
    def __init__(self, peers, buf, near, source=None):
        self.peers, self.buf, self.source = peers, buf, source
        if near:
            self.slots = (0, 1, 2, 2, 3)
        else:
            self.slots = (peers.own, peers.own, peers.own, peers.far, peers.far)

    def start(self):
        own, at_sib, at_far, unused, unused = self.slots
        source = self.buf.at[own] if self.source is None else self.source
        self.to_far = self.peers.send(source, self.buf.at[at_far], self.peers.far)
        self.to_sib = self.peers.send(source, self.buf.at[at_sib], self.peers.sib)

    def wait_near(self):
        self.to_sib.wait_recv()

    def relay(self):
        unused, unused, unused, far, far_at_sib = self.slots
        self.to_far.wait_recv()
        self.relayed = self.peers.send(
            self.buf.at[far], self.buf.at[far_at_sib], self.peers.sib
        )

    def wait_far(self):
        self.relayed.wait_recv()


def attend(queries, kv, bias_of, allowed, weights_out, mixed_out):
    rows = queries.shape[0]
    total = kv.shape[0] * kv.shape[1]
    first = lax.broadcasted_iota(jnp.int32, (rows, PAIR), 1) < HEAD
    for pair in range(PAIRS):
        lanes = slice(pair * PAIR, (pair + 1) * PAIR)
        keys = kv[:, :, lanes].reshape(total, PAIR)
        values = kv[:, :, INNER + pair * PAIR : INNER + (pair + 1) * PAIR].reshape(total, PAIR)
        both = queries[:, lanes].astype(F32)
        mixed = []
        for half in range(2):
            head = 2 * pair + half
            here = to_low(jnp.where(first if half == 0 else ~first, both, 0.0))
            scores = dot_last(here, keys)
            if bias_of is not None:
                scores = scores + bias_of(head)
            scores = jnp.where(allowed, scores, MASKED)
            shifted = jnp.exp(scores - jnp.max(scores, axis=-1, keepdims=True))
            weights = shifted / jnp.sum(shifted, axis=-1, keepdims=True)
            weights_out[head] = weights
            mixed.append(dot(to_low(weights), values))
        mixed_out[:, lanes] = to_low(jnp.where(first, mixed[0], mixed[1]))


def attend_back(queries, kv, weights_in, grad_out, grad_q_out, grad_kv_out, grad_s_out):
    rows = queries.shape[0]
    total = kv.shape[0] * kv.shape[1]
    block = kv.shape[1]
    first = lax.broadcasted_iota(jnp.int32, (rows, PAIR), 1) < HEAD
    first_key = lax.broadcasted_iota(jnp.int32, (total, PAIR), 1) < HEAD
    for pair in range(PAIRS):
        lanes = slice(pair * PAIR, (pair + 1) * PAIR)
        value_lanes = slice(INNER + pair * PAIR, INNER + (pair + 1) * PAIR)
        keys = kv[:, :, lanes].reshape(total, PAIR)
        values = kv[:, :, value_lanes].reshape(total, PAIR)
        query = queries[:, lanes]
        grad = grad_out[:, lanes]
        grad_wide = grad.astype(F32)
        grad_q, grad_k, grad_v = [], [], []
        for half in range(2):
            head = 2 * pair + half
            here = to_low(jnp.where(first if half == 0 else ~first, grad_wide, 0.0))
            weights = weights_in[head]
            grad_weights = dot_last(here, values)
            weighted = jnp.sum(weights * grad_weights, axis=-1, keepdims=True)
            grad_scores = to_low(weights * (grad_weights - weighted))
            if grad_s_out is not None:
                grad_s_out[head] = grad_scores
            grad_q.append(dot(grad_scores, keys))
            grad_k.append(dot_first(grad_scores, query))
            grad_v.append(dot_first(to_low(weights), grad))
        grad_q_out[:, lanes] = to_low(jnp.where(first, grad_q[0], grad_q[1]))
        grad_kv_out[:, :, lanes] = jnp.where(first_key, grad_k[0], grad_k[1]).reshape(
            4, block, PAIR
        )
        grad_kv_out[:, :, value_lanes] = jnp.where(first_key, grad_v[0], grad_v[1]).reshape(
            4, block, PAIR
        )


class Exchange:
    def __init__(self, peers, whole, rows, place=0):
        partner = peers.across(place)
        self.rows = [
            (peers.send(own.at[0], other.at[0], partner), Gather(peers, other, True))
            for own, other in rows
        ]
        self.whole = [peers.send(own, other, partner) for own, other in whole]

    def spread(self):
        for copy, gather in self.rows:
            copy.wait_recv()
            gather.start()

    def relay(self):
        for unused, gather in self.rows:
            gather.wait_near()
            gather.relay()

    def finish_rows(self):
        for unused, gather in self.rows:
            gather.wait_far()

    def finish_first(self):
        self.whole.pop(0).wait_recv()

    def finish_whole(self):
        for copy in self.whole:
            copy.wait_recv()
        self.whole = []


class Loads:
    def __init__(self, sems):
        self.sems, self.used = sems, 0

    def start(self, source, target):
        copy = pltpu.make_async_copy(source, target, self.sems.at[self.used])
        self.used += 1
        copy.start()
        return copy


def wait_all(copies):
    for copy in copies:
        copy.wait()
    copies.clear()


def project_kv(rows, wqk, wvo, target):
    target[:, :INNER] = to_low(dot(rows, wqk[:, INNER:]))
    target[:, INNER:] = to_low(dot(rows, wvo[:, :INNER]))


def ff_up(rows, w_in, gelu_out, slope_out, hidden_out, slots):
    count, block = slots.stop - slots.start, gelu_out.shape[1]
    for low, high in tiles(gelu_out.shape[2]):
        gate = dot(rows, w_in[0, :, low:high])
        up_proj = dot(rows, w_in[1, :, low:high])
        gelu, slope = act_parts(gate, up_proj)
        shape = (count, block, high - low)
        gelu_out[slots, :, low:high] = gelu.reshape(shape)
        slope_out[slots, :, low:high] = slope.reshape(shape)
        hidden_out[slots, :, low:high] = to_low(gelu * up_proj).reshape(shape)


def reduce_far(peers, diag_part, far_part, send, recv):
    width = send.shape[2]
    for low, high in tiles(width):
        send[0, :, low:high] = to_low(diag_part(low, high))
    first = peers.send(send.at[0], recv.at[0], peers.sib)
    first.wait_recv()
    for low, high in tiles(width):
        send[2, :, low:high] = to_low(
            far_part(low, high) + recv[0, :, low:high].astype(F32)
        )
    return peers.send(send.at[2], recv.at[2], peers.far)


def ka_kernel(
    enc_x, dec_x_short, dec_cot_short, gains, enc_terms, self_bias, item_count, enc_mask, dec_mask,
    qk_all, vo_all, fi_all, fo_all,
    h0, enc_q, enc_kv_out, enc_p_out, enc_o, enc_mid_out, h1_out, enc_gelu_out, enc_slope_out,
    enc_hidden_out, enc_end_out, memory, cross_kv_out, hs, self_q, self_kv, self_p, self_o,
    dec_one, hc, cross_q, cross_p, cross_o, dec_two, hf, dec_gy, dec_gg, dec_gu, dec_hidden,
    dec_x, dec_cot, x_h1, x_enc_hidden,
    wqk, wvo, wfi, wfo, part, send, recv, dec_gelu, dec_slope, dec_gh,
    enc_kv, enc_p, enc_mid, h1, enc_gelu, enc_slope, enc_hidden, enc_end, cross_kv,
    send_sem, recv_sem, load_sem, store_sem,
):
    peers = Peers(send_sem, recv_sem)
    loads, stores, stored = Loads(load_sem), Loads(store_sem), []
    get_qk, get_vo, get_fi, get_fo = {}, {}, {}, {}
    for a in (0, 1):
        get_qk[a] = loads.start(qk_all.at[a], wqk.at[a])
        get_vo[a] = loads.start(vo_all.at[a], wvo.at[a])
    get_fi[0] = loads.start(fi_all.at[0], wfi.at[0])
    get_fo[0] = loads.start(fo_all.at[0], wfo.at[0])
    get_qk[2] = loads.start(qk_all.at[2], wqk.at[2])
    get_vo[2] = loads.start(vo_all.at[2], wvo.at[2])
    get_fi[1] = loads.start(fi_all.at[1], wfi.at[1])
    get_fo[1] = loads.start(fo_all.at[1], wfo.at[1])
    peers.greet([peers.across(0)])

    enc_rows, dec_rows, real_rows = enc_x.shape[0], dec_x.shape[0], dec_x_short.shape[0]
    enc_total, dec_total = 4 * enc_rows, 4 * real_rows

    def item_of(place, total):
        scaled = place * item_count[...]
        return sum((scaled >= part * total).astype(jnp.int32) for part in (1, 2, 3))

    def counted(rows, columns, axis):
        return lax.broadcasted_iota(jnp.int32, (rows, columns), axis)

    enc_code = jnp.where(enc_mask[...] == 1, item_of(counted(1, enc_total, 1), enc_total), -1)
    enc_item = item_of(counted(enc_rows, 1, 0) + peers.own * enc_rows, enc_total)
    slot = counted(1, 4 * dec_rows, 1)
    inside = lax.rem(slot, dec_rows)
    key_place = lax.div(slot, dec_rows) * real_rows + inside
    key_item = jnp.where(
        (inside < real_rows) & (dec_mask[...] == 1), item_of(key_place, dec_total), -1
    )
    row = counted(dec_rows, 1, 0)
    row_place = row + peers.own * real_rows
    dec_item = jnp.where(row < real_rows, item_of(row_place, dec_total), -2)
    self_allowed = (dec_item == key_item) & (key_place <= row_place)

    fill = jnp.zeros((dec_rows - real_rows, dec_x.shape[1]), F32)
    for short, padded in ((dec_x_short, dec_x), (dec_cot_short, dec_cot)):
        padded[...] = to_low(jnp.concatenate([short[...].astype(F32), fill], axis=0))

    normed = to_low(norm_gain(enc_x[...].astype(F32), gains[0:1]))
    h0[...] = normed
    get_qk[0].wait()
    get_vo[0].wait()
    project_kv(normed, wqk.at[0], wvo.at[0], enc_kv.at[peers.own])
    enc_gather = Gather(peers, enc_kv, False)
    enc_gather.start()
    normed_dec = to_low(norm_gain(dec_x[...].astype(F32), gains[3:4]))
    hs[...] = normed_dec
    get_qk[1].wait()
    get_vo[1].wait()
    project_kv(normed_dec, wqk.at[1], wvo.at[1], self_kv.at[peers.own])
    self_gather = Gather(peers, self_kv, False)
    self_gather.start()
    dec_gy[0] = dec_cot[...]
    gy_gather = Gather(peers, dec_gy, True)
    gy_gather.start()
    enc_q[...] = to_low(dot(normed, wqk[0, :, :INNER]))
    self_q[...] = to_low(dot(normed_dec, wqk[1, :, :INNER]))

    enc_gather.wait_near()
    enc_gather.relay()
    enc_allowed = enc_item == enc_code

    def enc_bias(head):
        own_rows, period = h0.shape[0], enc_terms.shape[1]
        spread = jnp.broadcast_to(enc_terms[head : head + 1, :], (own_rows, period))
        rolled = pltpu.roll(spread, 0, 1, stride=1, stride_axis=0)
        return rolled[:, : period // 2]

    enc_gather.wait_far()
    attend(enc_q[...], enc_kv, enc_bias, enc_allowed, enc_p, enc_o)
    stored += [stores.start(enc_kv, enc_kv_out), stores.start(enc_p, enc_p_out)]
    for low, high in tiles(enc_mid.shape[1]):
        enc_mid[:, low:high] = enc_x[:, low:high].astype(F32) + dot_last(
            enc_o[...], wvo[0, low:high, INNER:]
        )
    h1[0] = to_low(norm_gain(enc_mid[...], gains[1:2]))
    h1_gather = Gather(peers, h1, True)
    h1_gather.start()
    exchanges = [Exchange(peers, [(h1.at[0], x_h1)], [])]

    def hidden_part(low, high):
        return [(enc_hidden.at[slot], x_enc_hidden.at[slot]) for slot in range(low, high)]

    self_gather.wait_near()
    self_gather.relay()
    gy_gather.wait_near()
    gy_gather.relay()
    self_gather.wait_far()
    gy_gather.wait_far()
    attend(
        self_q[...], self_kv, lambda head: self_bias[head], self_allowed, self_p, self_o
    )
    for low, high in tiles(dec_one.shape[1]):
        dec_one[:, low:high] = dec_x[:, low:high].astype(F32) + dot_last(
            self_o[...], wvo[1, low:high, INNER:]
        )
    normed_dec = to_low(norm_gain(dec_one[...], gains[4:5]))
    hc[...] = normed_dec

    h1_gather.wait_near()
    get_fi[0].wait()
    get_fo[0].wait()
    block, width = h1.shape[1], h1.shape[2]

    def both(buf, slots):
        return buf[slots].reshape((slots.stop - slots.start) * block, buf.shape[2])

    near, away = slice(0, 2), slice(2, 4)
    ff_up(both(h1, near), wfi.at[0], enc_gelu, enc_slope, enc_hidden, near)
    exchanges.append(Exchange(peers, hidden_part(0, 2), []))
    h1_gather.relay()
    h1_gather.wait_far()
    ff_up(both(h1, away), wfi.at[0], enc_gelu, enc_slope, enc_hidden, away)
    stored += [
        stores.start(h1, h1_out), stores.start(enc_gelu, enc_gelu_out),
        stores.start(enc_slope, enc_slope_out), stores.start(enc_hidden, enc_hidden_out),
        stores.start(enc_mid, enc_mid_out),
    ]
    hidden = both(enc_hidden, away)
    for low, high in tiles(width):
        value = dot_last(hidden, wfo[0, low:high, :])
        part[:, low:high] = value[:block]
        send[0, :, low:high] = to_low(value[block:])
    first = peers.send(send.at[0], recv.at[0], peers.sib)
    exchanges.append(Exchange(peers, hidden_part(2, 4), []))
    get_qk[2].wait()
    get_vo[2].wait()
    cross_q[...] = to_low(dot(hc[...], wqk[2, :, :INNER]))
    first.wait_recv()
    send[2] = to_low(part[...] + recv[0].astype(F32))
    second = peers.send(send.at[2], recv.at[2], peers.far)
    hidden = both(enc_hidden, near)
    for low, high in tiles(width):
        value = dot_last(hidden, wfo[0, low:high, :])
        part[:, low:high] = value[:block] + enc_mid[:, low:high]
        send[1, :, low:high] = to_low(value[block:])
    third = peers.send(send.at[1], recv.at[1], peers.sib)
    get_fi[1].wait()
    get_fo[1].wait()
    grad_y = dec_gy[...].reshape(4 * dec_rows, width)
    for low, high in tiles(dec_gh.shape[2]):
        dec_gh[:, :, low:high] = dot(grad_y, wfo[1, :, low:high]).reshape(4, dec_rows, high - low)
    third.wait_recv()
    part[...] = part[...] + recv[1].astype(F32)
    second.wait_recv()
    ended = part[...] + recv[2].astype(F32)
    enc_end[...] = ended
    stored.append(stores.start(enc_end, enc_end_out))
    normed = to_low(norm_gain(ended, gains[2:3]))
    memory[...] = normed

    project_kv(normed, wqk.at[2], wvo.at[2], cross_kv.at[peers.own])
    cross_gather = Gather(peers, cross_kv, False)
    cross_gather.start()
    cross_allowed = dec_item == enc_code
    cross_gather.wait_near()
    cross_gather.relay()
    cross_gather.wait_far()
    attend(cross_q[...], cross_kv, None, cross_allowed, cross_p, cross_o)
    stored.append(stores.start(cross_kv, cross_kv_out))
    for low, high in tiles(dec_two.shape[1]):
        dec_two[:, low:high] = dec_one[:, low:high] + dot_last(
            cross_o[...], wvo[2, low:high, INNER:]
        )
    hf[0] = to_low(norm_gain(dec_two[...], gains[5:6]))
    hf_gather = Gather(peers, hf, True)
    hf_gather.start()

    rows = hf.shape[0] * hf.shape[1]
    hf_gather.wait_near()
    hf_gather.relay()
    hf_gather.wait_far()
    ff_up(hf[...].reshape(rows, width), wfi.at[1], dec_gelu, dec_slope, dec_hidden, slice(0, 4))
    dec_gg[...] = to_low(dec_gh[...] * dec_slope[...])
    dec_gu[...] = to_low(dec_gh[...] * dec_gelu[...])
    for exchange in exchanges:
        exchange.finish_whole()
    wait_all(stored)
    peers.finish()


def ka_call(enc_x, dec_x, dec_cot, gains, enc_terms, self_bias, item_count, enc_mask, dec_mask, attn_qk, attn_vo, ff_in, ff_out):
    rows, width = enc_x.shape
    dec_rows = DEC_PAD
    units = ff_in.shape[3]
    total = enc_mask.shape[1]
    kv_width = 2 * INNER
    shape = jax.ShapeDtypeStruct
    outs = [
        shape((rows, width), LOW), shape((rows, INNER), LOW), shape((4, rows, kv_width), LOW),
        shape((HEADS, rows, total), F32), shape((rows, INNER), LOW), shape((rows, width), F32),
        shape((4, rows, width), LOW), shape((4, rows, units), F32), shape((4, rows, units), F32),
        shape((4, rows, units), LOW), shape((rows, width), F32), shape((rows, width), LOW),
        shape((4, rows, kv_width), LOW),
        shape((dec_rows, width), LOW), shape((dec_rows, INNER), LOW),
        shape((4, dec_rows, kv_width), LOW), shape((HEADS, dec_rows, 4 * dec_rows), F32),
        shape((dec_rows, INNER), LOW), shape((dec_rows, width), F32),
        shape((dec_rows, width), LOW), shape((dec_rows, INNER), LOW),
        shape((HEADS, dec_rows, total), F32), shape((dec_rows, INNER), LOW),
        shape((dec_rows, width), F32),
        shape((4, dec_rows, width), LOW), shape((4, dec_rows, width), LOW),
        shape((4, dec_rows, units), LOW), shape((4, dec_rows, units), LOW),
        shape((4, dec_rows, units), LOW), shape((dec_rows, width), LOW),
        shape((dec_rows, width), LOW),
    ]
    traded = [shape((rows, width), LOW), shape((4, rows, units), LOW)]
    vmem = pl.BlockSpec(memory_space=pltpu.VMEM)
    hbm = pl.BlockSpec(memory_space=pltpu.HBM)
    copies = 3 * 6 + 3 + 1 + 4
    apart = (2, 3, 5, 6, 7, 8, 9, 10, 12)
    return pl.pallas_call(
        ka_kernel,
        out_shape=outs + traded,
        in_specs=[vmem] * 9 + [hbm] * 4,
        out_specs=[hbm if place in apart else vmem for place in range(len(outs))]
        + [hbm] * len(traded),
        scratch_shapes=[
            pltpu.VMEM(attn_qk.shape, LOW), pltpu.VMEM(attn_vo.shape, LOW),
            pltpu.VMEM(ff_in.shape, LOW), pltpu.VMEM(ff_out.shape, LOW),
            pltpu.VMEM((rows, width), F32), pltpu.VMEM((3, rows, width), LOW),
            pltpu.VMEM((3, rows, width), LOW), pltpu.VMEM((4, dec_rows, units), F32),
            pltpu.VMEM((4, dec_rows, units), F32), pltpu.VMEM((4, dec_rows, units), F32),
            *[pltpu.VMEM(outs[place].shape, outs[place].dtype) for place in apart],
            pltpu.SemaphoreType.DMA((copies,)), pltpu.SemaphoreType.DMA((copies,)),
            pltpu.SemaphoreType.DMA((10,)), pltpu.SemaphoreType.DMA((len(apart),)),
        ],
        compiler_params=pltpu.CompilerParams(
            collective_id=0, has_side_effects=True, vmem_limit_bytes=VMEM_BYTES
        ),
        name="forward_chain",
    )(enc_x, dec_x, dec_cot, gains, enc_terms, self_bias, item_count, enc_mask, dec_mask,
      attn_qk, attn_vo, ff_in, ff_out)


def prepare(item_count, enc_mask, dec_mask, enc_buckets, dec_buckets, tables, enc_own, dec_own):
    tensor_id = lax.axis_index("tensor")
    enc_total, dec_total = enc_mask.shape[0], dec_mask.shape[0]
    slot = jnp.arange(4 * DEC_PAD)
    place = slot // DEC_PAD * dec_own + slot % DEC_PAD
    row_place = tensor_id * dec_own + jnp.arange(DEC_PAD)
    dec_live = jnp.pad(dec_mask.reshape(4, dec_own), ((0, 0), (0, DEC_PAD - dec_own)))
    onehot = (enc_buckets[:, None] == jnp.arange(BUCKETS)[None, :]).astype(F32)
    terms = jnp.dot(tables[0].T, onehot.T, precision=HIGH)
    terms = jnp.pad(terms, ((0, 2), (0, 1)))
    period = 2 * enc_total
    doubled = jnp.concatenate([terms, terms], axis=1)
    shift = (enc_total - 1 - tensor_id * enc_own + period) % period
    enc_terms = lax.dynamic_slice_in_dim(doubled, shift, period, 1)
    far_back = jnp.clip(row_place[:, None] - place[None, :], 0, dec_total - 1)
    far_back = (far_back[None] == jnp.arange(dec_total)[:, None, None]).astype(F32)
    far_back = far_back.reshape(dec_total, -1)
    dec_onehot = (dec_buckets[:, None] == jnp.arange(BUCKETS)[None, :]).astype(F32)
    dec_terms = jnp.dot(tables[1].T, dec_onehot.T, precision=HIGH)
    self_bias = jnp.dot(dec_terms, far_back, precision=HIGH).reshape(
        HEADS, DEC_PAD, 4 * DEC_PAD
    )
    spots = jnp.pad(onehot, ((0, 1), (0, 0)))
    enc_spots = lax.dynamic_slice_in_dim(
        spots, enc_total - enc_own - tensor_id * enc_own, enc_total + enc_own, 0
    )
    self_bucket = jnp.dot(
        dec_buckets.astype(F32)[None, :], far_back, precision=HIGH
    ).reshape(DEC_PAD, 4 * DEC_PAD)
    return (
        enc_terms, self_bias, item_count.reshape(1, 1), enc_mask.reshape(1, enc_total),
        dec_live.reshape(1, 4 * DEC_PAD),
    ), (enc_spots, self_bucket)


RING = 4


def chunk_of(size):
    return 512 if size <= 8 else 256


def lag_of(steps):
    return 2 if steps <= 3 else 1


class Reduce:
    def __init__(self, peers, places, product, columns, total, send, recv, slot, finish, ships):
        self.ships = ships
        self.peers, self.places, self.product, self.columns = peers, places, product, columns
        self.total, self.send, self.recv, self.slot, self.done = total, send, recv, slot, finish
        self.steps = len(places) + 1

    def buffers(self, step):
        lanes = pl.ds(0, self.columns)
        return (
            self.send[step].at[self.slot % self.send[step].shape[0], :, lanes],
            self.recv[step].at[self.slot, :, lanes],
        )

    def ship(self, step, value, place):
        source, target = self.buffers(step)
        key = (id(self.send), step, self.slot % self.send[step].shape[0])
        if key in self.ships:
            self.ships[key].wait_send()
            self.peers.copies = [c for c in self.peers.copies if c is not self.ships[key]]
        source[...] = to_low(value)
        self.copy = self.peers.send(source, target, self.peers.across(place))
        self.ships[key] = self.copy

    def run(self, step):
        lanes = pl.ds(0, self.columns)
        if step == 0:
            here = self.peers.bit(self.places[0])
            self.ship(0, self.product(1 - here), self.places[0])
            self.height = self.send[0].shape[1]
            self.start = 0
            self.total[: self.height, lanes] = self.product(here)
            return
        self.copy.wait_recv()
        arrived = self.buffers(step - 1)[1]
        if step == self.steps - 1:
            rows = pl.ds(self.start, self.height)
            self.done(self.total[rows, lanes] + arrived[...].astype(F32))
            return
        self.height //= 2
        place = self.places[step]
        here = self.peers.bit(place)
        away = pl.multiple_of(self.start + (1 - here) * self.height, 16)
        kept = pl.multiple_of(self.start + here * self.height, 16)
        from_away = pl.multiple_of((1 - here) * self.height, 16)
        from_kept = pl.multiple_of(here * self.height, 16)
        self.ship(
            step,
            self.total[pl.ds(away, self.height), lanes]
            + arrived[pl.ds(from_away, self.height), :].astype(F32),
            place,
        )
        self.total[pl.ds(kept, self.height), lanes] += arrived[
            pl.ds(from_kept, self.height), :
        ].astype(F32)
        self.start = kept


class Stream:
    def __init__(self, items, lag):
        self.items, self.lag, self.now = items, lag, 0
        self.last = max(place + lag * (item.steps - 1) for place, item in enumerate(items))

    def pump(self, ticks=1):
        for unused in range(ticks):
            now = self.now
            if now > self.last:
                return
            self.now += 1
            for place, item in reversed(list(enumerate(self.items))):
                step, odd = divmod(now - place, self.lag)
                if odd == 0 and 0 < step < item.steps:
                    item.run(step)
            if now < len(self.items):
                for action in self.items[now].before:
                    if action is not None:
                        action()
                self.items[now].run(0)

    def drain(self):
        self.pump(self.last + 1 - self.now)


def flat(value):
    return value.reshape(value.shape[0] * value.shape[1], value.shape[2])


def choose_rows(peers, layout, first, rows, chosen, start):
    size, block, padded = layout
    bits = size.bit_length() - 1
    width = rows.shape[1]
    for known in range(2**first):

        def run(known=known):
            for half in range(2):
                for place in range(chosen.shape[1] // padded):
                    owner = known + (half << first)
                    for bit in range(first + 1, bits):
                        owner += ((place >> (bits - 1 - bit)) & 1) << bit
                    left = owner * block // 128 * 128
                    right = min(-(-(owner + 1) * block // 128) * 128, width)
                    inside = lax.broadcasted_iota(jnp.int32, (padded, right - left), 0)
                    lane = lax.broadcasted_iota(jnp.int32, (padded, right - left), 1)
                    picked = (lane - inside == owner * block - left) & (inside < block)
                    pick = to_low(jnp.where(picked, 1.0, 0.0))
                    for low, high in tiles(rows.shape[0]):
                        chosen[
                            half, place * padded : (place + 1) * padded,
                            start + low : start + high,
                        ] = to_low(dot_last(pick, rows[low:high, left:right]))

        if first:
            same = peers.bit(0) == known % 2
            for bit in range(1, first):
                same = same & (peers.bit(bit) == (known >> bit) % 2)
            pl.when(same)(run)
        else:
            run()


class Products:
    def __init__(self, peers, layout, first, steps, chosen, total, *buffers):
        self.peers, self.layout, self.first = peers, layout, first
        self.chosen, self.total = chosen, total
        self.places = list(range(first, steps))
        self.send, self.recv = buffers[: steps - first], buffers[steps - first :]
        self.items, self.ships = [], {}

    def choose(self, lefts, before):
        def run():
            if before is not None:
                before()
            rows = lefts[0].shape[0] * lefts[0].shape[1]
            for part, left in enumerate(lefts):
                choose_rows(
                    self.peers, self.layout, self.first, flat(left[...]), self.chosen, part * rows
                )

        return run

    def add(self, lefts, rights, out, before=None, ready=()):
        actions = [] if lefts is None else [self.choose(lefts, before)]
        for kind, parts in enumerate(rights):
            rows = parts[0].shape[0] * parts[0].shape[1]
            if ready:
                actions.append(ready[kind])
            for low, high in tiles(parts[0].shape[2], self.total.shape[2]):

                def product(half, parts=parts, low=low, high=high):
                    value = None
                    for part, right in enumerate(parts):
                        here = dot(
                            self.chosen[half, :, part * rows : (part + 1) * rows],
                            flat(right[:, :, low:high]),
                        )
                        value = here if value is None else value + here
                    return value

                def finish(value, kind=kind, low=low, high=high):
                    out[kind, :, low:high] = value[: out.shape[1]]

                count = len(self.items)
                item = Reduce(
                    self.peers, self.places, product, high - low,
                    self.total.at[count % self.total.shape[0]], self.send, self.recv, count,
                    finish, self.ships,
                )
                item.before, actions = actions, []
                self.items.append(item)


def product_scratch(size, padded, rows, items, first, chunk):
    chosen = size * padded >> first
    steps = size.bit_length() - 1
    heights = [chosen >> (step + 1) for step in range(steps - first)]
    return [
        pltpu.VMEM((2, chosen // 2, rows), LOW),
        pltpu.VMEM((lag_of(steps) * (steps - first) + 1, chosen // 2, chunk), F32),
        *[pltpu.VMEM((RING, height, chunk), LOW) for height in heights],
        *[pltpu.VMEM((items, height, chunk), LOW) for height in heights],
    ]


def to_owners(peers, sources, target, rows_of, own_sem):
    sends = []
    for peer in (peers.far, peers.diag, peers.sib):
        place = peers.used
        peers.used += 1
        for role in range(4):
            rows = rows_of[role]

            def copy(role=role, rows=rows, place=place, peer=peer):
                return pltpu.make_async_remote_copy(
                    src_ref=sources[role],
                    dst_ref=target.at[peers.own, pl.ds(0, rows)],
                    send_sem=peers.send_sem.at[place],
                    recv_sem=peers.recv_sem.at[place],
                    device_id=peers.device(peer),
                    device_id_type=pl.DeviceIdType.MESH,
                )

            @pl.when(peer == role)
            def _(copy=copy):
                copy().start()

            sends.append((peer, role, copy))
    for role in range(4):

        def keep(role=role):
            return pltpu.make_async_copy(
                sources[role], target.at[peers.own, pl.ds(0, rows_of[role])], own_sem
            )

        @pl.when(peers.own == role)
        def _(keep=keep):
            keep().start()

        sends.append((None, role, keep))
    return sends


def owners_done(peers, sends):
    for peer, role, copy in sends:

        @pl.when(peers.own == role)
        def _(copy=copy, peer=peer):
            copy().wait() if peer is None else copy().wait_recv()

        if peer is not None:

            @pl.when(peer == role)
            def _(copy=copy):
                copy().wait_send()


def kv_back(grad_kv, wqk, wvo, low, high):
    return dot_last(grad_kv[:, :INNER], wqk[low:high, INNER:]) + dot_last(
        grad_kv[:, INNER:], wvo[low:high, :INNER]
    )


class SumBlocks:
    def __init__(self, peers, buf, send, recv):
        self.peers, self.buf, self.send, self.recv = peers, buf, send, recv
        send[0] = to_low(buf[peers.diag])
        send[1] = to_low(buf[peers.sib])
        self.first = peers.send(send.at[0], recv.at[0], peers.sib)
        self.third = peers.send(send.at[1], recv.at[1], peers.sib)

    def cross(self):
        peers = self.peers
        self.first.wait_recv()
        self.send[2] = to_low(self.buf[peers.far] + self.recv[0].astype(F32))
        self.second = peers.send(self.send.at[2], self.recv.at[2], peers.far)

    def result(self):
        self.third.wait_recv()
        value = self.buf[self.peers.own] + self.recv[1].astype(F32)
        self.second.wait_recv()
        return value + self.recv[2].astype(F32)


class SumNear:
    def __init__(self, peers, part_of, block, total, send, recv):
        self.peers, self.total, self.send, self.recv = peers, total, send, recv
        for low, high in tiles(send.shape[2]):
            value = part_of(low, high)
            total[0, :, low:high] = value[:block]
            send[1, :, low:high] = to_low(value[block : 2 * block])
            total[1, :, low:high] = value[2 * block : 3 * block]
            send[0, :, low:high] = to_low(value[3 * block :])
        self.first = peers.send(send.at[0], recv.at[0], peers.sib)
        self.third = peers.send(send.at[1], recv.at[1], peers.sib)

    def cross(self):
        self.first.wait_recv()
        self.send[2] = to_low(self.total[1] + self.recv[0].astype(F32))
        self.second = self.peers.send(self.send.at[2], self.recv.at[2], self.peers.far)

    def result(self):
        self.third.wait_recv()
        value = self.total[0] + self.recv[1].astype(F32)
        self.second.wait_recv()
        return value + self.recv[2].astype(F32)


def kb_kernel(
    dec_gg, dec_gu, dec_hidden, dec_cot, dec_two, dec_one, gains, cross_q, hf,
    qk_all, vo_all, fi_all, fo_all, dec_gy, cross_kv_all, cross_p_all, enc_end_all,
    enc_gelu_all, enc_slope_all,
    dec_out, cross_gy, cross_gq, cross_gk, cross_gv, dec_one_grad, enc_end_grad, enc_gy, enc_gg, enc_gu,
    gains_grad, dec_gate, x_dec_hidden, x_dec_gy, x_dec_gu, x_hf,
    wqk, wvo, wfi, wfo, grad_kv, kv_send, kv_recv, row_total, row_send, row_recv, out_total,
    out_send, out_recv, x_dec_gg, cross_kv, cross_p, enc_end, enc_gelu, enc_slope,
    *rest,
    layout, steps,
):
    scratch, (send_sem, recv_sem, load_sem) = rest[:-3], rest[-3:]
    peers = Peers(send_sem, recv_sem)
    loads = Loads(load_sem)
    get_fi = loads.start(fi_all.at[1], wfi)
    get_cross = [
        loads.start(vo_all.at[2], wvo), loads.start(cross_kv_all, cross_kv),
        loads.start(cross_p_all, cross_p), loads.start(qk_all.at[2], wqk),
        loads.start(enc_end_all, enc_end),
    ]
    get_fo1 = loads.start(fo_all.at[1], wfo.at[1])
    get_up = [
        loads.start(fo_all.at[0], wfo.at[0]), loads.start(enc_gelu_all, enc_gelu),
        loads.start(enc_slope_all, enc_slope),
    ]
    peers.greet([peers.across(place) for place in range(steps)])
    first = Exchange(peers, [(dec_gg, x_dec_gg)], [(hf, x_hf)])
    later = [
        Exchange(
            peers, [(dec_gu, x_dec_gu), (dec_hidden, x_dec_hidden)], [(dec_gy, x_dec_gy)]
        )
    ]

    def arrived():
        first.finish_rows()
        first.finish_whole()

    products = Products(peers, layout, 1, steps, *scratch)
    products.add(
        [hf, x_hf], [(dec_gg, x_dec_gg)], dec_gate, before=arrived
    )
    stream = Stream(products.items, lag_of(steps))
    width = dec_two.shape[1]
    block = dec_two.shape[0]
    units = dec_gg.shape[2]
    gains_grad[...] = jnp.zeros_like(gains_grad)

    get_fi.wait()
    gate, up_proj = dec_gg[...].reshape(4 * block, units), dec_gu[...].reshape(4 * block, units)

    def grad_rows_part(low, high):
        return dot_last(gate, wfi[0, low:high, :]) + dot_last(up_proj, wfi[1, low:high, :])

    grad_rows = SumNear(peers, grad_rows_part, block, row_total, row_send, row_recv)
    grad_rows.cross()
    wait_all(get_cross)
    first.spread()
    value, gain_row = norm_back(dec_two[...], gains[5:6], grad_rows.result())
    gains_grad[5:6] = gain_row
    residual = dec_cot[...].astype(F32) + value
    grad_y = to_low(residual)
    cross_gy[...] = grad_y

    grad_out = to_low(dot(grad_y, wvo[:, INNER:]))
    first.relay()
    stream.pump(1)
    attend_back(cross_q[...], cross_kv, cross_p, grad_out, cross_gq, grad_kv, None)
    kv_sum = SumBlocks(peers, grad_kv, kv_send, kv_recv)
    kv_sum.cross()
    stream.pump(1)
    for low, high in tiles(width):
        row_total[0, :, low:high] = dot_last(cross_gq[...], wqk[low:high, :INNER])
    value, gain_row = norm_back(dec_one[...], gains[4:5], row_total[0])
    gains_grad[4:5] = gain_row
    dec_one_grad[...] = residual + value
    stream.pump(1)
    own_kv = to_low(kv_sum.result())
    cross_gk[...] = own_kv[:, :INNER]
    cross_gv[...] = own_kv[:, INNER:]
    for low, high in tiles(width):
        enc_end_grad[:, low:high] = kv_back(own_kv, wqk, wvo, low, high)
    value, gain_row = norm_back(enc_end[...], gains[2:3], enc_end_grad[...])
    gains_grad[2:3] = gain_row
    enc_end_grad[...] = value
    enc_gy[0] = to_low(value)
    gy_gather = Gather(peers, enc_gy, True)
    gy_gather.start()

    get_fo1.wait()
    hidden = dec_hidden[...].reshape(4 * block, units)
    out_sum = SumNear(
        peers, lambda low, high: dot_last(hidden, wfo[1, low:high, :]), block, out_total,
        out_send, out_recv,
    )

    stream.pump(1)
    for exchange in later:
        exchange.spread()
    wait_all(get_up)
    rows = enc_gy.shape[1]

    def gate_grads(slots):
        grad_y = enc_gy[slots].reshape(2 * rows, width)
        for low, high in tiles(units):
            grad_h = dot(grad_y, wfo[0, :, low:high]).reshape(2, rows, high - low)
            enc_gg[slots, :, low:high] = to_low(grad_h * enc_slope[slots, :, low:high])
            enc_gu[slots, :, low:high] = to_low(grad_h * enc_gelu[slots, :, low:high])

    gy_gather.wait_near()
    stream.pump(1)
    gate_grads(slice(0, 2))
    gy_gather.relay()
    out_sum.cross()
    stream.pump(1)
    gy_gather.wait_far()
    gate_grads(slice(2, 4))
    stream.pump(1)
    for exchange in later:
        exchange.relay()
    stream.pump(1)
    dec_out[...] = to_low(dec_two[...] + out_sum.result())
    stream.drain()
    for exchange in later:
        exchange.finish_rows()
        exchange.finish_whole()
    peers.finish()


def kb_call(dec_gg, dec_gu, dec_hidden, dec_cot, dec_two, dec_one, gains, cross_q, cross_kv,
            cross_p, enc_end, enc_gelu, enc_slope, attn_qk, attn_vo, ff_in, ff_out, hf, dec_gy,
            size, block, padded):
    rows, width = enc_end.shape
    dec_rows = dec_two.shape[0]
    units = ff_in.shape[3]
    kv_width = 2 * INNER
    shape = jax.ShapeDtypeStruct
    outs = [
        shape((dec_rows, width), LOW), shape((dec_rows, width), LOW),
        shape((dec_rows, INNER), LOW), shape((rows, INNER), LOW), shape((rows, INNER), LOW),
        shape((dec_rows, width), F32), shape((rows, width), F32), shape((4, rows, width), LOW), shape((4, rows, units), LOW),
        shape((4, rows, units), LOW), shape((8, width), F32), shape((1, block, units), F32),
    ]
    traded = [
        shape(value.shape, LOW)
        for value in (dec_hidden, dec_gy, dec_gu, hf)
    ]
    steps = size.bit_length() - 1
    items = len(tiles(units, 256))
    vmem = pl.BlockSpec(memory_space=pltpu.VMEM)
    hbm = pl.BlockSpec(memory_space=pltpu.HBM)
    copies = 3 * 3 + 3 + 5 + 6 + items * (steps - 1)
    return pl.pallas_call(
        functools.partial(kb_kernel, layout=(size, block, padded), steps=steps),
        out_shape=outs + traded,
        in_specs=[vmem] * 9 + [hbm] * 10,
        out_specs=[vmem] * len(outs) + [hbm] * (len(traded) - 1) + [vmem],
        scratch_shapes=[
            pltpu.VMEM(attn_qk.shape[1:], LOW), pltpu.VMEM(attn_vo.shape[1:], LOW),
            pltpu.VMEM(ff_in.shape[1:], LOW), pltpu.VMEM(ff_out.shape, LOW),
            pltpu.VMEM((4, rows, kv_width), F32), pltpu.VMEM((3, rows, kv_width), LOW),
            pltpu.VMEM((3, rows, kv_width), LOW), pltpu.VMEM((2, dec_rows, width), F32),
            pltpu.VMEM((3, dec_rows, width), LOW), pltpu.VMEM((3, dec_rows, width), LOW),
            pltpu.VMEM((2, dec_rows, width), F32), pltpu.VMEM((3, dec_rows, width), LOW),
            pltpu.VMEM((3, dec_rows, width), LOW),
            pltpu.VMEM(dec_gg.shape, LOW),
            pltpu.VMEM(cross_kv.shape, LOW), pltpu.VMEM(cross_p.shape, F32),
            pltpu.VMEM(enc_end.shape, F32), pltpu.VMEM(enc_gelu.shape, F32),
            pltpu.VMEM(enc_slope.shape, F32),
            *product_scratch(size, padded, 2 * 4 * dec_rows, items, 1, 256),
            pltpu.SemaphoreType.DMA((copies,)), pltpu.SemaphoreType.DMA((copies,)),
            pltpu.SemaphoreType.DMA((10,)),
        ],
        compiler_params=pltpu.CompilerParams(
            collective_id=1, has_side_effects=True, vmem_limit_bytes=VMEM_BYTES
        ),
        name="middle_chain",
    )(dec_gg, dec_gu, dec_hidden, dec_cot, dec_two, dec_one, gains, cross_q, hf,
      attn_qk, attn_vo, ff_in, ff_out, dec_gy, cross_kv, cross_p, enc_end,
      enc_gelu, enc_slope)


def kc_kernel(
    enc_gg, enc_gu, gains, gains_mid, enc_q, dec_one_grad, dec_x, self_q, self_kv, self_p,
    enc_spots, self_bucket,
    qk_all, vo_all, fi_all, enc_end_grad_all, enc_mid_all, enc_x_all, enc_kv_all, enc_p_all,
    enc_gy_all, hf_all, x_hf_all, dec_gu_all, x_dec_gu_all, dec_gy_all, x_dec_gy_all,
    dec_hidden_all, x_dec_hidden_all, enc_hidden_all,
    x_enc_hidden_all, h1_all, x_h1_rows, hs, hc, memory, cross_gy, cross_gq, cross_gk, cross_gv,
    cross_o,
    enc_grad, enc_ay, enc_gq, enc_gk, enc_gv, dec_grad, self_gy, self_gq, self_gk, self_gv,
    small, ffout, dec_up, chosen_h1, left_cross, right_cross, left_self, x_enc_gg, x_enc_gu, x_h1,
    wqk, wvo, wfi, enc_gs, self_gs, part, send, recv, enc_gkv_full, kv_send, kv_recv,
    self_gkv_full, self_send, self_recv, x_enc_gy, enc_end_grad, enc_mid, enc_x, enc_kv, enc_p,
    enc_gy, hfs, dec_gus, dec_gys, dec_hiddens, enc_hidden, x_enc_hidden, stage, *rest,
    layout, steps,
):
    dec_scratch, enc_scratch = rest[: 2 * steps], rest[2 * steps : -4]
    send_sem, recv_sem, load_sem, own_sem = rest[-4:]
    peers = Peers(send_sem, recv_sem)
    loads = Loads(load_sem)
    get_dec = [
        loads.start(source, target.at[place])
        for sources, target in (
            ((hf_all, x_hf_all), hfs), ((dec_gu_all, x_dec_gu_all), dec_gus),
            ((dec_gy_all, x_dec_gy_all), dec_gys), ((dec_hidden_all, x_dec_hidden_all), dec_hiddens),
        )
        for place, source in enumerate(sources)
    ]
    get_fi = loads.start(fi_all.at[0], wfi)
    get_vo1 = loads.start(vo_all.at[1], wvo.at[1])
    get_mid = [
        loads.start(enc_mid_all, enc_mid), loads.start(enc_end_grad_all, enc_end_grad),
        loads.start(vo_all.at[0], wvo.at[0]), loads.start(enc_kv_all, enc_kv),
        loads.start(enc_p_all, enc_p),
    ]
    get_out = [
        loads.start(enc_gy_all, enc_gy), loads.start(enc_hidden_all, enc_hidden),
        loads.start(x_enc_hidden_all, x_enc_hidden),
    ]
    get_last = [
        loads.start(qk_all.at[0], wqk.at[0]), loads.start(qk_all.at[1], wqk.at[1]),
        loads.start(enc_x_all, enc_x),
    ]
    for buf in (left_cross, right_cross):
        buf[...] = jnp.zeros_like(buf)
    peers.greet([peers.diag] + [peers.across(place) for place in range(steps)])
    exchange = Exchange(
        peers, [(enc_gg, x_enc_gg), (enc_gu, x_enc_gu)], [(enc_gy_all, x_enc_gy)]
    )
    dec_rows, enc_rows = hs.shape[0], memory.shape[0]
    short = (dec_rows,) * 4
    mixed = (dec_rows, enc_rows, enc_rows, dec_rows)
    owned = [
        to_owners(peers, (hc, memory, memory, cross_gy), left_cross, mixed, own_sem.at[0]),
        to_owners(
            peers, (cross_gq, cross_gk, cross_gv, cross_o), right_cross, mixed, own_sem.at[1]
        ),
    ]

    h1_gather = Gather(peers, x_h1, True, x_h1_rows)

    def arrived():
        wait_all(get_out)
        exchange.relay()
        exchange.finish_rows()

    def ready():
        wait_all(get_dec)

    dec_products = Products(peers, layout, 1, steps, *dec_scratch)
    dec_products.add(
        [hfs.at[place] for place in range(2)], [[dec_gus.at[place] for place in range(2)]], dec_up,
        before=ready,
    )
    dec_products.add(
        [dec_gys.at[place] for place in range(2)], [[dec_hiddens.at[place] for place in range(2)]],
        ffout.at[pl.ds(1, 1)],
    )
    enc_products = Products(peers, layout, 1, steps, *enc_scratch)
    enc_products.add(
        [enc_gy, x_enc_gy], [(enc_hidden, x_enc_hidden)], ffout.at[pl.ds(0, 1)], before=arrived
    )
    stream = Stream(dec_products.items + enc_products.items, lag_of(steps))
    staged = []

    def fetch_rows(place):
        if place == 5:
            h1_gather.wait_near()
            h1_gather.relay()
        if place == 7:
            h1_gather.wait_far()
        source = x_h1_rows if place == 4 else (h1_all, x_h1)[place // 4].at[place % 4]
        staged.append(loads.start(source, stage.at[place % 2]))

    def choose_next(place):
        staged.pop(0).wait()
        choose_rows(peers, layout, 1, stage[place % 2], chosen_h1, place * enc_rows)
        if place + 2 < 8:
            fetch_rows(place + 2)

    rows, width = enc_mid.shape
    units = enc_gg.shape[2]
    small[...] = jnp.zeros_like(small)
    small[:8] = gains_mid[...]

    stream.pump(2)
    get_fi.wait()

    def grad_part(slots, low, high):
        gate = enc_gg[slots].reshape(2 * rows, units)
        up_proj = enc_gu[slots].reshape(2 * rows, units)
        return dot_last(gate, wfi[0, low:high, :]) + dot_last(up_proj, wfi[1, low:high, :])

    for low, high in tiles(width):
        value = grad_part(slice(2, 4), low, high)
        part[:, low:high] = value[:rows]
        send[0, :, low:high] = to_low(value[rows:])
    for place in range(2):
        fetch_rows(place)
    first = peers.send(send.at[0], recv.at[0], peers.sib)
    stream.pump(1)
    get_vo1.wait()
    residual_dec = dec_one_grad[...]
    grad_y = to_low(residual_dec)
    self_gy[...] = grad_y
    owned.append(to_owners(peers, (hs, hs, hs, self_gy), left_self, short, own_sem.at[2]))
    grad_out_dec = to_low(dot(grad_y, wvo[1, :, INNER:]))
    exchange.spread()
    first.wait_recv()
    send[2] = to_low(part[...] + recv[0].astype(F32))
    second = peers.send(send.at[2], recv.at[2], peers.far)
    for low, high in tiles(width):
        value = grad_part(slice(0, 2), low, high)
        part[:, low:high] = value[:rows]
        send[1, :, low:high] = to_low(value[rows:])
    third = peers.send(send.at[1], recv.at[1], peers.sib)

    stream.pump(1)
    attend_back(self_q[...], self_kv, self_p, grad_out_dec, self_gq, self_gkv_full, self_gs)
    self_sum = SumBlocks(peers, self_gkv_full, self_send, self_recv)
    self_sum.cross()

    stream.pump(1)
    for place in range(3):
        choose_next(place)

    columns = []
    for bucket in range(BUCKETS):
        here = jnp.where(self_bucket[...] == bucket, 1.0, 0.0)
        sums = jnp.sum(self_gs[...].astype(F32) * here[None], axis=1)
        columns.append(jnp.sum(sums, axis=1, keepdims=True))
    self_table = jnp.concatenate(columns, axis=1)

    stream.pump(1)
    third.wait_recv()
    part[...] = part[...] + recv[1].astype(F32)
    second.wait_recv()
    wait_all(get_mid)
    value, gain_row = norm_back(enc_mid[...], gains[1:2], part[...] + recv[2].astype(F32))
    small[1:2] = gain_row
    residual = enc_end_grad[...] + value
    grad_y = to_low(residual)
    enc_ay[...] = grad_y
    enc_grad[...] = residual

    h1_gather.start()
    grad_out = to_low(dot(grad_y, wvo[0, :, INNER:]))
    attend_back(enc_q[...], enc_kv, enc_p, grad_out, enc_gq, enc_gkv_full, enc_gs)
    enc_sum = SumBlocks(peers, enc_gkv_full, kv_send, kv_recv)
    stream.pump(2)
    wait_all(get_last)
    for low, high in tiles(width):
        part[:, low:high] = dot_last(enc_gq[...], wqk[0, low:high, :INNER])
    enc_sum.cross()

    stream.pump(1)
    choose_next(3)
    own_kv = to_low(self_sum.result())
    self_gk[...] = own_kv[:, :INNER]
    self_gv[...] = own_kv[:, INNER:]
    for low, high in tiles(width):
        dec_grad[:, low:high] = dot_last(self_gq[...], wqk[1, low:high, :INNER]) + kv_back(
            own_kv, wqk.at[1], wvo.at[1], low, high
        )
    value, gain_row = norm_back(dec_x[...].astype(F32), gains[3:4], dec_grad[...])
    small[3:4] = gain_row
    dec_grad[...] = residual_dec + value

    turn = lax.broadcasted_iota(jnp.int32, (rows, rows), 0) + lax.broadcasted_iota(
        jnp.int32, (rows, rows), 1
    )
    turn = jnp.where(turn == rows - 1, 1.0, 0.0).astype(LOW)
    offsets = []
    for head in range(HEADS):
        turned = dot(turn, enc_gs[head])
        spread = jnp.concatenate([turned, jnp.zeros((rows, rows), F32)], axis=1)
        spread = pltpu.roll(spread, 0, 1, stride=1, stride_axis=0)
        offsets.append(jnp.sum(spread, axis=0, keepdims=True))
    enc_table = jnp.dot(
        jnp.concatenate(offsets + [jnp.zeros((2, offsets[0].shape[1]), F32)], axis=0),
        enc_spots[...], precision=HIGH, preferred_element_type=F32,
    )
    small[8:, :BUCKETS] = enc_table
    small[8 : 8 + HEADS, PAIR : PAIR + BUCKETS] = self_table

    stream.pump(2)
    own_kv = to_low(enc_sum.result())
    enc_gk[...] = own_kv[:, :INNER]
    enc_gv[...] = own_kv[:, INNER:]
    for low, high in tiles(width):
        part[:, low:high] += kv_back(own_kv, wqk.at[0], wvo.at[0], low, high)
    value, gain_row = norm_back(enc_x[...].astype(F32), gains[0:1], part[...])
    small[0:1] = gain_row
    enc_grad[...] += value
    for place in range(4, 8):
        stream.pump(1)
        choose_next(place)
    stream.drain()
    exchange.finish_whole()
    for sends in owned:
        owners_done(peers, sends)
    peers.finish()


def kc_call(size, block, padded, near, streamed):
    enc_gg, dec_x = near[0], near[6]
    attn_qk, attn_vo, ff_in = streamed[:3]
    rows, width = streamed[4].shape
    dec_rows = dec_x.shape[0]
    units = ff_in.shape[3]
    kv_width = 2 * INNER
    total = 4 * rows
    half = size * padded // 2
    steps = size.bit_length() - 1
    items = len(tiles(units, chunk_of(size)))
    shape = jax.ShapeDtypeStruct
    outs = [
        shape((rows, width), F32), shape((rows, width), LOW), shape((rows, INNER), LOW),
        shape((rows, INNER), LOW), shape((rows, INNER), LOW),
        shape((dec_rows, width), F32), shape((dec_rows, width), LOW),
        shape((dec_rows, INNER), LOW), shape((dec_rows, INNER), LOW),
        shape((dec_rows, INNER), LOW),
        shape((16, width), F32), shape((2, block, units), F32), shape((1, block, units), F32),
        shape((2, half // 2, 2 * total), LOW), shape((4, rows, width), LOW),
        shape((4, rows, INNER), LOW),
    ]
    apart = [
        shape((4, dec_rows, width), LOW),
        shape(enc_gg.shape, LOW), shape(enc_gg.shape, LOW), shape((4, rows, width), LOW),
    ]
    vmem = pl.BlockSpec(memory_space=pltpu.VMEM)
    hbm = pl.BlockSpec(memory_space=pltpu.HBM)
    copies = 3 * 3 + 3 + 3 + 3 * 3 + 3 + 3 * items * (steps - 1)
    return pl.pallas_call(
        functools.partial(kc_kernel, layout=(size, block, padded), steps=steps),
        out_shape=outs + apart,
        in_specs=[vmem] * len(near) + [hbm] * len(streamed),
        out_specs=[vmem] * len(outs) + [hbm] * len(apart),
        scratch_shapes=[
            pltpu.VMEM((2,) + attn_qk.shape[1:], LOW), pltpu.VMEM((2,) + attn_vo.shape[1:], LOW),
            pltpu.VMEM(ff_in.shape[1:], LOW), pltpu.VMEM((HEADS, rows, total), LOW),
            pltpu.VMEM((HEADS, dec_rows, 4 * dec_rows), LOW),
            pltpu.VMEM((rows, width), F32), pltpu.VMEM((3, rows, width), LOW),
            pltpu.VMEM((3, rows, width), LOW),
            pltpu.VMEM((4, rows, kv_width), F32), pltpu.VMEM((3, rows, kv_width), LOW),
            pltpu.VMEM((3, rows, kv_width), LOW),
            pltpu.VMEM((4, dec_rows, kv_width), F32), pltpu.VMEM((3, dec_rows, kv_width), LOW),
            pltpu.VMEM((3, dec_rows, kv_width), LOW), pltpu.VMEM((4, rows, width), LOW),
            pltpu.VMEM((rows, width), F32), pltpu.VMEM((rows, width), F32),
            pltpu.VMEM((rows, width), LOW), pltpu.VMEM((4, rows, kv_width), LOW),
            pltpu.VMEM((HEADS, rows, total), F32), pltpu.VMEM((4, rows, width), LOW),
            *[pltpu.VMEM((2, 4, dec_rows, width), LOW), pltpu.VMEM((2, 4, dec_rows, units), LOW)] * 2,
            pltpu.VMEM((4, rows, units), LOW), pltpu.VMEM((4, rows, units), LOW),
            pltpu.VMEM((2, rows, width), LOW),
            *product_scratch(size, padded, 2 * 4 * dec_rows, 2 * items, 1, chunk_of(size)),
            *product_scratch(size, padded, 2 * total, items, 1, chunk_of(size)),
            pltpu.SemaphoreType.DMA((copies,)), pltpu.SemaphoreType.DMA((copies,)),
            pltpu.SemaphoreType.DMA((2 + 8 + 5 + 3 + 3 + 8,)), pltpu.SemaphoreType.DMA((3,)),
        ],
        compiler_params=pltpu.CompilerParams(
            collective_id=2, has_side_effects=True, vmem_limit_bytes=62 * 1024 * 1024
        ),
        name="last_chain",
    )(*near, *streamed)
class Spread:
    def __init__(self, peers, partners, total, recv):
        self.peers, self.partners, self.total, self.recv = peers, partners, total, recv
        self.steps = len(partners) + 1

    def run(self, step):
        if step:
            self.copy.wait_recv()
            self.total[step] = self.total[step - 1] + self.recv[step - 1]
        if step < len(self.partners):
            self.copy = self.peers.send(
                self.total.at[step], self.recv.at[step], self.partners[step]
            )


def kd_kernel(
    small,
    chosen_h1, enc_gg_all, x_enc_gg_all, enc_gu_all, x_enc_gu_all,
    left_cross_all, right_cross_all, left_self_all, h0, enc_ay,
    enc_gq, enc_gk, enc_gv, enc_o, self_gq, self_gk, self_gv, self_o, dec_gate,
    dec_up,
    ffin, qk, vo, small_out,
    enc_ffin, enc_gg, x_enc_gg, enc_gu, x_enc_gu, chosen_attn, left_enc, left_cross,
    left_self, right_enc, right_cross, right_self, attn_total, attn, small_total, small_recv,
    *rest,
    layout, steps,
):
    size, block, padded = layout
    scratch, rest = rest[: 2 * steps], rest[2 * steps :]
    at_send, at_recv = rest[:steps], rest[steps : 2 * steps]
    send_sem, recv_sem, load_sem, own_sem = rest[2 * steps :]
    peers = Peers(send_sem, recv_sem)
    loads = Loads(load_sem)
    get_gate = [
        loads.start(chosen_h1, scratch[0]), loads.start(enc_gg_all, enc_gg),
        loads.start(x_enc_gg_all, x_enc_gg),
    ]
    get_cross = [
        loads.start(left_cross_all, left_cross), loads.start(right_cross_all, right_cross),
    ]
    get_up = [loads.start(enc_gu_all, enc_gu), loads.start(x_enc_gu_all, x_enc_gu)]
    get_self = [loads.start(left_self_all, left_self)]
    passed = [
        loads.start(dec_gate, ffin.at[1, pl.ds(0, 1)]), loads.start(dec_up, ffin.at[1, pl.ds(1, 1)])
    ]
    partners = [peers.across(place) for place in range(steps)]
    peers.greet([peers.diag] + partners)
    dec_rows, enc_rows = self_gq.shape[0], enc_gq.shape[0]
    own_self = to_owners(
        peers, (self_gq, self_gk, self_gv, self_o), right_self, (dec_rows,) * 4, own_sem.at[0]
    )
    own_enc = to_owners(
        peers, (enc_gq, enc_gk, enc_gv, enc_o), right_enc, (enc_rows,) * 4, own_sem.at[1]
    )
    own_left = to_owners(peers, (h0, h0, h0, enc_ay), left_enc, (enc_rows,) * 4, own_sem.at[3])
    spread = Spread(peers, [peers.sib, peers.far] + partners, small_total, small_recv)
    small_total[0] = small[...]
    spread.run(0)

    products = Products(peers, layout, 1, steps, *scratch)
    products.add(
        None, [(enc_gg, x_enc_gg), (enc_gu, x_enc_gu)], enc_ffin,
        ready=(lambda: wait_all(get_gate), lambda: wait_all(get_up)),
    )

    def wait_self():
        wait_all(get_self)
        owners_done(peers, own_self)

    def wait_enc():
        owners_done(peers, own_enc)
        owners_done(peers, own_left)

    kinds = (
        (2, left_cross, right_cross, lambda: wait_all(get_cross)),
        (1, left_self, right_self, wait_self), (0, left_enc, right_enc, wait_enc),
    )
    attn_items, gathers = [], []
    for a, left, right, arrived in kinds:
        rows = left.shape[0] * left.shape[1]

        def before(left=left, right=right, arrived=arrived):
            arrived()
            if block % 8:
                choose_rows(peers, layout, 0, flat(left[...]), chosen_attn, 0)
                return
            for low, high in tiles(INNER, chunk_of(size)):
                chosen_attn[:, low:high] = dot_first(flat(left[...]), flat(right[:, :, low:high]))

        for place, (low, high) in enumerate(tiles(INNER, chunk_of(size))):

            def product(half, right=right, rows=rows, low=low, high=high):
                if block % 8:
                    return dot(chosen_attn[half, :, :rows], flat(right[:, :, low:high]))
                parts = []
                for place in range(size // 2):
                    owner = half
                    for bit in range(1, steps):
                        owner = owner + (((place >> (steps - 1 - bit)) & 1) << bit)
                    start = pl.multiple_of(owner * block, 8)
                    parts.append(chosen_attn[pl.ds(start, block), low:high])
                    if padded > block:
                        parts.append(jnp.zeros((padded - block, high - low), F32))
                return jnp.concatenate(parts, axis=0)

            def finish(value, a=a, low=low, high=high, last=high == INNER):
                attn[a, peers.own, :, low:high] = to_low(value)
                if last:
                    gathers.append((a, Gather(peers, attn.at[a], False)))
                    gathers[-1][1].start()

            slot = len(attn_items)
            item = Reduce(
                peers, list(range(steps)), product, high - low, attn_total.at[slot], at_send,
                at_recv, slot, finish, products.ships,
            )
            item.before = [before] if place == 0 else []
            attn_items.append(item)

    items = []
    for place in range(max(len(products.items), len(attn_items) + 2)):
        if 2 <= place < len(attn_items) + 2:
            items.append(attn_items[place - 2])
        if place < len(products.items):
            items.append(products.items[place])
    stream = Stream(items, lag_of(steps))
    spreading = []

    def settle(relay, write):
        for entry in spreading:
            a, gather, begun, relayed = entry
            if not relayed and stream.now - begun >= relay:
                gather.wait_near()
                gather.relay()
                entry[3] = True
        for entry in list(spreading):
            a, gather, begun, relayed = entry
            if relayed and stream.now - begun >= write:
                gather.wait_far()
                for place, out in enumerate((qk, qk, vo, vo)):
                    lanes = slice(place % 2 * INNER, (place % 2 + 1) * INNER)
                    out[a, :, lanes] = attn[a, place, :, :].astype(F32)[:block]
                spreading.remove(entry)

    while stream.now <= stream.last:
        stream.pump()
        spreading += [[a, gather, stream.now, False] for a, gather in gathers]
        gathers.clear()
        settle(1, 2)
        if stream.now < 2 * spread.steps:
            if stream.now % 2 == 0:
                spread.run(stream.now // 2)
    for step in range(1, spread.steps):
        if 2 * step > stream.last + 1:
            spread.run(step)
    small_out[...] = small_total[spread.steps - 1]
    left = pltpu.make_async_copy(enc_ffin, ffin.at[0], own_sem.at[2])
    left.start()
    settle(0, 0)
    settle(0, 0)
    left.wait()
    wait_all(passed)
    peers.finish()


def kd_call(size, block, padded, width, small, streamed):
    gate, self_q = streamed[1], streamed[14]
    units, enc_rows, dec_rows = gate.shape[2], gate.shape[1], self_q.shape[0]
    steps = size.bit_length() - 1
    shape = jax.ShapeDtypeStruct
    outs = [
        shape((2, 2, block, units), F32), shape((3, block, 2 * INNER), F32),
        shape((3, block, 2 * INNER), F32), shape(small.shape, F32),
    ]
    vmem = pl.BlockSpec(memory_space=pltpu.VMEM)
    hbm = pl.BlockSpec(memory_space=pltpu.HBM)
    half = size * padded // 2
    ff_items = 2 * len(tiles(units, chunk_of(size)))
    at_items = 3 * len(tiles(INNER, chunk_of(size)))
    at_heights = [half >> step for step in range(steps)]

    def bufs(items, heights):
        return [pltpu.VMEM((items, height, chunk_of(size)), LOW) for height in heights]

    copies = ff_items * (steps - 1) + at_items * steps + 3 * 3 + (2 + steps) + 9
    return pl.pallas_call(
        functools.partial(kd_kernel, layout=(size, block, padded), steps=steps),
        out_shape=outs,
        in_specs=[vmem] + [hbm] * len(streamed),
        out_specs=[hbm] + [vmem] * 3,
        scratch_shapes=[
            pltpu.VMEM((2, block, units), F32),
            *[pltpu.VMEM(gate.shape, LOW)] * 4,
            pltpu.VMEM((2, half, 4 * enc_rows), LOW) if block % 8 else pltpu.VMEM((width, INNER), F32),
            pltpu.VMEM((4, enc_rows, width), LOW), pltpu.VMEM((4, enc_rows, width), LOW),
            pltpu.VMEM((4, dec_rows, width), LOW),
            pltpu.VMEM((4, enc_rows, INNER), LOW), pltpu.VMEM((4, enc_rows, INNER), LOW),
            pltpu.VMEM((4, dec_rows, INNER), LOW),
            pltpu.VMEM((at_items, half, chunk_of(size)), F32),
            pltpu.VMEM((3, 4, padded, INNER), LOW),
            pltpu.VMEM((3 + steps,) + small.shape, F32),
            pltpu.VMEM((2 + steps,) + small.shape, F32),
            *product_scratch(size, padded, 8 * enc_rows, ff_items, 1, chunk_of(size)),
            *bufs(2, at_heights), *bufs(at_items, at_heights),
            pltpu.SemaphoreType.DMA((copies,)), pltpu.SemaphoreType.DMA((copies,)),
            pltpu.SemaphoreType.DMA((10,)), pltpu.SemaphoreType.DMA((4,)),
        ],
        compiler_params=pltpu.CompilerParams(
            collective_id=3, has_side_effects=True, vmem_limit_bytes=62 * 1024 * 1024
        ),
        name="weight_sums",
    )(small, *streamed)


def out_kernel(
    qk, vo, ffin, ffout, enc_grad_all, dec_grad, sums, decoded,
    qk_out, vo_out, ffin_out, ffout_out, enc_out_all, dec_out, gains_out, decoded_out,
    enc_grad, enc_out, *rest,
):
    held, sems = rest[:-1], rest[-1]
    loads = Loads(sems)
    get_enc = loads.start(enc_grad_all, enc_grad)
    pieces = []
    for source, buf, target in zip(
        (qk, vo, ffin, ffout), held, (qk_out, vo_out, ffin_out, ffout_out)
    ):
        for place in range(source.shape[0]):
            pieces.append(
                (loads.start(source.at[place], buf.at[place]), buf.at[place], target.at[place])
            )
    get_enc.wait()
    enc_out[...] = enc_grad[...].T
    leaving = [loads.start(enc_out, enc_out_all)]
    for copy, buf, target in pieces:
        copy.wait()
        leaving.append(loads.start(buf, target))
    dec_out[...] = dec_grad[: dec_out.shape[0]]
    gains_out[...] = sums[: gains_out.shape[0]]
    decoded_out[...] = to_low(decoded[...].astype(F32)[: decoded_out.shape[0]])
    wait_all(leaving)


def out_call(qk, vo, ffin, ffout, enc_grad, dec_grad, sums, decoded, dec_rows, gain_rows):
    shape = jax.ShapeDtypeStruct
    large = (qk, vo, ffin, ffout)
    width = sums.shape[1]
    vmem = pl.BlockSpec(memory_space=pltpu.VMEM)
    hbm = pl.BlockSpec(memory_space=pltpu.HBM)
    return pl.pallas_call(
        out_kernel,
        out_shape=[
            *[shape(value.shape, F32) for value in large],
            shape(enc_grad.shape[::-1], F32), shape((dec_rows, width), F32),
            shape((gain_rows, width), F32), shape((dec_rows, width), LOW),
        ],
        in_specs=[hbm] * 5 + [vmem] * 3,
        out_specs=[hbm] * 5 + [vmem] * 3,
        scratch_shapes=[
            pltpu.VMEM(enc_grad.shape, F32), pltpu.VMEM(enc_grad.shape[::-1], F32),
            *[pltpu.VMEM(value.shape, F32) for value in large],
            pltpu.SemaphoreType.DMA((2 + 2 * sum(value.shape[0] for value in large),)),
        ],
        compiler_params=pltpu.CompilerParams(vmem_limit_bytes=VMEM_BYTES),
        name="results",
    )(qk, vo, ffin, ffout, enc_grad, dec_grad, sums, decoded)


def on_device(
    enc_x, dec_x, dec_cot, item_count, enc_mask, dec_mask, enc_buckets, dec_buckets,
    gains, tables, attn_qk, attn_vo, ff_in, ff_out,
):
    tensor_id = lax.axis_index("tensor")
    size = lax.axis_size("dp")
    enc_own, dec_own = enc_x.shape[0], dec_x.shape[0]
    width = enc_x.shape[1]
    block = width // size
    padded = (block + 15) // 16 * 16
    small, (enc_spots, self_bucket) = prepare(
        item_count, enc_mask, dec_mask, enc_buckets, dec_buckets, tables, enc_own, dec_own
    )
    ff_out_t = jnp.swapaxes(ff_out, 1, 2)
    (
        h0, enc_q, enc_kv, enc_p, enc_o, enc_mid, h1, enc_gelu, enc_slope, enc_hidden, enc_end,
        memory, cross_kv, hs, self_q, self_kv, self_p, self_o, dec_one, hc, cross_q, cross_p,
        cross_o, dec_two, hf, dec_gy, dec_gg, dec_gu, dec_hidden, dec_x, dec_cot,
        x_h1_rows, x_enc_hidden,
    ) = ka_call(enc_x, dec_x, dec_cot, gains, *small, attn_qk, attn_vo, ff_in, ff_out_t)
    (
        dec_out, cross_gy, cross_gq, cross_gk, cross_gv, dec_one_grad, enc_end_grad, enc_gy,
        enc_gg, enc_gu, gains_mid, dec_gate, x_dec_hidden, x_dec_gy, x_dec_gu, x_hf,
    ) = kb_call(
        dec_gg, dec_gu, dec_hidden, dec_cot, dec_two, dec_one, gains, cross_q, cross_kv, cross_p,
        enc_end, enc_gelu, enc_slope, attn_qk, attn_vo, ff_in, ff_out_t, hf, dec_gy,
        size, block, padded,
    )
    (
        enc_grad, enc_ay, enc_gq, enc_gk, enc_gv, dec_grad, self_gy, self_gq, self_gk, self_gv,
        sums, ffout_sum, dec_up, chosen_h1, left_cross, right_cross, left_self, x_enc_gg,
        x_enc_gu, unused,
    ) = kc_call(
        size, block, padded,
        [
            enc_gg, enc_gu, gains, gains_mid, enc_q, dec_one_grad, dec_x, self_q, self_kv, self_p,
            enc_spots, self_bucket,
        ],
        [
            attn_qk, attn_vo, ff_in, enc_end_grad, enc_mid, enc_x, enc_kv, enc_p, enc_gy, hf, x_hf,
            dec_gu, x_dec_gu, dec_gy, x_dec_gy, dec_hidden, x_dec_hidden, enc_hidden, x_enc_hidden, h1, x_h1_rows, hs, hc, memory, cross_gy, cross_gq,
            cross_gk, cross_gv, cross_o,
        ],
    )
    ffin_sum, qk_sum, vo_sum, sums = kd_call(
        size, block, padded, width, sums,
        [
            chosen_h1, enc_gg, x_enc_gg, enc_gu, x_enc_gu, left_cross, right_cross,
            left_self, h0, enc_ay, enc_gq, enc_gk, enc_gv, enc_o, self_gq, self_gk, self_gv, self_o,
            dec_gate, dec_up,
        ],
    )
    qk_sum, vo_sum, ffin_sum, ffout_sum, enc_grad, dec_grad, gains_sum, dec_out = out_call(
        qk_sum, vo_sum, ffin_sum, ffout_sum, enc_grad, dec_grad, sums, dec_out, dec_own,
        gains.shape[0],
    )
    ffout_sum = jnp.swapaxes(ffout_sum, 1, 2)
    table_rows = sums[8 : 8 + HEADS]
    tables_sum = jnp.stack(
        [table_rows[:, :BUCKETS].T, table_rows[:, PAIR : PAIR + BUCKETS].T]
    )
    return (
        dec_out, enc_grad.T, dec_grad, gains_sum, tables_sum, qk_sum, vo_sum, ffin_sum,
        ffout_sum,
    )


def solution(mesh):
    rows = P(("dp", "tensor"), None)
    return jax.shard_map(
        on_device,
        mesh=mesh,
        in_specs=(
            rows, rows, rows, P("dp"), P("dp"), P("dp"), P(), P(), P(), P(), P(), P(),
            P(None, None, None, "tensor"), P(None, "tensor", None),
        ),
        out_specs=(
            rows, rows, rows, P(), P(), P(None, "dp", None), P(None, "dp", None),
            P(None, None, "dp", "tensor"), P(None, "tensor", "dp"),
        ),
        check_vma=False,
    )
```

```python
import functools

import jax
import jax.numpy as jnp
from jax import lax
from jax.experimental import pallas as pl
from jax.experimental.pallas import tpu as pltpu
from jax.sharding import PartitionSpec as P

HEADS = 6
HEAD = 64
INNER = HEADS * HEAD
PAIRS = HEADS // 2
PAIR = 2 * HEAD
BUCKETS = 32
EPSILON = 1e-06
MASKED = -1000000000.0
HIGH = lax.Precision.HIGHEST
F32 = jnp.float32
LOW = jnp.bfloat16
DEC_PAD = 32
VMEM_BYTES = 60 * 1024 * 1024
ROOT = 0.7978845608028654
CUBE = 0.044715


def to_low(value):
    return value.astype(LOW)


def dot(left, right):
    return jnp.dot(left, right, preferred_element_type=F32)


def dot_first(left, right):
    return lax.dot_general(left, right, (((0,), (0,)), ((), ())), preferred_element_type=F32)


def dot_last(left, right):
    return lax.dot_general(left, right, (((1,), (1,)), ((), ())), preferred_element_type=F32)


def norm_gain(rows, gain):
    return rows * lax.rsqrt(jnp.mean(rows * rows, axis=-1, keepdims=True) + EPSILON) * gain


def norm_back(rows, gain, grad_rows):
    scale = lax.rsqrt(jnp.mean(rows * rows, axis=-1, keepdims=True) + EPSILON)
    normed = rows * scale
    scaled = grad_rows * gain
    inner = jnp.mean(scaled * normed, axis=-1, keepdims=True)
    grad_gain = jnp.sum(grad_rows * normed, axis=0, keepdims=True)
    return scale * (scaled - normed * inner), grad_gain


def act_parts(gate, up_proj):
    square = gate * gate
    curve = jnp.tanh(ROOT * gate * (1.0 + CUBE * square))
    half = 0.5 * (1.0 + curve)
    slope = half + 0.5 * gate * (1.0 - curve * curve) * (ROOT * (1.0 + 3.0 * CUBE * square))
    return gate * half, up_proj * slope


def tiles(width, step=256):
    return [(start, min(start + step, width)) for start in range(0, width, step)]


class Peers:
    def __init__(self, send_sem, recv_sem):
        dp, tensor = lax.axis_index("dp"), lax.axis_index("tensor")
        chip, core = lax.div(tensor, 2), lax.rem(tensor, 2)
        self.dp = dp
        self.own = tensor
        self.sib = chip * 2 + (1 - core)
        self.far = (1 - chip) * 2 + core
        self.diag = (1 - chip) * 2 + (1 - core)
        self.send_sem, self.recv_sem = send_sem, recv_sem
        self.used = 0
        self.copies = []

    def bit(self, place):
        return lax.rem(lax.div(self.dp, 2**place), 2)

    def across(self, place):
        return (self.dp + (1 - 2 * self.bit(place)) * 2**place, self.own)

    def device(self, peer):
        return peer if isinstance(peer, tuple) else (self.dp, peer)

    def greet(self, more=()):
        barrier = pltpu.get_barrier_semaphore()
        for peer in (self.sib, self.far) + tuple(more):
            pl.semaphore_signal(
                barrier, inc=1, device_id=self.device(peer), device_id_type=pl.DeviceIdType.MESH
            )
        pl.semaphore_wait(barrier, 2 + len(more))

    def send(self, source, target, peer):
        place = self.used
        self.used += 1
        assert place < self.send_sem.shape[0]
        copy = pltpu.make_async_remote_copy(
            src_ref=source,
            dst_ref=target,
            send_sem=self.send_sem.at[place],
            recv_sem=self.recv_sem.at[place],
            device_id=self.device(peer),
            device_id_type=pl.DeviceIdType.MESH,
        )
        copy.start()
        self.copies.append(copy)
        return copy

    def finish(self):
        for copy in self.copies:
            copy.wait_send()


class Gather:
    def __init__(self, peers, buf, near, source=None):
        self.peers, self.buf, self.source = peers, buf, source
        if near:
            self.slots = (0, 1, 2, 2, 3)
        else:
            self.slots = (peers.own, peers.own, peers.own, peers.far, peers.far)

    def start(self):
        own, at_sib, at_far, unused, unused = self.slots
        source = self.buf.at[own] if self.source is None else self.source
        self.to_far = self.peers.send(source, self.buf.at[at_far], self.peers.far)
        self.to_sib = self.peers.send(source, self.buf.at[at_sib], self.peers.sib)

    def wait_near(self):
        self.to_sib.wait_recv()

    def relay(self):
        unused, unused, unused, far, far_at_sib = self.slots
        self.to_far.wait_recv()
        self.relayed = self.peers.send(
            self.buf.at[far], self.buf.at[far_at_sib], self.peers.sib
        )

    def wait_far(self):
        self.relayed.wait_recv()


def attend(queries, kv, bias_of, allowed, weights_out, mixed_out):
    rows = queries.shape[0]
    total = kv.shape[0] * kv.shape[1]
    first = lax.broadcasted_iota(jnp.int32, (rows, PAIR), 1) < HEAD
    for pair in range(PAIRS):
        lanes = slice(pair * PAIR, (pair + 1) * PAIR)
        keys = kv[:, :, lanes].reshape(total, PAIR)
        values = kv[:, :, INNER + pair * PAIR : INNER + (pair + 1) * PAIR].reshape(total, PAIR)
        both = queries[:, lanes].astype(F32)
        mixed = []
        for half in range(2):
            head = 2 * pair + half
            here = to_low(jnp.where(first if half == 0 else ~first, both, 0.0))
            scores = dot_last(here, keys)
            if bias_of is not None:
                scores = scores + bias_of(head)
            scores = jnp.where(allowed, scores, MASKED)
            shifted = jnp.exp(scores - jnp.max(scores, axis=-1, keepdims=True))
            weights = shifted / jnp.sum(shifted, axis=-1, keepdims=True)
            weights_out[head] = weights
            mixed.append(dot(to_low(weights), values))
        mixed_out[:, lanes] = to_low(jnp.where(first, mixed[0], mixed[1]))


def attend_back(queries, kv, weights_in, grad_out, grad_q_out, grad_kv_out, grad_s_out):
    rows = queries.shape[0]
    total = kv.shape[0] * kv.shape[1]
    block = kv.shape[1]
    first = lax.broadcasted_iota(jnp.int32, (rows, PAIR), 1) < HEAD
    first_key = lax.broadcasted_iota(jnp.int32, (total, PAIR), 1) < HEAD
    for pair in range(PAIRS):
        lanes = slice(pair * PAIR, (pair + 1) * PAIR)
        value_lanes = slice(INNER + pair * PAIR, INNER + (pair + 1) * PAIR)
        keys = kv[:, :, lanes].reshape(total, PAIR)
        values = kv[:, :, value_lanes].reshape(total, PAIR)
        query = queries[:, lanes]
        grad = grad_out[:, lanes]
        grad_wide = grad.astype(F32)
        grad_q, grad_k, grad_v = [], [], []
        for half in range(2):
            head = 2 * pair + half
            here = to_low(jnp.where(first if half == 0 else ~first, grad_wide, 0.0))
            weights = weights_in[head]
            grad_weights = dot_last(here, values)
            weighted = jnp.sum(weights * grad_weights, axis=-1, keepdims=True)
            grad_scores = to_low(weights * (grad_weights - weighted))
            if grad_s_out is not None:
                grad_s_out[head] = grad_scores
            grad_q.append(dot(grad_scores, keys))
            grad_k.append(dot_first(grad_scores, query))
            grad_v.append(dot_first(to_low(weights), grad))
        grad_q_out[:, lanes] = to_low(jnp.where(first, grad_q[0], grad_q[1]))
        grad_kv_out[:, :, lanes] = jnp.where(first_key, grad_k[0], grad_k[1]).reshape(
            4, block, PAIR
        )
        grad_kv_out[:, :, value_lanes] = jnp.where(first_key, grad_v[0], grad_v[1]).reshape(
            4, block, PAIR
        )


class Exchange:
    def __init__(self, peers, whole, rows, place=0):
        partner = peers.across(place)
        self.rows = [
            (peers.send(own.at[0], other.at[0], partner), Gather(peers, other, True))
            for own, other in rows
        ]
        self.whole = [peers.send(own, other, partner) for own, other in whole]

    def spread(self):
        for copy, gather in self.rows:
            copy.wait_recv()
            gather.start()

    def relay(self):
        for unused, gather in self.rows:
            gather.wait_near()
            gather.relay()

    def finish_rows(self):
        for unused, gather in self.rows:
            gather.wait_far()

    def finish_first(self):
        self.whole.pop(0).wait_recv()

    def finish_whole(self):
        for copy in self.whole:
            copy.wait_recv()
        self.whole = []


class Loads:
    def __init__(self, sems):
        self.sems, self.used = sems, 0

    def start(self, source, target):
        copy = pltpu.make_async_copy(source, target, self.sems.at[self.used])
        self.used += 1
        copy.start()
        return copy


def wait_all(copies):
    for copy in copies:
        copy.wait()
    copies.clear()


def project_kv(rows, wqk, wvo, target):
    target[:, :INNER] = to_low(dot(rows, wqk[:, INNER:]))
    target[:, INNER:] = to_low(dot(rows, wvo[:, :INNER]))


def ff_up(rows, w_in, gelu_out, slope_out, hidden_out, slots):
    count, block = slots.stop - slots.start, gelu_out.shape[1]
    for low, high in tiles(gelu_out.shape[2]):
        gate = dot(rows, w_in[0, :, low:high])
        up_proj = dot(rows, w_in[1, :, low:high])
        gelu, slope = act_parts(gate, up_proj)
        shape = (count, block, high - low)
        gelu_out[slots, :, low:high] = gelu.reshape(shape)
        slope_out[slots, :, low:high] = slope.reshape(shape)
        hidden_out[slots, :, low:high] = to_low(gelu * up_proj).reshape(shape)


def reduce_far(peers, diag_part, far_part, send, recv):
    width = send.shape[2]
    for low, high in tiles(width):
        send[0, :, low:high] = to_low(diag_part(low, high))
    first = peers.send(send.at[0], recv.at[0], peers.sib)
    first.wait_recv()
    for low, high in tiles(width):
        send[2, :, low:high] = to_low(
            far_part(low, high) + recv[0, :, low:high].astype(F32)
        )
    return peers.send(send.at[2], recv.at[2], peers.far)


def ka_kernel(
    enc_x, dec_x_short, dec_cot_short, gains, enc_terms, self_bias, item_count, enc_mask, dec_mask,
    qk_all, vo_all, fi_all, fo_all,
    h0, enc_q, enc_kv_out, enc_p_out, enc_o, enc_mid_out, h1_out, enc_gelu_out, enc_slope_out,
    enc_hidden_out, enc_end_out, memory, cross_kv_out, hs, self_q, self_kv, self_p, self_o,
    dec_one, hc, cross_q, cross_p, cross_o, dec_two, hf, dec_gy, dec_gg, dec_gu, dec_hidden,
    dec_x, dec_cot, x_h1, x_enc_hidden,
    wqk, wvo, wfi, wfo, part, send, recv, dec_gelu, dec_slope, dec_gh,
    enc_kv, enc_p, enc_mid, h1, enc_gelu, enc_slope, enc_hidden, enc_end, cross_kv,
    send_sem, recv_sem, load_sem, store_sem,
):
    peers = Peers(send_sem, recv_sem)
    loads, stores, stored = Loads(load_sem), Loads(store_sem), []
    get_qk, get_vo, get_fi, get_fo = {}, {}, {}, {}
    for a in (0, 1):
        get_qk[a] = loads.start(qk_all.at[a], wqk.at[a])
        get_vo[a] = loads.start(vo_all.at[a], wvo.at[a])
    get_fi[0] = loads.start(fi_all.at[0], wfi.at[0])
    get_fo[0] = loads.start(fo_all.at[0], wfo.at[0])
    get_qk[2] = loads.start(qk_all.at[2], wqk.at[2])
    get_vo[2] = loads.start(vo_all.at[2], wvo.at[2])
    get_fi[1] = loads.start(fi_all.at[1], wfi.at[1])
    get_fo[1] = loads.start(fo_all.at[1], wfo.at[1])
    peers.greet([peers.across(0)])

    enc_rows, dec_rows, real_rows = enc_x.shape[0], dec_x.shape[0], dec_x_short.shape[0]
    enc_total, dec_total = 4 * enc_rows, 4 * real_rows

    def item_of(place, total):
        scaled = place * item_count[...]
        return sum((scaled >= part * total).astype(jnp.int32) for part in (1, 2, 3))

    def counted(rows, columns, axis):
        return lax.broadcasted_iota(jnp.int32, (rows, columns), axis)

    enc_code = jnp.where(enc_mask[...] == 1, item_of(counted(1, enc_total, 1), enc_total), -1)
    enc_item = item_of(counted(enc_rows, 1, 0) + peers.own * enc_rows, enc_total)
    slot = counted(1, 4 * dec_rows, 1)
    inside = lax.rem(slot, dec_rows)
    key_place = lax.div(slot, dec_rows) * real_rows + inside
    key_item = jnp.where(
        (inside < real_rows) & (dec_mask[...] == 1), item_of(key_place, dec_total), -1
    )
    row = counted(dec_rows, 1, 0)
    row_place = row + peers.own * real_rows
    dec_item = jnp.where(row < real_rows, item_of(row_place, dec_total), -2)
    self_allowed = (dec_item == key_item) & (key_place <= row_place)

    fill = jnp.zeros((dec_rows - real_rows, dec_x.shape[1]), F32)
    for short, padded in ((dec_x_short, dec_x), (dec_cot_short, dec_cot)):
        padded[...] = to_low(jnp.concatenate([short[...].astype(F32), fill], axis=0))

    normed = to_low(norm_gain(enc_x[...].astype(F32), gains[0:1]))
    h0[...] = normed
    get_qk[0].wait()
    get_vo[0].wait()
    project_kv(normed, wqk.at[0], wvo.at[0], enc_kv.at[peers.own])
    enc_gather = Gather(peers, enc_kv, False)
    enc_gather.start()
    normed_dec = to_low(norm_gain(dec_x[...].astype(F32), gains[3:4]))
    hs[...] = normed_dec
    get_qk[1].wait()
    get_vo[1].wait()
    project_kv(normed_dec, wqk.at[1], wvo.at[1], self_kv.at[peers.own])
    self_gather = Gather(peers, self_kv, False)
    self_gather.start()
    dec_gy[0] = dec_cot[...]
    gy_gather = Gather(peers, dec_gy, True)
    gy_gather.start()
    enc_q[...] = to_low(dot(normed, wqk[0, :, :INNER]))
    self_q[...] = to_low(dot(normed_dec, wqk[1, :, :INNER]))

    enc_gather.wait_near()
    enc_gather.relay()
    enc_allowed = enc_item == enc_code

    def enc_bias(head):
        own_rows, period = h0.shape[0], enc_terms.shape[1]
        spread = jnp.broadcast_to(enc_terms[head : head + 1, :], (own_rows, period))
        rolled = pltpu.roll(spread, 0, 1, stride=1, stride_axis=0)
        return rolled[:, : period // 2]

    enc_gather.wait_far()
    attend(enc_q[...], enc_kv, enc_bias, enc_allowed, enc_p, enc_o)
    stored += [stores.start(enc_kv, enc_kv_out), stores.start(enc_p, enc_p_out)]
    for low, high in tiles(enc_mid.shape[1]):
        enc_mid[:, low:high] = enc_x[:, low:high].astype(F32) + dot_last(
            enc_o[...], wvo[0, low:high, INNER:]
        )
    h1[0] = to_low(norm_gain(enc_mid[...], gains[1:2]))
    h1_gather = Gather(peers, h1, True)
    h1_gather.start()
    exchanges = [Exchange(peers, [(h1.at[0], x_h1)], [])]

    def hidden_part(low, high):
        return [(enc_hidden.at[slot], x_enc_hidden.at[slot]) for slot in range(low, high)]

    self_gather.wait_near()
    self_gather.relay()
    gy_gather.wait_near()
    gy_gather.relay()
    self_gather.wait_far()
    gy_gather.wait_far()
    attend(
        self_q[...], self_kv, lambda head: self_bias[head], self_allowed, self_p, self_o
    )
    for low, high in tiles(dec_one.shape[1]):
        dec_one[:, low:high] = dec_x[:, low:high].astype(F32) + dot_last(
            self_o[...], wvo[1, low:high, INNER:]
        )
    normed_dec = to_low(norm_gain(dec_one[...], gains[4:5]))
    hc[...] = normed_dec

    h1_gather.wait_near()
    get_fi[0].wait()
    get_fo[0].wait()
    block, width = h1.shape[1], h1.shape[2]

    def both(buf, slots):
        return buf[slots].reshape((slots.stop - slots.start) * block, buf.shape[2])

    near, away = slice(0, 2), slice(2, 4)
    ff_up(both(h1, near), wfi.at[0], enc_gelu, enc_slope, enc_hidden, near)
    exchanges.append(Exchange(peers, hidden_part(0, 2), []))
    h1_gather.relay()
    h1_gather.wait_far()
    ff_up(both(h1, away), wfi.at[0], enc_gelu, enc_slope, enc_hidden, away)
    stored += [
        stores.start(h1, h1_out), stores.start(enc_gelu, enc_gelu_out),
        stores.start(enc_slope, enc_slope_out), stores.start(enc_hidden, enc_hidden_out),
        stores.start(enc_mid, enc_mid_out),
    ]
    hidden = both(enc_hidden, away)
    for low, high in tiles(width):
        value = dot_last(hidden, wfo[0, low:high, :])
        part[:, low:high] = value[:block]
        send[0, :, low:high] = to_low(value[block:])
    first = peers.send(send.at[0], recv.at[0], peers.sib)
    exchanges.append(Exchange(peers, hidden_part(2, 4), []))
    get_qk[2].wait()
    get_vo[2].wait()
    cross_q[...] = to_low(dot(hc[...], wqk[2, :, :INNER]))
    first.wait_recv()
    send[2] = to_low(part[...] + recv[0].astype(F32))
    second = peers.send(send.at[2], recv.at[2], peers.far)
    hidden = both(enc_hidden, near)
    for low, high in tiles(width):
        value = dot_last(hidden, wfo[0, low:high, :])
        part[:, low:high] = value[:block] + enc_mid[:, low:high]
        send[1, :, low:high] = to_low(value[block:])
    third = peers.send(send.at[1], recv.at[1], peers.sib)
    get_fi[1].wait()
    get_fo[1].wait()
    grad_y = dec_gy[...].reshape(4 * dec_rows, width)
    for low, high in tiles(dec_gh.shape[2]):
        dec_gh[:, :, low:high] = dot(grad_y, wfo[1, :, low:high]).reshape(4, dec_rows, high - low)
    third.wait_recv()
    part[...] = part[...] + recv[1].astype(F32)
    second.wait_recv()
    ended = part[...] + recv[2].astype(F32)
    enc_end[...] = ended
    stored.append(stores.start(enc_end, enc_end_out))
    normed = to_low(norm_gain(ended, gains[2:3]))
    memory[...] = normed

    project_kv(normed, wqk.at[2], wvo.at[2], cross_kv.at[peers.own])
    cross_gather = Gather(peers, cross_kv, False)
    cross_gather.start()
    cross_allowed = dec_item == enc_code
    cross_gather.wait_near()
    cross_gather.relay()
    cross_gather.wait_far()
    attend(cross_q[...], cross_kv, None, cross_allowed, cross_p, cross_o)
    stored.append(stores.start(cross_kv, cross_kv_out))
    for low, high in tiles(dec_two.shape[1]):
        dec_two[:, low:high] = dec_one[:, low:high] + dot_last(
            cross_o[...], wvo[2, low:high, INNER:]
        )
    hf[0] = to_low(norm_gain(dec_two[...], gains[5:6]))
    hf_gather = Gather(peers, hf, True)
    hf_gather.start()

    rows = hf.shape[0] * hf.shape[1]
    hf_gather.wait_near()
    hf_gather.relay()
    hf_gather.wait_far()
    ff_up(hf[...].reshape(rows, width), wfi.at[1], dec_gelu, dec_slope, dec_hidden, slice(0, 4))
    dec_gg[...] = to_low(dec_gh[...] * dec_slope[...])
    dec_gu[...] = to_low(dec_gh[...] * dec_gelu[...])
    for exchange in exchanges:
        exchange.finish_whole()
    wait_all(stored)
    peers.finish()


def ka_call(enc_x, dec_x, dec_cot, gains, enc_terms, self_bias, item_count, enc_mask, dec_mask, attn_qk, attn_vo, ff_in, ff_out):
    rows, width = enc_x.shape
    dec_rows = DEC_PAD
    units = ff_in.shape[3]
    total = enc_mask.shape[1]
    kv_width = 2 * INNER
    shape = jax.ShapeDtypeStruct
    outs = [
        shape((rows, width), LOW), shape((rows, INNER), LOW), shape((4, rows, kv_width), LOW),
        shape((HEADS, rows, total), F32), shape((rows, INNER), LOW), shape((rows, width), F32),
        shape((4, rows, width), LOW), shape((4, rows, units), F32), shape((4, rows, units), F32),
        shape((4, rows, units), LOW), shape((rows, width), F32), shape((rows, width), LOW),
        shape((4, rows, kv_width), LOW),
        shape((dec_rows, width), LOW), shape((dec_rows, INNER), LOW),
        shape((4, dec_rows, kv_width), LOW), shape((HEADS, dec_rows, 4 * dec_rows), F32),
        shape((dec_rows, INNER), LOW), shape((dec_rows, width), F32),
        shape((dec_rows, width), LOW), shape((dec_rows, INNER), LOW),
        shape((HEADS, dec_rows, total), F32), shape((dec_rows, INNER), LOW),
        shape((dec_rows, width), F32),
        shape((4, dec_rows, width), LOW), shape((4, dec_rows, width), LOW),
        shape((4, dec_rows, units), LOW), shape((4, dec_rows, units), LOW),
        shape((4, dec_rows, units), LOW), shape((dec_rows, width), LOW),
        shape((dec_rows, width), LOW),
    ]
    traded = [shape((rows, width), LOW), shape((4, rows, units), LOW)]
    vmem = pl.BlockSpec(memory_space=pltpu.VMEM)
    hbm = pl.BlockSpec(memory_space=pltpu.HBM)
    copies = 3 * 6 + 3 + 1 + 4
    apart = (2, 3, 5, 6, 7, 8, 9, 10, 12)
    return pl.pallas_call(
        ka_kernel,
        out_shape=outs + traded,
        in_specs=[vmem] * 9 + [hbm] * 4,
        out_specs=[hbm if place in apart else vmem for place in range(len(outs))]
        + [hbm] * len(traded),
        scratch_shapes=[
            pltpu.VMEM(attn_qk.shape, LOW), pltpu.VMEM(attn_vo.shape, LOW),
            pltpu.VMEM(ff_in.shape, LOW), pltpu.VMEM(ff_out.shape, LOW),
            pltpu.VMEM((rows, width), F32), pltpu.VMEM((3, rows, width), LOW),
            pltpu.VMEM((3, rows, width), LOW), pltpu.VMEM((4, dec_rows, units), F32),
            pltpu.VMEM((4, dec_rows, units), F32), pltpu.VMEM((4, dec_rows, units), F32),
            *[pltpu.VMEM(outs[place].shape, outs[place].dtype) for place in apart],
            pltpu.SemaphoreType.DMA((copies,)), pltpu.SemaphoreType.DMA((copies,)),
            pltpu.SemaphoreType.DMA((10,)), pltpu.SemaphoreType.DMA((len(apart),)),
        ],
        compiler_params=pltpu.CompilerParams(
            collective_id=0, has_side_effects=True, vmem_limit_bytes=VMEM_BYTES
        ),
        name="forward_chain",
    )(enc_x, dec_x, dec_cot, gains, enc_terms, self_bias, item_count, enc_mask, dec_mask,
      attn_qk, attn_vo, ff_in, ff_out)


def prepare(item_count, enc_mask, dec_mask, enc_buckets, dec_buckets, tables, enc_own, dec_own):
    tensor_id = lax.axis_index("tensor")
    enc_total, dec_total = enc_mask.shape[0], dec_mask.shape[0]
    slot = jnp.arange(4 * DEC_PAD)
    place = slot // DEC_PAD * dec_own + slot % DEC_PAD
    row_place = tensor_id * dec_own + jnp.arange(DEC_PAD)
    dec_live = jnp.pad(dec_mask.reshape(4, dec_own), ((0, 0), (0, DEC_PAD - dec_own)))
    onehot = (enc_buckets[:, None] == jnp.arange(BUCKETS)[None, :]).astype(F32)
    terms = jnp.dot(tables[0].T, onehot.T, precision=HIGH)
    terms = jnp.pad(terms, ((0, 2), (0, 1)))
    period = 2 * enc_total
    doubled = jnp.concatenate([terms, terms], axis=1)
    shift = (enc_total - 1 - tensor_id * enc_own + period) % period
    enc_terms = lax.dynamic_slice_in_dim(doubled, shift, period, 1)
    far_back = jnp.clip(row_place[:, None] - place[None, :], 0, dec_total - 1)
    far_back = (far_back[None] == jnp.arange(dec_total)[:, None, None]).astype(F32)
    far_back = far_back.reshape(dec_total, -1)
    dec_onehot = (dec_buckets[:, None] == jnp.arange(BUCKETS)[None, :]).astype(F32)
    dec_terms = jnp.dot(tables[1].T, dec_onehot.T, precision=HIGH)
    self_bias = jnp.dot(dec_terms, far_back, precision=HIGH).reshape(
        HEADS, DEC_PAD, 4 * DEC_PAD
    )
    spots = jnp.pad(onehot, ((0, 1), (0, 0)))
    enc_spots = lax.dynamic_slice_in_dim(
        spots, enc_total - enc_own - tensor_id * enc_own, enc_total + enc_own, 0
    )
    self_bucket = jnp.dot(
        dec_buckets.astype(F32)[None, :], far_back, precision=HIGH
    ).reshape(DEC_PAD, 4 * DEC_PAD)
    return (
        enc_terms, self_bias, item_count.reshape(1, 1), enc_mask.reshape(1, enc_total),
        dec_live.reshape(1, 4 * DEC_PAD),
    ), (enc_spots, self_bucket)


RING = 4


def chunk_of(size):
    return 512 if size <= 8 else 256


def lag_of(steps):
    return 2 if steps <= 3 else 1


class Reduce:
    def __init__(self, peers, places, product, columns, total, send, recv, slot, finish, ships):
        self.ships = ships
        self.peers, self.places, self.product, self.columns = peers, places, product, columns
        self.total, self.send, self.recv, self.slot, self.done = total, send, recv, slot, finish
        self.steps = len(places) + 1

    def buffers(self, step):
        lanes = pl.ds(0, self.columns)
        return (
            self.send[step].at[self.slot % self.send[step].shape[0], :, lanes],
            self.recv[step].at[self.slot, :, lanes],
        )

    def ship(self, step, value, place):
        source, target = self.buffers(step)
        key = (id(self.send), step, self.slot % self.send[step].shape[0])
        if key in self.ships:
            self.ships[key].wait_send()
            self.peers.copies = [c for c in self.peers.copies if c is not self.ships[key]]
        source[...] = to_low(value)
        self.copy = self.peers.send(source, target, self.peers.across(place))
        self.ships[key] = self.copy

    def run(self, step):
        lanes = pl.ds(0, self.columns)
        if step == 0:
            here = self.peers.bit(self.places[0])
            self.ship(0, self.product(1 - here), self.places[0])
            self.height = self.send[0].shape[1]
            self.start = 0
            self.total[: self.height, lanes] = self.product(here)
            return
        self.copy.wait_recv()
        arrived = self.buffers(step - 1)[1]
        if step == self.steps - 1:
            rows = pl.ds(self.start, self.height)
            self.done(self.total[rows, lanes] + arrived[...].astype(F32))
            return
        self.height //= 2
        place = self.places[step]
        here = self.peers.bit(place)
        away = pl.multiple_of(self.start + (1 - here) * self.height, 16)
        kept = pl.multiple_of(self.start + here * self.height, 16)
        from_away = pl.multiple_of((1 - here) * self.height, 16)
        from_kept = pl.multiple_of(here * self.height, 16)
        self.ship(
            step,
            self.total[pl.ds(away, self.height), lanes]
            + arrived[pl.ds(from_away, self.height), :].astype(F32),
            place,
        )
        self.total[pl.ds(kept, self.height), lanes] += arrived[
            pl.ds(from_kept, self.height), :
        ].astype(F32)
        self.start = kept


class Stream:
    def __init__(self, items, lag):
        self.items, self.lag, self.now = items, lag, 0
        self.last = max(place + lag * (item.steps - 1) for place, item in enumerate(items))

    def pump(self, ticks=1):
        for unused in range(ticks):
            now = self.now
            if now > self.last:
                return
            self.now += 1
            for place, item in reversed(list(enumerate(self.items))):
                step, odd = divmod(now - place, self.lag)
                if odd == 0 and 0 < step < item.steps:
                    item.run(step)
            if now < len(self.items):
                for action in self.items[now].before:
                    if action is not None:
                        action()
                self.items[now].run(0)

    def drain(self):
        self.pump(self.last + 1 - self.now)


def flat(value):
    return value.reshape(value.shape[0] * value.shape[1], value.shape[2])


def choose_rows(peers, layout, first, rows, chosen, start):
    size, block, padded = layout
    bits = size.bit_length() - 1
    width = rows.shape[1]
    for known in range(2**first):

        def run(known=known):
            for half in range(2):
                for place in range(chosen.shape[1] // padded):
                    owner = known + (half << first)
                    for bit in range(first + 1, bits):
                        owner += ((place >> (bits - 1 - bit)) & 1) << bit
                    left = owner * block // 128 * 128
                    right = min(-(-(owner + 1) * block // 128) * 128, width)
                    inside = lax.broadcasted_iota(jnp.int32, (padded, right - left), 0)
                    lane = lax.broadcasted_iota(jnp.int32, (padded, right - left), 1)
                    picked = (lane - inside == owner * block - left) & (inside < block)
                    pick = to_low(jnp.where(picked, 1.0, 0.0))
                    for low, high in tiles(rows.shape[0]):
                        chosen[
                            half, place * padded : (place + 1) * padded,
                            start + low : start + high,
                        ] = to_low(dot_last(pick, rows[low:high, left:right]))

        if first:
            same = peers.bit(0) == known % 2
            for bit in range(1, first):
                same = same & (peers.bit(bit) == (known >> bit) % 2)
            pl.when(same)(run)
        else:
            run()


class Products:
    def __init__(self, peers, layout, first, steps, chosen, total, *buffers):
        self.peers, self.layout, self.first = peers, layout, first
        self.chosen, self.total = chosen, total
        self.places = list(range(first, steps))
        self.send, self.recv = buffers[: steps - first], buffers[steps - first :]
        self.items, self.ships = [], {}

    def choose(self, lefts, before):
        def run():
            if before is not None:
                before()
            rows = lefts[0].shape[0] * lefts[0].shape[1]
            for part, left in enumerate(lefts):
                choose_rows(
                    self.peers, self.layout, self.first, flat(left[...]), self.chosen, part * rows
                )

        return run

    def add(self, lefts, rights, out, before=None, ready=()):
        actions = [] if lefts is None else [self.choose(lefts, before)]
        for kind, parts in enumerate(rights):
            rows = parts[0].shape[0] * parts[0].shape[1]
            if ready:
                actions.append(ready[kind])
            for low, high in tiles(parts[0].shape[2], self.total.shape[2]):

                def product(half, parts=parts, low=low, high=high):
                    value = None
                    for part, right in enumerate(parts):
                        here = dot(
                            self.chosen[half, :, part * rows : (part + 1) * rows],
                            flat(right[:, :, low:high]),
                        )
                        value = here if value is None else value + here
                    return value

                def finish(value, kind=kind, low=low, high=high):
                    out[kind, :, low:high] = value[: out.shape[1]]

                count = len(self.items)
                item = Reduce(
                    self.peers, self.places, product, high - low,
                    self.total.at[count % self.total.shape[0]], self.send, self.recv, count,
                    finish, self.ships,
                )
                item.before, actions = actions, []
                self.items.append(item)


def product_scratch(size, padded, rows, items, first, chunk):
    chosen = size * padded >> first
    steps = size.bit_length() - 1
    heights = [chosen >> (step + 1) for step in range(steps - first)]
    return [
        pltpu.VMEM((2, chosen // 2, rows), LOW),
        pltpu.VMEM((lag_of(steps) * (steps - first) + 1, chosen // 2, chunk), F32),
        *[pltpu.VMEM((RING, height, chunk), LOW) for height in heights],
        *[pltpu.VMEM((items, height, chunk), LOW) for height in heights],
    ]


def to_owners(peers, sources, target, rows_of, own_sem):
    sends = []
    for peer in (peers.far, peers.diag, peers.sib):
        place = peers.used
        peers.used += 1
        for role in range(4):
            rows = rows_of[role]

            def copy(role=role, rows=rows, place=place, peer=peer):
                return pltpu.make_async_remote_copy(
                    src_ref=sources[role],
                    dst_ref=target.at[peers.own, pl.ds(0, rows)],
                    send_sem=peers.send_sem.at[place],
                    recv_sem=peers.recv_sem.at[place],
                    device_id=peers.device(peer),
                    device_id_type=pl.DeviceIdType.MESH,
                )

            @pl.when(peer == role)
            def _(copy=copy):
                copy().start()

            sends.append((peer, role, copy))
    for role in range(4):

        def keep(role=role):
            return pltpu.make_async_copy(
                sources[role], target.at[peers.own, pl.ds(0, rows_of[role])], own_sem
            )

        @pl.when(peers.own == role)
        def _(keep=keep):
            keep().start()

        sends.append((None, role, keep))
    return sends


def owners_done(peers, sends):
    for peer, role, copy in sends:

        @pl.when(peers.own == role)
        def _(copy=copy, peer=peer):
            copy().wait() if peer is None else copy().wait_recv()

        if peer is not None:

            @pl.when(peer == role)
            def _(copy=copy):
                copy().wait_send()


def kv_back(grad_kv, wqk, wvo, low, high):
    return dot_last(grad_kv[:, :INNER], wqk[low:high, INNER:]) + dot_last(
        grad_kv[:, INNER:], wvo[low:high, :INNER]
    )


class SumBlocks:
    def __init__(self, peers, buf, send, recv):
        self.peers, self.buf, self.send, self.recv = peers, buf, send, recv
        send[0] = to_low(buf[peers.diag])
        send[1] = to_low(buf[peers.sib])
        self.first = peers.send(send.at[0], recv.at[0], peers.sib)
        self.third = peers.send(send.at[1], recv.at[1], peers.sib)

    def cross(self):
        peers = self.peers
        self.first.wait_recv()
        self.send[2] = to_low(self.buf[peers.far] + self.recv[0].astype(F32))
        self.second = peers.send(self.send.at[2], self.recv.at[2], peers.far)

    def result(self):
        self.third.wait_recv()
        value = self.buf[self.peers.own] + self.recv[1].astype(F32)
        self.second.wait_recv()
        return value + self.recv[2].astype(F32)


class SumNear:
    def __init__(self, peers, part_of, block, total, send, recv):
        self.peers, self.total, self.send, self.recv = peers, total, send, recv
        for low, high in tiles(send.shape[2]):
            value = part_of(low, high)
            total[0, :, low:high] = value[:block]
            send[1, :, low:high] = to_low(value[block : 2 * block])
            total[1, :, low:high] = value[2 * block : 3 * block]
            send[0, :, low:high] = to_low(value[3 * block :])
        self.first = peers.send(send.at[0], recv.at[0], peers.sib)
        self.third = peers.send(send.at[1], recv.at[1], peers.sib)

    def cross(self):
        self.first.wait_recv()
        self.send[2] = to_low(self.total[1] + self.recv[0].astype(F32))
        self.second = self.peers.send(self.send.at[2], self.recv.at[2], self.peers.far)

    def result(self):
        self.third.wait_recv()
        value = self.total[0] + self.recv[1].astype(F32)
        self.second.wait_recv()
        return value + self.recv[2].astype(F32)


def kb_kernel(
    dec_gg, dec_gu, dec_hidden, dec_cot, dec_two, dec_one, gains, cross_q, hf,
    qk_all, vo_all, fi_all, fo_all, dec_gy, cross_kv_all, cross_p_all, enc_end_all,
    enc_gelu_all, enc_slope_all,
    dec_out, cross_gy, cross_gq, cross_gk, cross_gv, dec_one_grad, enc_end_grad, enc_gy, enc_gg, enc_gu,
    gains_grad, dec_gate, x_dec_hidden, x_dec_gy, x_dec_gu, x_hf,
    wqk, wvo, wfi, wfo, grad_kv, kv_send, kv_recv, row_total, row_send, row_recv, out_total,
    out_send, out_recv, x_dec_gg, cross_kv, cross_p, enc_end, enc_gelu, enc_slope,
    *rest,
    layout, steps,
):
    scratch, (send_sem, recv_sem, load_sem) = rest[:-3], rest[-3:]
    peers = Peers(send_sem, recv_sem)
    loads = Loads(load_sem)
    get_fi = loads.start(fi_all.at[1], wfi)
    get_cross = [
        loads.start(vo_all.at[2], wvo), loads.start(cross_kv_all, cross_kv),
        loads.start(cross_p_all, cross_p), loads.start(qk_all.at[2], wqk),
        loads.start(enc_end_all, enc_end),
    ]
    get_fo1 = loads.start(fo_all.at[1], wfo.at[1])
    get_up = [
        loads.start(fo_all.at[0], wfo.at[0]), loads.start(enc_gelu_all, enc_gelu),
        loads.start(enc_slope_all, enc_slope),
    ]
    peers.greet([peers.across(place) for place in range(steps)])
    first = Exchange(peers, [(dec_gg, x_dec_gg)], [(hf, x_hf)])
    later = [
        Exchange(
            peers, [(dec_gu, x_dec_gu), (dec_hidden, x_dec_hidden)], [(dec_gy, x_dec_gy)]
        )
    ]

    def arrived():
        first.finish_rows()
        first.finish_whole()

    products = Products(peers, layout, 1, steps, *scratch)
    products.add(
        [hf, x_hf], [(dec_gg, x_dec_gg)], dec_gate, before=arrived
    )
    stream = Stream(products.items, lag_of(steps))
    width = dec_two.shape[1]
    block = dec_two.shape[0]
    units = dec_gg.shape[2]
    gains_grad[...] = jnp.zeros_like(gains_grad)

    get_fi.wait()
    gate, up_proj = dec_gg[...].reshape(4 * block, units), dec_gu[...].reshape(4 * block, units)

    def grad_rows_part(low, high):
        return dot_last(gate, wfi[0, low:high, :]) + dot_last(up_proj, wfi[1, low:high, :])

    grad_rows = SumNear(peers, grad_rows_part, block, row_total, row_send, row_recv)
    grad_rows.cross()
    wait_all(get_cross)
    first.spread()
    value, gain_row = norm_back(dec_two[...], gains[5:6], grad_rows.result())
    gains_grad[5:6] = gain_row
    residual = dec_cot[...].astype(F32) + value
    grad_y = to_low(residual)
    cross_gy[...] = grad_y

    grad_out = to_low(dot(grad_y, wvo[:, INNER:]))
    first.relay()
    stream.pump(1)
    attend_back(cross_q[...], cross_kv, cross_p, grad_out, cross_gq, grad_kv, None)
    kv_sum = SumBlocks(peers, grad_kv, kv_send, kv_recv)
    kv_sum.cross()
    stream.pump(1)
    for low, high in tiles(width):
        row_total[0, :, low:high] = dot_last(cross_gq[...], wqk[low:high, :INNER])
    value, gain_row = norm_back(dec_one[...], gains[4:5], row_total[0])
    gains_grad[4:5] = gain_row
    dec_one_grad[...] = residual + value
    stream.pump(1)
    own_kv = to_low(kv_sum.result())
    cross_gk[...] = own_kv[:, :INNER]
    cross_gv[...] = own_kv[:, INNER:]
    for low, high in tiles(width):
        enc_end_grad[:, low:high] = kv_back(own_kv, wqk, wvo, low, high)
    value, gain_row = norm_back(enc_end[...], gains[2:3], enc_end_grad[...])
    gains_grad[2:3] = gain_row
    enc_end_grad[...] = value
    enc_gy[0] = to_low(value)
    gy_gather = Gather(peers, enc_gy, True)
    gy_gather.start()

    get_fo1.wait()
    hidden = dec_hidden[...].reshape(4 * block, units)
    out_sum = SumNear(
        peers, lambda low, high: dot_last(hidden, wfo[1, low:high, :]), block, out_total,
        out_send, out_recv,
    )

    stream.pump(1)
    for exchange in later:
        exchange.spread()
    wait_all(get_up)
    rows = enc_gy.shape[1]

    def gate_grads(slots):
        grad_y = enc_gy[slots].reshape(2 * rows, width)
        for low, high in tiles(units):
            grad_h = dot(grad_y, wfo[0, :, low:high]).reshape(2, rows, high - low)
            enc_gg[slots, :, low:high] = to_low(grad_h * enc_slope[slots, :, low:high])
            enc_gu[slots, :, low:high] = to_low(grad_h * enc_gelu[slots, :, low:high])

    gy_gather.wait_near()
    stream.pump(1)
    gate_grads(slice(0, 2))
    gy_gather.relay()
    out_sum.cross()
    stream.pump(1)
    gy_gather.wait_far()
    gate_grads(slice(2, 4))
    stream.pump(1)
    for exchange in later:
        exchange.relay()
    stream.pump(1)
    dec_out[...] = to_low(dec_two[...] + out_sum.result())
    stream.drain()
    for exchange in later:
        exchange.finish_rows()
        exchange.finish_whole()
    peers.finish()


def kb_call(dec_gg, dec_gu, dec_hidden, dec_cot, dec_two, dec_one, gains, cross_q, cross_kv,
            cross_p, enc_end, enc_gelu, enc_slope, attn_qk, attn_vo, ff_in, ff_out, hf, dec_gy,
            size, block, padded):
    rows, width = enc_end.shape
    dec_rows = dec_two.shape[0]
    units = ff_in.shape[3]
    kv_width = 2 * INNER
    shape = jax.ShapeDtypeStruct
    outs = [
        shape((dec_rows, width), LOW), shape((dec_rows, width), LOW),
        shape((dec_rows, INNER), LOW), shape((rows, INNER), LOW), shape((rows, INNER), LOW),
        shape((dec_rows, width), F32), shape((rows, width), F32), shape((4, rows, width), LOW), shape((4, rows, units), LOW),
        shape((4, rows, units), LOW), shape((8, width), F32), shape((1, block, units), F32),
    ]
    traded = [
        shape(value.shape, LOW)
        for value in (dec_hidden, dec_gy, dec_gu, hf)
    ]
    steps = size.bit_length() - 1
    items = len(tiles(units, 256))
    vmem = pl.BlockSpec(memory_space=pltpu.VMEM)
    hbm = pl.BlockSpec(memory_space=pltpu.HBM)
    copies = 3 * 3 + 3 + 5 + 6 + items * (steps - 1)
    return pl.pallas_call(
        functools.partial(kb_kernel, layout=(size, block, padded), steps=steps),
        out_shape=outs + traded,
        in_specs=[vmem] * 9 + [hbm] * 10,
        out_specs=[vmem] * len(outs) + [hbm] * (len(traded) - 1) + [vmem],
        scratch_shapes=[
            pltpu.VMEM(attn_qk.shape[1:], LOW), pltpu.VMEM(attn_vo.shape[1:], LOW),
            pltpu.VMEM(ff_in.shape[1:], LOW), pltpu.VMEM(ff_out.shape, LOW),
            pltpu.VMEM((4, rows, kv_width), F32), pltpu.VMEM((3, rows, kv_width), LOW),
            pltpu.VMEM((3, rows, kv_width), LOW), pltpu.VMEM((2, dec_rows, width), F32),
            pltpu.VMEM((3, dec_rows, width), LOW), pltpu.VMEM((3, dec_rows, width), LOW),
            pltpu.VMEM((2, dec_rows, width), F32), pltpu.VMEM((3, dec_rows, width), LOW),
            pltpu.VMEM((3, dec_rows, width), LOW),
            pltpu.VMEM(dec_gg.shape, LOW),
            pltpu.VMEM(cross_kv.shape, LOW), pltpu.VMEM(cross_p.shape, F32),
            pltpu.VMEM(enc_end.shape, F32), pltpu.VMEM(enc_gelu.shape, F32),
            pltpu.VMEM(enc_slope.shape, F32),
            *product_scratch(size, padded, 2 * 4 * dec_rows, items, 1, 256),
            pltpu.SemaphoreType.DMA((copies,)), pltpu.SemaphoreType.DMA((copies,)),
            pltpu.SemaphoreType.DMA((10,)),
        ],
        compiler_params=pltpu.CompilerParams(
            collective_id=1, has_side_effects=True, vmem_limit_bytes=VMEM_BYTES
        ),
        name="middle_chain",
    )(dec_gg, dec_gu, dec_hidden, dec_cot, dec_two, dec_one, gains, cross_q, hf,
      attn_qk, attn_vo, ff_in, ff_out, dec_gy, cross_kv, cross_p, enc_end,
      enc_gelu, enc_slope)


def kc_kernel(
    enc_gg, enc_gu, gains, gains_mid, enc_q, dec_one_grad, dec_x, self_q, self_kv, self_p,
    enc_spots, self_bucket,
    qk_all, vo_all, fi_all, enc_end_grad_all, enc_mid_all, enc_x_all, enc_kv_all, enc_p_all,
    enc_gy_all, hf_all, x_hf_all, dec_gu_all, x_dec_gu_all, dec_gy_all, x_dec_gy_all,
    dec_hidden_all, x_dec_hidden_all, enc_hidden_all,
    x_enc_hidden_all, h1_all, x_h1_rows, hs, hc, memory, cross_gy, cross_gq, cross_gk, cross_gv,
    cross_o,
    enc_grad, enc_ay, enc_gq, enc_gk, enc_gv, dec_grad, self_gy, self_gq, self_gk, self_gv,
    small, ffout, dec_up, chosen_h1, left_cross, right_cross, left_self, x_enc_gg, x_enc_gu, x_h1,
    wqk, wvo, wfi, enc_gs, self_gs, part, send, recv, enc_gkv_full, kv_send, kv_recv,
    self_gkv_full, self_send, self_recv, x_enc_gy, enc_end_grad, enc_mid, enc_x, enc_kv, enc_p,
    enc_gy, hfs, dec_gus, dec_gys, dec_hiddens, enc_hidden, x_enc_hidden, stage, *rest,
    layout, steps,
):
    dec_scratch, enc_scratch = rest[: 2 * steps], rest[2 * steps : -4]
    send_sem, recv_sem, load_sem, own_sem = rest[-4:]
    peers = Peers(send_sem, recv_sem)
    loads = Loads(load_sem)
    get_dec = [
        loads.start(source, target.at[place])
        for sources, target in (
            ((hf_all, x_hf_all), hfs), ((dec_gu_all, x_dec_gu_all), dec_gus),
            ((dec_gy_all, x_dec_gy_all), dec_gys), ((dec_hidden_all, x_dec_hidden_all), dec_hiddens),
        )
        for place, source in enumerate(sources)
    ]
    get_fi = loads.start(fi_all.at[0], wfi)
    get_vo1 = loads.start(vo_all.at[1], wvo.at[1])
    get_mid = [
        loads.start(enc_mid_all, enc_mid), loads.start(enc_end_grad_all, enc_end_grad),
        loads.start(vo_all.at[0], wvo.at[0]), loads.start(enc_kv_all, enc_kv),
        loads.start(enc_p_all, enc_p),
    ]
    get_out = [
        loads.start(enc_gy_all, enc_gy), loads.start(enc_hidden_all, enc_hidden),
        loads.start(x_enc_hidden_all, x_enc_hidden),
    ]
    get_last = [
        loads.start(qk_all.at[0], wqk.at[0]), loads.start(qk_all.at[1], wqk.at[1]),
        loads.start(enc_x_all, enc_x),
    ]
    for buf in (left_cross, right_cross):
        buf[...] = jnp.zeros_like(buf)
    peers.greet([peers.diag] + [peers.across(place) for place in range(steps)])
    exchange = Exchange(
        peers, [(enc_gg, x_enc_gg), (enc_gu, x_enc_gu)], [(enc_gy_all, x_enc_gy)]
    )
    dec_rows, enc_rows = hs.shape[0], memory.shape[0]
    short = (dec_rows,) * 4
    mixed = (dec_rows, enc_rows, enc_rows, dec_rows)
    owned = [
        to_owners(peers, (hc, memory, memory, cross_gy), left_cross, mixed, own_sem.at[0]),
        to_owners(
            peers, (cross_gq, cross_gk, cross_gv, cross_o), right_cross, mixed, own_sem.at[1]
        ),
    ]

    h1_gather = Gather(peers, x_h1, True, x_h1_rows)

    def arrived():
        wait_all(get_out)
        exchange.relay()
        exchange.finish_rows()

    def ready():
        wait_all(get_dec)

    dec_products = Products(peers, layout, 1, steps, *dec_scratch)
    dec_products.add(
        [hfs.at[place] for place in range(2)], [[dec_gus.at[place] for place in range(2)]], dec_up,
        before=ready,
    )
    dec_products.add(
        [dec_gys.at[place] for place in range(2)], [[dec_hiddens.at[place] for place in range(2)]],
        ffout.at[pl.ds(1, 1)],
    )
    enc_products = Products(peers, layout, 1, steps, *enc_scratch)
    enc_products.add(
        [enc_gy, x_enc_gy], [(enc_hidden, x_enc_hidden)], ffout.at[pl.ds(0, 1)], before=arrived
    )
    stream = Stream(dec_products.items + enc_products.items, lag_of(steps))
    staged = []

    def fetch_rows(place):
        if place == 5:
            h1_gather.wait_near()
            h1_gather.relay()
        if place == 7:
            h1_gather.wait_far()
        source = x_h1_rows if place == 4 else (h1_all, x_h1)[place // 4].at[place % 4]
        staged.append(loads.start(source, stage.at[place % 2]))

    def choose_next(place):
        staged.pop(0).wait()
        choose_rows(peers, layout, 1, stage[place % 2], chosen_h1, place * enc_rows)
        if place + 2 < 8:
            fetch_rows(place + 2)

    rows, width = enc_mid.shape
    units = enc_gg.shape[2]
    small[...] = jnp.zeros_like(small)
    small[:8] = gains_mid[...]

    stream.pump(2)
    get_fi.wait()

    def grad_part(slots, low, high):
        gate = enc_gg[slots].reshape(2 * rows, units)
        up_proj = enc_gu[slots].reshape(2 * rows, units)
        return dot_last(gate, wfi[0, low:high, :]) + dot_last(up_proj, wfi[1, low:high, :])

    for low, high in tiles(width):
        value = grad_part(slice(2, 4), low, high)
        part[:, low:high] = value[:rows]
        send[0, :, low:high] = to_low(value[rows:])
    for place in range(2):
        fetch_rows(place)
    first = peers.send(send.at[0], recv.at[0], peers.sib)
    stream.pump(1)
    get_vo1.wait()
    residual_dec = dec_one_grad[...]
    grad_y = to_low(residual_dec)
    self_gy[...] = grad_y
    owned.append(to_owners(peers, (hs, hs, hs, self_gy), left_self, short, own_sem.at[2]))
    grad_out_dec = to_low(dot(grad_y, wvo[1, :, INNER:]))
    exchange.spread()
    first.wait_recv()
    send[2] = to_low(part[...] + recv[0].astype(F32))
    second = peers.send(send.at[2], recv.at[2], peers.far)
    for low, high in tiles(width):
        value = grad_part(slice(0, 2), low, high)
        part[:, low:high] = value[:rows]
        send[1, :, low:high] = to_low(value[rows:])
    third = peers.send(send.at[1], recv.at[1], peers.sib)

    stream.pump(1)
    attend_back(self_q[...], self_kv, self_p, grad_out_dec, self_gq, self_gkv_full, self_gs)
    self_sum = SumBlocks(peers, self_gkv_full, self_send, self_recv)
    self_sum.cross()

    stream.pump(1)
    for place in range(3):
        choose_next(place)

    columns = []
    for bucket in range(BUCKETS):
        here = jnp.where(self_bucket[...] == bucket, 1.0, 0.0)
        sums = jnp.sum(self_gs[...].astype(F32) * here[None], axis=1)
        columns.append(jnp.sum(sums, axis=1, keepdims=True))
    self_table = jnp.concatenate(columns, axis=1)

    stream.pump(1)
    third.wait_recv()
    part[...] = part[...] + recv[1].astype(F32)
    second.wait_recv()
    wait_all(get_mid)
    value, gain_row = norm_back(enc_mid[...], gains[1:2], part[...] + recv[2].astype(F32))
    small[1:2] = gain_row
    residual = enc_end_grad[...] + value
    grad_y = to_low(residual)
    enc_ay[...] = grad_y
    enc_grad[...] = residual

    h1_gather.start()
    grad_out = to_low(dot(grad_y, wvo[0, :, INNER:]))
    attend_back(enc_q[...], enc_kv, enc_p, grad_out, enc_gq, enc_gkv_full, enc_gs)
    enc_sum = SumBlocks(peers, enc_gkv_full, kv_send, kv_recv)
    stream.pump(2)
    wait_all(get_last)
    for low, high in tiles(width):
        part[:, low:high] = dot_last(enc_gq[...], wqk[0, low:high, :INNER])
    enc_sum.cross()

    stream.pump(1)
    choose_next(3)
    own_kv = to_low(self_sum.result())
    self_gk[...] = own_kv[:, :INNER]
    self_gv[...] = own_kv[:, INNER:]
    for low, high in tiles(width):
        dec_grad[:, low:high] = dot_last(self_gq[...], wqk[1, low:high, :INNER]) + kv_back(
            own_kv, wqk.at[1], wvo.at[1], low, high
        )
    value, gain_row = norm_back(dec_x[...].astype(F32), gains[3:4], dec_grad[...])
    small[3:4] = gain_row
    dec_grad[...] = residual_dec + value

    turn = lax.broadcasted_iota(jnp.int32, (rows, rows), 0) + lax.broadcasted_iota(
        jnp.int32, (rows, rows), 1
    )
    turn = jnp.where(turn == rows - 1, 1.0, 0.0).astype(LOW)
    offsets = []
    for head in range(HEADS):
        turned = dot(turn, enc_gs[head])
        spread = jnp.concatenate([turned, jnp.zeros((rows, rows), F32)], axis=1)
        spread = pltpu.roll(spread, 0, 1, stride=1, stride_axis=0)
        offsets.append(jnp.sum(spread, axis=0, keepdims=True))
    enc_table = jnp.dot(
        jnp.concatenate(offsets + [jnp.zeros((2, offsets[0].shape[1]), F32)], axis=0),
        enc_spots[...], precision=HIGH, preferred_element_type=F32,
    )
    small[8:, :BUCKETS] = enc_table
    small[8 : 8 + HEADS, PAIR : PAIR + BUCKETS] = self_table

    stream.pump(2)
    own_kv = to_low(enc_sum.result())
    enc_gk[...] = own_kv[:, :INNER]
    enc_gv[...] = own_kv[:, INNER:]
    for low, high in tiles(width):
        part[:, low:high] += kv_back(own_kv, wqk.at[0], wvo.at[0], low, high)
    value, gain_row = norm_back(enc_x[...].astype(F32), gains[0:1], part[...])
    small[0:1] = gain_row
    enc_grad[...] += value
    for place in range(4, 8):
        stream.pump(1)
        choose_next(place)
    stream.drain()
    exchange.finish_whole()
    for sends in owned:
        owners_done(peers, sends)
    peers.finish()


def kc_call(size, block, padded, near, streamed):
    enc_gg, dec_x = near[0], near[6]
    attn_qk, attn_vo, ff_in = streamed[:3]
    rows, width = streamed[4].shape
    dec_rows = dec_x.shape[0]
    units = ff_in.shape[3]
    kv_width = 2 * INNER
    total = 4 * rows
    half = size * padded // 2
    steps = size.bit_length() - 1
    items = len(tiles(units, chunk_of(size)))
    shape = jax.ShapeDtypeStruct
    outs = [
        shape((rows, width), F32), shape((rows, width), LOW), shape((rows, INNER), LOW),
        shape((rows, INNER), LOW), shape((rows, INNER), LOW),
        shape((dec_rows, width), F32), shape((dec_rows, width), LOW),
        shape((dec_rows, INNER), LOW), shape((dec_rows, INNER), LOW),
        shape((dec_rows, INNER), LOW),
        shape((16, width), F32), shape((2, block, units), F32), shape((1, block, units), F32),
        shape((2, half // 2, 2 * total), LOW), shape((4, rows, width), LOW),
        shape((4, rows, INNER), LOW),
    ]
    apart = [
        shape((4, dec_rows, width), LOW),
        shape(enc_gg.shape, LOW), shape(enc_gg.shape, LOW), shape((4, rows, width), LOW),
    ]
    vmem = pl.BlockSpec(memory_space=pltpu.VMEM)
    hbm = pl.BlockSpec(memory_space=pltpu.HBM)
    copies = 3 * 3 + 3 + 3 + 3 * 3 + 3 + 3 * items * (steps - 1)
    return pl.pallas_call(
        functools.partial(kc_kernel, layout=(size, block, padded), steps=steps),
        out_shape=outs + apart,
        in_specs=[vmem] * len(near) + [hbm] * len(streamed),
        out_specs=[vmem] * len(outs) + [hbm] * len(apart),
        scratch_shapes=[
            pltpu.VMEM((2,) + attn_qk.shape[1:], LOW), pltpu.VMEM((2,) + attn_vo.shape[1:], LOW),
            pltpu.VMEM(ff_in.shape[1:], LOW), pltpu.VMEM((HEADS, rows, total), LOW),
            pltpu.VMEM((HEADS, dec_rows, 4 * dec_rows), LOW),
            pltpu.VMEM((rows, width), F32), pltpu.VMEM((3, rows, width), LOW),
            pltpu.VMEM((3, rows, width), LOW),
            pltpu.VMEM((4, rows, kv_width), F32), pltpu.VMEM((3, rows, kv_width), LOW),
            pltpu.VMEM((3, rows, kv_width), LOW),
            pltpu.VMEM((4, dec_rows, kv_width), F32), pltpu.VMEM((3, dec_rows, kv_width), LOW),
            pltpu.VMEM((3, dec_rows, kv_width), LOW), pltpu.VMEM((4, rows, width), LOW),
            pltpu.VMEM((rows, width), F32), pltpu.VMEM((rows, width), F32),
            pltpu.VMEM((rows, width), LOW), pltpu.VMEM((4, rows, kv_width), LOW),
            pltpu.VMEM((HEADS, rows, total), F32), pltpu.VMEM((4, rows, width), LOW),
            *[pltpu.VMEM((2, 4, dec_rows, width), LOW), pltpu.VMEM((2, 4, dec_rows, units), LOW)] * 2,
            pltpu.VMEM((4, rows, units), LOW), pltpu.VMEM((4, rows, units), LOW),
            pltpu.VMEM((2, rows, width), LOW),
            *product_scratch(size, padded, 2 * 4 * dec_rows, 2 * items, 1, chunk_of(size)),
            *product_scratch(size, padded, 2 * total, items, 1, chunk_of(size)),
            pltpu.SemaphoreType.DMA((copies,)), pltpu.SemaphoreType.DMA((copies,)),
            pltpu.SemaphoreType.DMA((2 + 8 + 5 + 3 + 3 + 8,)), pltpu.SemaphoreType.DMA((3,)),
        ],
        compiler_params=pltpu.CompilerParams(
            collective_id=2, has_side_effects=True, vmem_limit_bytes=62 * 1024 * 1024
        ),
        name="last_chain",
    )(*near, *streamed)
class Spread:
    def __init__(self, peers, partners, total, recv):
        self.peers, self.partners, self.total, self.recv = peers, partners, total, recv
        self.steps = len(partners) + 1

    def run(self, step):
        if step:
            self.copy.wait_recv()
            self.total[step] = self.total[step - 1] + self.recv[step - 1]
        if step < len(self.partners):
            self.copy = self.peers.send(
                self.total.at[step], self.recv.at[step], self.partners[step]
            )


def kd_kernel(
    small,
    chosen_h1, enc_gg_all, x_enc_gg_all, enc_gu_all, x_enc_gu_all,
    left_cross_all, right_cross_all, left_self_all, h0, enc_ay,
    enc_gq, enc_gk, enc_gv, enc_o, self_gq, self_gk, self_gv, self_o, dec_gate,
    dec_up,
    ffin, attn, small_out,
    enc_ffin, enc_gg, x_enc_gg, enc_gu, x_enc_gu, chosen_attn, left_enc, left_cross,
    left_self, right_enc, right_cross, right_self, attn_total, small_total, small_recv,
    *rest,
    layout, steps,
):
    size, block, padded = layout
    scratch, rest = rest[: 2 * steps], rest[2 * steps :]
    at_send, at_recv = rest[:steps], rest[steps : 2 * steps]
    send_sem, recv_sem, load_sem, own_sem = rest[2 * steps :]
    peers = Peers(send_sem, recv_sem)
    loads = Loads(load_sem)
    get_gate = [
        loads.start(chosen_h1, scratch[0]), loads.start(enc_gg_all, enc_gg),
        loads.start(x_enc_gg_all, x_enc_gg),
    ]
    get_cross = [
        loads.start(left_cross_all, left_cross), loads.start(right_cross_all, right_cross),
    ]
    get_up = [loads.start(enc_gu_all, enc_gu), loads.start(x_enc_gu_all, x_enc_gu)]
    get_self = [loads.start(left_self_all, left_self)]
    passed = [
        loads.start(dec_gate, ffin.at[1, pl.ds(0, 1)]), loads.start(dec_up, ffin.at[1, pl.ds(1, 1)])
    ]
    partners = [peers.across(place) for place in range(steps)]
    peers.greet([peers.diag] + partners)
    dec_rows, enc_rows = self_gq.shape[0], enc_gq.shape[0]
    own_self = to_owners(
        peers, (self_gq, self_gk, self_gv, self_o), right_self, (dec_rows,) * 4, own_sem.at[0]
    )
    own_enc = to_owners(
        peers, (enc_gq, enc_gk, enc_gv, enc_o), right_enc, (enc_rows,) * 4, own_sem.at[1]
    )
    own_left = to_owners(peers, (h0, h0, h0, enc_ay), left_enc, (enc_rows,) * 4, own_sem.at[3])
    spread = Spread(peers, [peers.sib, peers.far] + partners, small_total, small_recv)
    small_total[0] = small[...]
    spread.run(0)

    products = Products(peers, layout, 1, steps, *scratch)
    products.add(
        None, [(enc_gg, x_enc_gg), (enc_gu, x_enc_gu)], enc_ffin,
        ready=(lambda: wait_all(get_gate), lambda: wait_all(get_up)),
    )

    def wait_self():
        wait_all(get_self)
        owners_done(peers, own_self)

    def wait_enc():
        owners_done(peers, own_enc)
        owners_done(peers, own_left)

    kinds = (
        (2, left_cross, right_cross, lambda: wait_all(get_cross)),
        (1, left_self, right_self, wait_self), (0, left_enc, right_enc, wait_enc),
    )
    attn_items, gathers = [], []
    for a, left, right, arrived in kinds:
        rows = left.shape[0] * left.shape[1]

        def before(left=left, right=right, arrived=arrived):
            arrived()
            if block % 8:
                choose_rows(peers, layout, 0, flat(left[...]), chosen_attn, 0)
                return
            for low, high in tiles(INNER, chunk_of(size)):
                chosen_attn[:, low:high] = dot_first(flat(left[...]), flat(right[:, :, low:high]))

        for place, (low, high) in enumerate(tiles(INNER, chunk_of(size))):

            def product(half, right=right, rows=rows, low=low, high=high):
                if block % 8:
                    return dot(chosen_attn[half, :, :rows], flat(right[:, :, low:high]))
                parts = []
                for place in range(size // 2):
                    owner = half
                    for bit in range(1, steps):
                        owner = owner + (((place >> (steps - 1 - bit)) & 1) << bit)
                    start = pl.multiple_of(owner * block, 8)
                    parts.append(chosen_attn[pl.ds(start, block), low:high])
                    if padded > block:
                        parts.append(jnp.zeros((padded - block, high - low), F32))
                return jnp.concatenate(parts, axis=0)

            def finish(value, a=a, low=low, high=high, last=high == INNER):
                attn[a, peers.own, :, low:high] = to_low(value)
                if last:
                    gathers.append((a, Gather(peers, attn.at[a], False)))
                    gathers[-1][1].start()

            slot = len(attn_items)
            item = Reduce(
                peers, list(range(steps)), product, high - low, attn_total.at[slot], at_send,
                at_recv, slot, finish, products.ships,
            )
            item.before = [before] if place == 0 else []
            attn_items.append(item)

    items = []
    for place in range(max(len(products.items), len(attn_items) + 2)):
        if 2 <= place < len(attn_items) + 2:
            items.append(attn_items[place - 2])
        if place < len(products.items):
            items.append(products.items[place])
    stream = Stream(items, lag_of(steps))
    spreading = []

    def settle(relay, write):
        for entry in spreading:
            a, gather, begun, relayed = entry
            if not relayed and stream.now - begun >= relay:
                gather.wait_near()
                gather.relay()
                entry[3] = True
        for entry in list(spreading):
            a, gather, begun, relayed = entry
            if relayed and stream.now - begun >= write:
                gather.wait_far()
                spreading.remove(entry)

    while stream.now <= stream.last:
        stream.pump()
        spreading += [[a, gather, stream.now, False] for a, gather in gathers]
        gathers.clear()
        settle(1, 2)
        if stream.now < 2 * spread.steps:
            if stream.now % 2 == 0:
                spread.run(stream.now // 2)
    for step in range(1, spread.steps):
        if 2 * step > stream.last + 1:
            spread.run(step)
    small_out[...] = small_total[spread.steps - 1]
    left = pltpu.make_async_copy(enc_ffin, ffin.at[0], own_sem.at[2])
    left.start()
    settle(0, 0)
    settle(0, 0)
    left.wait()
    wait_all(passed)
    peers.finish()


def kd_call(size, block, padded, width, small, streamed):
    gate, self_q = streamed[1], streamed[14]
    units, enc_rows, dec_rows = gate.shape[2], gate.shape[1], self_q.shape[0]
    steps = size.bit_length() - 1
    shape = jax.ShapeDtypeStruct
    outs = [
        shape((2, 2, block, units), F32), shape((3, 4, padded, INNER), LOW),
        shape(small.shape, F32),
    ]
    vmem = pl.BlockSpec(memory_space=pltpu.VMEM)
    hbm = pl.BlockSpec(memory_space=pltpu.HBM)
    half = size * padded // 2
    ff_items = 2 * len(tiles(units, chunk_of(size)))
    at_items = 3 * len(tiles(INNER, chunk_of(size)))
    at_heights = [half >> step for step in range(steps)]

    def bufs(items, heights):
        return [pltpu.VMEM((items, height, chunk_of(size)), LOW) for height in heights]

    copies = ff_items * (steps - 1) + at_items * steps + 3 * 3 + (2 + steps) + 9
    return pl.pallas_call(
        functools.partial(kd_kernel, layout=(size, block, padded), steps=steps),
        out_shape=outs,
        in_specs=[vmem] + [hbm] * len(streamed),
        out_specs=[hbm] + [vmem] * 2,
        scratch_shapes=[
            pltpu.VMEM((2, block, units), F32),
            *[pltpu.VMEM(gate.shape, LOW)] * 4,
            pltpu.VMEM((2, half, 4 * enc_rows), LOW) if block % 8 else pltpu.VMEM((width, INNER), F32),
            pltpu.VMEM((4, enc_rows, width), LOW), pltpu.VMEM((4, enc_rows, width), LOW),
            pltpu.VMEM((4, dec_rows, width), LOW),
            pltpu.VMEM((4, enc_rows, INNER), LOW), pltpu.VMEM((4, enc_rows, INNER), LOW),
            pltpu.VMEM((4, dec_rows, INNER), LOW),
            pltpu.VMEM((at_items, half, chunk_of(size)), F32),
            pltpu.VMEM((3 + steps,) + small.shape, F32),
            pltpu.VMEM((2 + steps,) + small.shape, F32),
            *product_scratch(size, padded, 8 * enc_rows, ff_items, 1, chunk_of(size)),
            *bufs(2, at_heights), *bufs(at_items, at_heights),
            pltpu.SemaphoreType.DMA((copies,)), pltpu.SemaphoreType.DMA((copies,)),
            pltpu.SemaphoreType.DMA((10,)), pltpu.SemaphoreType.DMA((4,)),
        ],
        compiler_params=pltpu.CompilerParams(
            collective_id=3, has_side_effects=True, vmem_limit_bytes=62 * 1024 * 1024
        ),
        name="weight_sums",
    )(small, *streamed)


def out_kernel(
    ffin, ffout, enc_grad_all, attn, dec_grad, sums, decoded,
    qk_out, vo_out, ffin_out, ffout_out, enc_out_all, dec_out, gains_out, decoded_out,
    enc_grad, enc_out, qk, vo, *rest,
):
    held, sems = rest[:-1], rest[-1]
    block = qk.shape[1]
    loads = Loads(sems)
    get_enc = loads.start(enc_grad_all, enc_grad)
    pieces = []
    for source, buf, target in zip((ffin, ffout), held, (ffin_out, ffout_out)):
        for place in range(source.shape[0]):
            pieces.append(
                (loads.start(source.at[place], buf.at[place]), buf.at[place], target.at[place])
            )
    leaving = []
    for buf, target, first in ((qk, qk_out, 0), (vo, vo_out, 2)):
        for a in range(3):
            for place in range(2):
                lanes = slice(place * INNER, (place + 1) * INNER)
                buf[a, :, lanes] = attn[a, first + place, :, :].astype(F32)[:block]
            leaving.append(loads.start(buf.at[a], target.at[a]))
    get_enc.wait()
    enc_out[...] = enc_grad[...].T
    leaving.append(loads.start(enc_out, enc_out_all))
    for copy, buf, target in pieces:
        copy.wait()
        leaving.append(loads.start(buf, target))
    dec_out[...] = dec_grad[: dec_out.shape[0]]
    gains_out[...] = sums[: gains_out.shape[0]]
    decoded_out[...] = to_low(decoded[...].astype(F32)[: decoded_out.shape[0]])
    wait_all(leaving)


def out_call(block, attn, ffin, ffout, enc_grad, dec_grad, sums, decoded, dec_rows, gain_rows):
    shape = jax.ShapeDtypeStruct
    large = (ffin, ffout)
    joined = (3, block, 2 * INNER)
    width = sums.shape[1]
    vmem = pl.BlockSpec(memory_space=pltpu.VMEM)
    hbm = pl.BlockSpec(memory_space=pltpu.HBM)
    return pl.pallas_call(
        out_kernel,
        out_shape=[
            shape(joined, F32), shape(joined, F32),
            *[shape(value.shape, F32) for value in large],
            shape(enc_grad.shape[::-1], F32), shape((dec_rows, width), F32),
            shape((gain_rows, width), F32), shape((dec_rows, width), LOW),
        ],
        in_specs=[hbm] * 3 + [vmem] * 4,
        out_specs=[hbm] * 5 + [vmem] * 3,
        scratch_shapes=[
            pltpu.VMEM(enc_grad.shape, F32), pltpu.VMEM(enc_grad.shape[::-1], F32),
            pltpu.VMEM(joined, F32), pltpu.VMEM(joined, F32),
            *[pltpu.VMEM(value.shape, F32) for value in large],
            pltpu.SemaphoreType.DMA((2 + 6 + 2 * sum(value.shape[0] for value in large),)),
        ],
        compiler_params=pltpu.CompilerParams(vmem_limit_bytes=VMEM_BYTES),
        name="results",
    )(ffin, ffout, enc_grad, attn, dec_grad, sums, decoded)


def on_device(
    enc_x, dec_x, dec_cot, item_count, enc_mask, dec_mask, enc_buckets, dec_buckets,
    gains, tables, attn_qk, attn_vo, ff_in, ff_out,
):
    tensor_id = lax.axis_index("tensor")
    size = lax.axis_size("dp")
    enc_own, dec_own = enc_x.shape[0], dec_x.shape[0]
    width = enc_x.shape[1]
    block = width // size
    padded = (block + 15) // 16 * 16
    small, (enc_spots, self_bucket) = prepare(
        item_count, enc_mask, dec_mask, enc_buckets, dec_buckets, tables, enc_own, dec_own
    )
    ff_out_t = jnp.swapaxes(ff_out, 1, 2)
    (
        h0, enc_q, enc_kv, enc_p, enc_o, enc_mid, h1, enc_gelu, enc_slope, enc_hidden, enc_end,
        memory, cross_kv, hs, self_q, self_kv, self_p, self_o, dec_one, hc, cross_q, cross_p,
        cross_o, dec_two, hf, dec_gy, dec_gg, dec_gu, dec_hidden, dec_x, dec_cot,
        x_h1_rows, x_enc_hidden,
    ) = ka_call(enc_x, dec_x, dec_cot, gains, *small, attn_qk, attn_vo, ff_in, ff_out_t)
    (
        dec_out, cross_gy, cross_gq, cross_gk, cross_gv, dec_one_grad, enc_end_grad, enc_gy,
        enc_gg, enc_gu, gains_mid, dec_gate, x_dec_hidden, x_dec_gy, x_dec_gu, x_hf,
    ) = kb_call(
        dec_gg, dec_gu, dec_hidden, dec_cot, dec_two, dec_one, gains, cross_q, cross_kv, cross_p,
        enc_end, enc_gelu, enc_slope, attn_qk, attn_vo, ff_in, ff_out_t, hf, dec_gy,
        size, block, padded,
    )
    (
        enc_grad, enc_ay, enc_gq, enc_gk, enc_gv, dec_grad, self_gy, self_gq, self_gk, self_gv,
        sums, ffout_sum, dec_up, chosen_h1, left_cross, right_cross, left_self, x_enc_gg,
        x_enc_gu, unused,
    ) = kc_call(
        size, block, padded,
        [
            enc_gg, enc_gu, gains, gains_mid, enc_q, dec_one_grad, dec_x, self_q, self_kv, self_p,
            enc_spots, self_bucket,
        ],
        [
            attn_qk, attn_vo, ff_in, enc_end_grad, enc_mid, enc_x, enc_kv, enc_p, enc_gy, hf, x_hf,
            dec_gu, x_dec_gu, dec_gy, x_dec_gy, dec_hidden, x_dec_hidden, enc_hidden, x_enc_hidden, h1, x_h1_rows, hs, hc, memory, cross_gy, cross_gq,
            cross_gk, cross_gv, cross_o,
        ],
    )
    ffin_sum, attn, sums = kd_call(
        size, block, padded, width, sums,
        [
            chosen_h1, enc_gg, x_enc_gg, enc_gu, x_enc_gu, left_cross, right_cross,
            left_self, h0, enc_ay, enc_gq, enc_gk, enc_gv, enc_o, self_gq, self_gk, self_gv, self_o,
            dec_gate, dec_up,
        ],
    )
    qk_sum, vo_sum, ffin_sum, ffout_sum, enc_grad, dec_grad, gains_sum, dec_out = out_call(
        block, attn, ffin_sum, ffout_sum, enc_grad, dec_grad, sums, dec_out, dec_own,
        gains.shape[0],
    )
    ffout_sum = jnp.swapaxes(ffout_sum, 1, 2)
    table_rows = sums[8 : 8 + HEADS]
    tables_sum = jnp.stack(
        [table_rows[:, :BUCKETS].T, table_rows[:, PAIR : PAIR + BUCKETS].T]
    )
    return (
        dec_out, enc_grad.T, dec_grad, gains_sum, tables_sum, qk_sum, vo_sum, ffin_sum,
        ffout_sum,
    )


def solution(mesh):
    rows = P(("dp", "tensor"), None)
    return jax.shard_map(
        on_device,
        mesh=mesh,
        in_specs=(
            rows, rows, rows, P("dp"), P("dp"), P("dp"), P(), P(), P(), P(), P(), P(),
            P(None, None, None, "tensor"), P(None, "tensor", None),
        ),
        out_specs=(
            rows, rows, rows, P(), P(), P(None, "dp", None), P(None, "dp", None),
            P(None, None, "dp", "tensor"), P(None, "tensor", "dp"),
        ),
        check_vma=False,
    )
```
